32 devices in a mesh: replica: 8 (over z, core), fsdp: 4 (over y, x).
Axes of the slice: x: 2, y: 2, z: 4, core: 2. Of those that a mesh axis runs over, the one named last changes fastest.
Arguments:
- hidden_in: bfloat16 [8192, 1152], P(('replica', 'fsdp')), may hold values from -6 to 6
- out_grad: bfloat16 [8192, 1152], P(('replica', 'fsdp')), may hold values from -6 to 6
- segments: int32 [8192], P('replica'), may hold values from 0 to 3, as said below
- positions: int32 [8192], P(('replica', 'fsdp')), may hold values from 0 to 8191, as said below
- norm_in: bfloat16 [1152], P('fsdp'), may hold values from 0.25 to 1.75
- query_weight: bfloat16 [1152, 1024], P('fsdp'), may hold values from -0.1875 to 0.1875
- key_weight: bfloat16 [1152, 256], P('fsdp'), may hold values from -0.1875 to 0.1875
- value_weight: bfloat16 [1152, 256], P('fsdp'), may hold values from -0.1875 to 0.1875
- out_weight: bfloat16 [1152, 1024], P('fsdp'), may hold values from -0.1875 to 0.1875
- norm_attn: bfloat16 [1152], P('fsdp'), may hold values from 0.25 to 1.75
- norm_ffn: bfloat16 [1152], P('fsdp'), may hold values from 0.25 to 1.75
- gate_weight: bfloat16 [6912, 1152], P('fsdp'), may hold values from -0.1875 to 0.1875
- up_weight: bfloat16 [6912, 1152], P('fsdp'), may hold values from -0.1875 to 0.1875
- down_weight: bfloat16 [6912, 1152], P('fsdp'), may hold values from -0.078125 to 0.078125
- norm_out: bfloat16 [1152], P('fsdp'), may hold values from 0.25 to 1.75
- query_gain: bfloat16 [256], P('fsdp'), may hold values from 0.25 to 1.75
- key_gain: bfloat16 [256], P('fsdp'), may hold values from 0.25 to 1.75
Outputs:
- hidden_out: bfloat16 [8192, 1152], P(('replica', 'fsdp'))
- grad_in: float32 [8192, 1152], P(('replica', 'fsdp'))
- grad_norm_in: float32 [1152], P('fsdp')
- grad_query_weight: float32 [1152, 1024], P('fsdp')
- grad_key_weight: float32 [1152, 256], P('fsdp')
- grad_value_weight: float32 [1152, 256], P('fsdp')
- grad_out_weight: float32 [1152, 1024], P('fsdp')
- grad_norm_attn: float32 [1152], P('fsdp')
- grad_norm_ffn: float32 [1152], P('fsdp')
- grad_gate_weight: float32 [6912, 1152], P('fsdp')
- grad_up_weight: float32 [6912, 1152], P('fsdp')
- grad_down_weight: float32 [6912, 1152], P('fsdp')
- grad_norm_out: float32 [1152], P('fsdp')
- grad_query_gain: float32 [256], P('fsdp')
- grad_key_gain: float32 [256], P('fsdp')
The draws below stay inside these ranges and needn't reach their ends.
Inputs may be any that keep to these rules, and one draw needn't show every extreme that they name: `segments`: within each sequence of 1024 tokens the numbers never fall; every sequence begins in document 0 and ends in document 3. `positions`: within a document the position rises by one from token to token; document 0 of every sequence starts at 0 and the last document of every sequence ends at 8191.
All inputs are finite; a program needn't handle non-finite values.
Results may differ from the reference program's by a relative error of at most 0.025.
Values may be sent and summed in bfloat16 or wider, within the bound.
No kernel may reach another device: no remote copies, remote signals or barrier semaphores. Data moves between devices by JAX's collectives and lax.ppermute only.
A program may use at most 192 MiB of HBM per device.

```python
import jax
import jax.numpy as jnp
from jax import lax

D = 1152
FF = 6912
HQ = 4
HD = 256
WINDOW = 512
LENGTH = 1024
SEQS = 8
TOKENS = 8192


def layout(key):
    cuts = jax.random.randint(key, (SEQS, 3), 1, LENGTH)
    index = jnp.arange(LENGTH, dtype=jnp.int32)
    after = cuts[:, None, :] <= index[None, :, None]
    document = jnp.sum(after.astype(jnp.int32), axis=-1)
    begin = jnp.max(jnp.where(after, cuts[:, None, :], 0), axis=-1)
    return (cuts, index, document, begin)


def draw_segments(key, part):
    cuts, index, document, begin = layout(key)
    return document.reshape(TOKENS).astype(jnp.int32)


def draw_positions(key, part):
    cuts, index, document, begin = layout(key)
    key = jax.random.fold_in(key, 23)
    offsets = jax.random.randint(key, (SEQS, 4), 0, 8193 - LENGTH)
    last_begin = jnp.max(cuts, axis=1)
    offsets = offsets.at[:, 0].set(0)
    offsets = offsets.at[:, 3].set(8191 - (LENGTH - 1) + last_begin)
    chosen = jnp.take_along_axis(offsets, document, axis=1)
    return (index[None, :] - begin + chosen).reshape(TOKENS).astype(jnp.int32)


def block_levels(own_key, shape, split, low, largest):
    level, own = 1.0, jax.random.fold_in(own_key, 6)
    for dim, shards_of in split:
        heights = jnp.exp(jax.random.uniform(jax.random.fold_in(own, dim), (shards_of,), jnp.float32, low / len(split), largest / len(split)))
        level = level * jnp.repeat(heights, shape[dim] // shards_of).reshape([-1 if axis == dim else 1 for axis in range(len(shape))])
    return level


def scatter_about(key, dims, width, most, shards=(), kind=jnp.bfloat16):
    values = width * jax.random.normal(key, dims, jnp.float32)
    if shards:
        values = values * block_levels(key, dims, shards, -0.22, 0.18)
    return jnp.clip(values, -most, most).astype(kind)


def setup_inputs(seed: int = 0) -> dict:
    streams_of = jax.random.split(jax.random.key(seed), 18)
    return {
        "hidden_in": scatter_about(streams_of[0], (TOKENS, D), 1.0, 6.0, ((0, 32),)),
        "out_grad": scatter_about(streams_of[1], (TOKENS, D), 1.0, 6.0, ((0, 32),)),
        "segments": draw_segments(jax.random.fold_in(streams_of[17], 71), 0),
        "positions": draw_positions(jax.random.fold_in(streams_of[17], 71), 0),
        "norm_in": jnp.clip(1.0 + 0.15 * jax.random.normal(streams_of[4], (D,), jnp.float32), 0.25, 1.75).astype(jnp.bfloat16),
        "query_weight": scatter_about(streams_of[5], (D, HQ * HD), D ** -0.5, 0.1875, ((0, 4),)),
        "key_weight": scatter_about(streams_of[6], (D, HD), D ** -0.5, 0.1875, ((0, 4),)),
        "value_weight": scatter_about(streams_of[7], (D, HD), D ** -0.5, 0.1875, ((0, 4),)),
        "out_weight": scatter_about(streams_of[8], (D, HQ * HD), (HQ * HD) ** -0.5, 0.1875, ((0, 4),)),
        "norm_attn": jnp.clip(1.0 + 0.15 * jax.random.normal(streams_of[9], (D,), jnp.float32), 0.25, 1.75).astype(jnp.bfloat16),
        "norm_ffn": jnp.clip(1.0 + 0.15 * jax.random.normal(streams_of[10], (D,), jnp.float32), 0.25, 1.75).astype(jnp.bfloat16),
        "gate_weight": scatter_about(streams_of[11], (FF, D), D ** -0.5, 0.1875, ((0, 4),)),
        "up_weight": scatter_about(streams_of[12], (FF, D), D ** -0.5, 0.1875, ((0, 4),)),
        "down_weight": scatter_about(streams_of[13], (FF, D), FF ** -0.5, 0.078125, ((0, 4),)),
        "norm_out": jnp.clip(1.0 + 0.15 * jax.random.normal(streams_of[14], (D,), jnp.float32), 0.25, 1.75).astype(jnp.bfloat16),
        "query_gain": jnp.clip(1.0 + 0.15 * jax.random.normal(streams_of[15], (HD,), jnp.float32), 0.25, 1.75).astype(jnp.bfloat16),
        "key_gain": jnp.clip(1.0 + 0.15 * jax.random.normal(streams_of[16], (HD,), jnp.float32), 0.25, 1.75).astype(jnp.bfloat16),
    }


EPS = 1e-06
NEG = -1e+30

@jax.custom_vjp
def low(v):
    return lax.optimization_barrier(v.astype(jnp.bfloat16)).astype(jnp.float32)

@jax.custom_vjp
def low_back(v):
    return v

def low_keep(v):
    return (low(v), None)

def low_pass(kept, grad):
    return (grad,)

def back_keep(v):
    return (v, None)

def back_low(kept, grad):
    return (low(grad),)
low.defvjp(low_keep, low_pass)
low_back.defvjp(back_keep, back_low)

def product(left, right):
    return jnp.dot(left, right, precision=lax.Precision.HIGHEST)

def normed(value, gain):
    return value * lax.rsqrt(lax.optimization_barrier(jnp.mean(value * value, axis=-1, keepdims=True)) + EPS) * gain

def tables(places):
    half = HD // 2
    freq = 10000.0 ** (-(2.0 * jnp.arange(half, dtype=jnp.float32)) / HD)
    angle = places.astype(jnp.float32)[:, None] * freq[None, :]
    return (jnp.cos(angle), jnp.sin(angle))

def rotate(value, cosine, sine):
    half = value.shape[-1] // 2
    first = value[..., :half]
    second = value[..., half:]
    return jnp.concatenate([first * cosine - second * sine, second * cosine + first * sine], axis=-1)

def attend(query, key, value, seg):
    block = min(512, LENGTH)
    seg_int = seg.astype(jnp.int32)
    pad_keys = jnp.concatenate([jnp.zeros((WINDOW, HD), key.dtype), key], axis=0)
    pad_values = jnp.concatenate([jnp.zeros((WINDOW, HD), value.dtype), value], axis=0)
    pad_seg = jnp.concatenate([jnp.full((WINDOW,), -1, jnp.int32), seg_int], axis=0)

    def one_block(index):
        start = (index * block).astype(jnp.int32)
        rows_q = lax.dynamic_slice_in_dim(query, start, block, 0)
        keys_b = lax.dynamic_slice_in_dim(pad_keys, start, block + WINDOW, 0)
        values_b = lax.dynamic_slice_in_dim(pad_values, start, block + WINDOW, 0)
        seg_k = lax.dynamic_slice_in_dim(pad_seg, start, block + WINDOW, 0)
        seg_q = lax.dynamic_slice_in_dim(seg_int, start, block, 0)
        gap = WINDOW + jnp.arange(block)[:, None] - jnp.arange(block + WINDOW)[None, :]
        allowed = (gap >= 0) & (gap < WINDOW) & (seg_q[:, None] == seg_k[None, :])
        scores = jnp.einsum('qhd,kd->qhk', rows_q, keys_b, precision=lax.Precision.HIGHEST) * HD ** (-0.5)
        scores = low_back(scores)
        scores = jnp.where(allowed[:, None, :], scores, NEG)
        probs = low(jax.nn.softmax(scores, axis=-1))
        return jnp.einsum('qhk,kd->qhd', probs, values_b, precision=lax.Precision.HIGHEST)
    outs = lax.map(jax.checkpoint(one_block), jnp.arange(LENGTH // block, dtype=jnp.int32))
    return outs.reshape(LENGTH, HQ * HD)

def layer(x, weights, seg, places):
    gain_in, w_query, w_key, w_value, w_out, gain_attn, gain_ffn, w_gate, w_up, w_down, gain_out, gain_query, gain_key = weights
    normed_in = low(normed(x, gain_in))
    query_raw = low_back(product(normed_in, w_query)).reshape(LENGTH, HQ, HD)
    key_raw = low_back(product(normed_in, w_key))
    value_new = low(low_back(product(normed_in, w_value)))
    cosine, sine = tables(places)
    query_new = low(rotate(normed(query_raw, gain_query), cosine[:, None, :], sine[:, None, :]))
    key_new = low(rotate(normed(key_raw, gain_key), cosine, sine))
    mixed = low(low_back(attend(query_new, key_new, value_new, seg)))
    attended = low_back(product(mixed, w_out.T))
    resid = x + normed(attended, gain_attn)
    ffn_in = low(normed(resid, gain_ffn))
    gate = low_back(product(ffn_in, w_gate.T))
    upper = low_back(product(ffn_in, w_up.T))
    hidden = low(jax.nn.gelu(gate, approximate=True) * upper)
    branch = low_back(product(hidden, w_down))
    return resid + normed(branch, gain_out)

def reference(hidden_in, out_grad, segments, positions, norm_in, query_weight, key_weight, value_weight, out_weight, norm_attn, norm_ffn, gate_weight, up_weight, down_weight, norm_out, query_gain, key_gain):
    params = (norm_in.astype(jnp.float32), query_weight.astype(jnp.float32), key_weight.astype(jnp.float32), value_weight.astype(jnp.float32), out_weight.astype(jnp.float32), norm_attn.astype(jnp.float32), norm_ffn.astype(jnp.float32), gate_weight.astype(jnp.float32), up_weight.astype(jnp.float32), down_weight.astype(jnp.float32), norm_out.astype(jnp.float32), query_gain.astype(jnp.float32), key_gain.astype(jnp.float32))
    inputs = hidden_in.astype(jnp.float32).reshape(SEQS, LENGTH, D)
    cotangents = out_grad.astype(jnp.float32).reshape(SEQS, LENGTH, D)
    seg_all = segments.reshape(SEQS, LENGTH)
    place_all = positions.reshape(SEQS, LENGTH)

    def one_sequence(carry, item):
        x_seq, grad_seq, seg_seq, place_seq = item

        def layer_of(x_value, weights):
            return layer(x_value, weights, seg_seq, place_seq)
        result, pull = jax.vjp(layer_of, x_seq, params)
        grad_x, grad_weights = pull(grad_seq)
        carry = jax.tree.map(lambda left, right: left + right, carry, grad_weights)
        return (carry, (result, grad_x))
    start_sums = jax.tree.map(jnp.zeros_like, params)
    sums, (results, grads_x) = lax.scan(one_sequence, start_sums, (inputs, cotangents, seg_all, place_all))
    return (results.reshape(TOKENS, D).astype(jnp.bfloat16), grads_x.reshape(TOKENS, D), sums[0], sums[1], sums[2], sums[3], sums[4], sums[5], sums[6], sums[7], sums[8], sums[9], sums[10], sums[11], sums[12])
```

```python
import jax
import jax.numpy as jnp
from jax import lax
from jax.sharding import PartitionSpec as P

WINDOW = 512


EPS = 1e-06
NEG = -1e30


def swapped(block, axis, mask):
    route = [(i, i ^ mask) for i in range(lax.axis_size(axis))]
    return lax.ppermute(block, axis, route)


def added(left, right):
    total = left.astype(jnp.float32) + right.astype(jnp.float32)
    return lax.optimization_barrier(total.astype(jnp.bfloat16))


def along_line(block, pairs):
    route = [(2 * a + core, 2 * b + core) for a, b in pairs for core in range(2)]
    return lax.ppermute(block, "replica", route)


def line_sum(block):
    places = lax.axis_size("replica") // 2
    place = lax.axis_index("replica") // 2
    middle = places // 2
    for hop in range(middle - 1):
        block = added(block, along_line(block, [(hop, hop + 1), (places - 1 - hop, places - 2 - hop)]))
    block = added(block, along_line(block, [(middle - 1, middle), (middle, middle - 1)]))
    for hop in reversed(range(middle - 1)):
        far = along_line(block, [(hop + 1, hop), (places - 2 - hop, places - 1 - hop)])
        block = jnp.where((place == hop) | (place == places - 1 - hop), far, block)
    return block


def halves(block, axis):
    core = lax.axis_index("replica") % 2
    half = block.shape[axis] // 2
    mine = lax.dynamic_slice_in_dim(block, core * half, half, axis)
    other = lax.dynamic_slice_in_dim(block, (1 - core) * half, half, axis)
    return mine, other


def joined(mine, other, axis):
    core = lax.axis_index("replica") % 2
    return jnp.where(
        core == 0,
        jnp.concatenate([mine, other], axis=axis),
        jnp.concatenate([other, mine], axis=axis),
    )


def core_sum(block, axis):
    mine, other = halves(block, axis)
    return added(mine, swapped(other, "replica", 1))


def core_join(block, axis):
    return joined(block, swapped(block, "replica", 1), axis)


def replica_sum(block):
    return core_join(line_sum(core_sum(block, 0)), 0).astype(jnp.float32)


def owner_sum(blocks):
    rank = lax.axis_index("fsdp")
    part = core_sum(blocks, 1)
    total = lax.dynamic_index_in_dim(part, rank, 0, keepdims=False).astype(jnp.float32)
    for mask in range(1, blocks.shape[0]):
        far = swapped(lax.dynamic_index_in_dim(part, rank ^ mask, 0, keepdims=False), "fsdp", mask)
        total = total + far.astype(jnp.float32)
    total = lax.optimization_barrier(total.astype(jnp.bfloat16))
    return core_join(line_sum(total), 0).astype(jnp.float32)


def in_order(blocks):
    rank = lax.axis_index("fsdp")
    stack = jnp.stack(blocks)
    return [lax.dynamic_index_in_dim(stack, rank ^ i, 0, keepdims=False) for i in range(len(blocks))]


def gathered_rows(own, extra=None):
    group = lax.axis_size("fsdp")
    half = own.shape[0] // 2
    block = halves(own, 0)[0]
    if extra is not None:
        block = jnp.concatenate([block, extra], axis=0)
    got = [swapped(block, "fsdp", mask) for mask in range(1, group)]
    mine = jnp.stack([part[:half] for part in got])
    whole = core_join(mine, 1)
    rows = jnp.concatenate(in_order([own] + list(whole)), axis=0)
    if extra is None:
        return rows
    return rows, in_order([extra] + [part[half:] for part in got])


def passed_along(block, axis, distance):
    devices = range(lax.axis_size(axis))
    route = [(i - distance, i) for i in devices if i - distance in devices]
    return lax.ppermute(block, axis, route)


def contract(left, right, left_dim, right_dim):
    return lax.dot_general(
        left, right, (((left_dim,), (right_dim,)), ((), ())), preferred_element_type=jnp.float32
    )


def normed(value, gain):
    return value * lax.rsqrt(jnp.mean(value * value, axis=-1, keepdims=True) + EPS) * gain


def norm_back(value, gain, grad):
    _, pull = jax.vjp(normed, value, gain)
    return pull(grad)


def tables(places, half):
    freq = 10000.0 ** (-(2.0 * jnp.arange(half, dtype=jnp.float32)) / (2 * half))
    angle = places.astype(jnp.float32)[:, None] * freq[None, :]
    return (jnp.cos(angle), jnp.sin(angle))


def rotate(value, cosine, sine):
    half = value.shape[-1] // 2
    first = value[..., :half]
    second = value[..., half:]
    return jnp.concatenate(
        [first * cosine - second * sine, second * cosine + first * sine], axis=-1
    )


def head_post(raw, gain, cosine, sine):
    return rotate(normed(raw, gain), cosine, sine)


def gated(gate, upper):
    return jax.nn.gelu(gate, approximate=True) * upper


def gated_back(gate, upper, grad):
    _, pull = jax.vjp(gated, gate, upper)
    grad_gate, grad_upper = pull(grad)
    return (grad_gate.astype(jnp.bfloat16), grad_upper.astype(jnp.bfloat16))


def per_device(
    hidden_in,
    out_grad,
    segments,
    positions,
    norm_in,
    query_weight,
    key_weight,
    value_weight,
    out_weight,
    norm_attn,
    norm_ffn,
    gate_weight,
    up_weight,
    down_weight,
    norm_out,
    query_gain,
    key_gain,
):
    rows = hidden_in.shape[0]
    rank = lax.axis_index("fsdp")
    group = lax.axis_size("fsdp")
    masks = range(1, group)
    head_size = key_weight.shape[1]
    heads = query_weight.shape[1] // head_size
    model = hidden_in.shape[1]
    own_model = norm_in.shape[0]
    own_head = query_gain.shape[0]
    hops = (WINDOW - 1) // rows + 1
    scale = head_size ** (-0.5)
    w_own = jnp.concatenate([query_weight, key_weight, value_weight], axis=1)
    wide = w_own.shape[1]
    sizes = [own_model] * 4 + [own_head] * 2
    gains = jnp.concatenate([norm_in, norm_attn, norm_ffn, norm_out, query_gain, key_gain])
    gains = jnp.pad(gains[None, :], ((0, 15), (0, wide - sum(sizes))))
    w_qkv, gain_rows = gathered_rows(w_own, gains)
    w_out = gathered_rows(out_weight)
    spots = [sum(sizes[:i]) for i in range(7)]
    gain_in, gain_attn, gain_ffn, gain_out, gain_query, gain_key = (
        jnp.concatenate([row[0, spots[i] : spots[i + 1]] for row in gain_rows]) for i in range(6)
    )
    residual_in = hidden_in.astype(jnp.float32)
    normed_in = normed(residual_in, gain_in).astype(jnp.bfloat16)
    qkv = jnp.dot(normed_in, w_qkv, preferred_element_type=jnp.float32)
    query_raw = qkv[:, : heads * head_size].reshape(rows, heads, head_size)
    key_raw = qkv[:, heads * head_size : (heads + 1) * head_size]
    value_new = qkv[:, (heads + 1) * head_size :].astype(jnp.bfloat16)
    cosine, sine = tables(positions, head_size // 2)
    cosine_heads = cosine[:, None, :]
    sine_heads = sine[:, None, :]
    query_new = head_post(query_raw, gain_query, cosine_heads, sine_heads).astype(jnp.bfloat16)
    key_new = head_post(key_raw, gain_key, cosine, sine).astype(jnp.bfloat16)
    pair_new = jnp.concatenate([key_new, value_new], axis=1)
    parts = [pair_new]
    for step in range(1, hops + 1):
        parts.insert(0, passed_along(pair_new, "fsdp", step))
    pairs = jnp.concatenate(parts, axis=0)
    keys = pairs[:, :head_size]
    values = pairs[:, head_size:]
    width = keys.shape[0]
    seg_padded = jnp.concatenate([jnp.full((hops * rows,), -1, jnp.int32), segments], axis=0)
    key_segs = lax.dynamic_slice_in_dim(seg_padded, rank * rows, width, 0)
    query_segs = lax.dynamic_slice_in_dim(segments, rank * rows, rows, 0)
    gap = hops * rows + jnp.arange(rows)[:, None] - jnp.arange(width)[None, :]
    allowed = (gap >= 0) & (gap < WINDOW) & (query_segs[:, None] == key_segs[None, :])
    query_rows = query_new.reshape(rows * heads, head_size)

    def scores_of():
        raw_scores = (contract(query_rows, keys, 1, 1) * scale).reshape(rows, heads, width)
        return jnp.where(allowed[:, None, :], raw_scores, NEG)

    scores = scores_of()
    highest = jnp.max(scores, axis=-1, keepdims=True)
    expo = jnp.exp(scores - highest)
    weight_sum = jnp.sum(expo, axis=-1, keepdims=True)
    probs = expo / weight_sum
    log_total = highest + jnp.log(weight_sum)
    probs_low = probs.astype(jnp.bfloat16).reshape(rows * heads, width)
    mixed = (
        jnp.dot(probs_low, values, preferred_element_type=jnp.float32)
        .reshape(rows, heads * head_size)
        .astype(jnp.bfloat16)
    )
    attended = contract(mixed, w_out, 1, 1)
    resid = residual_in + normed(attended, gain_attn)
    ffn_in = normed(resid, gain_ffn).astype(jnp.bfloat16)
    ffn_blocks = [ffn_in] + [swapped(ffn_in, "fsdp", mask) for mask in masks]
    gates, uppers, hiddens = [], [], []
    branch = None
    for mask in range(group):
        gate = contract(ffn_blocks[mask], gate_weight, 1, 1)
        upper = contract(ffn_blocks[mask], up_weight, 1, 1)
        hidden = gated(gate, upper).astype(jnp.bfloat16)
        part = jnp.dot(hidden, down_weight, preferred_element_type=jnp.float32).astype(jnp.bfloat16)
        part = swapped(part, "fsdp", mask) if mask else part
        branch = part.astype(jnp.float32) if mask == 0 else branch + part.astype(jnp.float32)
        gates.append(gate)
        uppers.append(upper)
        hiddens.append(hidden)
    result = resid + normed(branch, gain_out)
    hidden_out = result.astype(jnp.bfloat16)
    grad_result = out_grad.astype(jnp.float32)
    grad_branch, grad_gain_out = norm_back(branch, gain_out, grad_result)
    grad_branch_low = grad_branch.astype(jnp.bfloat16)
    pieces = [grad_branch_low] + [swapped(grad_branch_low, "fsdp", mask) for mask in masks]
    ffn_rows = jnp.concatenate(ffn_blocks, axis=0)
    grad_down = contract(jnp.concatenate(hiddens, axis=0), jnp.concatenate(pieces, axis=0), 0, 0)
    cut = grad_down.shape[0] // 2

    def cut_sum(grad):
        grad = grad.astype(jnp.bfloat16)
        return jnp.concatenate([replica_sum(grad[:cut]), replica_sum(grad[cut:])], axis=0)

    grad_down = cut_sum(grad_down)
    grad_gates, grad_uppers = [], []
    grad_ffn_in = None
    for mask in range(group):
        grad_hidden = contract(pieces[mask], down_weight, 1, 1)
        grad_gate, grad_upper = gated_back(gates[mask], uppers[mask], grad_hidden)
        part = (
            jnp.dot(grad_gate, gate_weight, preferred_element_type=jnp.float32)
            + jnp.dot(grad_upper, up_weight, preferred_element_type=jnp.float32)
        ).astype(jnp.bfloat16)
        part = swapped(part, "fsdp", mask) if mask else part
        grad_ffn_in = part.astype(jnp.float32) if mask == 0 else grad_ffn_in + part.astype(jnp.float32)
        grad_gates.append(grad_gate)
        grad_uppers.append(grad_upper)
    grad_gate_w = cut_sum(contract(jnp.concatenate(grad_gates, axis=0), ffn_rows, 0, 0))
    grad_up_w = cut_sum(contract(jnp.concatenate(grad_uppers, axis=0), ffn_rows, 0, 0))
    grad_resid_part, grad_gain_ffn = norm_back(resid, gain_ffn, grad_ffn_in)
    grad_resid = grad_result + grad_resid_part
    grad_attended, grad_gain_attn = norm_back(attended, gain_attn, grad_resid)
    grad_attended_low = grad_attended.astype(jnp.bfloat16)
    grad_wout = contract(grad_attended_low, mixed, 0, 0).astype(jnp.bfloat16)
    owned_out = owner_sum(grad_wout.reshape(group, own_model, -1))
    grad_mixed = jnp.dot(grad_attended_low, w_out, preferred_element_type=jnp.float32).astype(
        jnp.bfloat16
    )
    grad_mixed_rows = grad_mixed.reshape(rows * heads, head_size)
    scores = scores_of()
    probs = jnp.exp(scores - log_total)
    probs_low = probs.astype(jnp.bfloat16).reshape(rows * heads, width)
    grad_probs = contract(grad_mixed_rows, values, 1, 1).reshape(rows, heads, width)
    delta = jnp.sum(grad_probs * probs, axis=-1, keepdims=True)
    grad_scores = (probs * (grad_probs - delta)).astype(jnp.bfloat16).reshape(rows * heads, width)
    grad_query = (jnp.dot(grad_scores, keys, preferred_element_type=jnp.float32) * scale).reshape(
        rows, heads, head_size
    )
    grad_keys = contract(grad_scores, query_rows, 0, 0) * scale
    grad_values = contract(probs_low, grad_mixed_rows, 0, 0)
    grad_pairs = jnp.concatenate([grad_keys, grad_values], axis=1)
    grad_pair = grad_pairs[hops * rows :]
    for step in range(1, hops + 1):
        lower = (hops - step) * rows
        back = passed_along(grad_pairs[lower : lower + rows].astype(jnp.bfloat16), "fsdp", -step)
        grad_pair = grad_pair + back.astype(jnp.float32)
    grad_key = grad_pair[:, :head_size]
    grad_value = grad_pair[:, head_size:]
    _, pull_query = jax.vjp(
        lambda raw, gain: head_post(raw, gain, cosine_heads, sine_heads), query_raw, gain_query
    )
    grad_query_raw, grad_gain_query = pull_query(grad_query)
    _, pull_key = jax.vjp(lambda raw, gain: head_post(raw, gain, cosine, sine), key_raw, gain_key)
    grad_key_raw, grad_gain_key = pull_key(grad_key)
    grad_query_low = grad_query_raw.reshape(rows, heads * head_size).astype(jnp.bfloat16)
    grad_key_low = grad_key_raw.astype(jnp.bfloat16)
    grad_value_low = grad_value.astype(jnp.bfloat16)
    grad_qkv = jnp.concatenate([grad_query_low, grad_key_low, grad_value_low], axis=1)
    grad_wqkv = contract(normed_in, grad_qkv, 0, 0).astype(jnp.bfloat16)
    grad_normed_in = contract(grad_qkv, w_qkv, 1, 1)
    grad_input_part, grad_gain_in = norm_back(residual_in, gain_in, grad_normed_in)
    grad_in = grad_resid + grad_input_part
    gain_grads = jnp.concatenate(
        [
            grad.astype(jnp.bfloat16).reshape(group, -1)
            for grad in (
                grad_gain_in,
                grad_gain_attn,
                grad_gain_ffn,
                grad_gain_out,
                grad_gain_query,
                grad_gain_key,
            )
        ],
        axis=1,
    )
    gain_grads = jnp.pad(gain_grads[:, None, :], ((0, 0), (0, 31), (0, wide - sum(sizes))))
    owned = owner_sum(
        jnp.concatenate([grad_wqkv.reshape(group, own_model, wide), gain_grads], axis=1)
    )
    owned_query = owned[:own_model, : heads * head_size]
    owned_key = owned[:own_model, heads * head_size : (heads + 1) * head_size]
    owned_value = owned[:own_model, (heads + 1) * head_size :]
    owned_gain_in, owned_gain_attn, owned_gain_ffn, owned_gain_out, owned_gain_query, owned_gain_key = (
        owned[own_model, spots[i] : spots[i + 1]] for i in range(6)
    )
    return (
        hidden_out,
        grad_in,
        owned_gain_in,
        owned_query,
        owned_key,
        owned_value,
        owned_out,
        owned_gain_attn,
        owned_gain_ffn,
        grad_gate_w,
        grad_up_w,
        grad_down,
        owned_gain_out,
        owned_gain_query,
        owned_gain_key,
    )


def solution(mesh):
    return jax.shard_map(
        per_device,
        mesh=mesh,
        in_specs=(
            P(("replica", "fsdp"), None),
            P(("replica", "fsdp"), None),
            P("replica"),
            P(("replica", "fsdp")),
            P("fsdp"),
            P("fsdp", None),
            P("fsdp", None),
            P("fsdp", None),
            P("fsdp", None),
            P("fsdp"),
            P("fsdp"),
            P("fsdp", None),
            P("fsdp", None),
            P("fsdp", None),
            P("fsdp"),
            P("fsdp"),
            P("fsdp"),
        ),
        out_specs=(
            P(("replica", "fsdp"), None),
            P(("replica", "fsdp"), None),
            P("fsdp"),
            P("fsdp", None),
            P("fsdp", None),
            P("fsdp", None),
            P("fsdp", None),
            P("fsdp"),
            P("fsdp"),
            P("fsdp", None),
            P("fsdp", None),
            P("fsdp", None),
            P("fsdp"),
            P("fsdp"),
            P("fsdp"),
        ),
        check_vma=False,
    )
```

```python
import jax
import jax.numpy as jnp
from jax import lax
from jax.experimental import pallas as pl
from jax.sharding import PartitionSpec as P

WINDOW = 512


EPS = 1e-06
NEG = -1e30


def swapped(block, axis, mask):
    route = [(i, i ^ mask) for i in range(lax.axis_size(axis))]
    return lax.ppermute(block, axis, route)


def added(left, right):
    total = left.astype(jnp.float32) + right.astype(jnp.float32)
    return lax.optimization_barrier(total.astype(jnp.bfloat16))


def along_line(block, pairs):
    route = [(2 * a + core, 2 * b + core) for a, b in pairs for core in range(2)]
    return lax.ppermute(block, "replica", route)


def tied(arrays):
    place = pl.BlockSpec(memory_space=pl.ANY)
    return pl.pallas_call(
        lambda *refs: None,
        out_shape=[jax.ShapeDtypeStruct(array.shape, array.dtype) for array in arrays],
        in_specs=[place] * len(arrays),
        out_specs=[place] * len(arrays),
        input_output_aliases={i: i for i in range(len(arrays))},
        name="tie",
    )(*arrays)


def line_steps():
    places = lax.axis_size("replica") // 2
    middle = places // 2
    inward = [("add", [(hop, hop + 1), (places - 1 - hop, places - 2 - hop)]) for hop in range(middle - 1)]
    across = [("add", [(middle - 1, middle), (middle, middle - 1)])]
    outward = [
        ("take", [(hop + 1, hop), (places - 2 - hop, places - 1 - hop)])
        for hop in reversed(range(middle - 1))
    ]
    return inward + across + outward


def line_combine(step, block, far):
    kind, pairs = step
    if kind == "add":
        return added(block, far)
    place = lax.axis_index("replica") // 2
    ends = [b for _, b in pairs]
    return jnp.where((place == ends[0]) | (place == ends[1]), far, block)


class Line:
    def __init__(self):
        self.steps = line_steps()
        self.moving = []
        self.done = {}

    def advance(self, fresh, gate=None):
        arrays, state = [], []
        for name, block, far, step in self.moving:
            arrays.append(line_combine(self.steps[step], block, far))
            state.append((name, step + 1))
        for name, block in fresh:
            arrays.append(block)
            state.append((name, 0))
        if gate is not None:
            arrays.append(gate)
        arrays = tied(arrays)
        self.moving = []
        for (name, step), block in zip(state, arrays):
            if step == len(self.steps):
                self.done[name] = block
            else:
                self.moving.append((name, block, along_line(block, self.steps[step][1]), step))
        return arrays[-1]

    def finished(self, name):
        while name not in self.done:
            self.advance([])
        return self.done[name]


def halves(block, axis):
    core = lax.axis_index("replica") % 2
    half = block.shape[axis] // 2
    mine = lax.dynamic_slice_in_dim(block, core * half, half, axis)
    other = lax.dynamic_slice_in_dim(block, (1 - core) * half, half, axis)
    return mine, other


def joined(mine, other, axis):
    core = lax.axis_index("replica") % 2
    return jnp.where(
        core == 0,
        jnp.concatenate([mine, other], axis=axis),
        jnp.concatenate([other, mine], axis=axis),
    )


def core_sum(block, axis):
    mine, other = halves(block, axis)
    return added(mine, swapped(other, "replica", 1))


def core_join(block, axis):
    return joined(block, swapped(block, "replica", 1), axis)


def cut_sums(grad):
    grad = grad.reshape(2, grad.shape[0] // 2, grad.shape[1])
    mine, other = halves(grad, 1)
    far = swapped(other, "replica", 1)
    return added(mine[0], far[0]), added(mine[1], far[1])


def cut_join(first, second):
    mine = jnp.stack([first, second])
    whole = core_join(mine, 1).astype(jnp.float32)
    return whole.reshape(-1, whole.shape[2])


def owner_part(blocks):
    rank = lax.axis_index("fsdp")
    part = core_sum(blocks, 1)
    total = lax.dynamic_index_in_dim(part, rank, 0, keepdims=False).astype(jnp.float32)
    for mask in range(1, blocks.shape[0]):
        far = swapped(lax.dynamic_index_in_dim(part, rank ^ mask, 0, keepdims=False), "fsdp", mask)
        total = total + far.astype(jnp.float32)
    return lax.optimization_barrier(total.astype(jnp.bfloat16))


def in_order(blocks):
    rank = lax.axis_index("fsdp")
    stack = jnp.stack(blocks)
    return [lax.dynamic_index_in_dim(stack, rank ^ i, 0, keepdims=False) for i in range(len(blocks))]


def gathered_rows(own, extra=None):
    group = lax.axis_size("fsdp")
    half = own.shape[0] // 2
    block = halves(own, 0)[0]
    if extra is not None:
        block = jnp.concatenate([block, extra], axis=0)
    got = [swapped(block, "fsdp", mask) for mask in range(1, group)]
    mine = jnp.stack([part[:half] for part in got])
    whole = core_join(mine, 1)
    rows = jnp.concatenate(in_order([own] + list(whole)), axis=0)
    if extra is None:
        return rows
    return rows, in_order([extra] + [part[half:] for part in got])


def passed_along(block, axis, distance):
    devices = range(lax.axis_size(axis))
    route = [(i - distance, i) for i in devices if i - distance in devices]
    return lax.ppermute(block, axis, route)


def contract(left, right, left_dim, right_dim):
    return lax.dot_general(
        left, right, (((left_dim,), (right_dim,)), ((), ())), preferred_element_type=jnp.float32
    )


def normed(value, gain):
    return value * lax.rsqrt(jnp.mean(value * value, axis=-1, keepdims=True) + EPS) * gain


def norm_back(value, gain, grad):
    _, pull = jax.vjp(normed, value, gain)
    return pull(grad)


def tables(places, half):
    freq = 10000.0 ** (-(2.0 * jnp.arange(half, dtype=jnp.float32)) / (2 * half))
    angle = places.astype(jnp.float32)[:, None] * freq[None, :]
    return (jnp.cos(angle), jnp.sin(angle))


def rotate(value, cosine, sine):
    half = value.shape[-1] // 2
    first = value[..., :half]
    second = value[..., half:]
    return jnp.concatenate(
        [first * cosine - second * sine, second * cosine + first * sine], axis=-1
    )


def head_post(raw, gain, cosine, sine):
    return rotate(normed(raw, gain), cosine, sine)


def gated(gate, upper):
    return jax.nn.gelu(gate, approximate=True) * upper


def gated_back(gate, upper, grad):
    _, pull = jax.vjp(gated, gate, upper)
    grad_gate, grad_upper = pull(grad)
    return (grad_gate.astype(jnp.bfloat16), grad_upper.astype(jnp.bfloat16))


def per_device(
    hidden_in,
    out_grad,
    segments,
    positions,
    norm_in,
    query_weight,
    key_weight,
    value_weight,
    out_weight,
    norm_attn,
    norm_ffn,
    gate_weight,
    up_weight,
    down_weight,
    norm_out,
    query_gain,
    key_gain,
):
    rows = hidden_in.shape[0]
    rank = lax.axis_index("fsdp")
    group = lax.axis_size("fsdp")
    masks = range(1, group)
    head_size = key_weight.shape[1]
    heads = query_weight.shape[1] // head_size
    model = hidden_in.shape[1]
    own_model = norm_in.shape[0]
    own_head = query_gain.shape[0]
    hops = (WINDOW - 1) // rows + 1
    scale = head_size ** (-0.5)
    w_own = jnp.concatenate([query_weight, key_weight, value_weight], axis=1)
    wide = w_own.shape[1]
    sizes = [own_model] * 4 + [own_head] * 2
    gains = jnp.concatenate([norm_in, norm_attn, norm_ffn, norm_out, query_gain, key_gain])
    gains = jnp.pad(gains[None, :], ((0, 15), (0, wide - sum(sizes))))
    w_qkv, gain_rows = gathered_rows(w_own, gains)
    w_out = gathered_rows(out_weight)
    spots = [sum(sizes[:i]) for i in range(7)]
    gain_in, gain_attn, gain_ffn, gain_out, gain_query, gain_key = (
        jnp.concatenate([row[0, spots[i] : spots[i + 1]] for row in gain_rows]) for i in range(6)
    )
    residual_in = hidden_in.astype(jnp.float32)
    normed_in = normed(residual_in, gain_in).astype(jnp.bfloat16)
    qkv = jnp.dot(normed_in, w_qkv, preferred_element_type=jnp.float32)
    query_raw = qkv[:, : heads * head_size].reshape(rows, heads, head_size)
    key_raw = qkv[:, heads * head_size : (heads + 1) * head_size]
    value_new = qkv[:, (heads + 1) * head_size :].astype(jnp.bfloat16)
    cosine, sine = tables(positions, head_size // 2)
    cosine_heads = cosine[:, None, :]
    sine_heads = sine[:, None, :]
    query_new = head_post(query_raw, gain_query, cosine_heads, sine_heads).astype(jnp.bfloat16)
    key_new = head_post(key_raw, gain_key, cosine, sine).astype(jnp.bfloat16)
    pair_new = jnp.concatenate([key_new, value_new], axis=1)
    parts = [pair_new]
    for step in range(1, hops + 1):
        parts.insert(0, passed_along(pair_new, "fsdp", step))
    pairs = jnp.concatenate(parts, axis=0)
    keys = pairs[:, :head_size]
    values = pairs[:, head_size:]
    width = keys.shape[0]
    seg_padded = jnp.concatenate([jnp.full((hops * rows,), -1, jnp.int32), segments], axis=0)
    key_segs = lax.dynamic_slice_in_dim(seg_padded, rank * rows, width, 0)
    query_segs = lax.dynamic_slice_in_dim(segments, rank * rows, rows, 0)
    gap = hops * rows + jnp.arange(rows)[:, None] - jnp.arange(width)[None, :]
    allowed = (gap >= 0) & (gap < WINDOW) & (query_segs[:, None] == key_segs[None, :])
    query_rows = query_new.reshape(rows * heads, head_size)

    def scores_of():
        raw_scores = (contract(query_rows, keys, 1, 1) * scale).reshape(rows, heads, width)
        return jnp.where(allowed[:, None, :], raw_scores, NEG)

    scores = scores_of()
    highest = jnp.max(scores, axis=-1, keepdims=True)
    expo = jnp.exp(scores - highest)
    weight_sum = jnp.sum(expo, axis=-1, keepdims=True)
    probs = expo / weight_sum
    log_total = highest + jnp.log(weight_sum)
    probs_low = probs.astype(jnp.bfloat16).reshape(rows * heads, width)
    mixed = (
        jnp.dot(probs_low, values, preferred_element_type=jnp.float32)
        .reshape(rows, heads * head_size)
        .astype(jnp.bfloat16)
    )
    attended = contract(mixed, w_out, 1, 1)
    resid = residual_in + normed(attended, gain_attn)
    ffn_in = normed(resid, gain_ffn).astype(jnp.bfloat16)
    ffn_blocks = [ffn_in] + [swapped(ffn_in, "fsdp", mask) for mask in masks]
    gates, uppers, hiddens = [], [], []
    branch = None
    for mask in range(group):
        gate = contract(ffn_blocks[mask], gate_weight, 1, 1)
        upper = contract(ffn_blocks[mask], up_weight, 1, 1)
        hidden = gated(gate, upper).astype(jnp.bfloat16)
        part = jnp.dot(hidden, down_weight, preferred_element_type=jnp.float32).astype(jnp.bfloat16)
        part = swapped(part, "fsdp", mask) if mask else part
        branch = part.astype(jnp.float32) if mask == 0 else branch + part.astype(jnp.float32)
        gates.append(gate)
        uppers.append(upper)
        hiddens.append(hidden)
    result = resid + normed(branch, gain_out)
    hidden_out = result.astype(jnp.bfloat16)
    grad_result = out_grad.astype(jnp.float32)
    grad_branch, grad_gain_out = norm_back(branch, gain_out, grad_result)
    grad_branch_low = grad_branch.astype(jnp.bfloat16)
    pieces = [grad_branch_low] + [swapped(grad_branch_low, "fsdp", mask) for mask in masks]
    ffn_rows = jnp.concatenate(ffn_blocks, axis=0)
    grad_down = contract(jnp.concatenate(hiddens, axis=0), jnp.concatenate(pieces, axis=0), 0, 0)
    grad_down = grad_down.astype(jnp.bfloat16)
    line = Line()
    down_first, down_second = cut_sums(grad_down)
    grad_gates, grad_uppers = {}, {}
    order = list(masks) + [0]
    returned = []
    for mask in order:
        grad_hidden = contract(pieces[mask], down_weight, 1, 1)
        grad_gate, grad_upper = gated_back(gates[mask], uppers[mask], grad_hidden)
        part = (
            jnp.dot(grad_gate, gate_weight, preferred_element_type=jnp.float32)
            + jnp.dot(grad_upper, up_weight, preferred_element_type=jnp.float32)
        ).astype(jnp.bfloat16)
        returned.append(swapped(part, "fsdp", mask) if mask else part)
        grad_gates[mask] = grad_gate
        grad_uppers[mask] = grad_upper
        if mask == order[0]:
            pieces[order[1]] = line.advance([("down_first", down_first)], pieces[order[1]])
    grad_gates[0] = line.advance([("down_second", down_second)], grad_gates[0])
    grad_gate_w = contract(jnp.concatenate([grad_gates[i] for i in range(group)], axis=0), ffn_rows, 0, 0)
    grad_up_w = contract(jnp.concatenate([grad_uppers[i] for i in range(group)], axis=0), ffn_rows, 0, 0)
    gate_first, gate_second = cut_sums(grad_gate_w.astype(jnp.bfloat16))
    up_first, up_second = cut_sums(grad_up_w.astype(jnp.bfloat16))
    grad_ffn_in = sum(part.astype(jnp.float32) for part in returned)
    grad_resid_part, grad_gain_ffn = norm_back(resid, gain_ffn, grad_ffn_in)
    grad_resid = grad_result + grad_resid_part
    grad_attended, grad_gain_attn = norm_back(attended, gain_attn, grad_resid)
    grad_attended_low = grad_attended.astype(jnp.bfloat16)
    grad_attended_low = line.advance([("gate_first", gate_first)], grad_attended_low)
    grad_wout = contract(grad_attended_low, mixed, 0, 0).astype(jnp.bfloat16)
    out_part = owner_part(grad_wout.reshape(group, own_model, -1))
    grad_mixed = jnp.dot(grad_attended_low, w_out, preferred_element_type=jnp.float32).astype(
        jnp.bfloat16
    )
    grad_mixed_rows = grad_mixed.reshape(rows * heads, head_size)
    scores = scores_of()
    probs = jnp.exp(scores - log_total)
    probs_low = probs.astype(jnp.bfloat16).reshape(rows * heads, width)
    grad_probs = contract(grad_mixed_rows, values, 1, 1).reshape(rows, heads, width)
    delta = jnp.sum(grad_probs * probs, axis=-1, keepdims=True)
    grad_scores = (probs * (grad_probs - delta)).astype(jnp.bfloat16).reshape(rows * heads, width)
    grad_scores = line.advance([("gate_second", gate_second)], grad_scores)
    grad_query = (jnp.dot(grad_scores, keys, preferred_element_type=jnp.float32) * scale).reshape(
        rows, heads, head_size
    )
    grad_keys = contract(grad_scores, query_rows, 0, 0) * scale
    grad_values = contract(probs_low, grad_mixed_rows, 0, 0)
    grad_pairs = jnp.concatenate([grad_keys, grad_values], axis=1)
    grad_pair = grad_pairs[hops * rows :]
    for step in range(1, hops + 1):
        lower = (hops - step) * rows
        back = passed_along(grad_pairs[lower : lower + rows].astype(jnp.bfloat16), "fsdp", -step)
        grad_pair = grad_pair + back.astype(jnp.float32)
    grad_pair = line.advance([("up_first", up_first)], grad_pair)
    grad_key = grad_pair[:, :head_size]
    grad_value = grad_pair[:, head_size:]
    _, pull_query = jax.vjp(
        lambda raw, gain: head_post(raw, gain, cosine_heads, sine_heads), query_raw, gain_query
    )
    grad_query_raw, grad_gain_query = pull_query(grad_query)
    _, pull_key = jax.vjp(lambda raw, gain: head_post(raw, gain, cosine, sine), key_raw, gain_key)
    grad_key_raw, grad_gain_key = pull_key(grad_key)
    grad_query_low = grad_query_raw.reshape(rows, heads * head_size).astype(jnp.bfloat16)
    grad_key_low = grad_key_raw.astype(jnp.bfloat16)
    grad_value_low = grad_value.astype(jnp.bfloat16)
    grad_qkv = jnp.concatenate([grad_query_low, grad_key_low, grad_value_low], axis=1)
    grad_wqkv = contract(normed_in, grad_qkv, 0, 0).astype(jnp.bfloat16)
    grad_normed_in = contract(grad_qkv, w_qkv, 1, 1)
    grad_input_part, grad_gain_in = norm_back(residual_in, gain_in, grad_normed_in)
    grad_in = grad_resid + grad_input_part
    gain_grads = jnp.concatenate(
        [
            grad.astype(jnp.bfloat16).reshape(group, -1)
            for grad in (
                grad_gain_in,
                grad_gain_attn,
                grad_gain_ffn,
                grad_gain_out,
                grad_gain_query,
                grad_gain_key,
            )
        ],
        axis=1,
    )
    gain_grads = jnp.pad(gain_grads[:, None, :], ((0, 0), (0, 31), (0, wide - sum(sizes))))
    qkv_part = owner_part(
        jnp.concatenate([grad_wqkv.reshape(group, own_model, wide), gain_grads], axis=1)
    )
    line.advance([("up_second", up_second), ("out", out_part)])
    grad_down = cut_join(line.finished("down_first"), line.finished("down_second"))
    line.advance([("qkv", qkv_part)])
    grad_gate_w = cut_join(line.finished("gate_first"), line.finished("gate_second"))
    grad_up_w = cut_join(line.finished("up_first"), line.finished("up_second"))
    owned_out = core_join(line.finished("out"), 0).astype(jnp.float32)
    owned = core_join(line.finished("qkv"), 0).astype(jnp.float32)
    owned_query = owned[:own_model, : heads * head_size]
    owned_key = owned[:own_model, heads * head_size : (heads + 1) * head_size]
    owned_value = owned[:own_model, (heads + 1) * head_size :]
    owned_gain_in, owned_gain_attn, owned_gain_ffn, owned_gain_out, owned_gain_query, owned_gain_key = (
        owned[own_model, spots[i] : spots[i + 1]] for i in range(6)
    )
    return (
        hidden_out,
        grad_in,
        owned_gain_in,
        owned_query,
        owned_key,
        owned_value,
        owned_out,
        owned_gain_attn,
        owned_gain_ffn,
        grad_gate_w,
        grad_up_w,
        grad_down,
        owned_gain_out,
        owned_gain_query,
        owned_gain_key,
    )


def solution(mesh):
    return jax.shard_map(
        per_device,
        mesh=mesh,
        in_specs=(
            P(("replica", "fsdp"), None),
            P(("replica", "fsdp"), None),
            P("replica"),
            P(("replica", "fsdp")),
            P("fsdp"),
            P("fsdp", None),
            P("fsdp", None),
            P("fsdp", None),
            P("fsdp", None),
            P("fsdp"),
            P("fsdp"),
            P("fsdp", None),
            P("fsdp", None),
            P("fsdp", None),
            P("fsdp"),
            P("fsdp"),
            P("fsdp"),
        ),
        out_specs=(
            P(("replica", "fsdp"), None),
            P(("replica", "fsdp"), None),
            P("fsdp"),
            P("fsdp", None),
            P("fsdp", None),
            P("fsdp", None),
            P("fsdp", None),
            P("fsdp"),
            P("fsdp"),
            P("fsdp", None),
            P("fsdp", None),
            P("fsdp", None),
            P("fsdp"),
            P("fsdp"),
            P("fsdp"),
        ),
        check_vma=False,
    )
```

```python
import jax
import jax.numpy as jnp
from jax import lax
from jax.experimental import pallas as pl
from jax.experimental.pallas import tpu as pltpu
from jax.sharding import PartitionSpec as P

WINDOW = 512


EPS = 1e-06
NEG = -1e30


def swapped(block, axis, mask):
    route = [(i, i ^ mask) for i in range(lax.axis_size(axis))]
    return lax.ppermute(block, axis, route)


def added(left, right):
    total = left.astype(jnp.float32) + right.astype(jnp.float32)
    return lax.optimization_barrier(total.astype(jnp.bfloat16))


VMEM_LIMIT = 56 * 1024 * 1024


def params(*semantics):
    return pltpu.CompilerParams(vmem_limit_bytes=VMEM_LIMIT)


def dot(left, right, left_dim, right_dim):
    return lax.dot_general(
        left, right, (((left_dim,), (right_dim,)), ((), ())), preferred_element_type=jnp.float32
    )


def tile_of(size, most):
    return max(tile for tile in range(16, most + 1, 16) if size % tile == 0)


GELU_A = (2.0 / 3.141592653589793) ** 0.5
GELU_B = 0.044715


def ffn_forward_kernel(x_ref, gate_ref, up_ref, down_ref, hidden_ref, slope_ref, act_ref, out_ref, acc):
    step = pl.program_id(0)
    x = x_ref[...]
    gate = dot(gate_ref[...], x, 1, 1)
    upper = dot(up_ref[...], x, 1, 1)
    square = gate * gate
    bend = jnp.tanh(GELU_A * gate * (1.0 + GELU_B * square))
    half = 0.5 + 0.5 * bend
    act = gate * half
    slope = half + 0.5 * gate * (1.0 - bend * bend) * (GELU_A * (1.0 + 3.0 * GELU_B * square))
    hidden = (act * upper).astype(jnp.bfloat16)
    hidden_ref[...] = hidden
    slope_ref[...] = (slope * upper).astype(jnp.bfloat16)
    act_ref[...] = act.astype(jnp.bfloat16)
    part = dot(hidden, down_ref[...], 0, 0)

    @pl.when(step == 0)
    def _():
        acc[...] = part

    @pl.when(step > 0)
    def _():
        acc[...] += part

    @pl.when(step == pl.num_programs(0) - 1)
    def _():
        out_ref[...] = acc[...].astype(jnp.bfloat16)


def ffn_forward(x, gate_weight, up_weight, down_weight):
    rows, model = x.shape
    units = gate_weight.shape[0]
    tile = tile_of(units, 432)
    weight = pl.BlockSpec((tile, model), lambda i: (i, 0))
    flat = pl.BlockSpec((tile, rows), lambda i: (i, 0))
    whole = pl.BlockSpec((rows, model), lambda i: (0, 0))
    kept = jax.ShapeDtypeStruct((units, rows), jnp.bfloat16)
    return pl.pallas_call(
        ffn_forward_kernel,
        grid=(units // tile,),
        out_shape=[kept, kept, kept, jax.ShapeDtypeStruct((rows, model), jnp.bfloat16)],
        in_specs=[whole, weight, weight, weight],
        out_specs=[flat, flat, flat, whole],
        scratch_shapes=[pltpu.VMEM((rows, model), jnp.float32)],
        compiler_params=params(),
        name="ffn_forward",
    )(x, gate_weight, up_weight, down_weight)


def ffn_backward_kernel(
    grad_ref, gate_ref, up_ref, down_ref, slope_ref, act_ref, gate_grad_ref, up_grad_ref, out_ref, acc
):
    step = pl.program_id(0)
    grad_hidden = dot(down_ref[...], grad_ref[...], 1, 1)
    grad_gate = (grad_hidden * slope_ref[...].astype(jnp.float32)).astype(jnp.bfloat16)
    grad_upper = (grad_hidden * act_ref[...].astype(jnp.float32)).astype(jnp.bfloat16)
    gate_grad_ref[...] = grad_gate
    up_grad_ref[...] = grad_upper
    part = dot(grad_gate, gate_ref[...], 0, 0) + dot(grad_upper, up_ref[...], 0, 0)

    @pl.when(step == 0)
    def _():
        acc[...] = part

    @pl.when(step > 0)
    def _():
        acc[...] += part

    @pl.when(step == pl.num_programs(0) - 1)
    def _():
        out_ref[...] = acc[...].astype(jnp.bfloat16)


def ffn_backward(grad, gate_weight, up_weight, down_weight, slope, act):
    rows, model = grad.shape
    units = gate_weight.shape[0]
    tile = tile_of(units, 432)
    weight = pl.BlockSpec((tile, model), lambda i: (i, 0))
    flat = pl.BlockSpec((tile, rows), lambda i: (i, 0))
    whole = pl.BlockSpec((rows, model), lambda i: (0, 0))
    kept = jax.ShapeDtypeStruct((units, rows), jnp.bfloat16)
    return pl.pallas_call(
        ffn_backward_kernel,
        grid=(units // tile,),
        out_shape=[kept, kept, jax.ShapeDtypeStruct((rows, model), jnp.bfloat16)],
        in_specs=[whole, weight, weight, weight, flat, flat],
        out_specs=[flat, flat, whole],
        scratch_shapes=[pltpu.VMEM((rows, model), jnp.float32)],
        compiler_params=params(),
        name="ffn_backward",
    )(grad, gate_weight, up_weight, down_weight, slope, act)


def chunks_of(units):
    return 2 if units % 64 == 0 else 1


def weight_grad(lefts, rights):
    group = len(lefts)
    units, rows = lefts[0].shape
    model = rights[0].shape[1]
    chunks = chunks_of(units)
    tile = units // (2 * chunks)
    core = (lax.axis_index("replica") % 2).astype(jnp.int32).reshape(1)

    def kernel(core_ref, *refs):
        left = jnp.concatenate([ref[...] for ref in refs[:group]], axis=1)
        right = jnp.concatenate([ref[...] for ref in refs[group : 2 * group]], axis=0)
        value = dot(left, right, 1, 0).astype(jnp.bfloat16)
        other_ref, mine_ref = refs[2 * group :]

        @pl.when(pl.program_id(0) == 0)
        def _():
            other_ref[0] = value

        @pl.when(pl.program_id(0) == 1)
        def _():
            mine_ref[0] = value

    def left_map(side, chunk, core_ref):
        return (2 * chunk + jnp.where(side == 0, 1 - core_ref[0], core_ref[0]), 0)

    shape = jax.ShapeDtypeStruct((chunks, tile, model), jnp.bfloat16)
    return pl.pallas_call(
        kernel,
        grid_spec=pltpu.PrefetchScalarGridSpec(
            num_scalar_prefetch=1,
            grid=(2, chunks),
            in_specs=[pl.BlockSpec((tile, rows), left_map)] * group
            + [pl.BlockSpec((rows, model), lambda side, chunk, core_ref: (0, 0))] * group,
            out_specs=[
                pl.BlockSpec(
                    (1, tile, model),
                    lambda side, chunk, core_ref: (jnp.where(side == 0, chunk, chunks - 1), 0, 0),
                ),
                pl.BlockSpec(
                    (1, tile, model),
                    lambda side, chunk, core_ref: (jnp.where(side == 0, 0, chunk), 0, 0),
                ),
            ],
        ),
        out_shape=[shape, shape],
        compiler_params=params(),
        name="weight_grad",
    )(core, *lefts, *rights)


def line_edges():
    places = lax.axis_size("replica") // 2
    outer = places // 2 - 1
    return places, outer


def exchanged(block, pairs):
    route = [(2 * a + core, 2 * b + core) for a, b in pairs for core in range(2)]
    return lax.ppermute(block, "replica", route)


class Line:
    def __init__(self):
        self.places, self.outer = line_edges()
        self.steps = 2 * self.outer + 1
        self.moving = []
        self.done = {}

    def advance(self, fresh, gate=None):
        places, outer, steps = self.places, self.outer, self.steps
        place = (lax.axis_index("replica") // 2).astype(jnp.int32).reshape(1)
        operands, plan = [], []

        def operand(entry):
            array, index = entry if isinstance(entry, tuple) else (entry, None)
            for spot, (known, known_index) in enumerate(operands):
                if known is array and known_index == index:
                    return spot
            operands.append((array, index))
            return len(operands) - 1

        for name, block, step, far in self.moving:
            plan.append((name, step + 1, [operand(block), operand(far)], step))
        for name, terms in fresh:
            plan.append((name, 0, [operand(term) for term in terms], None))
        sizes = [operands[spots[0]][0].shape[-2:] for _, _, spots, _ in plan]
        by_step = {step: index for index, (_, step, _, _) in enumerate(plan)}
        pairs = []
        for edge in range(outer):
            inward, outward = by_step.get(edge), by_step.get(2 * outer - edge)
            if inward is not None and outward is not None and sizes[inward] == sizes[outward]:
                pairs.append((edge, inward, outward))
        cuts = 3 if all(size[0] % 48 == 0 for size in sizes) else 1

        def kernel(place_ref, *refs):
            here = place_ref[0]
            inputs = refs[: len(operands)]
            if gate is not None:
                refs = refs[: len(operands)] + refs[len(operands) + 1 :]
            outputs = refs[len(operands) :]
            states = []
            for spot, (_, _, terms, last) in enumerate(plan):
                value = inputs[terms[0]][...]
                if len(terms) == 2:
                    far = inputs[terms[1]][...]
                    total = (value.astype(jnp.float32) + far.astype(jnp.float32)).astype(jnp.bfloat16)
                    if last is None:
                        value = total
                    elif last <= outer:
                        edge = last
                        value = jnp.where((here == edge + 1) | (here == places - 2 - edge), total, value)
                    else:
                        edge = 2 * outer - last
                        value = jnp.where((here == edge) | (here == places - 1 - edge), far, value)
                states.append(value)
                outputs[spot][...] = value
            for spot, (edge, inward, outward) in enumerate(pairs):
                outputs[len(plan) + spot][...] = jnp.where(
                    (here == edge) | (here == places - 1 - edge), states[inward], states[outward]
                )

        def spec(size, index):
            if index is None:
                return pl.BlockSpec((size[0] // cuts, size[1]), lambda i, place_ref: (i, 0))
            return pl.BlockSpec((None, size[0] // cuts, size[1]), lambda i, place_ref: (index, i, 0))

        in_specs = [spec(array.shape[-2:], index) for array, index in operands]
        arrays = [array for array, _ in operands]
        out_sizes = sizes + [sizes[inward] for _, inward, _ in pairs]
        out_specs = [spec(size, None) for size in out_sizes]
        out_shape = [jax.ShapeDtypeStruct(size, jnp.bfloat16) for size in out_sizes]
        aliases = {}
        if gate is not None:
            aliases = {1 + len(arrays): len(out_shape)}
            in_specs.append(pl.BlockSpec(memory_space=pl.ANY))
            out_specs.append(pl.BlockSpec(memory_space=pl.ANY))
            out_shape.append(jax.ShapeDtypeStruct(gate.shape, gate.dtype))
            arrays.append(gate)
        outs = pl.pallas_call(
            kernel,
            grid_spec=pltpu.PrefetchScalarGridSpec(
                num_scalar_prefetch=1, grid=(cuts,), in_specs=in_specs, out_specs=out_specs
            ),
            out_shape=out_shape,
            input_output_aliases=aliases,
            compiler_params=params(),
            name="line_step",
        )(place, *arrays)
        received = {}
        for spot, (edge, inward, outward) in enumerate(pairs):
            ends = [(edge, edge + 1), (places - 1 - edge, places - 2 - edge)]
            far = exchanged(outs[len(plan) + spot], ends + [(b, a) for a, b in ends])
            received[inward] = received[outward] = far
        self.moving = []
        for index, (name, step, _, _) in enumerate(plan):
            block = outs[index]
            if step == steps:
                self.done[name] = block
                continue
            if index not in received:
                edge = step if step <= outer else 2 * outer - step
                route = [(edge, edge + 1), (places - 1 - edge, places - 2 - edge)]
                if step > outer:
                    route = [(b, a) for a, b in route]
                received[index] = exchanged(block, route)
            self.moving.append((name, block, step, received[index]))
        return outs[-1]

    def finished(self, name):
        while name not in self.done:
            self.advance([])
        return self.done[name]


def line_names(name, units):
    return [(name, chunk) for chunk in range(chunks_of(units))]


def whole_grad(line, name, units, dtype=jnp.float32):
    names = line_names(name, units)
    mines = [line.finished(chunk) for chunk in names]
    others = [swapped(mine, "replica", 1) for mine in mines]
    chunks = len(mines)
    tile, model = mines[0].shape
    core = (lax.axis_index("replica") % 2).astype(jnp.int32).reshape(1)

    def kernel(core_ref, *refs):
        out_ref = refs[-1]
        for chunk in range(chunks):
            for side in range(2):

                @pl.when((pl.program_id(0) == chunk) & (pl.program_id(1) == side))
                def _():
                    @pl.when(core_ref[0] == side)
                    def _():
                        out_ref[...] = refs[chunk][...].astype(dtype)

                    @pl.when(core_ref[0] != side)
                    def _():
                        out_ref[...] = refs[chunks + chunk][...].astype(dtype)

    return pl.pallas_call(
        kernel,
        grid_spec=pltpu.PrefetchScalarGridSpec(
            num_scalar_prefetch=1,
            grid=(chunks, 2),
            in_specs=[pl.BlockSpec((tile, model), lambda chunk, side, core_ref: (0, 0))] * (2 * chunks),
            out_specs=pl.BlockSpec((tile, model), lambda chunk, side, core_ref: (2 * chunk + side, 0)),
        ),
        out_shape=jax.ShapeDtypeStruct((units, model), dtype),
        compiler_params=params(),
        name="whole_grad",
    )(core, *mines, *others)


def halves(block, axis):
    core = lax.axis_index("replica") % 2
    half = block.shape[axis] // 2
    mine = lax.dynamic_slice_in_dim(block, core * half, half, axis)
    other = lax.dynamic_slice_in_dim(block, (1 - core) * half, half, axis)
    return mine, other


def joined(mine, other, axis):
    core = lax.axis_index("replica") % 2
    return jnp.where(
        core == 0,
        jnp.concatenate([mine, other], axis=axis),
        jnp.concatenate([other, mine], axis=axis),
    )


def core_sum(block, axis):
    mine, other = halves(block, axis)
    return added(mine, swapped(other, "replica", 1))


def core_join(block, axis):
    return joined(block, swapped(block, "replica", 1), axis)


def owner_part(blocks):
    rank = lax.axis_index("fsdp")
    part = core_sum(blocks, 1)
    total = lax.dynamic_index_in_dim(part, rank, 0, keepdims=False).astype(jnp.float32)
    for mask in range(1, blocks.shape[0]):
        far = swapped(lax.dynamic_index_in_dim(part, rank ^ mask, 0, keepdims=False), "fsdp", mask)
        total = total + far.astype(jnp.float32)
    return lax.optimization_barrier(total.astype(jnp.bfloat16))


def in_order(blocks):
    rank = lax.axis_index("fsdp")
    stack = jnp.stack(blocks)
    return [lax.dynamic_index_in_dim(stack, rank ^ i, 0, keepdims=False) for i in range(len(blocks))]


def gathered_rows(own, extra=None):
    group = lax.axis_size("fsdp")
    half = own.shape[0] // 2
    block = halves(own, 0)[0]
    if extra is not None:
        block = jnp.concatenate([block, extra], axis=0)
    got = [swapped(block, "fsdp", mask) for mask in range(1, group)]
    mine = jnp.stack([part[:half] for part in got])
    whole = core_join(mine, 1)
    rows = jnp.concatenate(in_order([own] + list(whole)), axis=0)
    if extra is None:
        return rows
    return rows, in_order([extra] + [part[half:] for part in got])


def passed_along(block, axis, distance):
    devices = range(lax.axis_size(axis))
    route = [(i - distance, i) for i in devices if i - distance in devices]
    return lax.ppermute(block, axis, route)


def contract(left, right, left_dim, right_dim):
    return lax.dot_general(
        left, right, (((left_dim,), (right_dim,)), ((), ())), preferred_element_type=jnp.float32
    )


def normed(value, gain):
    return value * lax.rsqrt(jnp.mean(value * value, axis=-1, keepdims=True) + EPS) * gain


def norm_back(value, gain, grad):
    _, pull = jax.vjp(normed, value, gain)
    return pull(grad)


def tables(places, half):
    freq = 10000.0 ** (-(2.0 * jnp.arange(half, dtype=jnp.float32)) / (2 * half))
    angle = places.astype(jnp.float32)[:, None] * freq[None, :]
    return (jnp.cos(angle), jnp.sin(angle))


def rotate(value, cosine, sine):
    half = value.shape[-1] // 2
    first = value[..., :half]
    second = value[..., half:]
    return jnp.concatenate(
        [first * cosine - second * sine, second * cosine + first * sine], axis=-1
    )


def head_post(raw, gain, cosine, sine):
    return rotate(normed(raw, gain), cosine, sine)


def per_device(
    hidden_in,
    out_grad,
    segments,
    positions,
    norm_in,
    query_weight,
    key_weight,
    value_weight,
    out_weight,
    norm_attn,
    norm_ffn,
    gate_weight,
    up_weight,
    down_weight,
    norm_out,
    query_gain,
    key_gain,
):
    rows = hidden_in.shape[0]
    rank = lax.axis_index("fsdp")
    group = lax.axis_size("fsdp")
    masks = range(1, group)
    head_size = key_weight.shape[1]
    heads = query_weight.shape[1] // head_size
    model = hidden_in.shape[1]
    own_model = norm_in.shape[0]
    own_head = query_gain.shape[0]
    hops = (WINDOW - 1) // rows + 1
    scale = head_size ** (-0.5)
    w_own = jnp.concatenate([query_weight, key_weight, value_weight], axis=1)
    wide = w_own.shape[1]
    sizes = [own_model] * 4 + [own_head] * 2
    gains = jnp.concatenate([norm_in, norm_attn, norm_ffn, norm_out, query_gain, key_gain])
    gains = jnp.pad(gains[None, :], ((0, 15), (0, wide - sum(sizes))))
    w_qkv, gain_rows = gathered_rows(w_own, gains)
    w_out = gathered_rows(out_weight)
    spots = [sum(sizes[:i]) for i in range(7)]
    gain_in, gain_attn, gain_ffn, gain_out, gain_query, gain_key = (
        jnp.concatenate([row[0, spots[i] : spots[i + 1]] for row in gain_rows]) for i in range(6)
    )
    residual_in = hidden_in.astype(jnp.float32)
    normed_in = normed(residual_in, gain_in).astype(jnp.bfloat16)
    qkv = jnp.dot(normed_in, w_qkv, preferred_element_type=jnp.float32)
    query_raw = qkv[:, : heads * head_size].reshape(rows, heads, head_size)
    key_raw = qkv[:, heads * head_size : (heads + 1) * head_size]
    value_new = qkv[:, (heads + 1) * head_size :].astype(jnp.bfloat16)
    cosine, sine = tables(positions, head_size // 2)
    cosine_heads = cosine[:, None, :]
    sine_heads = sine[:, None, :]
    query_new = head_post(query_raw, gain_query, cosine_heads, sine_heads).astype(jnp.bfloat16)
    key_new = head_post(key_raw, gain_key, cosine, sine).astype(jnp.bfloat16)
    pair_new = jnp.concatenate([key_new, value_new], axis=1)
    parts = [pair_new]
    for step in range(1, hops + 1):
        parts.insert(0, passed_along(pair_new, "fsdp", step))
    pairs = jnp.concatenate(parts, axis=0)
    keys = pairs[:, :head_size]
    values = pairs[:, head_size:]
    width = keys.shape[0]
    seg_padded = jnp.concatenate([jnp.full((hops * rows,), -1, jnp.int32), segments], axis=0)
    key_segs = lax.dynamic_slice_in_dim(seg_padded, rank * rows, width, 0)
    query_segs = lax.dynamic_slice_in_dim(segments, rank * rows, rows, 0)
    gap = hops * rows + jnp.arange(rows)[:, None] - jnp.arange(width)[None, :]
    allowed = (gap >= 0) & (gap < WINDOW) & (query_segs[:, None] == key_segs[None, :])
    query_rows = query_new.reshape(rows * heads, head_size)

    def scores_of():
        raw_scores = (contract(query_rows, keys, 1, 1) * scale).reshape(rows, heads, width)
        return jnp.where(allowed[:, None, :], raw_scores, NEG)

    scores = scores_of()
    highest = jnp.max(scores, axis=-1, keepdims=True)
    expo = jnp.exp(scores - highest)
    weight_sum = jnp.sum(expo, axis=-1, keepdims=True)
    probs = expo / weight_sum
    log_total = highest + jnp.log(weight_sum)
    probs_low = probs.astype(jnp.bfloat16).reshape(rows * heads, width)
    mixed = (
        jnp.dot(probs_low, values, preferred_element_type=jnp.float32)
        .reshape(rows, heads * head_size)
        .astype(jnp.bfloat16)
    )
    attended = contract(mixed, w_out, 1, 1)
    resid = residual_in + normed(attended, gain_attn)
    ffn_in = normed(resid, gain_ffn).astype(jnp.bfloat16)
    ffn_blocks = [ffn_in] + [swapped(ffn_in, "fsdp", mask) for mask in masks]
    hiddens, slopes, acts, parts = [], [], [], []
    for mask in range(group):
        hidden, slope, act, part = ffn_forward(ffn_blocks[mask], gate_weight, up_weight, down_weight)
        parts.append(swapped(part, "fsdp", mask) if mask else part)
        hiddens.append(hidden)
        slopes.append(slope)
        acts.append(act)
    branch = sum(part.astype(jnp.float32) for part in parts)
    result = resid + normed(branch, gain_out)
    hidden_out = result.astype(jnp.bfloat16)
    grad_result = out_grad.astype(jnp.float32)
    grad_branch, grad_gain_out = norm_back(branch, gain_out, grad_result)
    grad_branch_low = grad_branch.astype(jnp.bfloat16)
    pieces = [grad_branch_low] + [swapped(grad_branch_low, "fsdp", mask) for mask in masks]
    units = gate_weight.shape[0]
    line = Line()

    def fresh(name, other, mine):
        far = swapped(other, "replica", 1)
        return [(key, [(mine, key[1]), (far, key[1])]) for key in line_names(name, units)]

    waiting = fresh("down", *weight_grad(hiddens, pieces))
    grad_gates, grad_uppers = {}, {}
    order = list(masks) + [0]
    returned = {}
    for mask in order:
        grad_gates[mask], grad_uppers[mask], part = ffn_backward(
            pieces[mask], gate_weight, up_weight, down_weight, slopes[mask], acts[mask]
        )
        returned[mask] = swapped(part, "fsdp", mask) if mask else part
        if mask == order[0]:
            pieces[order[1]] = line.advance([waiting.pop(0)], pieces[order[1]])
    waiting += fresh("gate", *weight_grad([grad_gates[i] for i in range(group)], ffn_blocks))
    waiting += fresh("up", *weight_grad([grad_uppers[i] for i in range(group)], ffn_blocks))
    returned[0] = line.advance([waiting.pop(0)], returned[0])
    grad_ffn_in = sum(returned[i].astype(jnp.float32) for i in range(group))
    grad_resid_part, grad_gain_ffn = norm_back(resid, gain_ffn, grad_ffn_in)
    grad_resid = grad_result + grad_resid_part
    grad_attended, grad_gain_attn = norm_back(attended, gain_attn, grad_resid)
    grad_attended_low = grad_attended.astype(jnp.bfloat16)
    grad_attended_low = line.advance([waiting.pop(0)] if waiting else [], grad_attended_low)
    grad_wout = contract(grad_attended_low, mixed, 0, 0).astype(jnp.bfloat16)
    out_part = owner_part(grad_wout.reshape(group, own_model, -1))
    grad_mixed = jnp.dot(grad_attended_low, w_out, preferred_element_type=jnp.float32).astype(
        jnp.bfloat16
    )
    grad_mixed_rows = grad_mixed.reshape(rows * heads, head_size)
    scores = scores_of()
    probs = jnp.exp(scores - log_total)
    probs_low = probs.astype(jnp.bfloat16).reshape(rows * heads, width)
    grad_probs = contract(grad_mixed_rows, values, 1, 1).reshape(rows, heads, width)
    delta = jnp.sum(grad_probs * probs, axis=-1, keepdims=True)
    grad_scores = (probs * (grad_probs - delta)).astype(jnp.bfloat16).reshape(rows * heads, width)
    grad_scores = line.advance([waiting.pop(0)] if waiting else [], grad_scores)
    grad_query = (jnp.dot(grad_scores, keys, preferred_element_type=jnp.float32) * scale).reshape(
        rows, heads, head_size
    )
    grad_keys = contract(grad_scores, query_rows, 0, 0) * scale
    grad_values = contract(probs_low, grad_mixed_rows, 0, 0)
    grad_pairs = jnp.concatenate([grad_keys, grad_values], axis=1)
    grad_pair = grad_pairs[hops * rows :]
    for step in range(1, hops + 1):
        lower = (hops - step) * rows
        back = passed_along(grad_pairs[lower : lower + rows].astype(jnp.bfloat16), "fsdp", -step)
        grad_pair = grad_pair + back.astype(jnp.float32)
    grad_pair = line.advance([waiting.pop(0)] if waiting else [], grad_pair)
    grad_key = grad_pair[:, :head_size]
    grad_value = grad_pair[:, head_size:]
    _, pull_query = jax.vjp(
        lambda raw, gain: head_post(raw, gain, cosine_heads, sine_heads), query_raw, gain_query
    )
    grad_query_raw, grad_gain_query = pull_query(grad_query)
    _, pull_key = jax.vjp(lambda raw, gain: head_post(raw, gain, cosine, sine), key_raw, gain_key)
    grad_key_raw, grad_gain_key = pull_key(grad_key)
    grad_query_low = grad_query_raw.reshape(rows, heads * head_size).astype(jnp.bfloat16)
    grad_key_low = grad_key_raw.astype(jnp.bfloat16)
    grad_value_low = grad_value.astype(jnp.bfloat16)
    grad_qkv = jnp.concatenate([grad_query_low, grad_key_low, grad_value_low], axis=1)
    grad_wqkv = contract(normed_in, grad_qkv, 0, 0).astype(jnp.bfloat16)
    grad_normed_in = contract(grad_qkv, w_qkv, 1, 1)
    grad_input_part, grad_gain_in = norm_back(residual_in, gain_in, grad_normed_in)
    grad_in = grad_resid + grad_input_part
    gain_grads = jnp.concatenate(
        [
            grad.astype(jnp.bfloat16).reshape(group, -1)
            for grad in (
                grad_gain_in,
                grad_gain_attn,
                grad_gain_ffn,
                grad_gain_out,
                grad_gain_query,
                grad_gain_key,
            )
        ],
        axis=1,
    )
    gain_grads = jnp.pad(gain_grads[:, None, :], ((0, 0), (0, 31), (0, wide - sum(sizes))))
    qkv_part = owner_part(
        jnp.concatenate([grad_wqkv.reshape(group, own_model, wide), gain_grads], axis=1)
    )
    while waiting:
        line.advance([waiting.pop(0)])
    grad_down = whole_grad(line, "down", units)
    line.advance([("out", [out_part]), ("qkv", [qkv_part])])
    grad_gate_w = whole_grad(line, "gate", units)
    grad_up_w = whole_grad(line, "up", units)
    owned = core_join(line.finished("qkv"), 0).astype(jnp.float32)
    owned_out = core_join(line.finished("out"), 0).astype(jnp.float32)
    owned_query = owned[:own_model, : heads * head_size]
    owned_key = owned[:own_model, heads * head_size : (heads + 1) * head_size]
    owned_value = owned[:own_model, (heads + 1) * head_size :]
    owned_gain_in, owned_gain_attn, owned_gain_ffn, owned_gain_out, owned_gain_query, owned_gain_key = (
        owned[own_model, spots[i] : spots[i + 1]] for i in range(6)
    )
    return (
        hidden_out,
        grad_in,
        owned_gain_in,
        owned_query,
        owned_key,
        owned_value,
        owned_out,
        owned_gain_attn,
        owned_gain_ffn,
        grad_gate_w,
        grad_up_w,
        grad_down,
        owned_gain_out,
        owned_gain_query,
        owned_gain_key,
    )


def solution(mesh):
    return jax.shard_map(
        per_device,
        mesh=mesh,
        in_specs=(
            P(("replica", "fsdp"), None),
            P(("replica", "fsdp"), None),
            P("replica"),
            P(("replica", "fsdp")),
            P("fsdp"),
            P("fsdp", None),
            P("fsdp", None),
            P("fsdp", None),
            P("fsdp", None),
            P("fsdp"),
            P("fsdp"),
            P("fsdp", None),
            P("fsdp", None),
            P("fsdp", None),
            P("fsdp"),
            P("fsdp"),
            P("fsdp"),
        ),
        out_specs=(
            P(("replica", "fsdp"), None),
            P(("replica", "fsdp"), None),
            P("fsdp"),
            P("fsdp", None),
            P("fsdp", None),
            P("fsdp", None),
            P("fsdp", None),
            P("fsdp"),
            P("fsdp"),
            P("fsdp", None),
            P("fsdp", None),
            P("fsdp", None),
            P("fsdp"),
            P("fsdp"),
            P("fsdp"),
        ),
        check_vma=False,
    )
```

```python
import jax
import jax.numpy as jnp
from jax import lax
from jax.experimental import pallas as pl
from jax.experimental.pallas import tpu as pltpu
from jax.sharding import PartitionSpec as P

WINDOW = 512


EPS = 1e-06
NEG = -1e30


def swapped(block, axis, mask):
    route = [(i, i ^ mask) for i in range(lax.axis_size(axis))]
    return lax.ppermute(block, axis, route)


def added(left, right):
    total = left.astype(jnp.float32) + right.astype(jnp.float32)
    return lax.optimization_barrier(total.astype(jnp.bfloat16))


VMEM_LIMIT = 56 * 1024 * 1024


def params(*semantics):
    return pltpu.CompilerParams(vmem_limit_bytes=VMEM_LIMIT)


def dot(left, right, left_dim, right_dim):
    return lax.dot_general(
        left, right, (((left_dim,), (right_dim,)), ((), ())), preferred_element_type=jnp.float32
    )


def after(array, *others):
    place = pl.BlockSpec(memory_space=pl.ANY)
    return pl.pallas_call(
        lambda *refs: None,
        out_shape=jax.ShapeDtypeStruct(array.shape, array.dtype),
        in_specs=[place] * (1 + len(others)),
        out_specs=place,
        input_output_aliases={0: 0},
        name="after",
    )(array, *others)


def scalar(value):
    return value.astype(jnp.int32).reshape(1)


def packed(weights, extra=None):
    half = weights[0].shape[0] // 2
    wide = sum(weight.shape[1] for weight in weights)
    below = 0 if extra is None else extra.shape[0]

    def kernel(core_ref, *refs):
        out_ref = refs[-1]
        for side in range(2):

            @pl.when(core_ref[0] == side)
            def _():
                at = 0
                for ref in refs[: len(weights)]:
                    out_ref[:half, at : at + ref.shape[1]] = ref[side * half : (side + 1) * half, :]
                    at += ref.shape[1]

        if extra is not None:
            out_ref[half:, :] = refs[len(weights)][...]

    arrays = list(weights) + ([] if extra is None else [extra])
    return pl.pallas_call(
        kernel,
        grid_spec=pltpu.PrefetchScalarGridSpec(
            num_scalar_prefetch=1,
            grid=(1,),
            in_specs=[pl.BlockSpec(array.shape, lambda i, core_ref: (0, 0)) for array in arrays],
            out_specs=pl.BlockSpec((half + below, wide), lambda i, core_ref: (0, 0)),
        ),
        out_shape=jax.ShapeDtypeStruct((half + below, wide), jnp.bfloat16),
        compiler_params=params(),
        name="pack",
    )(scalar(lax.axis_index("replica") % 2), *arrays)


def unpacked(weights, got, peers):
    rows = weights[0].shape[0]
    half = rows // 2
    group = len(got) + 1
    wide = sum(weight.shape[1] for weight in weights)
    own = len(weights)

    def kernel(core_ref, rank_ref, *refs):
        out_ref = refs[-1]
        mask = rank_ref[0] ^ pl.program_id(0)

        @pl.when(mask == 0)
        def _():
            at = 0
            for ref in refs[:own]:
                out_ref[:, at : at + ref.shape[1]] = ref[...]
                at += ref.shape[1]

        for other in range(1, group):
            for side in range(2):

                @pl.when((mask == other) & (core_ref[0] == side))
                def _():
                    out_ref[side * half : (side + 1) * half, :] = refs[own + other - 1][:half, :]
                    out_ref[(1 - side) * half : (2 - side) * half, :] = refs[own + group - 2 + other][:half, :]

    arrays = list(weights) + list(got) + list(peers)
    return pl.pallas_call(
        kernel,
        grid_spec=pltpu.PrefetchScalarGridSpec(
            num_scalar_prefetch=2,
            grid=(group,),
            in_specs=[pl.BlockSpec(array.shape, lambda i, *refs: (0, 0)) for array in arrays],
            out_specs=pl.BlockSpec((rows, wide), lambda i, *refs: (i, 0)),
        ),
        out_shape=jax.ShapeDtypeStruct((group * rows, wide), jnp.bfloat16),
        compiler_params=params(),
        name="unpack",
    )(scalar(lax.axis_index("replica") % 2), scalar(lax.axis_index("fsdp")), *arrays)


GELU_A = (2.0 / 3.141592653589793) ** 0.5
GELU_B = 0.044715


def ffn_forward(x, gate_weight, up_weight, down_weight):
    gate = contract(gate_weight, x, 1, 1)
    upper = contract(up_weight, x, 1, 1)
    square = gate * gate
    bend = jnp.tanh(GELU_A * gate * (1.0 + GELU_B * square))
    half = 0.5 + 0.5 * bend
    act = gate * half
    slope = half + 0.5 * gate * (1.0 - bend * bend) * (GELU_A * (1.0 + 3.0 * GELU_B * square))
    hidden = (act * upper).astype(jnp.bfloat16)
    part = contract(hidden, down_weight, 0, 0).astype(jnp.bfloat16)
    return hidden, (slope * upper).astype(jnp.bfloat16), act.astype(jnp.bfloat16), part


def ffn_backward(grad, gate_weight, up_weight, down_weight, slope, act):
    grad_hidden = contract(down_weight, grad, 1, 1)
    grad_gate = (grad_hidden * slope.astype(jnp.float32)).astype(jnp.bfloat16)
    grad_upper = (grad_hidden * act.astype(jnp.float32)).astype(jnp.bfloat16)
    part = contract(grad_gate, gate_weight, 0, 0) + contract(grad_upper, up_weight, 0, 0)
    return grad_gate, grad_upper, part.astype(jnp.bfloat16)


def chunks_of(units):
    return 2 if units % 64 == 0 else 1


def weight_grad(lefts, rights):
    group = len(lefts)
    units, rows = lefts[0].shape
    model = rights[0].shape[1]
    chunks = chunks_of(units)
    tile = units // (2 * chunks)
    core = (lax.axis_index("replica") % 2).astype(jnp.int32).reshape(1)

    def kernel(core_ref, *refs):
        other_ref, mine_ref, left_ref, right_ref = refs[2 * group :]

        @pl.when((pl.program_id(0) == 0) & (pl.program_id(1) == 0))
        def _():
            for spot in range(group):
                right_ref[spot * rows : (spot + 1) * rows, :] = refs[group + spot][...]

        for spot in range(group):
            left_ref[:, spot * rows : (spot + 1) * rows] = refs[spot][...]
        value = dot(left_ref[...], right_ref[...], 1, 0).astype(jnp.bfloat16)

        @pl.when(pl.program_id(0) == 0)
        def _():
            other_ref[0] = value

        @pl.when(pl.program_id(0) == 1)
        def _():
            mine_ref[0] = value

    def left_map(side, chunk, core_ref):
        return (2 * chunk + jnp.where(side == 0, 1 - core_ref[0], core_ref[0]), 0)

    shape = jax.ShapeDtypeStruct((chunks, tile, model), jnp.bfloat16)
    return pl.pallas_call(
        kernel,
        grid_spec=pltpu.PrefetchScalarGridSpec(
            num_scalar_prefetch=1,
            grid=(2, chunks),
            in_specs=[pl.BlockSpec((tile, rows), left_map)] * group
            + [pl.BlockSpec((rows, model), lambda side, chunk, core_ref: (0, 0))] * group,
            out_specs=[
                pl.BlockSpec(
                    (1, tile, model),
                    lambda side, chunk, core_ref: (jnp.where(side == 0, chunk, chunks - 1), 0, 0),
                ),
                pl.BlockSpec(
                    (1, tile, model),
                    lambda side, chunk, core_ref: (jnp.where(side == 0, 0, chunk), 0, 0),
                ),
            ],
            scratch_shapes=[
                pltpu.VMEM((tile, group * rows), jnp.bfloat16),
                pltpu.VMEM((group * rows, model), jnp.bfloat16),
            ],
        ),
        out_shape=[shape, shape],
        compiler_params=params(),
        name="weight_grad",
    )(core, *lefts, *rights)


def line_edges():
    places = lax.axis_size("replica") // 2
    outer = places // 2 - 1
    return places, outer


def exchanged(block, pairs):
    route = [(2 * a + core, 2 * b + core) for a, b in pairs for core in range(2)]
    return lax.ppermute(block, "replica", route)


class Line:
    def __init__(self):
        self.places, self.outer = line_edges()
        self.steps = 2 * self.outer + 1
        self.moving = []
        self.done = {}

    def advance(self, fresh, gate=None):
        places, outer, steps = self.places, self.outer, self.steps
        place = (lax.axis_index("replica") // 2).astype(jnp.int32).reshape(1)
        operands, plan = [], []

        def operand(entry):
            array, index = entry if isinstance(entry, tuple) else (entry, None)
            for spot, (known, known_index) in enumerate(operands):
                if known is array and known_index == index:
                    return spot
            operands.append((array, index))
            return len(operands) - 1

        for name, block, step, far in self.moving:
            plan.append((name, step + 1, [operand(block), operand(far)], step))
        for name, terms in fresh:
            plan.append((name, 0, [operand(term) for term in terms], None))
        sizes = [operands[spots[0]][0].shape[-2:] for _, _, spots, _ in plan]
        by_step = {step: index for index, (_, step, _, _) in enumerate(plan)}
        pairs = []
        for edge in range(outer):
            inward, outward = by_step.get(edge), by_step.get(2 * outer - edge)
            if inward is not None and outward is not None and sizes[inward] == sizes[outward]:
                pairs.append((edge, inward, outward))
        cuts = 3 if all(size[0] % 48 == 0 for size in sizes) else 1

        def kernel(place_ref, *refs):
            here = place_ref[0]
            inputs = refs[: len(operands)]
            if gate is not None:
                refs = refs[: len(operands)] + refs[len(operands) + 1 :]
            outputs = refs[len(operands) :]
            states = []
            for spot, (_, _, terms, last) in enumerate(plan):
                value = inputs[terms[0]][...]
                if len(terms) == 2:
                    far = inputs[terms[1]][...]
                    total = (value.astype(jnp.float32) + far.astype(jnp.float32)).astype(jnp.bfloat16)
                    if last is None:
                        value = total
                    elif last <= outer:
                        edge = last
                        value = jnp.where((here == edge + 1) | (here == places - 2 - edge), total, value)
                    else:
                        edge = 2 * outer - last
                        value = jnp.where((here == edge) | (here == places - 1 - edge), far, value)
                states.append(value)
                outputs[spot][...] = value
            for spot, (edge, inward, outward) in enumerate(pairs):
                outputs[len(plan) + spot][...] = jnp.where(
                    (here == edge) | (here == places - 1 - edge), states[inward], states[outward]
                )

        def spec(size, index):
            if index is None:
                return pl.BlockSpec((size[0] // cuts, size[1]), lambda i, place_ref: (i, 0))
            return pl.BlockSpec((None, size[0] // cuts, size[1]), lambda i, place_ref: (index, i, 0))

        in_specs = [spec(array.shape[-2:], index) for array, index in operands]
        arrays = [array for array, _ in operands]
        out_sizes = sizes + [sizes[inward] for _, inward, _ in pairs]
        out_specs = [spec(size, None) for size in out_sizes]
        out_shape = [jax.ShapeDtypeStruct(size, jnp.bfloat16) for size in out_sizes]
        aliases = {}
        if gate is not None:
            aliases = {1 + len(arrays): len(out_shape)}
            in_specs.append(pl.BlockSpec(memory_space=pl.ANY))
            out_specs.append(pl.BlockSpec(memory_space=pl.ANY))
            out_shape.append(jax.ShapeDtypeStruct(gate.shape, gate.dtype))
            arrays.append(gate)
        outs = pl.pallas_call(
            kernel,
            grid_spec=pltpu.PrefetchScalarGridSpec(
                num_scalar_prefetch=1, grid=(cuts,), in_specs=in_specs, out_specs=out_specs
            ),
            out_shape=out_shape,
            input_output_aliases=aliases,
            compiler_params=params(),
            name="line_step",
        )(place, *arrays)
        received = {}
        for spot, (edge, inward, outward) in enumerate(pairs):
            ends = [(edge, edge + 1), (places - 1 - edge, places - 2 - edge)]
            far = exchanged(outs[len(plan) + spot], ends + [(b, a) for a, b in ends])
            received[inward] = received[outward] = far
        self.moving = []
        for index, (name, step, _, _) in enumerate(plan):
            block = outs[index]
            if step == steps:
                self.done[name] = block
                continue
            if index not in received:
                edge = step if step <= outer else 2 * outer - step
                route = [(edge, edge + 1), (places - 1 - edge, places - 2 - edge)]
                if step > outer:
                    route = [(b, a) for a, b in route]
                received[index] = exchanged(block, route)
            self.moving.append((name, block, step, received[index]))
        return outs[-1]

    def finished(self, name):
        while name not in self.done:
            self.advance([])
        return self.done[name]


def line_names(name, units):
    return [(name, chunk) for chunk in range(chunks_of(units))]


def whole_grad(line, name, units, dtype=jnp.float32):
    names = line_names(name, units)
    mines = [line.finished(chunk) for chunk in names]
    others = [swapped(mine, "replica", 1) for mine in mines]
    chunks = len(mines)
    tile, model = mines[0].shape
    core = (lax.axis_index("replica") % 2).astype(jnp.int32).reshape(1)

    def kernel(core_ref, *refs):
        out_ref = refs[-1]
        for chunk in range(chunks):
            for side in range(2):

                @pl.when((pl.program_id(0) == chunk) & (pl.program_id(1) == side))
                def _():
                    @pl.when(core_ref[0] == side)
                    def _():
                        out_ref[...] = refs[chunk][...].astype(dtype)

                    @pl.when(core_ref[0] != side)
                    def _():
                        out_ref[...] = refs[chunks + chunk][...].astype(dtype)

    return pl.pallas_call(
        kernel,
        grid_spec=pltpu.PrefetchScalarGridSpec(
            num_scalar_prefetch=1,
            grid=(chunks, 2),
            in_specs=[pl.BlockSpec((tile, model), lambda chunk, side, core_ref: (0, 0))] * (2 * chunks),
            out_specs=pl.BlockSpec((tile, model), lambda chunk, side, core_ref: (2 * chunk + side, 0)),
        ),
        out_shape=jax.ShapeDtypeStruct((units, model), dtype),
        compiler_params=params(),
        name="whole_grad",
    )(core, *mines, *others)


def halves(block, axis):
    core = lax.axis_index("replica") % 2
    half = block.shape[axis] // 2
    mine = lax.dynamic_slice_in_dim(block, core * half, half, axis)
    other = lax.dynamic_slice_in_dim(block, (1 - core) * half, half, axis)
    return mine, other


def joined(mine, other, axis):
    core = lax.axis_index("replica") % 2
    return jnp.where(
        core == 0,
        jnp.concatenate([mine, other], axis=axis),
        jnp.concatenate([other, mine], axis=axis),
    )


def core_sum(block, axis):
    mine, other = halves(block, axis)
    return added(mine, swapped(other, "replica", 1))


def core_join(block, axis):
    return joined(block, swapped(block, "replica", 1), axis)


def owner_part(blocks):
    rank = lax.axis_index("fsdp")
    part = core_sum(blocks, 1)
    total = lax.dynamic_index_in_dim(part, rank, 0, keepdims=False).astype(jnp.float32)
    for mask in range(1, blocks.shape[0]):
        far = swapped(lax.dynamic_index_in_dim(part, rank ^ mask, 0, keepdims=False), "fsdp", mask)
        total = total + far.astype(jnp.float32)
    return lax.optimization_barrier(total.astype(jnp.bfloat16))


def fetched(block):
    got = [swapped(block, "fsdp", mask) for mask in range(1, lax.axis_size("fsdp"))]
    return got, [swapped(part, "replica", 1) for part in got]


def passed_along(block, axis, distance):
    devices = range(lax.axis_size(axis))
    route = [(i - distance, i) for i in devices if i - distance in devices]
    return lax.ppermute(block, axis, route)


def contract(left, right, left_dim, right_dim):
    return lax.dot_general(
        left, right, (((left_dim,), (right_dim,)), ((), ())), preferred_element_type=jnp.float32
    )


def normed(value, gain):
    return value * lax.rsqrt(jnp.mean(value * value, axis=-1, keepdims=True) + EPS) * gain


def norm_back(value, gain, grad):
    _, pull = jax.vjp(normed, value, gain)
    return pull(grad)


def tables(places, half):
    freq = 10000.0 ** (-(2.0 * jnp.arange(half, dtype=jnp.float32)) / (2 * half))
    angle = places.astype(jnp.float32)[:, None] * freq[None, :]
    return (jnp.cos(angle), jnp.sin(angle))


def rotate(value, cosine, sine):
    half = value.shape[-1] // 2
    first = value[..., :half]
    second = value[..., half:]
    return jnp.concatenate(
        [first * cosine - second * sine, second * cosine + first * sine], axis=-1
    )


def head_post(raw, gain, cosine, sine):
    return rotate(normed(raw, gain), cosine, sine)


def per_device(
    hidden_in,
    out_grad,
    segments,
    positions,
    norm_in,
    query_weight,
    key_weight,
    value_weight,
    out_weight,
    norm_attn,
    norm_ffn,
    gate_weight,
    up_weight,
    down_weight,
    norm_out,
    query_gain,
    key_gain,
):
    rows = hidden_in.shape[0]
    rank = lax.axis_index("fsdp")
    group = lax.axis_size("fsdp")
    masks = range(1, group)
    head_size = key_weight.shape[1]
    heads = query_weight.shape[1] // head_size
    model = hidden_in.shape[1]
    own_model = norm_in.shape[0]
    own_head = query_gain.shape[0]
    hops = (WINDOW - 1) // rows + 1
    scale = head_size ** (-0.5)
    qkv_weights = (query_weight, key_weight, value_weight)
    wide = sum(weight.shape[1] for weight in qkv_weights)
    sizes = [own_model] * 4 + [own_head] * 2
    gains = jnp.concatenate([norm_in, norm_attn, norm_ffn, norm_out, query_gain, key_gain])
    gains = jnp.pad(gains[None, :], ((0, 15), (0, wide - sum(sizes))))
    got, peers = fetched(packed(qkv_weights, gains))
    w_qkv = unpacked(qkv_weights, got, peers)
    gain_stack = jnp.stack([gains[0]] + [part[-16] for part in got])
    gain_rows = [
        lax.dynamic_index_in_dim(gain_stack, rank ^ i, 0, keepdims=False) for i in range(group)
    ]
    got, peers = fetched(after(packed([out_weight]), w_qkv))
    spots = [sum(sizes[:i]) for i in range(7)]
    gain_in, gain_attn, gain_ffn, gain_out, gain_query, gain_key = (
        jnp.concatenate([row[spots[i] : spots[i + 1]] for row in gain_rows]) for i in range(6)
    )
    residual_in = hidden_in.astype(jnp.float32)
    normed_in = normed(residual_in, gain_in).astype(jnp.bfloat16)
    qkv = jnp.dot(normed_in, w_qkv, preferred_element_type=jnp.float32)
    query_raw = qkv[:, : heads * head_size].reshape(rows, heads, head_size)
    key_raw = qkv[:, heads * head_size : (heads + 1) * head_size]
    value_new = qkv[:, (heads + 1) * head_size :].astype(jnp.bfloat16)
    cosine, sine = tables(positions, head_size // 2)
    cosine_heads = cosine[:, None, :]
    sine_heads = sine[:, None, :]
    query_new = head_post(query_raw, gain_query, cosine_heads, sine_heads).astype(jnp.bfloat16)
    key_new = head_post(key_raw, gain_key, cosine, sine).astype(jnp.bfloat16)
    pair_new = jnp.concatenate([key_new, value_new], axis=1)
    parts = [pair_new]
    for step in range(1, hops + 1):
        parts.insert(0, passed_along(pair_new, "fsdp", step))
    pairs = jnp.concatenate(parts, axis=0)
    keys = pairs[:, :head_size]
    values = pairs[:, head_size:]
    width = keys.shape[0]
    seg_padded = jnp.concatenate([jnp.full((hops * rows,), -1, jnp.int32), segments], axis=0)
    key_segs = lax.dynamic_slice_in_dim(seg_padded, rank * rows, width, 0)
    query_segs = lax.dynamic_slice_in_dim(segments, rank * rows, rows, 0)
    gap = hops * rows + jnp.arange(rows)[:, None] - jnp.arange(width)[None, :]
    allowed = (gap >= 0) & (gap < WINDOW) & (query_segs[:, None] == key_segs[None, :])
    query_rows = query_new.reshape(rows * heads, head_size)

    def scores_of():
        raw_scores = (contract(query_rows, keys, 1, 1) * scale).reshape(rows, heads, width)
        return jnp.where(allowed[:, None, :], raw_scores, NEG)

    scores = scores_of()
    highest = jnp.max(scores, axis=-1, keepdims=True)
    expo = jnp.exp(scores - highest)
    weight_sum = jnp.sum(expo, axis=-1, keepdims=True)
    probs = expo / weight_sum
    log_total = highest + jnp.log(weight_sum)
    probs_low = probs.astype(jnp.bfloat16).reshape(rows * heads, width)
    mixed = (
        jnp.dot(probs_low, values, preferred_element_type=jnp.float32)
        .reshape(rows, heads * head_size)
        .astype(jnp.bfloat16)
    )
    w_out = unpacked([out_weight], got, peers)
    attended = contract(mixed, w_out, 1, 1)
    resid = residual_in + normed(attended, gain_attn)
    ffn_in = normed(resid, gain_ffn).astype(jnp.bfloat16)
    ffn_blocks = [ffn_in] + [swapped(ffn_in, "fsdp", mask) for mask in masks]
    hiddens, slopes, acts, parts = [], [], [], []
    for mask in range(group):
        hidden, slope, act, part = ffn_forward(ffn_blocks[mask], gate_weight, up_weight, down_weight)
        parts.append(part)
        hiddens.append(hidden)
        slopes.append(slope)
        acts.append(act)
    parts = parts[:1] + [swapped(parts[mask], "fsdp", mask) for mask in masks]
    branch = sum(part.astype(jnp.float32) for part in parts)
    result = resid + normed(branch, gain_out)
    hidden_out = result.astype(jnp.bfloat16)
    grad_result = out_grad.astype(jnp.float32)
    grad_branch, grad_gain_out = norm_back(branch, gain_out, grad_result)
    grad_branch_low = grad_branch.astype(jnp.bfloat16)
    pieces = [grad_branch_low] + [swapped(grad_branch_low, "fsdp", mask) for mask in masks]
    units = gate_weight.shape[0]
    line = Line()

    def fresh(name, other, mine):
        far = swapped(other, "replica", 1)
        return [(key, [(mine, key[1]), (far, key[1])]) for key in line_names(name, units)]

    grad_gates, grad_uppers, returned = {}, {}, {}
    last = group - 1
    for mask in range(group):
        if mask == last:
            waiting = fresh("down", *weight_grad(hiddens, pieces))
            pieces[mask] = line.advance([waiting.pop(0)], pieces[mask])
        grad_gates[mask], grad_uppers[mask], part = ffn_backward(
            pieces[mask], gate_weight, up_weight, down_weight, slopes[mask], acts[mask]
        )
        if mask < last:
            pieces[mask + 1] = after(pieces[mask + 1], part)
        returned[mask] = swapped(part, "fsdp", mask) if mask else part
    waiting += fresh("gate", *weight_grad([grad_gates[i] for i in range(group)], ffn_blocks))
    waiting += fresh("up", *weight_grad([grad_uppers[i] for i in range(group)], ffn_blocks))
    returned[0] = line.advance([waiting.pop(0)], returned[0])
    grad_ffn_in = sum(returned[i].astype(jnp.float32) for i in range(group))
    grad_resid_part, grad_gain_ffn = norm_back(resid, gain_ffn, grad_ffn_in)
    grad_resid = grad_result + grad_resid_part
    grad_attended, grad_gain_attn = norm_back(attended, gain_attn, grad_resid)
    grad_attended_low = grad_attended.astype(jnp.bfloat16)
    grad_attended_low = line.advance([waiting.pop(0)] if waiting else [], grad_attended_low)
    grad_wout = contract(grad_attended_low, mixed, 0, 0).astype(jnp.bfloat16)
    out_part = owner_part(grad_wout.reshape(group, own_model, -1))
    grad_mixed = jnp.dot(grad_attended_low, w_out, preferred_element_type=jnp.float32).astype(
        jnp.bfloat16
    )
    grad_mixed_rows = grad_mixed.reshape(rows * heads, head_size)
    scores = scores_of()
    probs = jnp.exp(scores - log_total)
    probs_low = probs.astype(jnp.bfloat16).reshape(rows * heads, width)
    grad_probs = contract(grad_mixed_rows, values, 1, 1).reshape(rows, heads, width)
    delta = jnp.sum(grad_probs * probs, axis=-1, keepdims=True)
    grad_scores = (probs * (grad_probs - delta)).astype(jnp.bfloat16).reshape(rows * heads, width)
    grad_scores = line.advance([waiting.pop(0)] if waiting else [], grad_scores)
    grad_query = (jnp.dot(grad_scores, keys, preferred_element_type=jnp.float32) * scale).reshape(
        rows, heads, head_size
    )
    grad_keys = contract(grad_scores, query_rows, 0, 0) * scale
    grad_values = contract(probs_low, grad_mixed_rows, 0, 0)
    grad_pairs = jnp.concatenate([grad_keys, grad_values], axis=1)
    grad_pair = grad_pairs[hops * rows :]
    for step in range(1, hops + 1):
        lower = (hops - step) * rows
        back = passed_along(grad_pairs[lower : lower + rows].astype(jnp.bfloat16), "fsdp", -step)
        grad_pair = grad_pair + back.astype(jnp.float32)
    grad_pair = line.advance([waiting.pop(0)] if waiting else [], grad_pair)
    grad_key = grad_pair[:, :head_size]
    grad_value = grad_pair[:, head_size:]
    _, pull_query = jax.vjp(
        lambda raw, gain: head_post(raw, gain, cosine_heads, sine_heads), query_raw, gain_query
    )
    grad_query_raw, grad_gain_query = pull_query(grad_query)
    _, pull_key = jax.vjp(lambda raw, gain: head_post(raw, gain, cosine, sine), key_raw, gain_key)
    grad_key_raw, grad_gain_key = pull_key(grad_key)
    grad_query_low = grad_query_raw.reshape(rows, heads * head_size).astype(jnp.bfloat16)
    grad_key_low = grad_key_raw.astype(jnp.bfloat16)
    grad_value_low = grad_value.astype(jnp.bfloat16)
    grad_qkv = jnp.concatenate([grad_query_low, grad_key_low, grad_value_low], axis=1)
    grad_wqkv = contract(normed_in, grad_qkv, 0, 0).astype(jnp.bfloat16)
    grad_normed_in = contract(grad_qkv, w_qkv, 1, 1)
    grad_input_part, grad_gain_in = norm_back(residual_in, gain_in, grad_normed_in)
    grad_in = grad_resid + grad_input_part
    gain_grads = jnp.concatenate(
        [
            grad.astype(jnp.bfloat16).reshape(group, -1)
            for grad in (
                grad_gain_in,
                grad_gain_attn,
                grad_gain_ffn,
                grad_gain_out,
                grad_gain_query,
                grad_gain_key,
            )
        ],
        axis=1,
    )
    gain_grads = jnp.pad(gain_grads[:, None, :], ((0, 0), (0, 31), (0, wide - sum(sizes))))
    qkv_part = owner_part(
        jnp.concatenate([grad_wqkv.reshape(group, own_model, wide), gain_grads], axis=1)
    )
    while waiting:
        line.advance([waiting.pop(0)])
    grad_down = whole_grad(line, "down", units)
    grad_down = line.advance([("out", [out_part]), ("qkv", [qkv_part])], grad_down)
    grad_gate_w = whole_grad(line, "gate", units)
    grad_gate_w = line.advance([], grad_gate_w)
    grad_up_w = whole_grad(line, "up", units)
    owned = core_join(line.finished("qkv"), 0).astype(jnp.float32)
    owned_out = core_join(line.finished("out"), 0).astype(jnp.float32)
    owned_query = owned[:own_model, : heads * head_size]
    owned_key = owned[:own_model, heads * head_size : (heads + 1) * head_size]
    owned_value = owned[:own_model, (heads + 1) * head_size :]
    owned_gain_in, owned_gain_attn, owned_gain_ffn, owned_gain_out, owned_gain_query, owned_gain_key = (
        owned[own_model, spots[i] : spots[i + 1]] for i in range(6)
    )
    return (
        hidden_out,
        grad_in,
        owned_gain_in,
        owned_query,
        owned_key,
        owned_value,
        owned_out,
        owned_gain_attn,
        owned_gain_ffn,
        grad_gate_w,
        grad_up_w,
        grad_down,
        owned_gain_out,
        owned_gain_query,
        owned_gain_key,
    )


def solution(mesh):
    return jax.shard_map(
        per_device,
        mesh=mesh,
        in_specs=(
            P(("replica", "fsdp"), None),
            P(("replica", "fsdp"), None),
            P("replica"),
            P(("replica", "fsdp")),
            P("fsdp"),
            P("fsdp", None),
            P("fsdp", None),
            P("fsdp", None),
            P("fsdp", None),
            P("fsdp"),
            P("fsdp"),
            P("fsdp", None),
            P("fsdp", None),
            P("fsdp", None),
            P("fsdp"),
            P("fsdp"),
            P("fsdp"),
        ),
        out_specs=(
            P(("replica", "fsdp"), None),
            P(("replica", "fsdp"), None),
            P("fsdp"),
            P("fsdp", None),
            P("fsdp", None),
            P("fsdp", None),
            P("fsdp", None),
            P("fsdp"),
            P("fsdp"),
            P("fsdp", None),
            P("fsdp", None),
            P("fsdp", None),
            P("fsdp"),
            P("fsdp"),
            P("fsdp"),
        ),
        check_vma=False,
    )
```

```python
import jax
import jax.numpy as jnp
from jax import lax
from jax.experimental import pallas as pl
from jax.experimental.pallas import tpu as pltpu
from jax.sharding import PartitionSpec as P

WINDOW = 512


EPS = 1e-06
NEG = -1e30


def swapped(block, axis, mask):
    route = [(i, i ^ mask) for i in range(lax.axis_size(axis))]
    return lax.ppermute(block, axis, route)


def added(left, right):
    total = left.astype(jnp.float32) + right.astype(jnp.float32)
    return lax.optimization_barrier(total.astype(jnp.bfloat16))


VMEM_LIMIT = 56 * 1024 * 1024


def params(*semantics):
    return pltpu.CompilerParams(vmem_limit_bytes=VMEM_LIMIT)


def dot(left, right, left_dim, right_dim):
    return lax.dot_general(
        left, right, (((left_dim,), (right_dim,)), ((), ())), preferred_element_type=jnp.float32
    )


def after(array, *others):
    place = pl.BlockSpec(memory_space=pl.ANY)
    return pl.pallas_call(
        lambda *refs: None,
        out_shape=jax.ShapeDtypeStruct(array.shape, array.dtype),
        in_specs=[place] * (1 + len(others)),
        out_specs=place,
        input_output_aliases={0: 0},
        name="after",
    )(array, *others)


def scalar(value):
    return value.astype(jnp.int32).reshape(1)


def packed(weights, extra=None):
    half = weights[0].shape[0] // 2
    wide = sum(weight.shape[1] for weight in weights)
    below = 0 if extra is None else extra.shape[0]

    def kernel(core_ref, *refs):
        out_ref = refs[-1]
        for side in range(2):

            @pl.when(core_ref[0] == side)
            def _():
                at = 0
                for ref in refs[: len(weights)]:
                    out_ref[:half, at : at + ref.shape[1]] = ref[side * half : (side + 1) * half, :]
                    at += ref.shape[1]

        if extra is not None:
            out_ref[half:, :] = refs[len(weights)][...]

    arrays = list(weights) + ([] if extra is None else [extra])
    return pl.pallas_call(
        kernel,
        grid_spec=pltpu.PrefetchScalarGridSpec(
            num_scalar_prefetch=1,
            grid=(1,),
            in_specs=[pl.BlockSpec(array.shape, lambda i, core_ref: (0, 0)) for array in arrays],
            out_specs=pl.BlockSpec((half + below, wide), lambda i, core_ref: (0, 0)),
        ),
        out_shape=jax.ShapeDtypeStruct((half + below, wide), jnp.bfloat16),
        compiler_params=params(),
        name="pack",
    )(scalar(lax.axis_index("replica") % 2), *arrays)


def unpacked(weights, got, peers):
    rows = weights[0].shape[0]
    half = rows // 2
    group = len(got) + 1
    wide = sum(weight.shape[1] for weight in weights)
    own = len(weights)

    def kernel(core_ref, rank_ref, *refs):
        out_ref = refs[-1]
        mask = rank_ref[0] ^ pl.program_id(0)

        @pl.when(mask == 0)
        def _():
            at = 0
            for ref in refs[:own]:
                out_ref[:, at : at + ref.shape[1]] = ref[...]
                at += ref.shape[1]

        for other in range(1, group):
            for side in range(2):

                @pl.when((mask == other) & (core_ref[0] == side))
                def _():
                    out_ref[side * half : (side + 1) * half, :] = refs[own + other - 1][:half, :]
                    out_ref[(1 - side) * half : (2 - side) * half, :] = refs[own + group - 2 + other][:half, :]

    arrays = list(weights) + list(got) + list(peers)
    return pl.pallas_call(
        kernel,
        grid_spec=pltpu.PrefetchScalarGridSpec(
            num_scalar_prefetch=2,
            grid=(group,),
            in_specs=[pl.BlockSpec(array.shape, lambda i, *refs: (0, 0)) for array in arrays],
            out_specs=pl.BlockSpec((rows, wide), lambda i, *refs: (i, 0)),
        ),
        out_shape=jax.ShapeDtypeStruct((group * rows, wide), jnp.bfloat16),
        compiler_params=params(),
        name="unpack",
    )(scalar(lax.axis_index("replica") % 2), scalar(lax.axis_index("fsdp")), *arrays)


GELU_A = (2.0 / 3.141592653589793) ** 0.5
GELU_B = 0.044715


def ffn_forward(x, gate_weight, up_weight, down_weight):
    gate = contract(gate_weight, x, 1, 1)
    upper = contract(up_weight, x, 1, 1)
    square = gate * gate
    bend = jnp.tanh(GELU_A * gate * (1.0 + GELU_B * square))
    half = 0.5 + 0.5 * bend
    act = gate * half
    slope = half + 0.5 * gate * (1.0 - bend * bend) * (GELU_A * (1.0 + 3.0 * GELU_B * square))
    hidden = (act * upper).astype(jnp.bfloat16)
    part = contract(hidden, down_weight, 0, 0).astype(jnp.bfloat16)
    return hidden, (slope * upper).astype(jnp.bfloat16), act.astype(jnp.bfloat16), part


def ffn_backward(grad, gate_weight, up_weight, down_weight, slope, act):
    grad_hidden = contract(down_weight, grad, 1, 1)
    grad_gate = (grad_hidden * slope.astype(jnp.float32)).astype(jnp.bfloat16)
    grad_upper = (grad_hidden * act.astype(jnp.float32)).astype(jnp.bfloat16)
    part = contract(grad_gate, gate_weight, 0, 0) + contract(grad_upper, up_weight, 0, 0)
    return grad_gate, grad_upper, part.astype(jnp.bfloat16)


def chunks_of(units):
    return 2 if units % 64 == 0 else 1


def weight_grad(lefts, rights):
    group = len(lefts)
    units, rows = lefts[0].shape
    model = rights[0].shape[1]
    chunks = chunks_of(units)
    tile = units // (2 * chunks)
    core = (lax.axis_index("replica") % 2).astype(jnp.int32).reshape(1)

    def kernel(core_ref, *refs):
        other_ref, mine_ref, left_ref, right_ref = refs[2 * group :]

        @pl.when((pl.program_id(0) == 0) & (pl.program_id(1) == 0))
        def _():
            for spot in range(group):
                right_ref[spot * rows : (spot + 1) * rows, :] = refs[group + spot][...]

        for spot in range(group):
            left_ref[:, spot * rows : (spot + 1) * rows] = refs[spot][...]
        value = dot(left_ref[...], right_ref[...], 1, 0).astype(jnp.bfloat16)

        @pl.when(pl.program_id(0) == 0)
        def _():
            other_ref[0] = value

        @pl.when(pl.program_id(0) == 1)
        def _():
            mine_ref[0] = value

    def left_map(side, chunk, core_ref):
        return (2 * chunk + jnp.where(side == 0, 1 - core_ref[0], core_ref[0]), 0)

    shape = jax.ShapeDtypeStruct((chunks, tile, model), jnp.bfloat16)
    return pl.pallas_call(
        kernel,
        grid_spec=pltpu.PrefetchScalarGridSpec(
            num_scalar_prefetch=1,
            grid=(2, chunks),
            in_specs=[pl.BlockSpec((tile, rows), left_map)] * group
            + [pl.BlockSpec((rows, model), lambda side, chunk, core_ref: (0, 0))] * group,
            out_specs=[
                pl.BlockSpec(
                    (1, tile, model),
                    lambda side, chunk, core_ref: (jnp.where(side == 0, chunk, chunks - 1), 0, 0),
                ),
                pl.BlockSpec(
                    (1, tile, model),
                    lambda side, chunk, core_ref: (jnp.where(side == 0, 0, chunk), 0, 0),
                ),
            ],
            scratch_shapes=[
                pltpu.VMEM((tile, group * rows), jnp.bfloat16),
                pltpu.VMEM((group * rows, model), jnp.bfloat16),
            ],
        ),
        out_shape=[shape, shape],
        compiler_params=params(),
        name="weight_grad",
    )(core, *lefts, *rights)


def allowed_mask(query_segs_ref, key_segs_ref, rows, width):
    gap = (
        width
        - rows
        + lax.broadcasted_iota(jnp.int32, (rows, width), 0)
        - lax.broadcasted_iota(jnp.int32, (rows, width), 1)
    )
    return (gap >= 0) & (gap < WINDOW) & (query_segs_ref[...] == key_segs_ref[...])


def head_probs(query, keys, allowed, scale):
    scores = jnp.where(allowed, dot(query, keys, 1, 1) * scale, NEG)
    expo = jnp.exp(scores - jnp.max(scores, axis=-1, keepdims=True))
    return expo / jnp.sum(expo, axis=-1, keepdims=True)


def attention_specs(rows, size, width, heads):
    head = pl.BlockSpec((rows, size), lambda h: (0, h))
    whole = lambda *shape: pl.BlockSpec(shape, lambda h: (0, 0))
    common = [
        head,
        whole(1, size),
        whole(rows, size // 2),
        whole(rows, size // 2),
        whole(width, 2 * size),
        whole(rows, 1),
        whole(1, width),
    ]
    return head, whole, common


def attention_forward(qkv, gain, cosine, sine, pairs, query_segs, key_segs, heads):
    rows, width, size = qkv.shape[0], pairs.shape[0], pairs.shape[1] // 2
    head, _, common = attention_specs(rows, size, width, heads)

    def kernel(raw_ref, gain_ref, cos_ref, sin_ref, pairs_ref, qseg_ref, kseg_ref, query_ref, mixed_ref):
        query = head_post(raw_ref[...], gain_ref[...], cos_ref[...], sin_ref[...]).astype(jnp.bfloat16)
        query_ref[...] = query
        allowed = allowed_mask(qseg_ref, kseg_ref, rows, width)
        probs = head_probs(query, pairs_ref[:, :size], allowed, size**-0.5).astype(jnp.bfloat16)
        mixed_ref[...] = dot(probs, pairs_ref[:, size:], 1, 0).astype(jnp.bfloat16)

    shape = jax.ShapeDtypeStruct((rows, heads * size), jnp.bfloat16)
    return pl.pallas_call(
        kernel,
        grid=(heads,),
        in_specs=common,
        out_specs=[head, head],
        out_shape=[shape, shape],
        compiler_params=params(),
        name="attention_forward",
    )(qkv, gain, cosine, sine, pairs, query_segs, key_segs)


def attention_backward(qkv, gain, cosine, sine, pairs, query_segs, key_segs, query, grad_mixed, heads):
    rows, width, size = qkv.shape[0], pairs.shape[0], pairs.shape[1] // 2
    head, whole, common = attention_specs(rows, size, width, heads)
    before = width - rows

    def kernel(
        raw_ref, gain_ref, cos_ref, sin_ref, pairs_ref, qseg_ref, kseg_ref, query_ref, grad_ref,
        raw_grad_ref, gain_grad_ref, far_ref, own_ref, acc,
    ):
        step = pl.program_id(0)
        query = query_ref[...]
        grad = grad_ref[...]
        allowed = allowed_mask(qseg_ref, kseg_ref, rows, width)
        keys = pairs_ref[:, :size]
        probs = head_probs(query, keys, allowed, size**-0.5)
        grad_probs = dot(grad, pairs_ref[:, size:], 1, 1)
        delta = jnp.sum(grad_probs * probs, axis=-1, keepdims=True)
        grad_scores = (probs * (grad_probs - delta)).astype(jnp.bfloat16)
        grad_query = dot(grad_scores, keys, 1, 0) * size**-0.5
        grad_keys = dot(grad_scores, query, 0, 0) * size**-0.5
        grad_values = dot(probs.astype(jnp.bfloat16), grad, 0, 0)

        @pl.when(step == 0)
        def _():
            acc[:, :size] = grad_keys
            acc[:, size:] = grad_values

        @pl.when(step > 0)
        def _():
            acc[:, :size] += grad_keys
            acc[:, size:] += grad_values

        first = grad_query[:, : size // 2]
        second = grad_query[:, size // 2 :]
        cosine_part, sine_part = cos_ref[...], sin_ref[...]
        turned = jnp.concatenate(
            [
                first * cosine_part + second * sine_part,
                second * cosine_part - first * sine_part,
            ],
            axis=-1,
        )
        raw = raw_ref[...]
        scale = lax.rsqrt(jnp.mean(raw * raw, axis=-1, keepdims=True) + EPS)
        unit = raw * scale
        inner = turned * gain_ref[...].astype(jnp.float32)
        raw_grad = scale * (inner - unit * jnp.mean(inner * unit, axis=-1, keepdims=True))
        raw_grad_ref[...] = raw_grad.astype(jnp.bfloat16)
        gain_grad = jnp.sum(turned * unit, axis=0, keepdims=True)

        @pl.when(step == 0)
        def _():
            gain_grad_ref[...] = gain_grad

        @pl.when(step > 0)
        def _():
            gain_grad_ref[...] += gain_grad

        @pl.when(step == heads - 1)
        def _():
            far_ref[...] = acc[:before, :].astype(jnp.bfloat16)
            own_ref[...] = acc[before:, :]

    return pl.pallas_call(
        kernel,
        grid=(heads,),
        in_specs=common + [head, head],
        out_specs=[head, whole(1, size), whole(before, 2 * size), whole(rows, 2 * size)],
        out_shape=[
            jax.ShapeDtypeStruct((rows, heads * size), jnp.bfloat16),
            jax.ShapeDtypeStruct((1, size), jnp.float32),
            jax.ShapeDtypeStruct((before, 2 * size), jnp.bfloat16),
            jax.ShapeDtypeStruct((rows, 2 * size), jnp.float32),
        ],
        scratch_shapes=[pltpu.VMEM((width, 2 * size), jnp.float32)],
        compiler_params=params(),
        name="attention_backward",
    )(qkv, gain, cosine, sine, pairs, query_segs, key_segs, query, grad_mixed)


def line_edges():
    places = lax.axis_size("replica") // 2
    outer = places // 2 - 1
    return places, outer


def exchanged(block, pairs):
    route = [(2 * a + core, 2 * b + core) for a, b in pairs for core in range(2)]
    return lax.ppermute(block, "replica", route)


class Line:
    def __init__(self):
        self.places, self.outer = line_edges()
        self.steps = 2 * self.outer + 1
        self.moving = []
        self.done = {}

    def advance(self, fresh, gate=None):
        places, outer, steps = self.places, self.outer, self.steps
        place = (lax.axis_index("replica") // 2).astype(jnp.int32).reshape(1)
        operands, plan = [], []

        def operand(entry):
            array, index = entry if isinstance(entry, tuple) else (entry, None)
            for spot, (known, known_index) in enumerate(operands):
                if known is array and known_index == index:
                    return spot
            operands.append((array, index))
            return len(operands) - 1

        for name, block, step, far in self.moving:
            plan.append((name, step + 1, [operand(block), operand(far)], step))
        for name, terms in fresh:
            plan.append((name, 0, [operand(term) for term in terms], None))
        if not plan:
            return gate
        sizes = [operands[spots[0]][0].shape[-2:] for _, _, spots, _ in plan]
        by_step = {step: index for index, (_, step, _, _) in enumerate(plan)}
        pairs = []
        for edge in range(outer):
            inward, outward = by_step.get(edge), by_step.get(2 * outer - edge)
            if inward is not None and outward is not None and sizes[inward] == sizes[outward]:
                pairs.append((edge, inward, outward))
        cuts = 3 if all(size[0] % 48 == 0 for size in sizes) else 1

        def kernel(place_ref, *refs):
            here = place_ref[0]
            inputs = refs[: len(operands)]
            if gate is not None:
                refs = refs[: len(operands)] + refs[len(operands) + 1 :]
            outputs = refs[len(operands) :]
            states = []
            for spot, (_, _, terms, last) in enumerate(plan):
                value = inputs[terms[0]][...]
                if len(terms) == 2:
                    far = inputs[terms[1]][...]
                    total = (value.astype(jnp.float32) + far.astype(jnp.float32)).astype(jnp.bfloat16)
                    if last is None:
                        value = total
                    elif last <= outer:
                        edge = last
                        value = jnp.where((here == edge + 1) | (here == places - 2 - edge), total, value)
                    else:
                        edge = 2 * outer - last
                        value = jnp.where((here == edge) | (here == places - 1 - edge), far, value)
                states.append(value)
                outputs[spot][...] = value
            for spot, (edge, inward, outward) in enumerate(pairs):
                outputs[len(plan) + spot][...] = jnp.where(
                    (here == edge) | (here == places - 1 - edge), states[inward], states[outward]
                )

        def spec(size, index):
            if index is None:
                return pl.BlockSpec((size[0] // cuts, size[1]), lambda i, place_ref: (i, 0))
            return pl.BlockSpec((None, size[0] // cuts, size[1]), lambda i, place_ref: (index, i, 0))

        in_specs = [spec(array.shape[-2:], index) for array, index in operands]
        arrays = [array for array, _ in operands]
        out_sizes = sizes + [sizes[inward] for _, inward, _ in pairs]
        out_specs = [spec(size, None) for size in out_sizes]
        out_shape = [jax.ShapeDtypeStruct(size, jnp.bfloat16) for size in out_sizes]
        aliases = {}
        if gate is not None:
            aliases = {1 + len(arrays): len(out_shape)}
            in_specs.append(pl.BlockSpec(memory_space=pl.ANY))
            out_specs.append(pl.BlockSpec(memory_space=pl.ANY))
            out_shape.append(jax.ShapeDtypeStruct(gate.shape, gate.dtype))
            arrays.append(gate)
        outs = pl.pallas_call(
            kernel,
            grid_spec=pltpu.PrefetchScalarGridSpec(
                num_scalar_prefetch=1, grid=(cuts,), in_specs=in_specs, out_specs=out_specs
            ),
            out_shape=out_shape,
            input_output_aliases=aliases,
            compiler_params=params(),
            name="line_step",
        )(place, *arrays)
        received = {}
        for spot, (edge, inward, outward) in enumerate(pairs):
            ends = [(edge, edge + 1), (places - 1 - edge, places - 2 - edge)]
            far = exchanged(outs[len(plan) + spot], ends + [(b, a) for a, b in ends])
            received[inward] = received[outward] = far
        self.moving = []
        for index, (name, step, _, _) in enumerate(plan):
            block = outs[index]
            if step == steps:
                self.done[name] = block
                continue
            if index not in received:
                edge = step if step <= outer else 2 * outer - step
                route = [(edge, edge + 1), (places - 1 - edge, places - 2 - edge)]
                if step > outer:
                    route = [(b, a) for a, b in route]
                received[index] = exchanged(block, route)
            self.moving.append((name, block, step, received[index]))
        return outs[-1]

    def finished(self, name):
        while name not in self.done:
            self.advance([])
        return self.done[name]


def line_names(name, units):
    return [(name, chunk) for chunk in range(chunks_of(units))]


def whole_grad(lines, name, units, dtype=jnp.float32):
    names = line_names(name, units)
    mines = [lines[chunk[1]].finished(chunk) for chunk in names]
    others = [swapped(mine, "replica", 1) for mine in mines]
    chunks = len(mines)
    tile, model = mines[0].shape
    core = (lax.axis_index("replica") % 2).astype(jnp.int32).reshape(1)

    def kernel(core_ref, *refs):
        out_ref = refs[-1]
        for chunk in range(chunks):
            for side in range(2):

                @pl.when((pl.program_id(0) == chunk) & (pl.program_id(1) == side))
                def _():
                    @pl.when(core_ref[0] == side)
                    def _():
                        out_ref[...] = refs[chunk][...].astype(dtype)

                    @pl.when(core_ref[0] != side)
                    def _():
                        out_ref[...] = refs[chunks + chunk][...].astype(dtype)

    return pl.pallas_call(
        kernel,
        grid_spec=pltpu.PrefetchScalarGridSpec(
            num_scalar_prefetch=1,
            grid=(chunks, 2),
            in_specs=[pl.BlockSpec((tile, model), lambda chunk, side, core_ref: (0, 0))] * (2 * chunks),
            out_specs=pl.BlockSpec((tile, model), lambda chunk, side, core_ref: (2 * chunk + side, 0)),
        ),
        out_shape=jax.ShapeDtypeStruct((units, model), dtype),
        compiler_params=params(),
        name="whole_grad",
    )(core, *mines, *others)


def halves(block, axis):
    core = lax.axis_index("replica") % 2
    half = block.shape[axis] // 2
    mine = lax.dynamic_slice_in_dim(block, core * half, half, axis)
    other = lax.dynamic_slice_in_dim(block, (1 - core) * half, half, axis)
    return mine, other


def joined(mine, other, axis):
    core = lax.axis_index("replica") % 2
    return jnp.where(
        core == 0,
        jnp.concatenate([mine, other], axis=axis),
        jnp.concatenate([other, mine], axis=axis),
    )


def core_sum(block, axis):
    mine, other = halves(block, axis)
    return added(mine, swapped(other, "replica", 1))


def core_join(block, axis):
    return joined(block, swapped(block, "replica", 1), axis)


def owner_part(blocks):
    rank = lax.axis_index("fsdp")
    part = core_sum(blocks, 1)
    total = lax.dynamic_index_in_dim(part, rank, 0, keepdims=False).astype(jnp.float32)
    for mask in range(1, blocks.shape[0]):
        far = swapped(lax.dynamic_index_in_dim(part, rank ^ mask, 0, keepdims=False), "fsdp", mask)
        total = total + far.astype(jnp.float32)
    return lax.optimization_barrier(total.astype(jnp.bfloat16))


def fetched(block):
    got = [swapped(block, "fsdp", mask) for mask in range(1, lax.axis_size("fsdp"))]
    return got, [swapped(part, "replica", 1) for part in got]


def passed_along(block, axis, distance):
    devices = range(lax.axis_size(axis))
    route = [(i - distance, i) for i in devices if i - distance in devices]
    return lax.ppermute(block, axis, route)


def contract(left, right, left_dim, right_dim):
    return lax.dot_general(
        left, right, (((left_dim,), (right_dim,)), ((), ())), preferred_element_type=jnp.float32
    )


def normed(value, gain):
    return value * lax.rsqrt(jnp.mean(value * value, axis=-1, keepdims=True) + EPS) * gain


def norm_back(value, gain, grad):
    _, pull = jax.vjp(normed, value, gain)
    return pull(grad)


def tables(places, half):
    freq = 10000.0 ** (-(2.0 * jnp.arange(half, dtype=jnp.float32)) / (2 * half))
    angle = places.astype(jnp.float32)[:, None] * freq[None, :]
    return (jnp.cos(angle), jnp.sin(angle))


def rotate(value, cosine, sine):
    half = value.shape[-1] // 2
    first = value[..., :half]
    second = value[..., half:]
    return jnp.concatenate(
        [first * cosine - second * sine, second * cosine + first * sine], axis=-1
    )


def head_post(raw, gain, cosine, sine):
    return rotate(normed(raw, gain), cosine, sine)


def per_device(
    hidden_in,
    out_grad,
    segments,
    positions,
    norm_in,
    query_weight,
    key_weight,
    value_weight,
    out_weight,
    norm_attn,
    norm_ffn,
    gate_weight,
    up_weight,
    down_weight,
    norm_out,
    query_gain,
    key_gain,
):
    rows = hidden_in.shape[0]
    rank = lax.axis_index("fsdp")
    group = lax.axis_size("fsdp")
    masks = range(1, group)
    head_size = key_weight.shape[1]
    heads = query_weight.shape[1] // head_size
    model = hidden_in.shape[1]
    own_model = norm_in.shape[0]
    own_head = query_gain.shape[0]
    hops = (WINDOW - 1) // rows + 1
    scale = head_size ** (-0.5)
    qkv_weights = (query_weight, key_weight, value_weight)
    wide = sum(weight.shape[1] for weight in qkv_weights)
    sizes = [own_model] * 4 + [own_head] * 2
    gains = jnp.concatenate([norm_in, norm_attn, norm_ffn, norm_out, query_gain, key_gain])
    gains = jnp.pad(gains[None, :], ((0, 15), (0, wide - sum(sizes))))
    got, peers = fetched(packed(qkv_weights, gains))
    w_qkv = unpacked(qkv_weights, got, peers)
    gain_stack = jnp.stack([gains[0]] + [part[-16] for part in got])
    gain_rows = [
        lax.dynamic_index_in_dim(gain_stack, rank ^ i, 0, keepdims=False) for i in range(group)
    ]
    got, peers = fetched(after(packed([out_weight]), w_qkv))
    spots = [sum(sizes[:i]) for i in range(7)]
    gain_in, gain_attn, gain_ffn, gain_out, gain_query, gain_key = (
        jnp.concatenate([row[spots[i] : spots[i + 1]] for row in gain_rows]) for i in range(6)
    )
    residual_in = hidden_in.astype(jnp.float32)
    normed_in = normed(residual_in, gain_in).astype(jnp.bfloat16)
    qkv = jnp.dot(normed_in, w_qkv, preferred_element_type=jnp.float32)
    key_raw = qkv[:, heads * head_size : (heads + 1) * head_size]
    value_new = qkv[:, (heads + 1) * head_size :].astype(jnp.bfloat16)
    cosine, sine = tables(positions, head_size // 2)
    key_new = head_post(key_raw, gain_key, cosine, sine).astype(jnp.bfloat16)
    pair_new = jnp.concatenate([key_new, value_new], axis=1)
    parts = [pair_new]
    for step in range(1, hops + 1):
        parts.insert(0, passed_along(pair_new, "fsdp", step))
    pairs = jnp.concatenate(parts, axis=0)
    width = pairs.shape[0]
    seg_padded = jnp.concatenate([jnp.full((hops * rows,), -1, jnp.int32), segments], axis=0)
    key_segs = lax.dynamic_slice_in_dim(seg_padded, rank * rows, width, 0)
    query_segs = lax.dynamic_slice_in_dim(segments, rank * rows, rows, 0)
    attention_args = (
        qkv,
        gain_query[None, :],
        cosine,
        sine,
        pairs,
        query_segs[:, None],
        key_segs[None, :],
    )
    query_new, mixed = attention_forward(*attention_args, heads)
    w_out = unpacked([out_weight], got, peers)
    attended = contract(mixed, w_out, 1, 1)
    resid = residual_in + normed(attended, gain_attn)
    ffn_in = normed(resid, gain_ffn).astype(jnp.bfloat16)
    ffn_blocks = [ffn_in] + [swapped(ffn_in, "fsdp", mask) for mask in masks]
    hiddens, slopes, acts, parts = [], [], [], []
    for mask in range(group):
        hidden, slope, act, part = ffn_forward(ffn_blocks[mask], gate_weight, up_weight, down_weight)
        parts.append(part)
        hiddens.append(hidden)
        slopes.append(slope)
        acts.append(act)
    parts = parts[:1] + [swapped(parts[mask], "fsdp", mask) for mask in masks]
    branch = sum(part.astype(jnp.float32) for part in parts)
    result = resid + normed(branch, gain_out)
    hidden_out = result.astype(jnp.bfloat16)
    grad_result = out_grad.astype(jnp.float32)
    grad_branch, grad_gain_out = norm_back(branch, gain_out, grad_result)
    grad_branch_low = grad_branch.astype(jnp.bfloat16)
    pieces = [grad_branch_low] + [swapped(grad_branch_low, "fsdp", mask) for mask in masks]
    units = gate_weight.shape[0]
    lines = [Line(), Line()]

    def fresh(name, other, mine):
        far = swapped(other, "replica", 1)
        return [(key, [(mine, key[1]), (far, key[1])]) for key in line_names(name, units)]

    grad_gates, grad_uppers, returned = {}, {}, {}
    early = group // 2
    for mask in range(group):
        if mask == early:
            pieces[mask] = after(pieces[mask], part)
            waiting = fresh("down", *weight_grad(hiddens, pieces))
            pieces[mask] = lines[0].advance([waiting.pop(0)], pieces[mask])
        if mask == early + 1 and waiting:
            pieces[mask] = lines[1].advance([waiting.pop(0)], pieces[mask])
        grad_gates[mask], grad_uppers[mask], part = ffn_backward(
            pieces[mask], gate_weight, up_weight, down_weight, slopes[mask], acts[mask]
        )
        if mask + 1 < early:
            pieces[mask + 1] = after(pieces[mask + 1], part)
        returned[mask] = swapped(part, "fsdp", mask) if mask else part
    waiting = []
    waiting += fresh("gate", *weight_grad([grad_gates[i] for i in range(group)], ffn_blocks))
    waiting += fresh("up", *weight_grad([grad_uppers[i] for i in range(group)], ffn_blocks))

    def advance(spot, gate=None):
        ready = [entry for entry in waiting if entry[0][1] == spot][:1]
        for entry in ready:
            waiting.remove(entry)
        return lines[spot].advance(ready, gate)

    returned[0] = advance(0, returned[0])
    grad_ffn_in = sum(returned[i].astype(jnp.float32) for i in range(group))
    grad_resid_part, grad_gain_ffn = norm_back(resid, gain_ffn, grad_ffn_in)
    grad_resid = grad_result + grad_resid_part
    grad_attended, grad_gain_attn = norm_back(attended, gain_attn, grad_resid)
    grad_attended_low = advance(1, grad_attended.astype(jnp.bfloat16))
    grad_wout = contract(grad_attended_low, mixed, 0, 0).astype(jnp.bfloat16)
    grad_mixed = jnp.dot(grad_attended_low, w_out, preferred_element_type=jnp.float32).astype(
        jnp.bfloat16
    )
    grad_query_low, grad_gain_query, grad_far, grad_pair = attention_backward(
        *attention_args, query_new, grad_mixed, heads
    )
    grad_gain_query = grad_gain_query[0]
    grad_far = advance(0, grad_far)
    for step in range(1, hops + 1):
        lower = (hops - step) * rows
        back = passed_along(grad_far[lower : lower + rows], "fsdp", -step)
        grad_pair = grad_pair + back.astype(jnp.float32)
    grad_pair = advance(1, grad_pair)
    grad_key = grad_pair[:, :head_size]
    grad_value_low = grad_pair[:, head_size:].astype(jnp.bfloat16)
    _, pull_key = jax.vjp(lambda raw, gain: head_post(raw, gain, cosine, sine), key_raw, gain_key)
    grad_key_raw, grad_gain_key = pull_key(grad_key)
    grad_key_low = grad_key_raw.astype(jnp.bfloat16)
    grad_qkv = jnp.concatenate([grad_query_low, grad_key_low, grad_value_low], axis=1)
    grad_wqkv = contract(normed_in, grad_qkv, 0, 0).astype(jnp.bfloat16)
    grad_normed_in = contract(grad_qkv, w_qkv, 1, 1)
    grad_input_part, grad_gain_in = norm_back(residual_in, gain_in, grad_normed_in)
    grad_in = grad_resid + grad_input_part
    gain_grads = jnp.concatenate(
        [
            grad.astype(jnp.bfloat16).reshape(group, -1)
            for grad in (
                grad_gain_in,
                grad_gain_attn,
                grad_gain_ffn,
                grad_gain_out,
                grad_gain_query,
                grad_gain_key,
            )
        ],
        axis=1,
    )
    gain_grads = jnp.pad(gain_grads[:, None, :], ((0, 0), (0, 31), (0, wide - sum(sizes))))
    grad_weights = jnp.concatenate([grad_wqkv, grad_wout], axis=1).reshape(group, own_model, -1)
    gain_grads = jnp.pad(gain_grads, ((0, 0), (0, 0), (0, grad_wout.shape[1])))
    weights_part = owner_part(jnp.concatenate([grad_weights, gain_grads], axis=1))
    advance(0)
    advance(1)
    lines[0].advance([("weights", [weights_part])])
    lines[1].advance([])
    grad_down = whole_grad(lines, "down", units)
    grad_down = lines[0].advance([], grad_down)
    grad_gate_w = whole_grad(lines, "gate", units)
    grad_gate_w = lines[1].advance([], grad_gate_w)
    grad_up_w = whole_grad(lines, "up", units)
    owned = core_join(lines[0].finished("weights"), 0).astype(jnp.float32)
    owned_out = owned[:own_model, wide:]
    owned_query = owned[:own_model, : heads * head_size]
    owned_key = owned[:own_model, heads * head_size : (heads + 1) * head_size]
    owned_value = owned[:own_model, (heads + 1) * head_size : wide]
    owned_gain_in, owned_gain_attn, owned_gain_ffn, owned_gain_out, owned_gain_query, owned_gain_key = (
        owned[own_model, spots[i] : spots[i + 1]] for i in range(6)
    )
    return (
        hidden_out,
        grad_in,
        owned_gain_in,
        owned_query,
        owned_key,
        owned_value,
        owned_out,
        owned_gain_attn,
        owned_gain_ffn,
        grad_gate_w,
        grad_up_w,
        grad_down,
        owned_gain_out,
        owned_gain_query,
        owned_gain_key,
    )


def solution(mesh):
    return jax.shard_map(
        per_device,
        mesh=mesh,
        in_specs=(
            P(("replica", "fsdp"), None),
            P(("replica", "fsdp"), None),
            P("replica"),
            P(("replica", "fsdp")),
            P("fsdp"),
            P("fsdp", None),
            P("fsdp", None),
            P("fsdp", None),
            P("fsdp", None),
            P("fsdp"),
            P("fsdp"),
            P("fsdp", None),
            P("fsdp", None),
            P("fsdp", None),
            P("fsdp"),
            P("fsdp"),
            P("fsdp"),
        ),
        out_specs=(
            P(("replica", "fsdp"), None),
            P(("replica", "fsdp"), None),
            P("fsdp"),
            P("fsdp", None),
            P("fsdp", None),
            P("fsdp", None),
            P("fsdp", None),
            P("fsdp"),
            P("fsdp"),
            P("fsdp", None),
            P("fsdp", None),
            P("fsdp", None),
            P("fsdp"),
            P("fsdp"),
            P("fsdp"),
        ),
        check_vma=False,
    )
```

```python
import jax
import jax.numpy as jnp
from jax import lax
from jax.experimental import pallas as pl
from jax.experimental.pallas import tpu as pltpu
from jax.sharding import PartitionSpec as P

WINDOW = 512


EPS = 1e-06
NEG = -1e30


def swapped(block, axis, mask):
    route = [(i, i ^ mask) for i in range(lax.axis_size(axis))]
    return lax.ppermute(block, axis, route)


def added(left, right):
    total = left.astype(jnp.float32) + right.astype(jnp.float32)
    return lax.optimization_barrier(total.astype(jnp.bfloat16))


VMEM_LIMIT = 56 * 1024 * 1024


def params(*semantics):
    return pltpu.CompilerParams(vmem_limit_bytes=VMEM_LIMIT)


def dot(left, right, left_dim, right_dim):
    return lax.dot_general(
        left, right, (((left_dim,), (right_dim,)), ((), ())), preferred_element_type=jnp.float32
    )


def after(array, *others):
    place = pl.BlockSpec(memory_space=pl.ANY)
    return pl.pallas_call(
        lambda *refs: None,
        out_shape=jax.ShapeDtypeStruct(array.shape, array.dtype),
        in_specs=[place] * (1 + len(others)),
        out_specs=place,
        input_output_aliases={0: 0},
        name="after",
    )(array, *others)


def scalar(value):
    return value.astype(jnp.int32).reshape(1)


def packed(weights, gains=()):
    half = weights[0].shape[0] // 2
    wide = sum(weight.shape[1] for weight in weights)
    below = 16 if gains else 0

    def kernel(core_ref, *refs):
        out_ref = refs[-1]
        if gains:
            out_ref[half:, :] = jnp.zeros((below, wide), jnp.bfloat16)
        for spot in range(len(gains)):
            ref = refs[len(weights) + spot]
            out_ref[half + spot : half + spot + 1, : ref.shape[1]] = ref[...]
        for side in range(2):

            @pl.when(core_ref[0] == side)
            def _():
                at = 0
                for ref in refs[: len(weights)]:
                    out_ref[:half, at : at + ref.shape[1]] = ref[side * half : (side + 1) * half, :]
                    at += ref.shape[1]

    arrays = list(weights) + [gain[None, :] for gain in gains]
    return pl.pallas_call(
        kernel,
        grid_spec=pltpu.PrefetchScalarGridSpec(
            num_scalar_prefetch=1,
            grid=(1,),
            in_specs=[pl.BlockSpec(array.shape, lambda i, core_ref: (0, 0)) for array in arrays],
            out_specs=pl.BlockSpec((half + below, wide), lambda i, core_ref: (0, 0)),
        ),
        out_shape=jax.ShapeDtypeStruct((half + below, wide), jnp.bfloat16),
        compiler_params=params(),
        name="pack",
    )(scalar(lax.axis_index("replica") % 2), *arrays)


def unpacked(weights, got, peers):
    rows = weights[0].shape[0]
    half = rows // 2
    group = len(got) + 1
    wide = sum(weight.shape[1] for weight in weights)
    own = len(weights)

    def kernel(core_ref, rank_ref, *refs):
        out_ref = refs[-1]
        mask = rank_ref[0] ^ pl.program_id(0)

        @pl.when(mask == 0)
        def _():
            at = 0
            for ref in refs[:own]:
                out_ref[:, at : at + ref.shape[1]] = ref[...]
                at += ref.shape[1]

        for other in range(1, group):
            for side in range(2):

                @pl.when((mask == other) & (core_ref[0] == side))
                def _():
                    out_ref[side * half : (side + 1) * half, :] = refs[own + other - 1][:half, :]
                    out_ref[(1 - side) * half : (2 - side) * half, :] = refs[own + group - 2 + other][:half, :]

    arrays = list(weights) + list(got) + list(peers)
    return pl.pallas_call(
        kernel,
        grid_spec=pltpu.PrefetchScalarGridSpec(
            num_scalar_prefetch=2,
            grid=(group,),
            in_specs=[pl.BlockSpec(array.shape, lambda i, *refs: (0, 0)) for array in arrays],
            out_specs=pl.BlockSpec((rows, wide), lambda i, *refs: (i, 0)),
        ),
        out_shape=jax.ShapeDtypeStruct((group * rows, wide), jnp.bfloat16),
        compiler_params=params(),
        name="unpack",
    )(scalar(lax.axis_index("replica") % 2), scalar(lax.axis_index("fsdp")), *arrays)


GELU_A = (2.0 / 3.141592653589793) ** 0.5
GELU_B = 0.044715


def ffn_forward(x, gate_weight, up_weight, down_weight):
    gate = contract(gate_weight, x, 1, 1)
    upper = contract(up_weight, x, 1, 1)
    square = gate * gate
    bend = jnp.tanh(GELU_A * gate * (1.0 + GELU_B * square))
    half = 0.5 + 0.5 * bend
    act = gate * half
    slope = half + 0.5 * gate * (1.0 - bend * bend) * (GELU_A * (1.0 + 3.0 * GELU_B * square))
    hidden = (act * upper).astype(jnp.bfloat16)
    part = contract(hidden, down_weight, 0, 0).astype(jnp.bfloat16)
    return hidden, (slope * upper).astype(jnp.bfloat16), act.astype(jnp.bfloat16), part


def ffn_backward(grad, gate_weight, up_weight, down_weight, slope, act):
    grad_hidden = contract(down_weight, grad, 1, 1)
    grad_gate = (grad_hidden * slope.astype(jnp.float32)).astype(jnp.bfloat16)
    grad_upper = (grad_hidden * act.astype(jnp.float32)).astype(jnp.bfloat16)
    part = contract(grad_gate, gate_weight, 0, 0) + contract(grad_upper, up_weight, 0, 0)
    return grad_gate, grad_upper, part.astype(jnp.bfloat16)


def tile_of(size, most):
    return max(tile for tile in range(16, most + 1, 16) if size % tile == 0)


def ffn_backward_blocks(grads, gate_weight, up_weight, down_weight, slopes, acts):
    count = len(grads)
    rows, model = grads[0].shape
    units = gate_weight.shape[0]
    tile = tile_of(units, 432)
    steps = units // tile

    def kernel(*refs):
        step = pl.program_id(0)
        grad_refs, refs = refs[:count], refs[count:]
        (gate_ref, up_ref, down_ref), refs = refs[:3], refs[3:]
        slope_refs, act_refs, refs = refs[:count], refs[count : 2 * count], refs[2 * count :]
        gate_outs, up_outs, part_outs, (grad_ref, acc) = (
            refs[:count],
            refs[count : 2 * count],
            refs[2 * count : 3 * count],
            refs[3 * count :],
        )

        @pl.when(step == 0)
        def _():
            for spot in range(count):
                grad_ref[spot * rows : (spot + 1) * rows, :] = grad_refs[spot][...]
            acc[...] = jnp.zeros_like(acc)

        grad_hidden = dot(down_ref[...], grad_ref[...], 1, 1)
        slope = jnp.concatenate([ref[...] for ref in slope_refs], axis=1).astype(jnp.float32)
        act = jnp.concatenate([ref[...] for ref in act_refs], axis=1).astype(jnp.float32)
        grad_gate = (grad_hidden * slope).astype(jnp.bfloat16)
        grad_upper = (grad_hidden * act).astype(jnp.bfloat16)
        for spot in range(count):
            gate_outs[spot][...] = grad_gate[:, spot * rows : (spot + 1) * rows]
            up_outs[spot][...] = grad_upper[:, spot * rows : (spot + 1) * rows]
        acc[...] += dot(grad_gate, gate_ref[...], 0, 0) + dot(grad_upper, up_ref[...], 0, 0)

        @pl.when(step == steps - 1)
        def _():
            for spot in range(count):
                part_outs[spot][...] = acc[spot * rows : (spot + 1) * rows, :].astype(jnp.bfloat16)

    weight = pl.BlockSpec((tile, model), lambda i: (i, 0))
    flat = pl.BlockSpec((tile, rows), lambda i: (i, 0))
    whole = pl.BlockSpec((rows, model), lambda i: (0, 0))
    kept = jax.ShapeDtypeStruct((units, rows), jnp.bfloat16)
    outs = pl.pallas_call(
        kernel,
        grid=(steps,),
        out_shape=[kept] * (2 * count) + [jax.ShapeDtypeStruct((rows, model), jnp.bfloat16)] * count,
        in_specs=[whole] * count + [weight] * 3 + [flat] * (2 * count),
        out_specs=[flat] * (2 * count) + [whole] * count,
        scratch_shapes=[
            pltpu.VMEM((count * rows, model), jnp.bfloat16),
            pltpu.VMEM((count * rows, model), jnp.float32),
        ],
        compiler_params=params(),
        name="ffn_backward",
    )(*grads, gate_weight, up_weight, down_weight, *slopes, *acts)
    return outs[:count], outs[count : 2 * count], outs[2 * count :]


def norm_pull(value, gain, grad):
    scale = lax.rsqrt(jnp.mean(value * value, axis=-1, keepdims=True) + EPS)
    unit = value * scale
    inner = grad * gain
    return scale * (inner - unit * jnp.mean(inner * unit, axis=-1, keepdims=True)), grad * unit


def resid_backward(parts, resid, attended, out_grad, gain_ffn, gain_attn, w_out):
    count = len(parts)
    rows, model = resid.shape
    tile = min(rows, 128)

    def kernel(*refs):
        part_refs, refs = refs[:count], refs[count:]
        resid_ref, attended_ref, out_ref, ffn_ref, attn_ref, weight_ref, refs = *refs[:6], refs[6:]
        grad_resid_ref, grad_attended_ref, grad_mixed_ref, ffn_grad_ref, attn_grad_ref = refs
        grad = sum(ref[...].astype(jnp.float32) for ref in part_refs)
        pulled, ffn_rows = norm_pull(resid_ref[...], ffn_ref[...].astype(jnp.float32), grad)
        grad_resid = out_ref[...].astype(jnp.float32) + pulled
        grad_resid_ref[...] = grad_resid
        pulled, attn_rows = norm_pull(attended_ref[...], attn_ref[...].astype(jnp.float32), grad_resid)
        grad_attended = pulled.astype(jnp.bfloat16)
        grad_attended_ref[...] = grad_attended
        grad_mixed_ref[...] = dot(grad_attended, weight_ref[...], 1, 0).astype(jnp.bfloat16)
        ffn_grad = jnp.sum(ffn_rows, axis=0, keepdims=True)
        attn_grad = jnp.sum(attn_rows, axis=0, keepdims=True)

        @pl.when(pl.program_id(0) == 0)
        def _():
            ffn_grad_ref[...] = ffn_grad
            attn_grad_ref[...] = attn_grad

        @pl.when(pl.program_id(0) > 0)
        def _():
            ffn_grad_ref[...] += ffn_grad
            attn_grad_ref[...] += attn_grad

    block = pl.BlockSpec((tile, model), lambda i: (i, 0))
    vector = pl.BlockSpec((1, model), lambda i: (0, 0))
    inner = w_out.shape[1]
    return pl.pallas_call(
        kernel,
        grid=(rows // tile,),
        in_specs=[block] * (count + 3) + [vector] * 2 + [pl.BlockSpec(w_out.shape, lambda i: (0, 0))],
        out_specs=[block, block, pl.BlockSpec((tile, inner), lambda i: (i, 0)), vector, vector],
        out_shape=[
            jax.ShapeDtypeStruct((rows, model), jnp.float32),
            jax.ShapeDtypeStruct((rows, model), jnp.bfloat16),
            jax.ShapeDtypeStruct((rows, inner), jnp.bfloat16),
            jax.ShapeDtypeStruct((1, model), jnp.float32),
            jax.ShapeDtypeStruct((1, model), jnp.float32),
        ],
        compiler_params=params(),
        name="resid_backward",
    )(*parts, resid, attended, out_grad, gain_ffn[None, :], gain_attn[None, :], w_out)


def input_backward(
    own_pair, backs, qkv, cosine, sine, gain_key, normed_in, grad_query, w_qkv, hidden_in, gain_in, grad_resid,
    grad_attended, mixed, gain_grads, group,
):
    rows, model = hidden_in.shape
    size = own_pair.shape[1] // 2
    inner = grad_query.shape[1]
    own_rows = model // group
    half = inner + size
    hops = len(backs)
    count = len(gain_grads)

    def kernel(core_ref, *refs):
        pair_ref, refs = refs[0], refs[1:]
        back_refs, refs = refs[:hops], refs[hops:]
        (
            raw_ref, cos_ref, sin_ref, key_gain_ref, normed_ref, query_ref, weight_ref, x_ref, gain_ref, resid_ref,
            attended_ref, mixed_ref, refs,
        ) = *refs[:12], refs[12:]
        gain_refs, refs = refs[:count], refs[count:]
        other_ref, mine_ref, grad_in_ref, rows_ref = refs
        pair = pair_ref[...] + sum(ref[...].astype(jnp.float32) for ref in back_refs)
        first = pair[:, : size // 2]
        second = pair[:, size // 2 : size]
        turned = jnp.concatenate(
            [
                first * cos_ref[...] + second * sin_ref[...],
                second * cos_ref[...] - first * sin_ref[...],
            ],
            axis=-1,
        )
        pulled, key_rows = norm_pull(raw_ref[...], key_gain_ref[...].astype(jnp.float32), turned)
        grad_key = pulled.astype(jnp.bfloat16)
        grad_value = pair[:, size:].astype(jnp.bfloat16)
        grad_normed = (
            dot(query_ref[...], weight_ref[:, :inner], 1, 1)
            + dot(grad_key, weight_ref[:, inner:half], 1, 1)
            + dot(grad_value, weight_ref[:, half:], 1, 1)
        )
        pulled, in_rows = norm_pull(
            x_ref[...].astype(jnp.float32), gain_ref[...].astype(jnp.float32), grad_normed
        )
        grad_in_ref[...] = resid_ref[...] + pulled
        rows_ref[...] = jnp.zeros_like(rows_ref)
        rows_ref[0:1, :model] = jnp.sum(in_rows, axis=0, keepdims=True)
        rows_ref[1:2, :size] = jnp.sum(key_rows, axis=0, keepdims=True)
        for spot in range(count):
            rows_ref[2 + spot : 3 + spot, : gain_refs[spot].shape[1]] = gain_refs[spot][...].astype(
                jnp.float32
            )
        gains = rows_ref[...].astype(jnp.bfloat16)

        def write(ref, side):
            pieces = (
                [(normed_ref, query_ref[...], 0, inner), (normed_ref, grad_key, inner, half)]
                if side == 0
                else [(normed_ref, grad_value, 0, size), (attended_ref, mixed_ref[...], size, half)]
            )
            for left, right, begin, end in pieces:
                value = dot(left[...], right, 0, 0).astype(jnp.bfloat16)
                for owner in range(group):
                    ref[owner, :own_rows, begin:end] = value[owner * own_rows : (owner + 1) * own_rows]
            for owner in range(group):
                ref[owner, own_rows:, :] = gains

        for core in range(2):

            @pl.when(core_ref[0] == core)
            def _():
                write(other_ref, 1 - core)
                write(mine_ref, core)

    def whole(array):
        return pl.BlockSpec(array.shape, lambda i, core_ref: (0,) * len(array.shape))

    arrays = [
        own_pair, *backs, qkv, cosine, sine, gain_key[None, :], normed_in, grad_query, w_qkv, hidden_in,
        gain_in[None, :], grad_resid, grad_attended, mixed, *gain_grads,
    ]
    in_specs = [whole(array) for array in arrays]
    in_specs[1 + hops] = pl.BlockSpec((rows, size), lambda i, core_ref: (0, inner // size))
    shape = jax.ShapeDtypeStruct((group, own_rows + 16, half), jnp.bfloat16)
    grad_in = jax.ShapeDtypeStruct((rows, model), jnp.float32)
    return pl.pallas_call(
        kernel,
        grid_spec=pltpu.PrefetchScalarGridSpec(
            num_scalar_prefetch=1,
            grid=(1,),
            in_specs=in_specs,
            out_specs=[whole(shape), whole(shape), whole(grad_in)],
            scratch_shapes=[pltpu.VMEM((16, half), jnp.float32)],
        ),
        out_shape=[shape, shape, grad_in],
        compiler_params=params(),
        name="input_backward",
    )(scalar(lax.axis_index("replica") % 2), *arrays)


def chunks_of(units):
    return 2 if units % 64 == 0 else 1


def weight_grad(sets, rights):
    group = len(rights)
    count = len(sets)
    units, rows = sets[0][0].shape
    model = rights[0].shape[1]
    chunks = chunks_of(units)
    tile = units // (2 * chunks)

    def kernel(core_ref, *refs):
        right_refs, left_refs = refs[:group], refs[group:-4]
        other_ref, mine_ref, left_ref, right_ref = refs[-4:]

        @pl.when((pl.program_id(0) == 0) & (pl.program_id(1) == 0))
        def _():
            for spot in range(group):
                right_ref[spot * rows : (spot + 1) * rows, :] = right_refs[spot][...]

        for index in range(count):

            @pl.when(pl.program_id(1) == index)
            def _():
                for chunk in range(chunks):
                    for spot in range(group):
                        left_ref[
                            chunk * tile : (chunk + 1) * tile, spot * rows : (spot + 1) * rows
                        ] = left_refs[(index * chunks + chunk) * group + spot][...]

        value = dot(left_ref[...], right_ref[...], 1, 0).astype(jnp.bfloat16)

        @pl.when(pl.program_id(0) == 0)
        def _():
            for chunk in range(chunks):
                other_ref[chunk] = value[chunk * tile : (chunk + 1) * tile]

        @pl.when(pl.program_id(0) == 1)
        def _():
            for chunk in range(chunks):
                mine_ref[chunk] = value[chunk * tile : (chunk + 1) * tile]

    def left_spec(chunk):
        def index(side, spot, core_ref):
            return (2 * chunk + jnp.where(side == 0, 1 - core_ref[0], core_ref[0]), 0)

        return pl.BlockSpec((tile, rows), index)

    shape = jax.ShapeDtypeStruct((count * chunks, tile, model), jnp.bfloat16)
    block = (chunks, tile, model)
    return pl.pallas_call(
        kernel,
        grid_spec=pltpu.PrefetchScalarGridSpec(
            num_scalar_prefetch=1,
            grid=(2, count),
            in_specs=[pl.BlockSpec((rows, model), lambda side, spot, core_ref: (0, 0))] * group
            + [left_spec(chunk) for _ in range(count) for chunk in range(chunks) for _ in range(group)],
            out_specs=[
                pl.BlockSpec(
                    block, lambda side, spot, core_ref: (jnp.where(side == 0, spot, count - 1), 0, 0)
                ),
                pl.BlockSpec(block, lambda side, spot, core_ref: (jnp.where(side == 0, 0, spot), 0, 0)),
            ],
            scratch_shapes=[
                pltpu.VMEM((chunks * tile, group * rows), jnp.bfloat16),
                pltpu.VMEM((group * rows, model), jnp.bfloat16),
            ],
        ),
        out_shape=[shape, shape],
        compiler_params=params(),
        name="weight_grad",
    )(
        scalar(lax.axis_index("replica") % 2),
        *rights,
        *[left for lefts in sets for _ in range(chunks) for left in lefts],
    )


def allowed_mask(query_segs_ref, key_segs_ref, rows, width):
    gap = (
        width
        - rows
        + lax.broadcasted_iota(jnp.int32, (rows, width), 0)
        - lax.broadcasted_iota(jnp.int32, (rows, width), 1)
    )
    return (gap >= 0) & (gap < WINDOW) & (query_segs_ref[...] == key_segs_ref[...])


def head_probs(query, keys, allowed, scale):
    scores = jnp.where(allowed, dot(query, keys, 1, 1) * scale, NEG)
    expo = jnp.exp(scores - jnp.max(scores, axis=-1, keepdims=True))
    return expo / jnp.sum(expo, axis=-1, keepdims=True)


def attention_specs(rows, size, width, heads):
    head = pl.BlockSpec((rows, size), lambda h: (0, h))
    whole = lambda *shape: pl.BlockSpec(shape, lambda h: (0, 0))
    common = [
        head,
        whole(1, size),
        whole(rows, size // 2),
        whole(rows, size // 2),
        whole(width, 2 * size),
        whole(rows, 1),
        whole(1, width),
    ]
    return head, whole, common


def attention_forward(qkv, gain, cosine, sine, pairs, query_segs, key_segs, heads):
    rows, width, size = qkv.shape[0], pairs.shape[0], pairs.shape[1] // 2
    head, _, common = attention_specs(rows, size, width, heads)

    def kernel(raw_ref, gain_ref, cos_ref, sin_ref, pairs_ref, qseg_ref, kseg_ref, query_ref, mixed_ref):
        query = head_post(raw_ref[...], gain_ref[...], cos_ref[...], sin_ref[...]).astype(jnp.bfloat16)
        query_ref[...] = query
        allowed = allowed_mask(qseg_ref, kseg_ref, rows, width)
        probs = head_probs(query, pairs_ref[:, :size], allowed, size**-0.5).astype(jnp.bfloat16)
        mixed_ref[...] = dot(probs, pairs_ref[:, size:], 1, 0).astype(jnp.bfloat16)

    shape = jax.ShapeDtypeStruct((rows, heads * size), jnp.bfloat16)
    return pl.pallas_call(
        kernel,
        grid=(heads,),
        in_specs=common,
        out_specs=[head, head],
        out_shape=[shape, shape],
        compiler_params=params(),
        name="attention_forward",
    )(qkv, gain, cosine, sine, pairs, query_segs, key_segs)


def attention_backward(qkv, gain, cosine, sine, pairs, query_segs, key_segs, query, grad_mixed, heads):
    rows, width, size = qkv.shape[0], pairs.shape[0], pairs.shape[1] // 2
    head, whole, common = attention_specs(rows, size, width, heads)
    before = width - rows

    def kernel(
        raw_ref, gain_ref, cos_ref, sin_ref, pairs_ref, qseg_ref, kseg_ref, query_ref, grad_ref,
        raw_grad_ref, gain_grad_ref, far_ref, own_ref, acc,
    ):
        step = pl.program_id(0)
        query = query_ref[...]
        grad = grad_ref[...]
        allowed = allowed_mask(qseg_ref, kseg_ref, rows, width)
        keys = pairs_ref[:, :size]
        probs = head_probs(query, keys, allowed, size**-0.5)
        grad_probs = dot(grad, pairs_ref[:, size:], 1, 1)
        delta = jnp.sum(grad_probs * probs, axis=-1, keepdims=True)
        grad_scores = (probs * (grad_probs - delta)).astype(jnp.bfloat16)
        grad_query = dot(grad_scores, keys, 1, 0) * size**-0.5
        grad_keys = dot(grad_scores, query, 0, 0) * size**-0.5
        grad_values = dot(probs.astype(jnp.bfloat16), grad, 0, 0)

        @pl.when(step == 0)
        def _():
            acc[:, :size] = grad_keys
            acc[:, size:] = grad_values

        @pl.when(step > 0)
        def _():
            acc[:, :size] += grad_keys
            acc[:, size:] += grad_values

        first = grad_query[:, : size // 2]
        second = grad_query[:, size // 2 :]
        cosine_part, sine_part = cos_ref[...], sin_ref[...]
        turned = jnp.concatenate(
            [
                first * cosine_part + second * sine_part,
                second * cosine_part - first * sine_part,
            ],
            axis=-1,
        )
        raw = raw_ref[...]
        scale = lax.rsqrt(jnp.mean(raw * raw, axis=-1, keepdims=True) + EPS)
        unit = raw * scale
        inner = turned * gain_ref[...].astype(jnp.float32)
        raw_grad = scale * (inner - unit * jnp.mean(inner * unit, axis=-1, keepdims=True))
        raw_grad_ref[...] = raw_grad.astype(jnp.bfloat16)
        gain_grad = jnp.sum(turned * unit, axis=0, keepdims=True)

        @pl.when(step == 0)
        def _():
            gain_grad_ref[...] = gain_grad

        @pl.when(step > 0)
        def _():
            gain_grad_ref[...] += gain_grad

        @pl.when(step == heads - 1)
        def _():
            far_ref[...] = acc[:before, :].astype(jnp.bfloat16)
            own_ref[...] = acc[before:, :]

    return pl.pallas_call(
        kernel,
        grid=(heads,),
        in_specs=common + [head, head],
        out_specs=[head, whole(1, size), whole(before, 2 * size), whole(rows, 2 * size)],
        out_shape=[
            jax.ShapeDtypeStruct((rows, heads * size), jnp.bfloat16),
            jax.ShapeDtypeStruct((1, size), jnp.float32),
            jax.ShapeDtypeStruct((before, 2 * size), jnp.bfloat16),
            jax.ShapeDtypeStruct((rows, 2 * size), jnp.float32),
        ],
        scratch_shapes=[pltpu.VMEM((width, 2 * size), jnp.float32)],
        compiler_params=params(),
        name="attention_backward",
    )(qkv, gain, cosine, sine, pairs, query_segs, key_segs, query, grad_mixed)


def line_edges():
    places = lax.axis_size("replica") // 2
    outer = places // 2 - 1
    return places, outer


def exchanged(block, pairs):
    route = [(2 * a + core, 2 * b + core) for a, b in pairs for core in range(2)]
    return lax.ppermute(block, "replica", route)


class Line:
    def __init__(self):
        self.places, self.outer = line_edges()
        self.steps = 2 * self.outer + 1
        self.moving = []
        self.done = {}

    def advance(self, fresh, gate=None):
        places, outer, steps = self.places, self.outer, self.steps
        place = (lax.axis_index("replica") // 2).astype(jnp.int32).reshape(1)
        operands, plan = [], []

        def operand(entry):
            array, index = entry if isinstance(entry, tuple) else (entry, None)
            for spot, (known, known_index) in enumerate(operands):
                if known is array and known_index == index:
                    return spot
            operands.append((array, index))
            return len(operands) - 1

        for name, block, step, far in self.moving:
            plan.append((name, step + 1, [operand(block), operand(far)], step))
        for name, terms in fresh:
            plan.append((name, 0, [operand(term) for term in terms], None))
        if not plan:
            return gate
        sizes = [operands[spots[0]][0].shape[-2:] for _, _, spots, _ in plan]
        by_step = {step: index for index, (_, step, _, _) in enumerate(plan)}
        pairs = []
        for edge in range(outer):
            inward, outward = by_step.get(edge), by_step.get(2 * outer - edge)
            if inward is not None and outward is not None and sizes[inward] == sizes[outward]:
                pairs.append((edge, inward, outward))
        cuts = 3 if all(size[0] % 48 == 0 for size in sizes) else 1

        def kernel(place_ref, *refs):
            here = place_ref[0]
            inputs = refs[: len(operands)]
            if gate is not None:
                refs = refs[: len(operands)] + refs[len(operands) + 1 :]
            outputs = refs[len(operands) :]
            states = []
            for spot, (_, _, terms, last) in enumerate(plan):
                value = inputs[terms[0]][...]
                if len(terms) > 1:
                    far = inputs[terms[1]][...]
                    total = value.astype(jnp.float32)
                    for term in terms[1:]:
                        total = total + inputs[term][...].astype(jnp.float32)
                    total = total.astype(jnp.bfloat16)
                    if last is None:
                        value = total
                    elif last <= outer:
                        edge = last
                        value = jnp.where((here == edge + 1) | (here == places - 2 - edge), total, value)
                    else:
                        edge = 2 * outer - last
                        value = jnp.where((here == edge) | (here == places - 1 - edge), far, value)
                states.append(value)
                outputs[spot][...] = value
            for spot, (edge, inward, outward) in enumerate(pairs):
                outputs[len(plan) + spot][...] = jnp.where(
                    (here == edge) | (here == places - 1 - edge), states[inward], states[outward]
                )

        def spec(size, index):
            if index is None:
                return pl.BlockSpec((size[0] // cuts, size[1]), lambda i, place_ref: (i, 0))
            return pl.BlockSpec((None, size[0] // cuts, size[1]), lambda i, place_ref: (index, i, 0))

        in_specs = [spec(array.shape[-2:], index) for array, index in operands]
        arrays = [array for array, _ in operands]
        out_sizes = sizes + [sizes[inward] for _, inward, _ in pairs]
        out_specs = [spec(size, None) for size in out_sizes]
        out_shape = [jax.ShapeDtypeStruct(size, jnp.bfloat16) for size in out_sizes]
        aliases = {}
        if gate is not None:
            aliases = {1 + len(arrays): len(out_shape)}
            in_specs.append(pl.BlockSpec(memory_space=pl.ANY))
            out_specs.append(pl.BlockSpec(memory_space=pl.ANY))
            out_shape.append(jax.ShapeDtypeStruct(gate.shape, gate.dtype))
            arrays.append(gate)
        outs = pl.pallas_call(
            kernel,
            grid_spec=pltpu.PrefetchScalarGridSpec(
                num_scalar_prefetch=1, grid=(cuts,), in_specs=in_specs, out_specs=out_specs
            ),
            out_shape=out_shape,
            input_output_aliases=aliases,
            compiler_params=params(),
            name="line_step",
        )(place, *arrays)
        received = {}
        for spot, (edge, inward, outward) in enumerate(pairs):
            ends = [(edge, edge + 1), (places - 1 - edge, places - 2 - edge)]
            far = exchanged(outs[len(plan) + spot], ends + [(b, a) for a, b in ends])
            received[inward] = received[outward] = far
        self.moving = []
        for index, (name, step, _, _) in enumerate(plan):
            block = outs[index]
            if step == steps:
                self.done[name] = block
                continue
            if index not in received:
                edge = step if step <= outer else 2 * outer - step
                route = [(edge, edge + 1), (places - 1 - edge, places - 2 - edge)]
                if step > outer:
                    route = [(b, a) for a, b in route]
                received[index] = exchanged(block, route)
            self.moving.append((name, block, step, received[index]))
        return outs[-1]

    def arrived(self):
        return [far for _, _, _, far in self.moving]

    def finished(self, name):
        while name not in self.done:
            self.advance([])
        return self.done[name]


def line_names(name, units):
    return [(name, chunk) for chunk in range(chunks_of(units))]


def whole_grad(lines, name, units, dtype=jnp.float32):
    names = line_names(name, units)
    mines = [lines[chunk[1]].finished(chunk) for chunk in names]
    others = [swapped(mine, "replica", 1) for mine in mines]
    chunks = len(mines)
    tile, model = mines[0].shape
    core = (lax.axis_index("replica") % 2).astype(jnp.int32).reshape(1)

    def kernel(core_ref, *refs):
        out_ref = refs[-1]
        for chunk in range(chunks):
            for side in range(2):

                @pl.when((pl.program_id(0) == chunk) & (pl.program_id(1) == side))
                def _():
                    @pl.when(core_ref[0] == side)
                    def _():
                        out_ref[...] = refs[chunk][...].astype(dtype)

                    @pl.when(core_ref[0] != side)
                    def _():
                        out_ref[...] = refs[chunks + chunk][...].astype(dtype)

    return pl.pallas_call(
        kernel,
        grid_spec=pltpu.PrefetchScalarGridSpec(
            num_scalar_prefetch=1,
            grid=(chunks, 2),
            in_specs=[pl.BlockSpec((tile, model), lambda chunk, side, core_ref: (0, 0))] * (2 * chunks),
            out_specs=pl.BlockSpec((tile, model), lambda chunk, side, core_ref: (2 * chunk + side, 0)),
        ),
        out_shape=jax.ShapeDtypeStruct((units, model), dtype),
        compiler_params=params(),
        name="whole_grad",
    )(core, *mines, *others)


def joined(mine, other, axis):
    core = lax.axis_index("replica") % 2
    return jnp.where(
        core == 0,
        jnp.concatenate([mine, other], axis=axis),
        jnp.concatenate([other, mine], axis=axis),
    )


def core_join(block, axis):
    return joined(block, swapped(block, "replica", 1), axis)


def fetched(block):
    got = [swapped(block, "fsdp", mask) for mask in range(1, lax.axis_size("fsdp"))]
    return got, [swapped(part, "replica", 1) for part in got]


def passed_along(block, axis, distance):
    devices = range(lax.axis_size(axis))
    route = [(i - distance, i) for i in devices if i - distance in devices]
    return lax.ppermute(block, axis, route)


def contract(left, right, left_dim, right_dim):
    return lax.dot_general(
        left, right, (((left_dim,), (right_dim,)), ((), ())), preferred_element_type=jnp.float32
    )


def normed(value, gain):
    return value * lax.rsqrt(jnp.mean(value * value, axis=-1, keepdims=True) + EPS) * gain


def norm_back(value, gain, grad):
    _, pull = jax.vjp(normed, value, gain)
    return pull(grad)


def tables(places, half):
    freq = 10000.0 ** (-(2.0 * jnp.arange(half, dtype=jnp.float32)) / (2 * half))
    angle = places.astype(jnp.float32)[:, None] * freq[None, :]
    return (jnp.cos(angle), jnp.sin(angle))


def rotate(value, cosine, sine):
    half = value.shape[-1] // 2
    first = value[..., :half]
    second = value[..., half:]
    return jnp.concatenate(
        [first * cosine - second * sine, second * cosine + first * sine], axis=-1
    )


def head_post(raw, gain, cosine, sine):
    return rotate(normed(raw, gain), cosine, sine)


def per_device(
    hidden_in,
    out_grad,
    segments,
    positions,
    norm_in,
    query_weight,
    key_weight,
    value_weight,
    out_weight,
    norm_attn,
    norm_ffn,
    gate_weight,
    up_weight,
    down_weight,
    norm_out,
    query_gain,
    key_gain,
):
    rows = hidden_in.shape[0]
    rank = lax.axis_index("fsdp")
    group = lax.axis_size("fsdp")
    masks = range(1, group)
    head_size = key_weight.shape[1]
    heads = query_weight.shape[1] // head_size
    model = hidden_in.shape[1]
    own_model = norm_in.shape[0]
    own_head = query_gain.shape[0]
    hops = (WINDOW - 1) // rows + 1
    scale = head_size ** (-0.5)
    qkv_weights = (query_weight, key_weight, value_weight)
    wide = sum(weight.shape[1] for weight in qkv_weights)
    gains = (norm_in, norm_attn, norm_ffn, norm_out, query_gain, key_gain)
    block = packed(qkv_weights, gains)
    got, peers = fetched(block)
    w_qkv = unpacked(qkv_weights, got, peers)
    gain_stack = jnp.stack([part[-16:, :own_model] for part in [block] + got])
    gain_rows = jnp.stack(
        [lax.dynamic_index_in_dim(gain_stack, rank ^ i, 0, keepdims=False) for i in range(group)], axis=1
    )
    gain_in, gain_attn, gain_ffn, gain_out = (gain_rows[i].reshape(-1) for i in range(4))
    gain_query, gain_key = (gain_rows[i, :, :own_head].reshape(-1) for i in (4, 5))
    got, peers = fetched(after(packed([out_weight]), w_qkv))
    residual_in = hidden_in.astype(jnp.float32)
    normed_in = normed(residual_in, gain_in).astype(jnp.bfloat16)
    qkv = jnp.dot(normed_in, w_qkv, preferred_element_type=jnp.float32)
    key_raw = qkv[:, heads * head_size : (heads + 1) * head_size]
    value_new = qkv[:, (heads + 1) * head_size :].astype(jnp.bfloat16)
    cosine, sine = tables(positions, head_size // 2)
    key_new = head_post(key_raw, gain_key, cosine, sine).astype(jnp.bfloat16)
    pair_new = jnp.concatenate([key_new, value_new], axis=1)
    parts = [pair_new]
    for step in range(1, hops + 1):
        parts.insert(0, passed_along(pair_new, "fsdp", step))
    pairs = jnp.concatenate(parts, axis=0)
    width = pairs.shape[0]
    seg_padded = jnp.concatenate([jnp.full((hops * rows,), -1, jnp.int32), segments], axis=0)
    key_segs = lax.dynamic_slice_in_dim(seg_padded, rank * rows, width, 0)
    query_segs = lax.dynamic_slice_in_dim(segments, rank * rows, rows, 0)
    attention_args = (
        qkv,
        gain_query[None, :],
        cosine,
        sine,
        pairs,
        query_segs[:, None],
        key_segs[None, :],
    )
    query_new, mixed = attention_forward(*attention_args, heads)
    w_out = unpacked([out_weight], got, peers)
    attended = contract(mixed, w_out, 1, 1)
    resid = residual_in + normed(attended, gain_attn)
    ffn_in = normed(resid, gain_ffn).astype(jnp.bfloat16)
    ffn_blocks = [ffn_in] + [swapped(ffn_in, "fsdp", mask) for mask in masks]
    hiddens, slopes, acts, parts = [], [], [], []
    for mask in range(group):
        hidden, slope, act, part = ffn_forward(ffn_blocks[mask], gate_weight, up_weight, down_weight)
        parts.append(part)
        hiddens.append(hidden)
        slopes.append(slope)
        acts.append(act)
    parts = parts[:1] + [swapped(parts[mask], "fsdp", mask) for mask in masks]
    branch = sum(part.astype(jnp.float32) for part in parts)
    result = resid + normed(branch, gain_out)
    hidden_out = result.astype(jnp.bfloat16)
    grad_result = out_grad.astype(jnp.float32)
    grad_branch, grad_gain_out = norm_back(branch, gain_out, grad_result)
    grad_branch_low = grad_branch.astype(jnp.bfloat16)
    pieces = [grad_branch_low] + [swapped(grad_branch_low, "fsdp", mask) for mask in masks]
    units = gate_weight.shape[0]
    lines = [Line(), Line()]

    def fresh(names, other, mine):
        far = swapped(other, "replica", 1)
        keys = [key for name in names for key in line_names(name, units)]
        return [(key, [(mine, spot), (far, spot)]) for spot, key in enumerate(keys)]

    grad_gates, grad_uppers, returned = {}, {}, {}
    early = group // 2
    for mask in range(early):
        grad_gates[mask], grad_uppers[mask], part = ffn_backward(
            pieces[mask], gate_weight, up_weight, down_weight, slopes[mask], acts[mask]
        )
        pieces[mask + 1] = after(pieces[mask + 1], part)
        returned[mask] = swapped(part, "fsdp", mask) if mask else part
    waiting = fresh(["down"], *weight_grad([hiddens], pieces))
    for mask in range(1, early):
        pieces[early] = after(pieces[early], returned[mask])
    pieces[early] = lines[0].advance([waiting.pop(0)], pieces[early])
    late = range(early, group)
    gate_parts, upper_parts, parts = ffn_backward_blocks(
        [pieces[mask] for mask in late],
        gate_weight,
        up_weight,
        down_weight,
        [slopes[mask] for mask in late],
        [acts[mask] for mask in late],
    )
    for spot, mask in enumerate(late):
        grad_gates[mask], grad_uppers[mask] = gate_parts[spot], upper_parts[spot]
        returned[mask] = swapped(parts[spot], "fsdp", mask)
    if waiting:
        grad_gates[early] = lines[1].advance([waiting.pop(0)], grad_gates[early])
    grad_gates[0] = after(grad_gates[0], *lines[0].arrived())
    other, mine = weight_grad(
        [[grad_gates[i] for i in range(group)], [grad_uppers[i] for i in range(group)]], ffn_blocks
    )
    other = after(other, *lines[1].arrived(), *[returned[mask] for mask in late])
    waiting = fresh(["gate", "up"], other, mine)

    def advance(spot, gate=None):
        ready = [entry for entry in waiting if entry[0][1] == spot][:1]
        for entry in ready:
            waiting.remove(entry)
        return lines[spot].advance(ready, gate)

    grad_resid, grad_attended_low, grad_mixed, grad_gain_ffn, grad_gain_attn = resid_backward(
        [returned[mask] for mask in range(group)], resid, attended, out_grad, gain_ffn, gain_attn, w_out
    )
    grad_mixed = advance(0, grad_mixed)
    grad_query_low, grad_gain_query, grad_far, grad_pair = attention_backward(
        *attention_args, query_new, grad_mixed, heads
    )
    grad_far = advance(1, grad_far)
    backs = []
    for step in range(1, hops + 1):
        grad_far = passed_along(grad_far, "fsdp", -1)
        backs.append(grad_far[-rows:])
        grad_far = grad_far[:-rows]
    grad_pair = advance(0, grad_pair)
    other, mine, grad_in = input_backward(
        grad_pair,
        backs,
        qkv,
        cosine,
        sine,
        gain_key,
        normed_in,
        grad_query_low,
        w_qkv,
        hidden_in,
        gain_in,
        grad_resid,
        grad_attended_low,
        mixed,
        [grad_gain_attn, grad_gain_ffn, grad_gain_out[None, :], grad_gain_query],
        group,
    )
    other = advance(1, other)
    chip = added(mine, swapped(other, "replica", 1))
    owned = lax.psum_scatter(chip, "fsdp", scatter_dimension=0, tiled=True)[0]
    places = lax.axis_size("replica") // 2
    cores = [[2 * place + core for place in range(places)] for core in range(2)]
    owned = lax.psum(owned, "replica", axis_index_groups=cores)
    advance(0)
    advance(1)
    advance(0)
    advance(1)
    while waiting:
        advance(0)
    grad_down = whole_grad(lines, "down", units)
    grad_down = lines[0].advance([], grad_down)
    grad_gate_w = whole_grad(lines, "gate", units)
    grad_gate_w = lines[1].advance([], grad_gate_w)
    grad_up_w = whole_grad(lines, "up", units)
    owned = core_join(owned, 1).astype(jnp.float32)
    inner = heads * head_size
    columns = [0, inner, inner + head_size, inner + 2 * head_size, wide + inner]
    owned_query, owned_key, owned_value, owned_out = (
        owned[:own_model, columns[i] : columns[i + 1]] for i in range(4)
    )

    def owned_gain(row, size):
        return lax.dynamic_slice_in_dim(owned[own_model + row], rank * size, size, 0)

    owned_gain_in, owned_gain_attn, owned_gain_ffn, owned_gain_out = (
        owned_gain(row, own_model) for row in (0, 2, 3, 4)
    )
    owned_gain_key, owned_gain_query = (owned_gain(row, own_head) for row in (1, 5))
    return (
        hidden_out,
        grad_in,
        owned_gain_in,
        owned_query,
        owned_key,
        owned_value,
        owned_out,
        owned_gain_attn,
        owned_gain_ffn,
        grad_gate_w,
        grad_up_w,
        grad_down,
        owned_gain_out,
        owned_gain_query,
        owned_gain_key,
    )


def solution(mesh):
    return jax.shard_map(
        per_device,
        mesh=mesh,
        in_specs=(
            P(("replica", "fsdp"), None),
            P(("replica", "fsdp"), None),
            P("replica"),
            P(("replica", "fsdp")),
            P("fsdp"),
            P("fsdp", None),
            P("fsdp", None),
            P("fsdp", None),
            P("fsdp", None),
            P("fsdp"),
            P("fsdp"),
            P("fsdp", None),
            P("fsdp", None),
            P("fsdp", None),
            P("fsdp"),
            P("fsdp"),
            P("fsdp"),
        ),
        out_specs=(
            P(("replica", "fsdp"), None),
            P(("replica", "fsdp"), None),
            P("fsdp"),
            P("fsdp", None),
            P("fsdp", None),
            P("fsdp", None),
            P("fsdp", None),
            P("fsdp"),
            P("fsdp"),
            P("fsdp", None),
            P("fsdp", None),
            P("fsdp", None),
            P("fsdp"),
            P("fsdp"),
            P("fsdp"),
        ),
        check_vma=False,
    )
```

```python
import jax
import jax.numpy as jnp
from jax import lax
from jax.experimental import pallas as pl
from jax.experimental.pallas import tpu as pltpu
from jax.sharding import PartitionSpec as P

WINDOW = 512


EPS = 1e-06
NEG = -1e30


def swapped(block, axis, mask):
    route = [(i, i ^ mask) for i in range(lax.axis_size(axis))]
    return lax.ppermute(block, axis, route)


def added(left, right):
    total = left.astype(jnp.float32) + right.astype(jnp.float32)
    return lax.optimization_barrier(total.astype(jnp.bfloat16))


VMEM_LIMIT = 56 * 1024 * 1024


def params(*semantics):
    return pltpu.CompilerParams(vmem_limit_bytes=VMEM_LIMIT)


def dot(left, right, left_dim, right_dim):
    return lax.dot_general(
        left, right, (((left_dim,), (right_dim,)), ((), ())), preferred_element_type=jnp.float32
    )


def after(array, *others):
    place = pl.BlockSpec(memory_space=pl.ANY)
    return pl.pallas_call(
        lambda *refs: None,
        out_shape=jax.ShapeDtypeStruct(array.shape, array.dtype),
        in_specs=[place] * (1 + len(others)),
        out_specs=place,
        input_output_aliases={0: 0},
        name="after",
    )(array, *others)


def scalar(value):
    return value.astype(jnp.int32).reshape(1)


def packed(weights):
    half = weights[0].shape[0] // 2
    wide = sum(weight.shape[1] for weight in weights)

    def kernel(core_ref, *refs):
        out_ref = refs[-1]
        for side in range(2):

            @pl.when(core_ref[0] == side)
            def _():
                at = 0
                for ref in refs[:-1]:
                    out_ref[:, at : at + ref.shape[1]] = ref[side * half : (side + 1) * half, :]
                    at += ref.shape[1]

    return pl.pallas_call(
        kernel,
        grid_spec=pltpu.PrefetchScalarGridSpec(
            num_scalar_prefetch=1,
            grid=(1,),
            in_specs=[pl.BlockSpec(weight.shape, lambda i, core_ref: (0, 0)) for weight in weights],
            out_specs=pl.BlockSpec((half, wide), lambda i, core_ref: (0, 0)),
        ),
        out_shape=jax.ShapeDtypeStruct((half, wide), jnp.bfloat16),
        compiler_params=params(),
        name="pack",
    )(scalar(lax.axis_index("replica") % 2), *weights)


def unpacked(weights, got, peers):
    rows = weights[0].shape[0]
    half = rows // 2
    group = len(got) + 1
    wide = sum(weight.shape[1] for weight in weights)
    own = len(weights)

    def kernel(core_ref, rank_ref, *refs):
        out_ref = refs[-1]
        mask = rank_ref[0] ^ pl.program_id(0)

        @pl.when(mask == 0)
        def _():
            at = 0
            for ref in refs[:own]:
                out_ref[:, at : at + ref.shape[1]] = ref[...]
                at += ref.shape[1]

        for other in range(1, group):
            for side in range(2):

                @pl.when((mask == other) & (core_ref[0] == side))
                def _():
                    out_ref[side * half : (side + 1) * half, :] = refs[own + other - 1][:half, :]
                    out_ref[(1 - side) * half : (2 - side) * half, :] = refs[own + group - 2 + other][:half, :]

    arrays = list(weights) + list(got) + list(peers)
    return pl.pallas_call(
        kernel,
        grid_spec=pltpu.PrefetchScalarGridSpec(
            num_scalar_prefetch=2,
            grid=(group,),
            in_specs=[pl.BlockSpec(array.shape, lambda i, *refs: (0, 0)) for array in arrays],
            out_specs=pl.BlockSpec((rows, wide), lambda i, *refs: (i, 0)),
        ),
        out_shape=jax.ShapeDtypeStruct((group * rows, wide), jnp.bfloat16),
        compiler_params=params(),
        name="unpack",
    )(scalar(lax.axis_index("replica") % 2), scalar(lax.axis_index("fsdp")), *arrays)


GELU_A = (2.0 / 3.141592653589793) ** 0.5
GELU_B = 0.044715


def ffn_forward(x, gate_weight, up_weight, down_weight):
    gate = contract(gate_weight, x, 1, 1)
    upper = contract(up_weight, x, 1, 1)
    square = gate * gate
    bend = jnp.tanh(GELU_A * gate * (1.0 + GELU_B * square))
    half = 0.5 + 0.5 * bend
    act = gate * half
    slope = half + 0.5 * gate * (1.0 - bend * bend) * (GELU_A * (1.0 + 3.0 * GELU_B * square))
    hidden = (act * upper).astype(jnp.bfloat16)
    part = contract(hidden, down_weight, 0, 0).astype(jnp.bfloat16)
    return hidden, (slope * upper).astype(jnp.bfloat16), act.astype(jnp.bfloat16), part


def ffn_backward(grad, gate_weight, up_weight, down_weight, slope, act):
    grad_hidden = contract(down_weight, grad, 1, 1)
    grad_gate = (grad_hidden * slope.astype(jnp.float32)).astype(jnp.bfloat16)
    grad_upper = (grad_hidden * act.astype(jnp.float32)).astype(jnp.bfloat16)
    part = contract(grad_gate, gate_weight, 0, 0) + contract(grad_upper, up_weight, 0, 0)
    return grad_gate, grad_upper, part.astype(jnp.bfloat16)


def tile_of(size, most):
    return max(tile for tile in range(16, most + 1, 16) if size % tile == 0)


def ffn_backward_blocks(grads, gate_weight, up_weight, down_weight, slopes, acts):
    count = len(grads)
    rows, model = grads[0].shape
    units = gate_weight.shape[0]
    tile = tile_of(units, 432)
    steps = units // tile

    def kernel(*refs):
        step = pl.program_id(0)
        grad_refs, refs = refs[:count], refs[count:]
        (gate_ref, up_ref, down_ref), refs = refs[:3], refs[3:]
        slope_refs, act_refs, refs = refs[:count], refs[count : 2 * count], refs[2 * count :]
        gate_outs, up_outs, part_outs, (grad_ref, acc) = (
            refs[:count],
            refs[count : 2 * count],
            refs[2 * count : 3 * count],
            refs[3 * count :],
        )

        @pl.when(step == 0)
        def _():
            for spot in range(count):
                grad_ref[spot * rows : (spot + 1) * rows, :] = grad_refs[spot][...]
            acc[...] = jnp.zeros_like(acc)

        grad_hidden = dot(down_ref[...], grad_ref[...], 1, 1)
        slope = jnp.concatenate([ref[...] for ref in slope_refs], axis=1).astype(jnp.float32)
        act = jnp.concatenate([ref[...] for ref in act_refs], axis=1).astype(jnp.float32)
        grad_gate = (grad_hidden * slope).astype(jnp.bfloat16)
        grad_upper = (grad_hidden * act).astype(jnp.bfloat16)
        for spot in range(count):
            gate_outs[spot][...] = grad_gate[:, spot * rows : (spot + 1) * rows]
            up_outs[spot][...] = grad_upper[:, spot * rows : (spot + 1) * rows]
        acc[...] += dot(grad_gate, gate_ref[...], 0, 0) + dot(grad_upper, up_ref[...], 0, 0)

        @pl.when(step == steps - 1)
        def _():
            for spot in range(count):
                part_outs[spot][...] = acc[spot * rows : (spot + 1) * rows, :].astype(jnp.bfloat16)

    weight = pl.BlockSpec((tile, model), lambda i: (i, 0))
    flat = pl.BlockSpec((tile, rows), lambda i: (i, 0))
    whole = pl.BlockSpec((rows, model), lambda i: (0, 0))
    kept = jax.ShapeDtypeStruct((units, rows), jnp.bfloat16)
    outs = pl.pallas_call(
        kernel,
        grid=(steps,),
        out_shape=[kept] * (2 * count) + [jax.ShapeDtypeStruct((rows, model), jnp.bfloat16)] * count,
        in_specs=[whole] * count + [weight] * 3 + [flat] * (2 * count),
        out_specs=[flat] * (2 * count) + [whole] * count,
        scratch_shapes=[
            pltpu.VMEM((count * rows, model), jnp.bfloat16),
            pltpu.VMEM((count * rows, model), jnp.float32),
        ],
        compiler_params=params(),
        name="ffn_backward",
    )(*grads, gate_weight, up_weight, down_weight, *slopes, *acts)
    return outs[:count], outs[count : 2 * count], outs[2 * count :]


def norm_pull(value, gain, grad):
    scale = lax.rsqrt(jnp.mean(value * value, axis=-1, keepdims=True) + EPS)
    unit = value * scale
    inner = grad * gain
    return scale * (inner - unit * jnp.mean(inner * unit, axis=-1, keepdims=True)), grad * unit


def resid_backward(parts, resid, attended, out_grad, gain_ffn, gain_attn, w_out):
    count = len(parts)
    rows, model = resid.shape
    tile = min(rows, 128)

    def kernel(*refs):
        part_refs, refs = refs[:count], refs[count:]
        resid_ref, attended_ref, out_ref, ffn_ref, attn_ref, weight_ref, refs = *refs[:6], refs[6:]
        grad_resid_ref, grad_attended_ref, grad_mixed_ref, ffn_grad_ref, attn_grad_ref = refs
        grad = sum(ref[...].astype(jnp.float32) for ref in part_refs)
        pulled, ffn_rows = norm_pull(resid_ref[...], ffn_ref[...].astype(jnp.float32), grad)
        grad_resid = out_ref[...].astype(jnp.float32) + pulled
        grad_resid_ref[...] = grad_resid
        pulled, attn_rows = norm_pull(attended_ref[...], attn_ref[...].astype(jnp.float32), grad_resid)
        grad_attended = pulled.astype(jnp.bfloat16)
        grad_attended_ref[...] = grad_attended
        grad_mixed_ref[...] = dot(grad_attended, weight_ref[...], 1, 0).astype(jnp.bfloat16)
        ffn_grad = jnp.sum(ffn_rows, axis=0, keepdims=True)
        attn_grad = jnp.sum(attn_rows, axis=0, keepdims=True)

        @pl.when(pl.program_id(0) == 0)
        def _():
            ffn_grad_ref[...] = ffn_grad
            attn_grad_ref[...] = attn_grad

        @pl.when(pl.program_id(0) > 0)
        def _():
            ffn_grad_ref[...] += ffn_grad
            attn_grad_ref[...] += attn_grad

    block = pl.BlockSpec((tile, model), lambda i: (i, 0))
    vector = pl.BlockSpec((1, model), lambda i: (0, 0))
    inner = w_out.shape[1]
    return pl.pallas_call(
        kernel,
        grid=(rows // tile,),
        in_specs=[block] * (count + 3) + [vector] * 2 + [pl.BlockSpec(w_out.shape, lambda i: (0, 0))],
        out_specs=[block, block, pl.BlockSpec((tile, inner), lambda i: (i, 0)), vector, vector],
        out_shape=[
            jax.ShapeDtypeStruct((rows, model), jnp.float32),
            jax.ShapeDtypeStruct((rows, model), jnp.bfloat16),
            jax.ShapeDtypeStruct((rows, inner), jnp.bfloat16),
            jax.ShapeDtypeStruct((1, model), jnp.float32),
            jax.ShapeDtypeStruct((1, model), jnp.float32),
        ],
        compiler_params=params(),
        name="resid_backward",
    )(*parts, resid, attended, out_grad, gain_ffn[None, :], gain_attn[None, :], w_out)


def input_backward(
    own_pair, backs, qkv, cosine, sine, gain_key, normed_in, grad_query, w_qkv, hidden_in, gain_in, grad_resid,
    grad_attended, mixed, gain_grads, group,
):
    rows, model = hidden_in.shape
    size = own_pair.shape[1] // 2
    inner = grad_query.shape[1]
    own_rows = model // group
    half = inner + size
    hops = len(backs)
    count = len(gain_grads)

    def kernel(core_ref, *refs):
        pair_ref, refs = refs[0], refs[1:]
        back_refs, refs = refs[:hops], refs[hops:]
        (
            raw_ref, cos_ref, sin_ref, key_gain_ref, normed_ref, query_ref, weight_ref, x_ref, gain_ref, resid_ref,
            attended_ref, mixed_ref, refs,
        ) = *refs[:12], refs[12:]
        gain_refs, refs = refs[:count], refs[count:]
        other_ref, mine_ref, grad_in_ref, rows_ref = refs
        pair = pair_ref[...] + sum(ref[...].astype(jnp.float32) for ref in back_refs)
        first = pair[:, : size // 2]
        second = pair[:, size // 2 : size]
        turned = jnp.concatenate(
            [
                first * cos_ref[...] + second * sin_ref[...],
                second * cos_ref[...] - first * sin_ref[...],
            ],
            axis=-1,
        )
        pulled, key_rows = norm_pull(raw_ref[...], key_gain_ref[...].astype(jnp.float32), turned)
        grad_key = pulled.astype(jnp.bfloat16)
        grad_value = pair[:, size:].astype(jnp.bfloat16)
        grad_normed = (
            dot(query_ref[...], weight_ref[:, :inner], 1, 1)
            + dot(grad_key, weight_ref[:, inner:half], 1, 1)
            + dot(grad_value, weight_ref[:, half:], 1, 1)
        )
        pulled, in_rows = norm_pull(
            x_ref[...].astype(jnp.float32), gain_ref[...].astype(jnp.float32), grad_normed
        )
        grad_in_ref[...] = resid_ref[...] + pulled
        rows_ref[...] = jnp.zeros_like(rows_ref)
        rows_ref[0:1, :model] = jnp.sum(in_rows, axis=0, keepdims=True)
        rows_ref[1:2, :size] = jnp.sum(key_rows, axis=0, keepdims=True)
        for spot in range(count):
            rows_ref[2 + spot : 3 + spot, : gain_refs[spot].shape[1]] = gain_refs[spot][...].astype(
                jnp.float32
            )
        gains = rows_ref[...].astype(jnp.bfloat16)

        def write(ref, side):
            pieces = (
                [(normed_ref, query_ref[...], 0, inner), (normed_ref, grad_key, inner, half)]
                if side == 0
                else [(normed_ref, grad_value, 0, size), (attended_ref, mixed_ref[...], size, half)]
            )
            for left, right, begin, end in pieces:
                value = dot(left[...], right, 0, 0).astype(jnp.bfloat16)
                for owner in range(group):
                    ref[owner, :own_rows, begin:end] = value[owner * own_rows : (owner + 1) * own_rows]
            for owner in range(group):
                ref[owner, own_rows:, :] = gains

        for core in range(2):

            @pl.when(core_ref[0] == core)
            def _():
                write(other_ref, 1 - core)
                write(mine_ref, core)

    def whole(array):
        return pl.BlockSpec(array.shape, lambda i, core_ref: (0,) * len(array.shape))

    arrays = [
        own_pair, *backs, qkv, cosine, sine, gain_key[None, :], normed_in, grad_query, w_qkv, hidden_in,
        gain_in[None, :], grad_resid, grad_attended, mixed, *gain_grads,
    ]
    in_specs = [whole(array) for array in arrays]
    in_specs[1 + hops] = pl.BlockSpec((rows, size), lambda i, core_ref: (0, inner // size))
    shape = jax.ShapeDtypeStruct((group, own_rows + 16, half), jnp.bfloat16)
    grad_in = jax.ShapeDtypeStruct((rows, model), jnp.float32)
    return pl.pallas_call(
        kernel,
        grid_spec=pltpu.PrefetchScalarGridSpec(
            num_scalar_prefetch=1,
            grid=(1,),
            in_specs=in_specs,
            out_specs=[whole(shape), whole(shape), whole(grad_in)],
            scratch_shapes=[pltpu.VMEM((16, half), jnp.float32)],
        ),
        out_shape=[shape, shape, grad_in],
        compiler_params=params(),
        name="input_backward",
    )(scalar(lax.axis_index("replica") % 2), *arrays)


def chunks_of(units):
    return 2 if units % 64 == 0 else 1


def weight_grad(sets, rights):
    group = len(rights)
    count = len(sets)
    units, rows = sets[0][0].shape
    model = rights[0].shape[1]
    chunks = chunks_of(units)
    tile = units // (2 * chunks)

    def kernel(core_ref, *refs):
        right_refs, left_refs = refs[:group], refs[group:-4]
        other_ref, mine_ref, left_ref, right_ref = refs[-4:]

        @pl.when((pl.program_id(0) == 0) & (pl.program_id(1) == 0))
        def _():
            for spot in range(group):
                right_ref[spot * rows : (spot + 1) * rows, :] = right_refs[spot][...]

        for index in range(count):

            @pl.when(pl.program_id(1) == index)
            def _():
                for chunk in range(chunks):
                    for spot in range(group):
                        left_ref[
                            chunk * tile : (chunk + 1) * tile, spot * rows : (spot + 1) * rows
                        ] = left_refs[(index * chunks + chunk) * group + spot][...]

        value = dot(left_ref[...], right_ref[...], 1, 0).astype(jnp.bfloat16)

        @pl.when(pl.program_id(0) == 0)
        def _():
            for chunk in range(chunks):
                other_ref[chunk] = value[chunk * tile : (chunk + 1) * tile]

        @pl.when(pl.program_id(0) == 1)
        def _():
            for chunk in range(chunks):
                mine_ref[chunk] = value[chunk * tile : (chunk + 1) * tile]

    def left_spec(chunk):
        def index(side, spot, core_ref):
            return (2 * chunk + jnp.where(side == 0, 1 - core_ref[0], core_ref[0]), 0)

        return pl.BlockSpec((tile, rows), index)

    shape = jax.ShapeDtypeStruct((count * chunks, tile, model), jnp.bfloat16)
    block = (chunks, tile, model)
    return pl.pallas_call(
        kernel,
        grid_spec=pltpu.PrefetchScalarGridSpec(
            num_scalar_prefetch=1,
            grid=(2, count),
            in_specs=[pl.BlockSpec((rows, model), lambda side, spot, core_ref: (0, 0))] * group
            + [left_spec(chunk) for _ in range(count) for chunk in range(chunks) for _ in range(group)],
            out_specs=[
                pl.BlockSpec(
                    block, lambda side, spot, core_ref: (jnp.where(side == 0, spot, count - 1), 0, 0)
                ),
                pl.BlockSpec(block, lambda side, spot, core_ref: (jnp.where(side == 0, 0, spot), 0, 0)),
            ],
            scratch_shapes=[
                pltpu.VMEM((chunks * tile, group * rows), jnp.bfloat16),
                pltpu.VMEM((group * rows, model), jnp.bfloat16),
            ],
        ),
        out_shape=[shape, shape],
        compiler_params=params(),
        name="weight_grad",
    )(
        scalar(lax.axis_index("replica") % 2),
        *rights,
        *[left for lefts in sets for _ in range(chunks) for left in lefts],
    )


def allowed_mask(query_segs_ref, key_segs_ref, rows, width):
    gap = (
        width
        - rows
        + lax.broadcasted_iota(jnp.int32, (rows, width), 0)
        - lax.broadcasted_iota(jnp.int32, (rows, width), 1)
    )
    return (gap >= 0) & (gap < WINDOW) & (query_segs_ref[...] == key_segs_ref[...])


def head_probs(query, keys, allowed, scale):
    scores = jnp.where(allowed, dot(query, keys, 1, 1) * scale, NEG)
    expo = jnp.exp(scores - jnp.max(scores, axis=-1, keepdims=True))
    return expo / jnp.sum(expo, axis=-1, keepdims=True)


def attention_specs(rows, size, width, heads):
    head = pl.BlockSpec((rows, size), lambda h: (0, h))
    whole = lambda *shape: pl.BlockSpec(shape, lambda h: (0, 0))
    common = [
        head,
        whole(1, size),
        whole(rows, size // 2),
        whole(rows, size // 2),
        whole(width, 2 * size),
        whole(rows, 1),
        whole(1, width),
    ]
    return head, whole, common


def attention_forward(qkv, gain, cosine, sine, pairs, query_segs, key_segs, heads):
    rows, width, size = qkv.shape[0], pairs.shape[0], pairs.shape[1] // 2
    head, _, common = attention_specs(rows, size, width, heads)

    def kernel(raw_ref, gain_ref, cos_ref, sin_ref, pairs_ref, qseg_ref, kseg_ref, query_ref, mixed_ref):
        query = head_post(raw_ref[...], gain_ref[...], cos_ref[...], sin_ref[...]).astype(jnp.bfloat16)
        query_ref[...] = query
        allowed = allowed_mask(qseg_ref, kseg_ref, rows, width)
        probs = head_probs(query, pairs_ref[:, :size], allowed, size**-0.5).astype(jnp.bfloat16)
        mixed_ref[...] = dot(probs, pairs_ref[:, size:], 1, 0).astype(jnp.bfloat16)

    shape = jax.ShapeDtypeStruct((rows, heads * size), jnp.bfloat16)
    return pl.pallas_call(
        kernel,
        grid=(heads,),
        in_specs=common,
        out_specs=[head, head],
        out_shape=[shape, shape],
        compiler_params=params(),
        name="attention_forward",
    )(qkv, gain, cosine, sine, pairs, query_segs, key_segs)


def attention_backward(qkv, gain, cosine, sine, pairs, query_segs, key_segs, query, grad_mixed, heads):
    rows, width, size = qkv.shape[0], pairs.shape[0], pairs.shape[1] // 2
    head, whole, common = attention_specs(rows, size, width, heads)
    before = width - rows

    def kernel(
        raw_ref, gain_ref, cos_ref, sin_ref, pairs_ref, qseg_ref, kseg_ref, query_ref, grad_ref,
        raw_grad_ref, gain_grad_ref, far_ref, own_ref, acc,
    ):
        step = pl.program_id(0)
        query = query_ref[...]
        grad = grad_ref[...]
        allowed = allowed_mask(qseg_ref, kseg_ref, rows, width)
        keys = pairs_ref[:, :size]
        probs = head_probs(query, keys, allowed, size**-0.5)
        grad_probs = dot(grad, pairs_ref[:, size:], 1, 1)
        delta = jnp.sum(grad_probs * probs, axis=-1, keepdims=True)
        grad_scores = (probs * (grad_probs - delta)).astype(jnp.bfloat16)
        grad_query = dot(grad_scores, keys, 1, 0) * size**-0.5
        grad_keys = dot(grad_scores, query, 0, 0) * size**-0.5
        grad_values = dot(probs.astype(jnp.bfloat16), grad, 0, 0)

        @pl.when(step == 0)
        def _():
            acc[:, :size] = grad_keys
            acc[:, size:] = grad_values

        @pl.when(step > 0)
        def _():
            acc[:, :size] += grad_keys
            acc[:, size:] += grad_values

        first = grad_query[:, : size // 2]
        second = grad_query[:, size // 2 :]
        cosine_part, sine_part = cos_ref[...], sin_ref[...]
        turned = jnp.concatenate(
            [
                first * cosine_part + second * sine_part,
                second * cosine_part - first * sine_part,
            ],
            axis=-1,
        )
        raw = raw_ref[...]
        scale = lax.rsqrt(jnp.mean(raw * raw, axis=-1, keepdims=True) + EPS)
        unit = raw * scale
        inner = turned * gain_ref[...].astype(jnp.float32)
        raw_grad = scale * (inner - unit * jnp.mean(inner * unit, axis=-1, keepdims=True))
        raw_grad_ref[...] = raw_grad.astype(jnp.bfloat16)
        gain_grad = jnp.sum(turned * unit, axis=0, keepdims=True)

        @pl.when(step == 0)
        def _():
            gain_grad_ref[...] = gain_grad

        @pl.when(step > 0)
        def _():
            gain_grad_ref[...] += gain_grad

        @pl.when(step == heads - 1)
        def _():
            far_ref[...] = acc[:before, :].astype(jnp.bfloat16)
            own_ref[...] = acc[before:, :]

    return pl.pallas_call(
        kernel,
        grid=(heads,),
        in_specs=common + [head, head],
        out_specs=[head, whole(1, size), whole(before, 2 * size), whole(rows, 2 * size)],
        out_shape=[
            jax.ShapeDtypeStruct((rows, heads * size), jnp.bfloat16),
            jax.ShapeDtypeStruct((1, size), jnp.float32),
            jax.ShapeDtypeStruct((before, 2 * size), jnp.bfloat16),
            jax.ShapeDtypeStruct((rows, 2 * size), jnp.float32),
        ],
        scratch_shapes=[pltpu.VMEM((width, 2 * size), jnp.float32)],
        compiler_params=params(),
        name="attention_backward",
    )(qkv, gain, cosine, sine, pairs, query_segs, key_segs, query, grad_mixed)


def line_edges():
    places = lax.axis_size("replica") // 2
    outer = places // 2 - 1
    return places, outer


def exchanged(block, pairs):
    route = [(2 * a + core, 2 * b + core) for a, b in pairs for core in range(2)]
    return lax.ppermute(block, "replica", route)


class Line:
    def __init__(self):
        self.places, self.outer = line_edges()
        self.steps = 2 * self.outer + 1
        self.moving = []
        self.done = {}

    def advance(self, fresh, gate=None):
        places, outer, steps = self.places, self.outer, self.steps
        place = (lax.axis_index("replica") // 2).astype(jnp.int32).reshape(1)
        operands, plan = [], []

        def operand(entry):
            array, index = entry if isinstance(entry, tuple) else (entry, None)
            for spot, (known, known_index) in enumerate(operands):
                if known is array and known_index == index:
                    return spot
            operands.append((array, index))
            return len(operands) - 1

        for name, block, step, far in self.moving:
            plan.append((name, step + 1, [operand(block), operand(far)], step))
        for name, terms in fresh:
            plan.append((name, 0, [operand(term) for term in terms], None))
        if not plan:
            return gate
        sizes = [operands[spots[0]][0].shape[-2:] for _, _, spots, _ in plan]
        by_step = {step: index for index, (_, step, _, _) in enumerate(plan)}
        pairs = []
        for edge in range(outer):
            inward, outward = by_step.get(edge), by_step.get(2 * outer - edge)
            if inward is not None and outward is not None and sizes[inward] == sizes[outward]:
                pairs.append((edge, inward, outward))
        cuts = 3 if all(size[0] % 48 == 0 for size in sizes) else 1

        def kernel(place_ref, *refs):
            here = place_ref[0]
            inputs = refs[: len(operands)]
            if gate is not None:
                refs = refs[: len(operands)] + refs[len(operands) + 1 :]
            outputs = refs[len(operands) :]
            states = []
            for spot, (_, _, terms, last) in enumerate(plan):
                value = inputs[terms[0]][...]
                if len(terms) > 1:
                    far = inputs[terms[1]][...]
                    total = value.astype(jnp.float32)
                    for term in terms[1:]:
                        total = total + inputs[term][...].astype(jnp.float32)
                    total = total.astype(jnp.bfloat16)
                    if last is None:
                        value = total
                    elif last <= outer:
                        edge = last
                        value = jnp.where((here == edge + 1) | (here == places - 2 - edge), total, value)
                    else:
                        edge = 2 * outer - last
                        value = jnp.where((here == edge) | (here == places - 1 - edge), far, value)
                states.append(value)
                outputs[spot][...] = value
            for spot, (edge, inward, outward) in enumerate(pairs):
                outputs[len(plan) + spot][...] = jnp.where(
                    (here == edge) | (here == places - 1 - edge), states[inward], states[outward]
                )

        def spec(size, index):
            if index is None:
                return pl.BlockSpec((size[0] // cuts, size[1]), lambda i, place_ref: (i, 0))
            return pl.BlockSpec((None, size[0] // cuts, size[1]), lambda i, place_ref: (index, i, 0))

        in_specs = [spec(array.shape[-2:], index) for array, index in operands]
        arrays = [array for array, _ in operands]
        out_sizes = sizes + [sizes[inward] for _, inward, _ in pairs]
        out_specs = [spec(size, None) for size in out_sizes]
        out_shape = [jax.ShapeDtypeStruct(size, jnp.bfloat16) for size in out_sizes]
        aliases = {}
        if gate is not None:
            aliases = {1 + len(arrays): len(out_shape)}
            in_specs.append(pl.BlockSpec(memory_space=pl.ANY))
            out_specs.append(pl.BlockSpec(memory_space=pl.ANY))
            out_shape.append(jax.ShapeDtypeStruct(gate.shape, gate.dtype))
            arrays.append(gate)
        outs = pl.pallas_call(
            kernel,
            grid_spec=pltpu.PrefetchScalarGridSpec(
                num_scalar_prefetch=1, grid=(cuts,), in_specs=in_specs, out_specs=out_specs
            ),
            out_shape=out_shape,
            input_output_aliases=aliases,
            compiler_params=params(),
            name="line_step",
        )(place, *arrays)
        received = {}
        for spot, (edge, inward, outward) in enumerate(pairs):
            ends = [(edge, edge + 1), (places - 1 - edge, places - 2 - edge)]
            far = exchanged(outs[len(plan) + spot], ends + [(b, a) for a, b in ends])
            received[inward] = received[outward] = far
        self.moving = []
        for index, (name, step, _, _) in enumerate(plan):
            block = outs[index]
            if step == steps:
                self.done[name] = block
                continue
            if index not in received:
                edge = step if step <= outer else 2 * outer - step
                route = [(edge, edge + 1), (places - 1 - edge, places - 2 - edge)]
                if step > outer:
                    route = [(b, a) for a, b in route]
                received[index] = exchanged(block, route)
            self.moving.append((name, block, step, received[index]))
        return outs[-1]

    def arrived(self):
        return [far for _, _, _, far in self.moving]

    def finished(self, name):
        while name not in self.done:
            self.advance([])
        return self.done[name]


def line_names(name, units):
    return [(name, chunk) for chunk in range(chunks_of(units))]


def whole_grad(lines, name, units, dtype=jnp.float32):
    names = line_names(name, units)
    mines = [lines[chunk[1]].finished(chunk) for chunk in names]
    others = [swapped(mine, "replica", 1) for mine in mines]
    chunks = len(mines)
    tile, model = mines[0].shape
    core = (lax.axis_index("replica") % 2).astype(jnp.int32).reshape(1)

    def kernel(core_ref, *refs):
        out_ref = refs[-1]
        for chunk in range(chunks):
            for side in range(2):

                @pl.when((pl.program_id(0) == chunk) & (pl.program_id(1) == side))
                def _():
                    @pl.when(core_ref[0] == side)
                    def _():
                        out_ref[...] = refs[chunk][...].astype(dtype)

                    @pl.when(core_ref[0] != side)
                    def _():
                        out_ref[...] = refs[chunks + chunk][...].astype(dtype)

    return pl.pallas_call(
        kernel,
        grid_spec=pltpu.PrefetchScalarGridSpec(
            num_scalar_prefetch=1,
            grid=(chunks, 2),
            in_specs=[pl.BlockSpec((tile, model), lambda chunk, side, core_ref: (0, 0))] * (2 * chunks),
            out_specs=pl.BlockSpec((tile, model), lambda chunk, side, core_ref: (2 * chunk + side, 0)),
        ),
        out_shape=jax.ShapeDtypeStruct((units, model), dtype),
        compiler_params=params(),
        name="whole_grad",
    )(core, *mines, *others)


def joined(mine, other, axis):
    core = lax.axis_index("replica") % 2
    return jnp.where(
        core == 0,
        jnp.concatenate([mine, other], axis=axis),
        jnp.concatenate([other, mine], axis=axis),
    )


def core_join(block, axis):
    return joined(block, swapped(block, "replica", 1), axis)


def fetched(block):
    got = [swapped(block, "fsdp", mask) for mask in range(1, lax.axis_size("fsdp"))]
    return got, [swapped(part, "replica", 1) for part in got]


def gathered(block):
    group = lax.axis_size("fsdp")
    blocks, near = [block] + [None] * (group - 1), []
    for ring in range(1, group.bit_length()):
        masks = [mask for mask in range(1, group) if bin(mask).count("1") == ring]
        source = after(block, *near) if near else block
        near = [swapped(source, "fsdp", mask) for mask in masks]
        for mask, far in zip(masks, near):
            blocks[mask] = far
    return blocks


def passed_along(block, axis, distance):
    devices = range(lax.axis_size(axis))
    route = [(i - distance, i) for i in devices if i - distance in devices]
    return lax.ppermute(block, axis, route)


def contract(left, right, left_dim, right_dim):
    return lax.dot_general(
        left, right, (((left_dim,), (right_dim,)), ((), ())), preferred_element_type=jnp.float32
    )


def normed(value, gain):
    return value * lax.rsqrt(jnp.mean(value * value, axis=-1, keepdims=True) + EPS) * gain


def norm_back(value, gain, grad):
    _, pull = jax.vjp(normed, value, gain)
    return pull(grad)


def tables(places, half):
    freq = 10000.0 ** (-(2.0 * jnp.arange(half, dtype=jnp.float32)) / (2 * half))
    angle = places.astype(jnp.float32)[:, None] * freq[None, :]
    return (jnp.cos(angle), jnp.sin(angle))


def rotate(value, cosine, sine):
    half = value.shape[-1] // 2
    first = value[..., :half]
    second = value[..., half:]
    return jnp.concatenate(
        [first * cosine - second * sine, second * cosine + first * sine], axis=-1
    )


def head_post(raw, gain, cosine, sine):
    return rotate(normed(raw, gain), cosine, sine)


def per_device(
    hidden_in,
    out_grad,
    segments,
    positions,
    norm_in,
    query_weight,
    key_weight,
    value_weight,
    out_weight,
    norm_attn,
    norm_ffn,
    gate_weight,
    up_weight,
    down_weight,
    norm_out,
    query_gain,
    key_gain,
):
    rows = hidden_in.shape[0]
    rank = lax.axis_index("fsdp")
    group = lax.axis_size("fsdp")
    masks = range(1, group)
    head_size = key_weight.shape[1]
    heads = query_weight.shape[1] // head_size
    model = hidden_in.shape[1]
    own_model = norm_in.shape[0]
    own_head = query_gain.shape[0]
    hops = (WINDOW - 1) // rows + 1
    scale = head_size ** (-0.5)
    qkv_weights = (query_weight, key_weight, value_weight)
    wide = sum(weight.shape[1] for weight in qkv_weights)
    got, peers = fetched(packed(qkv_weights))
    gains = jnp.stack(
        [
            jnp.pad(gain, (0, own_model - gain.shape[0]))
            for gain in (norm_in, norm_attn, norm_ffn, norm_out, query_gain, key_gain)
        ]
    )
    gain_stack = jnp.stack([gains] + [swapped(gains, "fsdp", mask) for mask in masks])
    w_qkv = unpacked(qkv_weights, got, peers)
    gain_rows = jnp.stack(
        [lax.dynamic_index_in_dim(gain_stack, rank ^ i, 0, keepdims=False) for i in range(group)], axis=1
    )
    gain_in, gain_attn, gain_ffn, gain_out = (gain_rows[i].reshape(-1) for i in range(4))
    gain_query, gain_key = (gain_rows[i, :, :own_head].reshape(-1) for i in (4, 5))
    got, peers = fetched(after(packed([out_weight]), w_qkv))
    residual_in = hidden_in.astype(jnp.float32)
    normed_in = normed(residual_in, gain_in).astype(jnp.bfloat16)
    qkv = jnp.dot(normed_in, w_qkv, preferred_element_type=jnp.float32)
    key_raw = qkv[:, heads * head_size : (heads + 1) * head_size]
    value_new = qkv[:, (heads + 1) * head_size :].astype(jnp.bfloat16)
    cosine, sine = tables(positions, head_size // 2)
    key_new = head_post(key_raw, gain_key, cosine, sine).astype(jnp.bfloat16)
    pair_new = jnp.concatenate([key_new, value_new], axis=1)
    parts = [pair_new]
    for step in range(1, hops + 1):
        parts.insert(0, passed_along(pair_new, "fsdp", step))
    pairs = jnp.concatenate(parts, axis=0)
    width = pairs.shape[0]
    seg_padded = jnp.concatenate([jnp.full((hops * rows,), -1, jnp.int32), segments], axis=0)
    key_segs = lax.dynamic_slice_in_dim(seg_padded, rank * rows, width, 0)
    query_segs = lax.dynamic_slice_in_dim(segments, rank * rows, rows, 0)
    attention_args = (
        qkv,
        gain_query[None, :],
        cosine,
        sine,
        pairs,
        query_segs[:, None],
        key_segs[None, :],
    )
    query_new, mixed = attention_forward(*attention_args, heads)
    w_out = unpacked([out_weight], got, peers)
    attended = contract(mixed, w_out, 1, 1)
    resid = residual_in + normed(attended, gain_attn)
    ffn_in = normed(resid, gain_ffn).astype(jnp.bfloat16)
    ffn_blocks = gathered(ffn_in)
    hiddens, slopes, acts, parts = {}, {}, {}, {}
    rings = sorted(range(group), key=lambda mask: (bin(mask).count("1"), mask))
    last = None
    for mask in rings[1:] + [0]:
        if last is not None:
            ffn_blocks[mask] = after(ffn_blocks[mask], parts[last])
        hiddens[mask], slopes[mask], acts[mask], parts[mask] = ffn_forward(
            ffn_blocks[mask], gate_weight, up_weight, down_weight
        )
        last = mask
    branch = sum(
        (swapped(parts[mask], "fsdp", mask) if mask else parts[mask]).astype(jnp.float32)
        for mask in range(group)
    )
    result = resid + normed(branch, gain_out)
    hidden_out = result.astype(jnp.bfloat16)
    grad_result = out_grad.astype(jnp.float32)
    grad_branch, grad_gain_out = norm_back(branch, gain_out, grad_result)
    grad_branch_low = grad_branch.astype(jnp.bfloat16)
    pieces = gathered(grad_branch_low)
    units = gate_weight.shape[0]
    lines = [Line(), Line()]

    def fresh(names, other, mine):
        far = swapped(other, "replica", 1)
        keys = [key for name in names for key in line_names(name, units)]
        return [(key, [(mine, spot), (far, spot)]) for spot, key in enumerate(keys)]

    grad_gates, grad_uppers, returned = {}, {}, {}
    final = rings[-1]
    last = None
    for mask in rings[:-1]:
        if last is not None:
            pieces[mask] = after(pieces[mask], part)
        grad_gates[mask], grad_uppers[mask], part = ffn_backward(
            pieces[mask], gate_weight, up_weight, down_weight, slopes[mask], acts[mask]
        )
        returned[mask] = swapped(part, "fsdp", mask) if mask else part
        last = mask
    pieces[final] = after(pieces[final], part)
    waiting = fresh(
        ["down"], *weight_grad([[hiddens[i] for i in range(group)]], [pieces[i] for i in range(group)])
    )
    gate_parts, upper_parts, parts = ffn_backward_blocks(
        [pieces[final]], gate_weight, up_weight, down_weight, [slopes[final]], [acts[final]]
    )
    grad_gates[final], grad_uppers[final] = gate_parts[0], upper_parts[0]
    returned[final] = swapped(parts[0], "fsdp", final)
    grad_gates[final] = after(grad_gates[final], *[returned[mask] for mask in rings[1:-1]])
    grad_gates[final] = lines[0].advance([waiting.pop(0)], grad_gates[final])
    other, mine = weight_grad(
        [[grad_gates[i] for i in range(group)], [grad_uppers[i] for i in range(group)]], ffn_blocks
    )
    other = after(other, *lines[0].arrived(), returned[final])
    other = lines[1].advance([waiting.pop(0)] if waiting else [], other)
    waiting = fresh(["gate", "up"], other, mine)

    def advance(spot, gate=None):
        ready = [entry for entry in waiting if entry[0][1] == spot][:1]
        for entry in ready:
            waiting.remove(entry)
        return lines[spot].advance(ready, gate)

    grad_resid, grad_attended_low, grad_mixed, grad_gain_ffn, grad_gain_attn = resid_backward(
        [returned[mask] for mask in range(group)], resid, attended, out_grad, gain_ffn, gain_attn, w_out
    )
    grad_mixed = advance(0, grad_mixed)
    grad_query_low, grad_gain_query, grad_far, grad_pair = attention_backward(
        *attention_args, query_new, grad_mixed, heads
    )
    grad_far = advance(1, grad_far)
    backs = []
    for step in range(1, hops + 1):
        if step == 2:
            grad_far = after(grad_far, *lines[0].arrived())
        grad_far = passed_along(grad_far, "fsdp", -1)
        backs.append(grad_far[-rows:])
        grad_far = grad_far[:-rows]
    grad_pair = advance(0, grad_pair)
    other, mine, grad_in = input_backward(
        grad_pair,
        backs,
        qkv,
        cosine,
        sine,
        gain_key,
        normed_in,
        grad_query_low,
        w_qkv,
        hidden_in,
        gain_in,
        grad_resid,
        grad_attended_low,
        mixed,
        [grad_gain_attn, grad_gain_ffn, grad_gain_out[None, :], grad_gain_query],
        group,
    )
    other = advance(1, after(other, *lines[0].arrived()))
    chip = added(mine, swapped(other, "replica", 1))
    owned = lax.psum_scatter(chip, "fsdp", scatter_dimension=0, tiled=True)[0]
    advance(0)
    advance(1)
    while waiting:
        advance(0)
    lines[0].advance([("weights", [owned])])
    advance(1)
    grad_down = whole_grad(lines, "down", units)
    grad_down = lines[0].advance([], grad_down)
    grad_gate_w = whole_grad(lines, "gate", units)
    grad_gate_w = lines[1].advance([], grad_gate_w)
    grad_up_w = whole_grad(lines, "up", units)
    owned = core_join(lines[0].finished("weights"), 1).astype(jnp.float32)
    inner = heads * head_size
    columns = [0, inner, inner + head_size, inner + 2 * head_size, wide + inner]
    owned_query, owned_key, owned_value, owned_out = (
        owned[:own_model, columns[i] : columns[i + 1]] for i in range(4)
    )

    def owned_gain(row, size):
        return lax.dynamic_slice_in_dim(owned[own_model + row], rank * size, size, 0)

    owned_gain_in, owned_gain_attn, owned_gain_ffn, owned_gain_out = (
        owned_gain(row, own_model) for row in (0, 2, 3, 4)
    )
    owned_gain_key, owned_gain_query = (owned_gain(row, own_head) for row in (1, 5))
    return (
        hidden_out,
        grad_in,
        owned_gain_in,
        owned_query,
        owned_key,
        owned_value,
        owned_out,
        owned_gain_attn,
        owned_gain_ffn,
        grad_gate_w,
        grad_up_w,
        grad_down,
        owned_gain_out,
        owned_gain_query,
        owned_gain_key,
    )


def solution(mesh):
    return jax.shard_map(
        per_device,
        mesh=mesh,
        in_specs=(
            P(("replica", "fsdp"), None),
            P(("replica", "fsdp"), None),
            P("replica"),
            P(("replica", "fsdp")),
            P("fsdp"),
            P("fsdp", None),
            P("fsdp", None),
            P("fsdp", None),
            P("fsdp", None),
            P("fsdp"),
            P("fsdp"),
            P("fsdp", None),
            P("fsdp", None),
            P("fsdp", None),
            P("fsdp"),
            P("fsdp"),
            P("fsdp"),
        ),
        out_specs=(
            P(("replica", "fsdp"), None),
            P(("replica", "fsdp"), None),
            P("fsdp"),
            P("fsdp", None),
            P("fsdp", None),
            P("fsdp", None),
            P("fsdp", None),
            P("fsdp"),
            P("fsdp"),
            P("fsdp", None),
            P("fsdp", None),
            P("fsdp", None),
            P("fsdp"),
            P("fsdp"),
            P("fsdp"),
        ),
        check_vma=False,
    )
```

```python
import jax
import jax.numpy as jnp
from jax import lax
from jax.experimental import pallas as pl
from jax.experimental.pallas import tpu as pltpu
from jax.sharding import PartitionSpec as P

WINDOW = 512


EPS = 1e-06
NEG = -1e30


def swapped(block, axis, mask):
    route = [(i, i ^ mask) for i in range(lax.axis_size(axis))]
    return lax.ppermute(block, axis, route)


def added(left, right):
    total = left.astype(jnp.float32) + right.astype(jnp.float32)
    return lax.optimization_barrier(total.astype(jnp.bfloat16))


def params(mebibytes=48):
    return pltpu.CompilerParams(vmem_limit_bytes=mebibytes * 1024 * 1024)


def dot(left, right, left_dim, right_dim):
    return lax.dot_general(
        left, right, (((left_dim,), (right_dim,)), ((), ())), preferred_element_type=jnp.float32
    )


def after(array, *others):
    place = pl.BlockSpec(memory_space=pl.ANY)
    return pl.pallas_call(
        lambda *refs: None,
        out_shape=jax.ShapeDtypeStruct(array.shape, array.dtype),
        in_specs=[place] * (1 + len(others)),
        out_specs=place,
        input_output_aliases={0: 0},
        compiler_params=params(1),
        name="after",
    )(array, *others)


def scalar(value):
    return value.astype(jnp.int32).reshape(1)


def packed(weights):
    half = weights[0].shape[0] // 2
    wide = sum(weight.shape[1] for weight in weights)

    def kernel(core_ref, *refs):
        out_ref = refs[-1]
        for side in range(2):

            @pl.when(core_ref[0] == side)
            def _():
                at = 0
                for ref in refs[:-1]:
                    out_ref[:, at : at + ref.shape[1]] = ref[side * half : (side + 1) * half, :]
                    at += ref.shape[1]

    return pl.pallas_call(
        kernel,
        grid_spec=pltpu.PrefetchScalarGridSpec(
            num_scalar_prefetch=1,
            grid=(1,),
            in_specs=[pl.BlockSpec(weight.shape, lambda i, core_ref: (0, 0)) for weight in weights],
            out_specs=pl.BlockSpec((half, wide), lambda i, core_ref: (0, 0)),
        ),
        out_shape=jax.ShapeDtypeStruct((half, wide), jnp.bfloat16),
        compiler_params=params(16),
        name="pack",
    )(scalar(lax.axis_index("replica") % 2), *weights)


def unpacked(weights, got, peers):
    rows = weights[0].shape[0]
    half = rows // 2
    group = len(got) + 1
    wide = sum(weight.shape[1] for weight in weights)
    own = len(weights)

    def kernel(core_ref, rank_ref, *refs):
        out_ref = refs[-1]
        mask = rank_ref[0] ^ pl.program_id(0)

        @pl.when(mask == 0)
        def _():
            at = 0
            for ref in refs[:own]:
                out_ref[:, at : at + ref.shape[1]] = ref[...]
                at += ref.shape[1]

        for other in range(1, group):
            for side in range(2):

                @pl.when((mask == other) & (core_ref[0] == side))
                def _():
                    out_ref[side * half : (side + 1) * half, :] = refs[own + other - 1][:half, :]
                    out_ref[(1 - side) * half : (2 - side) * half, :] = refs[own + group - 2 + other][:half, :]

    arrays = list(weights) + list(got) + list(peers)
    return pl.pallas_call(
        kernel,
        grid_spec=pltpu.PrefetchScalarGridSpec(
            num_scalar_prefetch=2,
            grid=(group,),
            in_specs=[pl.BlockSpec(array.shape, lambda i, *refs: (0, 0)) for array in arrays],
            out_specs=pl.BlockSpec((rows, wide), lambda i, *refs: (i, 0)),
        ),
        out_shape=jax.ShapeDtypeStruct((group * rows, wide), jnp.bfloat16),
        compiler_params=params(24),
        name="unpack",
    )(scalar(lax.axis_index("replica") % 2), scalar(lax.axis_index("fsdp")), *arrays)


GELU_A = (2.0 / 3.141592653589793) ** 0.5
GELU_B = 0.044715


def ffn_forward(x, gate_weight, up_weight, down_weight):
    gate = contract(gate_weight, x, 1, 1)
    upper = contract(up_weight, x, 1, 1)
    square = gate * gate
    bend = jnp.tanh(GELU_A * gate * (1.0 + GELU_B * square))
    half = 0.5 + 0.5 * bend
    act = gate * half
    slope = half + 0.5 * gate * (1.0 - bend * bend) * (GELU_A * (1.0 + 3.0 * GELU_B * square))
    hidden = (act * upper).astype(jnp.bfloat16)
    part = contract(hidden, down_weight, 0, 0).astype(jnp.bfloat16)
    return hidden, (slope * upper).astype(jnp.bfloat16), act.astype(jnp.bfloat16), part


def ffn_backward(grad, gate_weight, up_weight, down_weight, slope, act):
    grad_hidden = contract(down_weight, grad, 1, 1)
    grad_gate = (grad_hidden * slope.astype(jnp.float32)).astype(jnp.bfloat16)
    grad_upper = (grad_hidden * act.astype(jnp.float32)).astype(jnp.bfloat16)
    part = contract(grad_gate, gate_weight, 0, 0) + contract(grad_upper, up_weight, 0, 0)
    return grad_gate, grad_upper, part.astype(jnp.bfloat16)


def tile_of(size, most):
    return max(tile for tile in range(16, most + 1, 16) if size % tile == 0)


def ffn_backward_blocks(grads, gate_weight, up_weight, down_weight, slopes, acts):
    count = len(grads)
    rows, model = grads[0].shape
    units = gate_weight.shape[0]
    tile = tile_of(units, 432)
    steps = units // tile

    def kernel(*refs):
        step = pl.program_id(0)
        grad_refs, refs = refs[:count], refs[count:]
        (gate_ref, up_ref, down_ref), refs = refs[:3], refs[3:]
        slope_refs, act_refs, refs = refs[:count], refs[count : 2 * count], refs[2 * count :]
        gate_outs, up_outs, part_outs, (grad_ref, acc) = (
            refs[:count],
            refs[count : 2 * count],
            refs[2 * count : 3 * count],
            refs[3 * count :],
        )

        @pl.when(step == 0)
        def _():
            for spot in range(count):
                grad_ref[spot * rows : (spot + 1) * rows, :] = grad_refs[spot][...]
            acc[...] = jnp.zeros_like(acc)

        grad_hidden = dot(down_ref[...], grad_ref[...], 1, 1)
        slope = jnp.concatenate([ref[...] for ref in slope_refs], axis=1).astype(jnp.float32)
        act = jnp.concatenate([ref[...] for ref in act_refs], axis=1).astype(jnp.float32)
        grad_gate = (grad_hidden * slope).astype(jnp.bfloat16)
        grad_upper = (grad_hidden * act).astype(jnp.bfloat16)
        for spot in range(count):
            gate_outs[spot][...] = grad_gate[:, spot * rows : (spot + 1) * rows]
            up_outs[spot][...] = grad_upper[:, spot * rows : (spot + 1) * rows]
        acc[...] += dot(grad_gate, gate_ref[...], 0, 0) + dot(grad_upper, up_ref[...], 0, 0)

        @pl.when(step == steps - 1)
        def _():
            for spot in range(count):
                part_outs[spot][...] = acc[spot * rows : (spot + 1) * rows, :].astype(jnp.bfloat16)

    weight = pl.BlockSpec((tile, model), lambda i: (i, 0))
    flat = pl.BlockSpec((tile, rows), lambda i: (i, 0))
    whole = pl.BlockSpec((rows, model), lambda i: (0, 0))
    kept = jax.ShapeDtypeStruct((units, rows), jnp.bfloat16)
    outs = pl.pallas_call(
        kernel,
        grid=(steps,),
        out_shape=[kept] * (2 * count) + [jax.ShapeDtypeStruct((rows, model), jnp.bfloat16)] * count,
        in_specs=[whole] * count + [weight] * 3 + [flat] * (2 * count),
        out_specs=[flat] * (2 * count) + [whole] * count,
        scratch_shapes=[
            pltpu.VMEM((count * rows, model), jnp.bfloat16),
            pltpu.VMEM((count * rows, model), jnp.float32),
        ],
        compiler_params=params(),
        name="ffn_backward",
    )(*grads, gate_weight, up_weight, down_weight, *slopes, *acts)
    return outs[:count], outs[count : 2 * count], outs[2 * count :]


def norm_pull(value, gain, grad):
    scale = lax.rsqrt(jnp.mean(value * value, axis=-1, keepdims=True) + EPS)
    unit = value * scale
    inner = grad * gain
    return scale * (inner - unit * jnp.mean(inner * unit, axis=-1, keepdims=True)), grad * unit


def resid_backward(parts, resid, attended, out_grad, gain_ffn, gain_attn, w_out):
    count = len(parts)
    rows, model = resid.shape
    tile = min(rows, 128)

    def kernel(*refs):
        part_refs, refs = refs[:count], refs[count:]
        resid_ref, attended_ref, out_ref, ffn_ref, attn_ref, weight_ref, refs = *refs[:6], refs[6:]
        grad_resid_ref, grad_attended_ref, grad_mixed_ref, ffn_grad_ref, attn_grad_ref = refs
        grad = sum(ref[...].astype(jnp.float32) for ref in part_refs)
        pulled, ffn_rows = norm_pull(resid_ref[...], ffn_ref[...].astype(jnp.float32), grad)
        grad_resid = out_ref[...].astype(jnp.float32) + pulled
        grad_resid_ref[...] = grad_resid
        pulled, attn_rows = norm_pull(attended_ref[...], attn_ref[...].astype(jnp.float32), grad_resid)
        grad_attended = pulled.astype(jnp.bfloat16)
        grad_attended_ref[...] = grad_attended
        grad_mixed_ref[...] = dot(grad_attended, weight_ref[...], 1, 0).astype(jnp.bfloat16)
        ffn_grad = jnp.sum(ffn_rows, axis=0, keepdims=True)
        attn_grad = jnp.sum(attn_rows, axis=0, keepdims=True)

        @pl.when(pl.program_id(0) == 0)
        def _():
            ffn_grad_ref[...] = ffn_grad
            attn_grad_ref[...] = attn_grad

        @pl.when(pl.program_id(0) > 0)
        def _():
            ffn_grad_ref[...] += ffn_grad
            attn_grad_ref[...] += attn_grad

    block = pl.BlockSpec((tile, model), lambda i: (i, 0))
    vector = pl.BlockSpec((1, model), lambda i: (0, 0))
    inner = w_out.shape[1]
    return pl.pallas_call(
        kernel,
        grid=(rows // tile,),
        in_specs=[block] * (count + 3) + [vector] * 2 + [pl.BlockSpec(w_out.shape, lambda i: (0, 0))],
        out_specs=[block, block, pl.BlockSpec((tile, inner), lambda i: (i, 0)), vector, vector],
        out_shape=[
            jax.ShapeDtypeStruct((rows, model), jnp.float32),
            jax.ShapeDtypeStruct((rows, model), jnp.bfloat16),
            jax.ShapeDtypeStruct((rows, inner), jnp.bfloat16),
            jax.ShapeDtypeStruct((1, model), jnp.float32),
            jax.ShapeDtypeStruct((1, model), jnp.float32),
        ],
        compiler_params=params(32),
        name="resid_backward",
    )(*parts, resid, attended, out_grad, gain_ffn[None, :], gain_attn[None, :], w_out)


def input_backward(
    own_pair, backs, qkv, cosine, sine, gain_key, normed_in, grad_query, w_qkv, hidden_in, gain_in, grad_resid,
    grad_attended, mixed, gain_grads, group,
):
    rows, model = hidden_in.shape
    size = own_pair.shape[1] // 2
    inner = grad_query.shape[1]
    own_rows = model // group
    half = inner + size
    hops = len(backs)
    count = len(gain_grads)

    def kernel(core_ref, *refs):
        pair_ref, refs = refs[0], refs[1:]
        back_refs, refs = refs[:hops], refs[hops:]
        (
            raw_ref, cos_ref, sin_ref, key_gain_ref, normed_ref, query_ref, weight_ref, x_ref, gain_ref, resid_ref,
            attended_ref, mixed_ref, refs,
        ) = *refs[:12], refs[12:]
        gain_refs, refs = refs[:count], refs[count:]
        other_ref, mine_ref, grad_in_ref, rows_ref = refs
        pair = pair_ref[...] + sum(ref[...].astype(jnp.float32) for ref in back_refs)
        first = pair[:, : size // 2]
        second = pair[:, size // 2 : size]
        turned = jnp.concatenate(
            [
                first * cos_ref[...] + second * sin_ref[...],
                second * cos_ref[...] - first * sin_ref[...],
            ],
            axis=-1,
        )
        pulled, key_rows = norm_pull(raw_ref[...], key_gain_ref[...].astype(jnp.float32), turned)
        grad_key = pulled.astype(jnp.bfloat16)
        grad_value = pair[:, size:].astype(jnp.bfloat16)
        grad_normed = (
            dot(query_ref[...], weight_ref[:, :inner], 1, 1)
            + dot(grad_key, weight_ref[:, inner:half], 1, 1)
            + dot(grad_value, weight_ref[:, half:], 1, 1)
        )
        pulled, in_rows = norm_pull(
            x_ref[...].astype(jnp.float32), gain_ref[...].astype(jnp.float32), grad_normed
        )
        grad_in_ref[...] = resid_ref[...] + pulled
        rows_ref[...] = jnp.zeros_like(rows_ref)
        rows_ref[0:1, :model] = jnp.sum(in_rows, axis=0, keepdims=True)
        rows_ref[1:2, :size] = jnp.sum(key_rows, axis=0, keepdims=True)
        for spot in range(count):
            rows_ref[2 + spot : 3 + spot, : gain_refs[spot].shape[1]] = gain_refs[spot][...].astype(
                jnp.float32
            )
        gains = rows_ref[...].astype(jnp.bfloat16)

        def write(ref, side):
            pieces = (
                [(normed_ref, query_ref[...], 0, inner), (normed_ref, grad_key, inner, half)]
                if side == 0
                else [(normed_ref, grad_value, 0, size), (attended_ref, mixed_ref[...], size, half)]
            )
            for left, right, begin, end in pieces:
                value = dot(left[...], right, 0, 0).astype(jnp.bfloat16)
                for owner in range(group):
                    ref[owner, :own_rows, begin:end] = value[owner * own_rows : (owner + 1) * own_rows]
            for owner in range(group):
                ref[owner, own_rows:, :] = gains

        for core in range(2):

            @pl.when(core_ref[0] == core)
            def _():
                write(other_ref, 1 - core)
                write(mine_ref, core)

    def whole(array):
        return pl.BlockSpec(array.shape, lambda i, core_ref: (0,) * len(array.shape))

    arrays = [
        own_pair, *backs, qkv, cosine, sine, gain_key[None, :], normed_in, grad_query, w_qkv, hidden_in,
        gain_in[None, :], grad_resid, grad_attended, mixed, *gain_grads,
    ]
    in_specs = [whole(array) for array in arrays]
    in_specs[1 + hops] = pl.BlockSpec((rows, size), lambda i, core_ref: (0, inner // size))
    shape = jax.ShapeDtypeStruct((group, own_rows + 16, half), jnp.bfloat16)
    grad_in = jax.ShapeDtypeStruct((rows, model), jnp.float32)
    return pl.pallas_call(
        kernel,
        grid_spec=pltpu.PrefetchScalarGridSpec(
            num_scalar_prefetch=1,
            grid=(1,),
            in_specs=in_specs,
            out_specs=[whole(shape), whole(shape), whole(grad_in)],
            scratch_shapes=[pltpu.VMEM((16, half), jnp.float32)],
        ),
        out_shape=[shape, shape, grad_in],
        compiler_params=params(),
        name="input_backward",
    )(scalar(lax.axis_index("replica") % 2), *arrays)


def owner_parts(other, mine):
    group, height, wide = mine.shape
    far = swapped(other, "replica", 1)

    def kernel(rank_ref, mine_ref, far_ref, *outs):
        total = mine_ref[...].astype(jnp.float32) + far_ref[...].astype(jnp.float32)
        for mask in range(group):

            @pl.when(pl.program_id(0) == mask)
            def _():
                outs[mask][...] = total.astype(jnp.bfloat16)

    block = pl.BlockSpec((None, height, wide), lambda i, rank_ref: (rank_ref[0] ^ i, 0, 0))
    parts = pl.pallas_call(
        kernel,
        grid_spec=pltpu.PrefetchScalarGridSpec(
            num_scalar_prefetch=1,
            grid=(group,),
            in_specs=[block, block],
            out_specs=[pl.BlockSpec((height, wide), lambda i, rank_ref: (0, 0))] * group,
        ),
        out_shape=[jax.ShapeDtypeStruct((height, wide), jnp.bfloat16)] * group,
        compiler_params=params(16),
        name="owner_parts",
    )(scalar(lax.axis_index("fsdp")), mine, far)
    return [parts[0]] + [swapped(parts[mask], "fsdp", mask) for mask in range(1, group)]


def weight_grad_whole(lefts, rights):
    group = len(rights)
    units, rows = lefts[0].shape
    model = rights[0].shape[1]
    tile = tile_of(units, 432)

    def kernel(*refs):
        right_refs, left_refs = refs[:group], refs[group : 2 * group]
        out_ref, left_ref, right_ref = refs[2 * group :]

        @pl.when(pl.program_id(0) == 0)
        def _():
            for spot in range(group):
                right_ref[spot * rows : (spot + 1) * rows, :] = right_refs[spot][...]

        for spot in range(group):
            left_ref[:, spot * rows : (spot + 1) * rows] = left_refs[spot][...]
        out_ref[...] = dot(left_ref[...], right_ref[...], 1, 0).astype(jnp.bfloat16)

    return pl.pallas_call(
        kernel,
        grid=(units // tile,),
        in_specs=[pl.BlockSpec((rows, model), lambda i: (0, 0))] * group
        + [pl.BlockSpec((tile, rows), lambda i: (i, 0))] * group,
        out_specs=pl.BlockSpec((tile, model), lambda i: (i, 0)),
        out_shape=jax.ShapeDtypeStruct((units, model), jnp.bfloat16),
        scratch_shapes=[
            pltpu.VMEM((tile, group * rows), jnp.bfloat16),
            pltpu.VMEM((group * rows, model), jnp.bfloat16),
        ],
        compiler_params=params(32),
        name="weight_grad",
    )(*rights, *lefts)


def chunks_of(units):
    return 2 if units % 64 == 0 else 1


def weight_grad(sets, rights):
    group = len(rights)
    count = len(sets)
    units, rows = sets[0][0].shape
    model = rights[0].shape[1]
    chunks = chunks_of(units)
    tile = units // (2 * chunks)

    def kernel(core_ref, *refs):
        right_refs, left_refs = refs[:group], refs[group:-4]
        other_ref, mine_ref, left_ref, right_ref = refs[-4:]

        @pl.when((pl.program_id(0) == 0) & (pl.program_id(1) == 0))
        def _():
            for spot in range(group):
                right_ref[spot * rows : (spot + 1) * rows, :] = right_refs[spot][...]

        for index in range(count):

            @pl.when(pl.program_id(1) == index)
            def _():
                for chunk in range(chunks):
                    for spot in range(group):
                        left_ref[
                            chunk * tile : (chunk + 1) * tile, spot * rows : (spot + 1) * rows
                        ] = left_refs[(index * chunks + chunk) * group + spot][...]

        value = dot(left_ref[...], right_ref[...], 1, 0).astype(jnp.bfloat16)

        @pl.when(pl.program_id(0) == 0)
        def _():
            for chunk in range(chunks):
                other_ref[chunk] = value[chunk * tile : (chunk + 1) * tile]

        @pl.when(pl.program_id(0) == 1)
        def _():
            for chunk in range(chunks):
                mine_ref[chunk] = value[chunk * tile : (chunk + 1) * tile]

    def left_spec(chunk):
        def index(side, spot, core_ref):
            return (2 * chunk + jnp.where(side == 0, 1 - core_ref[0], core_ref[0]), 0)

        return pl.BlockSpec((tile, rows), index)

    shape = jax.ShapeDtypeStruct((count * chunks, tile, model), jnp.bfloat16)
    block = (chunks, tile, model)
    return pl.pallas_call(
        kernel,
        grid_spec=pltpu.PrefetchScalarGridSpec(
            num_scalar_prefetch=1,
            grid=(2, count),
            in_specs=[pl.BlockSpec((rows, model), lambda side, spot, core_ref: (0, 0))] * group
            + [left_spec(chunk) for _ in range(count) for chunk in range(chunks) for _ in range(group)],
            out_specs=[
                pl.BlockSpec(
                    block, lambda side, spot, core_ref: (jnp.where(side == 0, spot, count - 1), 0, 0)
                ),
                pl.BlockSpec(block, lambda side, spot, core_ref: (jnp.where(side == 0, 0, spot), 0, 0)),
            ],
            scratch_shapes=[
                pltpu.VMEM((chunks * tile, group * rows), jnp.bfloat16),
                pltpu.VMEM((group * rows, model), jnp.bfloat16),
            ],
        ),
        out_shape=[shape, shape],
        compiler_params=params(),
        name="weight_grad",
    )(
        scalar(lax.axis_index("replica") % 2),
        *rights,
        *[left for lefts in sets for _ in range(chunks) for left in lefts],
    )


def allowed_mask(query_segs_ref, key_segs_ref, rows, width):
    gap = (
        width
        - rows
        + lax.broadcasted_iota(jnp.int32, (rows, width), 0)
        - lax.broadcasted_iota(jnp.int32, (rows, width), 1)
    )
    return (gap >= 0) & (gap < WINDOW) & (query_segs_ref[...] == key_segs_ref[...])


def head_probs(query, keys, allowed, scale):
    scores = jnp.where(allowed, dot(query, keys, 1, 1) * scale, NEG)
    expo = jnp.exp(scores - jnp.max(scores, axis=-1, keepdims=True))
    return expo / jnp.sum(expo, axis=-1, keepdims=True)


def attention_specs(rows, size, width, heads):
    head = pl.BlockSpec((rows, size), lambda h: (0, h))
    whole = lambda *shape: pl.BlockSpec(shape, lambda h: (0, 0))
    common = [
        head,
        whole(1, size),
        whole(rows, size // 2),
        whole(rows, size // 2),
        whole(width, 2 * size),
        whole(rows, 1),
        whole(1, width),
    ]
    return head, whole, common


def attention_forward(qkv, gain, cosine, sine, pairs, query_segs, key_segs, heads):
    rows, width, size = qkv.shape[0], pairs.shape[0], pairs.shape[1] // 2
    head, _, common = attention_specs(rows, size, width, heads)

    def kernel(raw_ref, gain_ref, cos_ref, sin_ref, pairs_ref, qseg_ref, kseg_ref, query_ref, mixed_ref):
        query = head_post(raw_ref[...], gain_ref[...], cos_ref[...], sin_ref[...]).astype(jnp.bfloat16)
        query_ref[...] = query
        allowed = allowed_mask(qseg_ref, kseg_ref, rows, width)
        probs = head_probs(query, pairs_ref[:, :size], allowed, size**-0.5).astype(jnp.bfloat16)
        mixed_ref[...] = dot(probs, pairs_ref[:, size:], 1, 0).astype(jnp.bfloat16)

    shape = jax.ShapeDtypeStruct((rows, heads * size), jnp.bfloat16)
    return pl.pallas_call(
        kernel,
        grid=(heads,),
        in_specs=common,
        out_specs=[head, head],
        out_shape=[shape, shape],
        compiler_params=params(32),
        name="attention_forward",
    )(qkv, gain, cosine, sine, pairs, query_segs, key_segs)


def attention_backward(qkv, gain, cosine, sine, pairs, query_segs, key_segs, query, grad_mixed, heads):
    rows, width, size = qkv.shape[0], pairs.shape[0], pairs.shape[1] // 2
    head, whole, common = attention_specs(rows, size, width, heads)
    before = width - rows

    def kernel(
        raw_ref, gain_ref, cos_ref, sin_ref, pairs_ref, qseg_ref, kseg_ref, query_ref, grad_ref,
        raw_grad_ref, gain_grad_ref, far_ref, own_ref, acc,
    ):
        step = pl.program_id(0)
        query = query_ref[...]
        grad = grad_ref[...]
        allowed = allowed_mask(qseg_ref, kseg_ref, rows, width)
        keys = pairs_ref[:, :size]
        probs = head_probs(query, keys, allowed, size**-0.5)
        grad_probs = dot(grad, pairs_ref[:, size:], 1, 1)
        delta = jnp.sum(grad_probs * probs, axis=-1, keepdims=True)
        grad_scores = (probs * (grad_probs - delta)).astype(jnp.bfloat16)
        grad_query = dot(grad_scores, keys, 1, 0) * size**-0.5
        grad_keys = dot(grad_scores, query, 0, 0) * size**-0.5
        grad_values = dot(probs.astype(jnp.bfloat16), grad, 0, 0)

        @pl.when(step == 0)
        def _():
            acc[:, :size] = grad_keys
            acc[:, size:] = grad_values

        @pl.when(step > 0)
        def _():
            acc[:, :size] += grad_keys
            acc[:, size:] += grad_values

        first = grad_query[:, : size // 2]
        second = grad_query[:, size // 2 :]
        cosine_part, sine_part = cos_ref[...], sin_ref[...]
        turned = jnp.concatenate(
            [
                first * cosine_part + second * sine_part,
                second * cosine_part - first * sine_part,
            ],
            axis=-1,
        )
        raw = raw_ref[...]
        scale = lax.rsqrt(jnp.mean(raw * raw, axis=-1, keepdims=True) + EPS)
        unit = raw * scale
        inner = turned * gain_ref[...].astype(jnp.float32)
        raw_grad = scale * (inner - unit * jnp.mean(inner * unit, axis=-1, keepdims=True))
        raw_grad_ref[...] = raw_grad.astype(jnp.bfloat16)
        gain_grad = jnp.sum(turned * unit, axis=0, keepdims=True)

        @pl.when(step == 0)
        def _():
            gain_grad_ref[...] = gain_grad

        @pl.when(step > 0)
        def _():
            gain_grad_ref[...] += gain_grad

        @pl.when(step == heads - 1)
        def _():
            far_ref[...] = acc[:before, :].astype(jnp.bfloat16)
            own_ref[...] = acc[before:, :]

    return pl.pallas_call(
        kernel,
        grid=(heads,),
        in_specs=common + [head, head],
        out_specs=[head, whole(1, size), whole(before, 2 * size), whole(rows, 2 * size)],
        out_shape=[
            jax.ShapeDtypeStruct((rows, heads * size), jnp.bfloat16),
            jax.ShapeDtypeStruct((1, size), jnp.float32),
            jax.ShapeDtypeStruct((before, 2 * size), jnp.bfloat16),
            jax.ShapeDtypeStruct((rows, 2 * size), jnp.float32),
        ],
        scratch_shapes=[pltpu.VMEM((width, 2 * size), jnp.float32)],
        compiler_params=params(32),
        name="attention_backward",
    )(qkv, gain, cosine, sine, pairs, query_segs, key_segs, query, grad_mixed)


def line_edges():
    places = lax.axis_size("replica") // 2
    outer = places // 2 - 1
    return places, outer


def exchanged(block, pairs):
    route = [(2 * a + core, 2 * b + core) for a, b in pairs for core in range(2)]
    return lax.ppermute(block, "replica", route)


class Line:
    def __init__(self):
        self.places, self.outer = line_edges()
        self.steps = 2 * self.outer + 1
        self.moving = []
        self.done = {}

    def advance(self, fresh, gate=None):
        places, outer, steps = self.places, self.outer, self.steps
        place = (lax.axis_index("replica") // 2).astype(jnp.int32).reshape(1)
        operands, plan = [], []

        def operand(entry):
            array, index = entry if isinstance(entry, tuple) else (entry, None)
            for spot, (known, known_index) in enumerate(operands):
                if known is array and known_index == index:
                    return spot
            operands.append((array, index))
            return len(operands) - 1

        for name, block, step, far in self.moving:
            plan.append((name, step + 1, [operand(block), operand(far)], step))
        for name, terms in fresh:
            plan.append((name, 0, [operand(term) for term in terms], None))
        if not plan:
            return gate
        sizes = [operands[spots[0]][0].shape[-2:] for _, _, spots, _ in plan]
        by_step = {step: index for index, (_, step, _, _) in enumerate(plan)}
        pairs = []
        for edge in range(outer):
            inward, outward = by_step.get(edge), by_step.get(2 * outer - edge)
            if inward is not None and outward is not None and sizes[inward] == sizes[outward]:
                pairs.append((edge, inward, outward))
        cuts = 3 if all(size[0] % 48 == 0 for size in sizes) else 1

        def kernel(place_ref, *refs):
            here = place_ref[0]
            inputs = refs[: len(operands)]
            if gate is not None:
                refs = refs[: len(operands)] + refs[len(operands) + 1 :]
            outputs = refs[len(operands) :]
            states = []
            for spot, (_, _, terms, last) in enumerate(plan):
                value = inputs[terms[0]][...]
                if len(terms) > 1:
                    far = inputs[terms[1]][...]
                    total = value.astype(jnp.float32)
                    for term in terms[1:]:
                        total = total + inputs[term][...].astype(jnp.float32)
                    total = total.astype(jnp.bfloat16)
                    if last is None:
                        value = total
                    elif last <= outer:
                        edge = last
                        value = jnp.where((here == edge + 1) | (here == places - 2 - edge), total, value)
                    else:
                        edge = 2 * outer - last
                        value = jnp.where((here == edge) | (here == places - 1 - edge), far, value)
                states.append(value)
                outputs[spot][...] = value
            for spot, (edge, inward, outward) in enumerate(pairs):
                outputs[len(plan) + spot][...] = jnp.where(
                    (here == edge) | (here == places - 1 - edge), states[inward], states[outward]
                )

        def spec(size, index):
            if index is None:
                return pl.BlockSpec((size[0] // cuts, size[1]), lambda i, place_ref: (i, 0))
            return pl.BlockSpec((None, size[0] // cuts, size[1]), lambda i, place_ref: (index, i, 0))

        in_specs = [spec(array.shape[-2:], index) for array, index in operands]
        arrays = [array for array, _ in operands]
        out_sizes = sizes + [sizes[inward] for _, inward, _ in pairs]
        out_specs = [spec(size, None) for size in out_sizes]
        out_shape = [jax.ShapeDtypeStruct(size, jnp.bfloat16) for size in out_sizes]
        aliases = {}
        if gate is not None:
            aliases = {1 + len(arrays): len(out_shape)}
            in_specs.append(pl.BlockSpec(memory_space=pl.ANY))
            out_specs.append(pl.BlockSpec(memory_space=pl.ANY))
            out_shape.append(jax.ShapeDtypeStruct(gate.shape, gate.dtype))
            arrays.append(gate)
        outs = pl.pallas_call(
            kernel,
            grid_spec=pltpu.PrefetchScalarGridSpec(
                num_scalar_prefetch=1, grid=(cuts,), in_specs=in_specs, out_specs=out_specs
            ),
            out_shape=out_shape,
            input_output_aliases=aliases,
            compiler_params=params(32),
            name="line_step",
        )(place, *arrays)
        received = {}
        for spot, (edge, inward, outward) in enumerate(pairs):
            ends = [(edge, edge + 1), (places - 1 - edge, places - 2 - edge)]
            far = exchanged(outs[len(plan) + spot], ends + [(b, a) for a, b in ends])
            received[inward] = received[outward] = far
        self.moving = []
        for index, (name, step, _, _) in enumerate(plan):
            block = outs[index]
            if step == steps:
                self.done[name] = block
                continue
            if index not in received:
                edge = step if step <= outer else 2 * outer - step
                route = [(edge, edge + 1), (places - 1 - edge, places - 2 - edge)]
                if step > outer:
                    route = [(b, a) for a, b in route]
                received[index] = exchanged(block, route)
            self.moving.append((name, block, step, received[index]))
        return outs[-1]

    def arrived(self):
        return [far for _, _, _, far in self.moving]

    def finished(self, name):
        while name not in self.done:
            self.advance([])
        return self.done[name]


def line_names(name, units):
    return [(name, chunk) for chunk in range(chunks_of(units))]


def whole_grad(line, name, units, dtype=jnp.float32):
    names = line_names(name, units)
    mines = [line.finished(chunk) for chunk in names]
    others = [swapped(mine, "replica", 1) for mine in mines]
    chunks = len(mines)
    tile, model = mines[0].shape
    core = (lax.axis_index("replica") % 2).astype(jnp.int32).reshape(1)

    def kernel(core_ref, *refs):
        out_ref = refs[-1]
        for chunk in range(chunks):
            for side in range(2):

                @pl.when((pl.program_id(0) == chunk) & (pl.program_id(1) == side))
                def _():
                    @pl.when(core_ref[0] == side)
                    def _():
                        out_ref[...] = refs[chunk][...].astype(dtype)

                    @pl.when(core_ref[0] != side)
                    def _():
                        out_ref[...] = refs[chunks + chunk][...].astype(dtype)

    return pl.pallas_call(
        kernel,
        grid_spec=pltpu.PrefetchScalarGridSpec(
            num_scalar_prefetch=1,
            grid=(chunks, 2),
            in_specs=[pl.BlockSpec((tile, model), lambda chunk, side, core_ref: (0, 0))] * (2 * chunks),
            out_specs=pl.BlockSpec((tile, model), lambda chunk, side, core_ref: (2 * chunk + side, 0)),
        ),
        out_shape=jax.ShapeDtypeStruct((units, model), dtype),
        compiler_params=params(24),
        name="whole_grad",
    )(core, *mines, *others)


def joined(mine, other, axis):
    core = lax.axis_index("replica") % 2
    return jnp.where(
        core == 0,
        jnp.concatenate([mine, other], axis=axis),
        jnp.concatenate([other, mine], axis=axis),
    )


def core_join(block, axis):
    return joined(block, swapped(block, "replica", 1), axis)


def fetched(block):
    got = [swapped(block, "fsdp", mask) for mask in range(1, lax.axis_size("fsdp"))]
    return got, [swapped(part, "replica", 1) for part in got]


def gathered(block):
    group = lax.axis_size("fsdp")
    blocks, near = [block] + [None] * (group - 1), []
    for ring in range(1, group.bit_length()):
        masks = [mask for mask in range(1, group) if bin(mask).count("1") == ring]
        source = after(block, *near) if near else block
        near = [swapped(source, "fsdp", mask) for mask in masks]
        for mask, far in zip(masks, near):
            blocks[mask] = far
    return blocks


def passed_along(block, axis, distance):
    devices = range(lax.axis_size(axis))
    route = [(i - distance, i) for i in devices if i - distance in devices]
    return lax.ppermute(block, axis, route)


def contract(left, right, left_dim, right_dim):
    return lax.dot_general(
        left, right, (((left_dim,), (right_dim,)), ((), ())), preferred_element_type=jnp.float32
    )


def normed(value, gain):
    return value * lax.rsqrt(jnp.mean(value * value, axis=-1, keepdims=True) + EPS) * gain


def norm_back(value, gain, grad):
    _, pull = jax.vjp(normed, value, gain)
    return pull(grad)


def tables(places, half):
    freq = 10000.0 ** (-(2.0 * jnp.arange(half, dtype=jnp.float32)) / (2 * half))
    angle = places.astype(jnp.float32)[:, None] * freq[None, :]
    return (jnp.cos(angle), jnp.sin(angle))


def rotate(value, cosine, sine):
    half = value.shape[-1] // 2
    first = value[..., :half]
    second = value[..., half:]
    return jnp.concatenate(
        [first * cosine - second * sine, second * cosine + first * sine], axis=-1
    )


def head_post(raw, gain, cosine, sine):
    return rotate(normed(raw, gain), cosine, sine)


def per_device(
    hidden_in,
    out_grad,
    segments,
    positions,
    norm_in,
    query_weight,
    key_weight,
    value_weight,
    out_weight,
    norm_attn,
    norm_ffn,
    gate_weight,
    up_weight,
    down_weight,
    norm_out,
    query_gain,
    key_gain,
):
    rows = hidden_in.shape[0]
    rank = lax.axis_index("fsdp")
    group = lax.axis_size("fsdp")
    masks = range(1, group)
    head_size = key_weight.shape[1]
    heads = query_weight.shape[1] // head_size
    model = hidden_in.shape[1]
    own_model = norm_in.shape[0]
    own_head = query_gain.shape[0]
    hops = (WINDOW - 1) // rows + 1
    scale = head_size ** (-0.5)
    qkv_weights = (query_weight, key_weight, value_weight)
    wide = sum(weight.shape[1] for weight in qkv_weights)
    qkv_block = packed(qkv_weights)
    got, peers = fetched(qkv_block)
    gains = jnp.stack(
        [
            jnp.pad(gain, (0, own_model - gain.shape[0]))
            for gain in (norm_in, norm_attn, norm_ffn, norm_out, query_gain, key_gain)
        ]
    )
    gains = after(gains, qkv_block)
    gain_stack = jnp.stack([gains] + [swapped(gains, "fsdp", mask) for mask in masks])
    w_qkv = unpacked(qkv_weights, got, peers)
    gain_rows = jnp.stack(
        [lax.dynamic_index_in_dim(gain_stack, rank ^ i, 0, keepdims=False) for i in range(group)], axis=1
    )
    gain_in, gain_attn, gain_ffn, gain_out = (gain_rows[i].reshape(-1) for i in range(4))
    gain_query, gain_key = (gain_rows[i, :, :own_head].reshape(-1) for i in (4, 5))
    residual_in = hidden_in.astype(jnp.float32)
    normed_in = normed(residual_in, gain_in).astype(jnp.bfloat16)
    qkv = jnp.dot(normed_in, w_qkv, preferred_element_type=jnp.float32)
    key_raw = qkv[:, heads * head_size : (heads + 1) * head_size]
    value_new = qkv[:, (heads + 1) * head_size :].astype(jnp.bfloat16)
    cosine, sine = tables(positions, head_size // 2)
    key_new = head_post(key_raw, gain_key, cosine, sine).astype(jnp.bfloat16)
    pair_new = jnp.concatenate([key_new, value_new], axis=1)
    got, peers = fetched(after(packed([out_weight]), pair_new))
    w_out = unpacked([out_weight], got, peers)
    parts = [pair_new]
    for step in range(1, hops + 1):
        parts.insert(0, passed_along(pair_new, "fsdp", step))
    pairs = after(jnp.concatenate(parts, axis=0), w_out)
    width = pairs.shape[0]
    seg_padded = jnp.concatenate([jnp.full((hops * rows,), -1, jnp.int32), segments], axis=0)
    key_segs = lax.dynamic_slice_in_dim(seg_padded, rank * rows, width, 0)
    query_segs = lax.dynamic_slice_in_dim(segments, rank * rows, rows, 0)
    attention_args = (
        qkv,
        gain_query[None, :],
        cosine,
        sine,
        pairs,
        query_segs[:, None],
        key_segs[None, :],
    )
    query_new, mixed = attention_forward(*attention_args, heads)
    attended = contract(mixed, w_out, 1, 1)
    resid = residual_in + normed(attended, gain_attn)
    ffn_in = normed(resid, gain_ffn).astype(jnp.bfloat16)
    ffn_blocks = gathered(ffn_in)
    hiddens, slopes, acts, parts = {}, {}, {}, {}
    rings = sorted(range(group), key=lambda mask: (bin(mask).count("1"), mask))
    last = None
    for mask in rings[1:] + [0]:
        if last is not None:
            ffn_blocks[mask] = after(ffn_blocks[mask], parts[last])
        hiddens[mask], slopes[mask], acts[mask], parts[mask] = ffn_forward(
            ffn_blocks[mask], gate_weight, up_weight, down_weight
        )
        last = mask
    branch = sum(
        (swapped(parts[mask], "fsdp", mask) if mask else parts[mask]).astype(jnp.float32)
        for mask in range(group)
    )
    result = resid + normed(branch, gain_out)
    hidden_out = result.astype(jnp.bfloat16)
    grad_result = out_grad.astype(jnp.float32)
    grad_branch, grad_gain_out = norm_back(branch, gain_out, grad_result)
    grad_branch_low = grad_branch.astype(jnp.bfloat16)
    pieces = gathered(grad_branch_low)
    units = gate_weight.shape[0]
    line = Line()

    def fresh(names, other, mine):
        far = swapped(other, "replica", 1)
        keys = [key for name in names for key in line_names(name, units)]
        return [(key, [(mine, spot), (far, spot)]) for spot, key in enumerate(keys)]

    grad_gates, grad_uppers, returned = {}, {}, {}
    final = rings[-1]
    last = None
    for mask in rings[:-1]:
        if last is not None:
            pieces[mask] = after(pieces[mask], part)
        grad_gates[mask], grad_uppers[mask], part = ffn_backward(
            pieces[mask], gate_weight, up_weight, down_weight, slopes[mask], acts[mask]
        )
        returned[mask] = swapped(part, "fsdp", mask) if mask else part
        last = mask
    pieces[final] = after(pieces[final], part)
    grad_down = weight_grad_whole(
        [hiddens[i] for i in range(group)], [pieces[i] for i in range(group)]
    )
    pieces[final] = after(pieces[final], grad_down)
    grad_down = lax.psum(grad_down, "replica").astype(jnp.float32)
    gate_parts, upper_parts, parts = ffn_backward_blocks(
        [pieces[final]], gate_weight, up_weight, down_weight, [slopes[final]], [acts[final]]
    )
    grad_gates[final], grad_uppers[final] = gate_parts[0], upper_parts[0]
    returned[final] = swapped(parts[0], "fsdp", final)
    grad_gates[final] = after(grad_gates[final], *[returned[mask] for mask in rings[1:-1]])
    other, mine = weight_grad(
        [[grad_gates[i] for i in range(group)], [grad_uppers[i] for i in range(group)]], ffn_blocks
    )
    other = after(other, returned[final])
    waiting = fresh(["gate", "up"], other, mine)

    def advance(gate=None):
        return line.advance([waiting.pop(0)] if waiting else [], gate)

    grad_resid, grad_attended_low, grad_mixed, grad_gain_ffn, grad_gain_attn = resid_backward(
        [returned[mask] for mask in range(group)], resid, attended, out_grad, gain_ffn, gain_attn, w_out
    )
    grad_mixed = advance(grad_mixed)
    grad_query_low, grad_gain_query, grad_far, grad_pair = attention_backward(
        *attention_args, query_new, grad_mixed, heads
    )
    backs = []
    for step in range(1, hops + 1):
        grad_far = passed_along(grad_far, "fsdp", -1)
        backs.append(grad_far[-rows:])
        grad_far = grad_far[:-rows]
    grad_pair = advance(grad_pair)
    other, mine, grad_in = input_backward(
        grad_pair,
        backs,
        qkv,
        cosine,
        sine,
        gain_key,
        normed_in,
        grad_query_low,
        w_qkv,
        hidden_in,
        gain_in,
        grad_resid,
        grad_attended_low,
        mixed,
        [grad_gain_attn, grad_gain_ffn, grad_gain_out[None, :], grad_gain_query],
        group,
    )
    other = advance(other)
    weight_parts = owner_parts(other, mine)
    while waiting:
        weight_parts[0] = advance(weight_parts[0])
    line.advance([("weights", weight_parts)])
    grad_gate_w = whole_grad(line, "gate", units)
    grad_gate_w = line.advance([], grad_gate_w)
    grad_up_w = whole_grad(line, "up", units)
    owned = core_join(line.finished("weights"), 1).astype(jnp.float32)
    inner = heads * head_size
    columns = [0, inner, inner + head_size, inner + 2 * head_size, wide + inner]
    owned_query, owned_key, owned_value, owned_out = (
        owned[:own_model, columns[i] : columns[i + 1]] for i in range(4)
    )

    def owned_gain(row, size):
        return lax.dynamic_slice_in_dim(owned[own_model + row], rank * size, size, 0)

    owned_gain_in, owned_gain_attn, owned_gain_ffn, owned_gain_out = (
        owned_gain(row, own_model) for row in (0, 2, 3, 4)
    )
    owned_gain_key, owned_gain_query = (owned_gain(row, own_head) for row in (1, 5))
    return (
        hidden_out,
        grad_in,
        owned_gain_in,
        owned_query,
        owned_key,
        owned_value,
        owned_out,
        owned_gain_attn,
        owned_gain_ffn,
        grad_gate_w,
        grad_up_w,
        grad_down,
        owned_gain_out,
        owned_gain_query,
        owned_gain_key,
    )


def solution(mesh):
    return jax.shard_map(
        per_device,
        mesh=mesh,
        in_specs=(
            P(("replica", "fsdp"), None),
            P(("replica", "fsdp"), None),
            P("replica"),
            P(("replica", "fsdp")),
            P("fsdp"),
            P("fsdp", None),
            P("fsdp", None),
            P("fsdp", None),
            P("fsdp", None),
            P("fsdp"),
            P("fsdp"),
            P("fsdp", None),
            P("fsdp", None),
            P("fsdp", None),
            P("fsdp"),
            P("fsdp"),
            P("fsdp"),
        ),
        out_specs=(
            P(("replica", "fsdp"), None),
            P(("replica", "fsdp"), None),
            P("fsdp"),
            P("fsdp", None),
            P("fsdp", None),
            P("fsdp", None),
            P("fsdp", None),
            P("fsdp"),
            P("fsdp"),
            P("fsdp", None),
            P("fsdp", None),
            P("fsdp", None),
            P("fsdp"),
            P("fsdp"),
            P("fsdp"),
        ),
        check_vma=False,
    )
```

```python
import jax
import jax.numpy as jnp
from jax import lax
from jax.experimental import pallas as pl
from jax.experimental.pallas import tpu as pltpu
from jax.sharding import PartitionSpec as P

WINDOW = 512


EPS = 1e-06
NEG = -1e30


def swapped(block, axis, mask):
    route = [(i, i ^ mask) for i in range(lax.axis_size(axis))]
    return lax.ppermute(block, axis, route)


def added(left, right):
    total = left.astype(jnp.float32) + right.astype(jnp.float32)
    return lax.optimization_barrier(total.astype(jnp.bfloat16))


def params(mebibytes=48):
    return pltpu.CompilerParams(vmem_limit_bytes=mebibytes * 1024 * 1024)


def dot(left, right, left_dim, right_dim):
    return lax.dot_general(
        left, right, (((left_dim,), (right_dim,)), ((), ())), preferred_element_type=jnp.float32
    )


def after(array, *others):
    place = pl.BlockSpec(memory_space=pl.ANY)
    return pl.pallas_call(
        lambda *refs: None,
        out_shape=jax.ShapeDtypeStruct(array.shape, array.dtype),
        in_specs=[place] * (1 + len(others)),
        out_specs=place,
        input_output_aliases={0: 0},
        compiler_params=params(1),
        name="after",
    )(array, *others)


def scalar(value):
    return value.astype(jnp.int32).reshape(1)


def packed(weights):
    half = weights[0].shape[0] // 2
    wide = sum(weight.shape[1] for weight in weights)

    def kernel(core_ref, *refs):
        out_ref = refs[-1]
        for side in range(2):

            @pl.when(core_ref[0] == side)
            def _():
                at = 0
                for ref in refs[:-1]:
                    out_ref[:, at : at + ref.shape[1]] = ref[side * half : (side + 1) * half, :]
                    at += ref.shape[1]

    return pl.pallas_call(
        kernel,
        grid_spec=pltpu.PrefetchScalarGridSpec(
            num_scalar_prefetch=1,
            grid=(1,),
            in_specs=[pl.BlockSpec(weight.shape, lambda i, core_ref: (0, 0)) for weight in weights],
            out_specs=pl.BlockSpec((half, wide), lambda i, core_ref: (0, 0)),
        ),
        out_shape=jax.ShapeDtypeStruct((half, wide), jnp.bfloat16),
        compiler_params=params(16),
        name="pack",
    )(scalar(lax.axis_index("replica") % 2), *weights)


def unpacked(weights, got, peers):
    rows = weights[0].shape[0]
    half = rows // 2
    group = len(got) + 1
    wide = sum(weight.shape[1] for weight in weights)
    own = len(weights)

    def kernel(core_ref, rank_ref, *refs):
        out_ref = refs[-1]
        mask = rank_ref[0] ^ pl.program_id(0)

        @pl.when(mask == 0)
        def _():
            at = 0
            for ref in refs[:own]:
                out_ref[:, at : at + ref.shape[1]] = ref[...]
                at += ref.shape[1]

        for other in range(1, group):
            for side in range(2):

                @pl.when((mask == other) & (core_ref[0] == side))
                def _():
                    out_ref[side * half : (side + 1) * half, :] = refs[own + other - 1][:half, :]
                    out_ref[(1 - side) * half : (2 - side) * half, :] = refs[own + group - 2 + other][:half, :]

    arrays = list(weights) + list(got) + list(peers)
    return pl.pallas_call(
        kernel,
        grid_spec=pltpu.PrefetchScalarGridSpec(
            num_scalar_prefetch=2,
            grid=(group,),
            in_specs=[pl.BlockSpec(array.shape, lambda i, *refs: (0, 0)) for array in arrays],
            out_specs=pl.BlockSpec((rows, wide), lambda i, *refs: (i, 0)),
        ),
        out_shape=jax.ShapeDtypeStruct((group * rows, wide), jnp.bfloat16),
        compiler_params=params(24),
        name="unpack",
    )(scalar(lax.axis_index("replica") % 2), scalar(lax.axis_index("fsdp")), *arrays)


GELU_A = (2.0 / 3.141592653589793) ** 0.5
GELU_B = 0.044715


def ffn_forward(x, gate_weight, up_weight, down_weight):
    gate = contract(gate_weight, x, 1, 1)
    upper = contract(up_weight, x, 1, 1)
    square = gate * gate
    bend = jnp.tanh(GELU_A * gate * (1.0 + GELU_B * square))
    half = 0.5 + 0.5 * bend
    act = gate * half
    slope = half + 0.5 * gate * (1.0 - bend * bend) * (GELU_A * (1.0 + 3.0 * GELU_B * square))
    hidden = (act * upper).astype(jnp.bfloat16)
    part = contract(hidden, down_weight, 0, 0).astype(jnp.bfloat16)
    return hidden, (slope * upper).astype(jnp.bfloat16), act.astype(jnp.bfloat16), part


def ffn_backward(grad, gate_weight, up_weight, down_weight, slope, act):
    grad_hidden = contract(down_weight, grad, 1, 1)
    grad_gate = (grad_hidden * slope.astype(jnp.float32)).astype(jnp.bfloat16)
    grad_upper = (grad_hidden * act.astype(jnp.float32)).astype(jnp.bfloat16)
    part = contract(grad_gate, gate_weight, 0, 0) + contract(grad_upper, up_weight, 0, 0)
    return grad_gate, grad_upper, part.astype(jnp.bfloat16)


def tile_of(size, most):
    return max(tile for tile in range(16, most + 1, 16) if size % tile == 0)


def ffn_backward_blocks(grads, gate_weight, up_weight, down_weight, slopes, acts):
    count = len(grads)
    rows, model = grads[0].shape
    units = gate_weight.shape[0]
    tile = tile_of(units, 432)
    steps = units // tile

    def kernel(*refs):
        step = pl.program_id(0)
        grad_refs, refs = refs[:count], refs[count:]
        (gate_ref, up_ref, down_ref), refs = refs[:3], refs[3:]
        slope_refs, act_refs, refs = refs[:count], refs[count : 2 * count], refs[2 * count :]
        gate_outs, up_outs, part_outs, (grad_ref, acc) = (
            refs[:count],
            refs[count : 2 * count],
            refs[2 * count : 3 * count],
            refs[3 * count :],
        )

        @pl.when(step == 0)
        def _():
            for spot in range(count):
                grad_ref[spot * rows : (spot + 1) * rows, :] = grad_refs[spot][...]
            acc[...] = jnp.zeros_like(acc)

        grad_hidden = dot(down_ref[...], grad_ref[...], 1, 1)
        slope = jnp.concatenate([ref[...] for ref in slope_refs], axis=1).astype(jnp.float32)
        act = jnp.concatenate([ref[...] for ref in act_refs], axis=1).astype(jnp.float32)
        grad_gate = (grad_hidden * slope).astype(jnp.bfloat16)
        grad_upper = (grad_hidden * act).astype(jnp.bfloat16)
        for spot in range(count):
            gate_outs[spot][...] = grad_gate[:, spot * rows : (spot + 1) * rows]
            up_outs[spot][...] = grad_upper[:, spot * rows : (spot + 1) * rows]
        acc[...] += dot(grad_gate, gate_ref[...], 0, 0) + dot(grad_upper, up_ref[...], 0, 0)

        @pl.when(step == steps - 1)
        def _():
            for spot in range(count):
                part_outs[spot][...] = acc[spot * rows : (spot + 1) * rows, :].astype(jnp.bfloat16)

    weight = pl.BlockSpec((tile, model), lambda i: (i, 0))
    flat = pl.BlockSpec((tile, rows), lambda i: (i, 0))
    whole = pl.BlockSpec((rows, model), lambda i: (0, 0))
    kept = jax.ShapeDtypeStruct((units, rows), jnp.bfloat16)
    outs = pl.pallas_call(
        kernel,
        grid=(steps,),
        out_shape=[kept] * (2 * count) + [jax.ShapeDtypeStruct((rows, model), jnp.bfloat16)] * count,
        in_specs=[whole] * count + [weight] * 3 + [flat] * (2 * count),
        out_specs=[flat] * (2 * count) + [whole] * count,
        scratch_shapes=[
            pltpu.VMEM((count * rows, model), jnp.bfloat16),
            pltpu.VMEM((count * rows, model), jnp.float32),
        ],
        compiler_params=params(),
        name="ffn_backward",
    )(*grads, gate_weight, up_weight, down_weight, *slopes, *acts)
    return outs[:count], outs[count : 2 * count], outs[2 * count :]


def norm_pull(value, gain, grad):
    scale = lax.rsqrt(jnp.mean(value * value, axis=-1, keepdims=True) + EPS)
    unit = value * scale
    inner = grad * gain
    return scale * (inner - unit * jnp.mean(inner * unit, axis=-1, keepdims=True)), grad * unit


def resid_backward(parts, resid, attended, out_grad, gain_ffn, gain_attn, w_out):
    count = len(parts)
    rows, model = resid.shape
    tile = min(rows, 128)

    def kernel(*refs):
        part_refs, refs = refs[:count], refs[count:]
        resid_ref, attended_ref, out_ref, ffn_ref, attn_ref, weight_ref, refs = *refs[:6], refs[6:]
        grad_resid_ref, grad_attended_ref, grad_mixed_ref, ffn_grad_ref, attn_grad_ref = refs
        grad = sum(ref[...].astype(jnp.float32) for ref in part_refs)
        pulled, ffn_rows = norm_pull(resid_ref[...], ffn_ref[...].astype(jnp.float32), grad)
        grad_resid = out_ref[...].astype(jnp.float32) + pulled
        grad_resid_ref[...] = grad_resid
        pulled, attn_rows = norm_pull(attended_ref[...], attn_ref[...].astype(jnp.float32), grad_resid)
        grad_attended = pulled.astype(jnp.bfloat16)
        grad_attended_ref[...] = grad_attended
        grad_mixed_ref[...] = dot(grad_attended, weight_ref[...], 1, 0).astype(jnp.bfloat16)
        ffn_grad = jnp.sum(ffn_rows, axis=0, keepdims=True)
        attn_grad = jnp.sum(attn_rows, axis=0, keepdims=True)

        @pl.when(pl.program_id(0) == 0)
        def _():
            ffn_grad_ref[...] = ffn_grad
            attn_grad_ref[...] = attn_grad

        @pl.when(pl.program_id(0) > 0)
        def _():
            ffn_grad_ref[...] += ffn_grad
            attn_grad_ref[...] += attn_grad

    block = pl.BlockSpec((tile, model), lambda i: (i, 0))
    vector = pl.BlockSpec((1, model), lambda i: (0, 0))
    inner = w_out.shape[1]
    return pl.pallas_call(
        kernel,
        grid=(rows // tile,),
        in_specs=[block] * (count + 3) + [vector] * 2 + [pl.BlockSpec(w_out.shape, lambda i: (0, 0))],
        out_specs=[block, block, pl.BlockSpec((tile, inner), lambda i: (i, 0)), vector, vector],
        out_shape=[
            jax.ShapeDtypeStruct((rows, model), jnp.float32),
            jax.ShapeDtypeStruct((rows, model), jnp.bfloat16),
            jax.ShapeDtypeStruct((rows, inner), jnp.bfloat16),
            jax.ShapeDtypeStruct((1, model), jnp.float32),
            jax.ShapeDtypeStruct((1, model), jnp.float32),
        ],
        compiler_params=params(32),
        name="resid_backward",
    )(*parts, resid, attended, out_grad, gain_ffn[None, :], gain_attn[None, :], w_out)


def input_backward(
    own_pair, backs, qkv, cosine, sine, gain_key, normed_in, grad_query, w_qkv, hidden_in, gain_in, grad_resid,
    grad_attended, mixed, gain_grads, group,
):
    rows, model = hidden_in.shape
    size = own_pair.shape[1] // 2
    inner = grad_query.shape[1]
    own_rows = model // group
    half = inner + size
    hops = len(backs)
    count = len(gain_grads)

    def kernel(core_ref, *refs):
        pair_ref, refs = refs[0], refs[1:]
        back_refs, refs = refs[:hops], refs[hops:]
        (
            raw_ref, cos_ref, sin_ref, key_gain_ref, normed_ref, query_ref, weight_ref, x_ref, gain_ref, resid_ref,
            attended_ref, mixed_ref, refs,
        ) = *refs[:12], refs[12:]
        gain_refs, refs = refs[:count], refs[count:]
        other_ref, mine_ref, grad_in_ref, rows_ref = refs
        pair = pair_ref[...] + sum(ref[...].astype(jnp.float32) for ref in back_refs)
        first = pair[:, : size // 2]
        second = pair[:, size // 2 : size]
        turned = jnp.concatenate(
            [
                first * cos_ref[...] + second * sin_ref[...],
                second * cos_ref[...] - first * sin_ref[...],
            ],
            axis=-1,
        )
        pulled, key_rows = norm_pull(raw_ref[...], key_gain_ref[...].astype(jnp.float32), turned)
        grad_key = pulled.astype(jnp.bfloat16)
        grad_value = pair[:, size:].astype(jnp.bfloat16)
        grad_normed = (
            dot(query_ref[...], weight_ref[:, :inner], 1, 1)
            + dot(grad_key, weight_ref[:, inner:half], 1, 1)
            + dot(grad_value, weight_ref[:, half:], 1, 1)
        )
        pulled, in_rows = norm_pull(
            x_ref[...].astype(jnp.float32), gain_ref[...].astype(jnp.float32), grad_normed
        )
        grad_in_ref[...] = resid_ref[...] + pulled
        rows_ref[...] = jnp.zeros_like(rows_ref)
        rows_ref[0:1, :model] = jnp.sum(in_rows, axis=0, keepdims=True)
        rows_ref[1:2, :size] = jnp.sum(key_rows, axis=0, keepdims=True)
        for spot in range(count):
            rows_ref[2 + spot : 3 + spot, : gain_refs[spot].shape[1]] = gain_refs[spot][...].astype(
                jnp.float32
            )
        gains = rows_ref[...].astype(jnp.bfloat16)

        def write(ref, side):
            pieces = (
                [(normed_ref, query_ref[...], 0, inner), (normed_ref, grad_key, inner, half)]
                if side == 0
                else [(normed_ref, grad_value, 0, size), (attended_ref, mixed_ref[...], size, half)]
            )
            for left, right, begin, end in pieces:
                value = dot(left[...], right, 0, 0).astype(jnp.bfloat16)
                for owner in range(group):
                    ref[owner, :own_rows, begin:end] = value[owner * own_rows : (owner + 1) * own_rows]
            for owner in range(group):
                ref[owner, own_rows:, :] = gains

        for core in range(2):

            @pl.when(core_ref[0] == core)
            def _():
                write(other_ref, 1 - core)
                write(mine_ref, core)

    def whole(array):
        return pl.BlockSpec(array.shape, lambda i, core_ref: (0,) * len(array.shape))

    arrays = [
        own_pair, *backs, qkv, cosine, sine, gain_key[None, :], normed_in, grad_query, w_qkv, hidden_in,
        gain_in[None, :], grad_resid, grad_attended, mixed, *gain_grads,
    ]
    in_specs = [whole(array) for array in arrays]
    in_specs[1 + hops] = pl.BlockSpec((rows, size), lambda i, core_ref: (0, inner // size))
    shape = jax.ShapeDtypeStruct((group, own_rows + 16, half), jnp.bfloat16)
    grad_in = jax.ShapeDtypeStruct((rows, model), jnp.float32)
    return pl.pallas_call(
        kernel,
        grid_spec=pltpu.PrefetchScalarGridSpec(
            num_scalar_prefetch=1,
            grid=(1,),
            in_specs=in_specs,
            out_specs=[whole(shape), whole(shape), whole(grad_in)],
            scratch_shapes=[pltpu.VMEM((16, half), jnp.float32)],
        ),
        out_shape=[shape, shape, grad_in],
        compiler_params=params(),
        name="input_backward",
    )(scalar(lax.axis_index("replica") % 2), *arrays)


def owner_parts(other, mine):
    group, height, wide = mine.shape
    far = swapped(other, "replica", 1)

    def kernel(rank_ref, mine_ref, far_ref, *outs):
        total = mine_ref[...].astype(jnp.float32) + far_ref[...].astype(jnp.float32)
        for mask in range(group):

            @pl.when(pl.program_id(0) == mask)
            def _():
                outs[mask][...] = total.astype(jnp.bfloat16)

    block = pl.BlockSpec((None, height, wide), lambda i, rank_ref: (rank_ref[0] ^ i, 0, 0))
    parts = pl.pallas_call(
        kernel,
        grid_spec=pltpu.PrefetchScalarGridSpec(
            num_scalar_prefetch=1,
            grid=(group,),
            in_specs=[block, block],
            out_specs=[pl.BlockSpec((height, wide), lambda i, rank_ref: (0, 0))] * group,
        ),
        out_shape=[jax.ShapeDtypeStruct((height, wide), jnp.bfloat16)] * group,
        compiler_params=params(16),
        name="owner_parts",
    )(scalar(lax.axis_index("fsdp")), mine, far)
    return [parts[0]] + [swapped(parts[mask], "fsdp", mask) for mask in range(1, group)]


def chunks_of(units):
    return 2 if units % 64 == 0 else 1


def weight_grad(sets, rights):
    group = len(rights)
    count = len(sets)
    units, rows = sets[0][0].shape
    model = rights[0].shape[1]
    chunks = chunks_of(units)
    tile = units // (2 * chunks)

    def kernel(core_ref, *refs):
        right_refs, left_refs = refs[:group], refs[group:-4]
        other_ref, mine_ref, left_ref, right_ref = refs[-4:]

        @pl.when((pl.program_id(0) == 0) & (pl.program_id(1) == 0))
        def _():
            for spot in range(group):
                right_ref[spot * rows : (spot + 1) * rows, :] = right_refs[spot][...]

        for index in range(count):

            @pl.when(pl.program_id(1) == index)
            def _():
                for chunk in range(chunks):
                    for spot in range(group):
                        left_ref[
                            chunk * tile : (chunk + 1) * tile, spot * rows : (spot + 1) * rows
                        ] = left_refs[(index * chunks + chunk) * group + spot][...]

        value = dot(left_ref[...], right_ref[...], 1, 0).astype(jnp.bfloat16)

        @pl.when(pl.program_id(0) == 0)
        def _():
            for chunk in range(chunks):
                other_ref[chunk] = value[chunk * tile : (chunk + 1) * tile]

        @pl.when(pl.program_id(0) == 1)
        def _():
            for chunk in range(chunks):
                mine_ref[chunk] = value[chunk * tile : (chunk + 1) * tile]

    def left_spec(chunk):
        def index(side, spot, core_ref):
            return (2 * chunk + jnp.where(side == 0, 1 - core_ref[0], core_ref[0]), 0)

        return pl.BlockSpec((tile, rows), index)

    shape = jax.ShapeDtypeStruct((count * chunks, tile, model), jnp.bfloat16)
    block = (chunks, tile, model)
    return pl.pallas_call(
        kernel,
        grid_spec=pltpu.PrefetchScalarGridSpec(
            num_scalar_prefetch=1,
            grid=(2, count),
            in_specs=[pl.BlockSpec((rows, model), lambda side, spot, core_ref: (0, 0))] * group
            + [left_spec(chunk) for _ in range(count) for chunk in range(chunks) for _ in range(group)],
            out_specs=[
                pl.BlockSpec(
                    block, lambda side, spot, core_ref: (jnp.where(side == 0, spot, count - 1), 0, 0)
                ),
                pl.BlockSpec(block, lambda side, spot, core_ref: (jnp.where(side == 0, 0, spot), 0, 0)),
            ],
            scratch_shapes=[
                pltpu.VMEM((chunks * tile, group * rows), jnp.bfloat16),
                pltpu.VMEM((group * rows, model), jnp.bfloat16),
            ],
        ),
        out_shape=[shape, shape],
        compiler_params=params(),
        name="weight_grad",
    )(
        scalar(lax.axis_index("replica") % 2),
        *rights,
        *[left for lefts in sets for _ in range(chunks) for left in lefts],
    )


def allowed_mask(query_segs_ref, key_segs_ref, rows, width):
    gap = (
        width
        - rows
        + lax.broadcasted_iota(jnp.int32, (rows, width), 0)
        - lax.broadcasted_iota(jnp.int32, (rows, width), 1)
    )
    return (gap >= 0) & (gap < WINDOW) & (query_segs_ref[...] == key_segs_ref[...])


def head_probs(query, keys, allowed, scale):
    scores = jnp.where(allowed, dot(query, keys, 1, 1) * scale, NEG)
    expo = jnp.exp(scores - jnp.max(scores, axis=-1, keepdims=True))
    return expo / jnp.sum(expo, axis=-1, keepdims=True)


def attention_specs(rows, size, width, heads):
    head = pl.BlockSpec((rows, size), lambda h: (0, h))
    whole = lambda *shape: pl.BlockSpec(shape, lambda h: (0, 0))
    common = [
        head,
        whole(1, size),
        whole(rows, size // 2),
        whole(rows, size // 2),
        whole(width, 2 * size),
        whole(rows, 1),
        whole(1, width),
    ]
    return head, whole, common


def attention_forward(qkv, gain, cosine, sine, pairs, query_segs, key_segs, heads):
    rows, width, size = qkv.shape[0], pairs.shape[0], pairs.shape[1] // 2
    head, _, common = attention_specs(rows, size, width, heads)

    def kernel(raw_ref, gain_ref, cos_ref, sin_ref, pairs_ref, qseg_ref, kseg_ref, query_ref, mixed_ref):
        query = head_post(raw_ref[...], gain_ref[...], cos_ref[...], sin_ref[...]).astype(jnp.bfloat16)
        query_ref[...] = query
        allowed = allowed_mask(qseg_ref, kseg_ref, rows, width)
        probs = head_probs(query, pairs_ref[:, :size], allowed, size**-0.5).astype(jnp.bfloat16)
        mixed_ref[...] = dot(probs, pairs_ref[:, size:], 1, 0).astype(jnp.bfloat16)

    shape = jax.ShapeDtypeStruct((rows, heads * size), jnp.bfloat16)
    return pl.pallas_call(
        kernel,
        grid=(heads,),
        in_specs=common,
        out_specs=[head, head],
        out_shape=[shape, shape],
        compiler_params=params(32),
        name="attention_forward",
    )(qkv, gain, cosine, sine, pairs, query_segs, key_segs)


def attention_backward(qkv, gain, cosine, sine, pairs, query_segs, key_segs, query, grad_mixed, heads):
    rows, width, size = qkv.shape[0], pairs.shape[0], pairs.shape[1] // 2
    head, whole, common = attention_specs(rows, size, width, heads)
    before = width - rows

    def kernel(
        raw_ref, gain_ref, cos_ref, sin_ref, pairs_ref, qseg_ref, kseg_ref, query_ref, grad_ref,
        raw_grad_ref, gain_grad_ref, far_ref, own_ref, acc,
    ):
        step = pl.program_id(0)
        query = query_ref[...]
        grad = grad_ref[...]
        allowed = allowed_mask(qseg_ref, kseg_ref, rows, width)
        keys = pairs_ref[:, :size]
        probs = head_probs(query, keys, allowed, size**-0.5)
        grad_probs = dot(grad, pairs_ref[:, size:], 1, 1)
        delta = jnp.sum(grad_probs * probs, axis=-1, keepdims=True)
        grad_scores = (probs * (grad_probs - delta)).astype(jnp.bfloat16)
        grad_query = dot(grad_scores, keys, 1, 0) * size**-0.5
        grad_keys = dot(grad_scores, query, 0, 0) * size**-0.5
        grad_values = dot(probs.astype(jnp.bfloat16), grad, 0, 0)

        @pl.when(step == 0)
        def _():
            acc[:, :size] = grad_keys
            acc[:, size:] = grad_values

        @pl.when(step > 0)
        def _():
            acc[:, :size] += grad_keys
            acc[:, size:] += grad_values

        first = grad_query[:, : size // 2]
        second = grad_query[:, size // 2 :]
        cosine_part, sine_part = cos_ref[...], sin_ref[...]
        turned = jnp.concatenate(
            [
                first * cosine_part + second * sine_part,
                second * cosine_part - first * sine_part,
            ],
            axis=-1,
        )
        raw = raw_ref[...]
        scale = lax.rsqrt(jnp.mean(raw * raw, axis=-1, keepdims=True) + EPS)
        unit = raw * scale
        inner = turned * gain_ref[...].astype(jnp.float32)
        raw_grad = scale * (inner - unit * jnp.mean(inner * unit, axis=-1, keepdims=True))
        raw_grad_ref[...] = raw_grad.astype(jnp.bfloat16)
        gain_grad = jnp.sum(turned * unit, axis=0, keepdims=True)

        @pl.when(step == 0)
        def _():
            gain_grad_ref[...] = gain_grad

        @pl.when(step > 0)
        def _():
            gain_grad_ref[...] += gain_grad

        @pl.when(step == heads - 1)
        def _():
            far_ref[...] = acc[:before, :].astype(jnp.bfloat16)
            own_ref[...] = acc[before:, :]

    return pl.pallas_call(
        kernel,
        grid=(heads,),
        in_specs=common + [head, head],
        out_specs=[head, whole(1, size), whole(before, 2 * size), whole(rows, 2 * size)],
        out_shape=[
            jax.ShapeDtypeStruct((rows, heads * size), jnp.bfloat16),
            jax.ShapeDtypeStruct((1, size), jnp.float32),
            jax.ShapeDtypeStruct((before, 2 * size), jnp.bfloat16),
            jax.ShapeDtypeStruct((rows, 2 * size), jnp.float32),
        ],
        scratch_shapes=[pltpu.VMEM((width, 2 * size), jnp.float32)],
        compiler_params=params(32),
        name="attention_backward",
    )(qkv, gain, cosine, sine, pairs, query_segs, key_segs, query, grad_mixed)


def line_edges():
    places = lax.axis_size("replica") // 2
    outer = places // 2 - 1
    return places, outer


def exchanged(block, pairs):
    route = [(2 * a + core, 2 * b + core) for a, b in pairs for core in range(2)]
    return lax.ppermute(block, "replica", route)


class Line:
    def __init__(self):
        self.places, self.outer = line_edges()
        self.steps = 2 * self.outer + 1
        self.moving = []
        self.done = {}

    def advance(self, fresh, gate=None):
        places, outer, steps = self.places, self.outer, self.steps
        place = (lax.axis_index("replica") // 2).astype(jnp.int32).reshape(1)
        operands, plan = [], []

        def operand(entry):
            array, index = entry if isinstance(entry, tuple) else (entry, None)
            for spot, (known, known_index) in enumerate(operands):
                if known is array and known_index == index:
                    return spot
            operands.append((array, index))
            return len(operands) - 1

        for name, block, step, far in self.moving:
            plan.append((name, step + 1, [operand(block), operand(far)], step))
        for name, terms in fresh:
            plan.append((name, 0, [operand(term) for term in terms], None))
        if not plan:
            return gate
        sizes = [operands[spots[0]][0].shape[-2:] for _, _, spots, _ in plan]
        by_step = {step: index for index, (_, step, _, _) in enumerate(plan)}
        pairs = []
        for edge in range(outer):
            inward, outward = by_step.get(edge), by_step.get(2 * outer - edge)
            if inward is not None and outward is not None and sizes[inward] == sizes[outward]:
                pairs.append((edge, inward, outward))
        cuts = 3 if all(size[0] % 48 == 0 for size in sizes) else 1

        def kernel(place_ref, *refs):
            here = place_ref[0]
            inputs = refs[: len(operands)]
            if gate is not None:
                refs = refs[: len(operands)] + refs[len(operands) + 1 :]
            outputs = refs[len(operands) :]
            states = []
            for spot, (_, _, terms, last) in enumerate(plan):
                value = inputs[terms[0]][...]
                if len(terms) > 1:
                    far = inputs[terms[1]][...]
                    total = value.astype(jnp.float32)
                    for term in terms[1:]:
                        total = total + inputs[term][...].astype(jnp.float32)
                    total = total.astype(jnp.bfloat16)
                    if last is None:
                        value = total
                    elif last <= outer:
                        edge = last
                        value = jnp.where((here == edge + 1) | (here == places - 2 - edge), total, value)
                    else:
                        edge = 2 * outer - last
                        value = jnp.where((here == edge) | (here == places - 1 - edge), far, value)
                states.append(value)
                outputs[spot][...] = value
            for spot, (edge, inward, outward) in enumerate(pairs):
                outputs[len(plan) + spot][...] = jnp.where(
                    (here == edge) | (here == places - 1 - edge), states[inward], states[outward]
                )

        def spec(size, index):
            if index is None:
                return pl.BlockSpec((size[0] // cuts, size[1]), lambda i, place_ref: (i, 0))
            return pl.BlockSpec((None, size[0] // cuts, size[1]), lambda i, place_ref: (index, i, 0))

        in_specs = [spec(array.shape[-2:], index) for array, index in operands]
        arrays = [array for array, _ in operands]
        out_sizes = sizes + [sizes[inward] for _, inward, _ in pairs]
        out_specs = [spec(size, None) for size in out_sizes]
        out_shape = [jax.ShapeDtypeStruct(size, jnp.bfloat16) for size in out_sizes]
        aliases = {}
        if gate is not None:
            aliases = {1 + len(arrays): len(out_shape)}
            in_specs.append(pl.BlockSpec(memory_space=pl.ANY))
            out_specs.append(pl.BlockSpec(memory_space=pl.ANY))
            out_shape.append(jax.ShapeDtypeStruct(gate.shape, gate.dtype))
            arrays.append(gate)
        outs = pl.pallas_call(
            kernel,
            grid_spec=pltpu.PrefetchScalarGridSpec(
                num_scalar_prefetch=1, grid=(cuts,), in_specs=in_specs, out_specs=out_specs
            ),
            out_shape=out_shape,
            input_output_aliases=aliases,
            compiler_params=params(32),
            name="line_step",
        )(place, *arrays)
        received = {}
        for spot, (edge, inward, outward) in enumerate(pairs):
            ends = [(edge, edge + 1), (places - 1 - edge, places - 2 - edge)]
            far = exchanged(outs[len(plan) + spot], ends + [(b, a) for a, b in ends])
            received[inward] = received[outward] = far
        self.moving = []
        for index, (name, step, _, _) in enumerate(plan):
            block = outs[index]
            if step == steps:
                self.done[name] = block
                continue
            if index not in received:
                edge = step if step <= outer else 2 * outer - step
                route = [(edge, edge + 1), (places - 1 - edge, places - 2 - edge)]
                if step > outer:
                    route = [(b, a) for a, b in route]
                received[index] = exchanged(block, route)
            self.moving.append((name, block, step, received[index]))
        return outs[-1]

    def arrived(self):
        return [far for _, _, _, far in self.moving]

    def finished(self, name):
        while name not in self.done:
            self.advance([])
        return self.done[name]


def line_names(name, units):
    return [(name, chunk) for chunk in range(chunks_of(units))]


def whole_grad(line, name, units, dtype=jnp.float32):
    names = line_names(name, units)
    mines = [line.finished(chunk) for chunk in names]
    others = [swapped(mine, "replica", 1) for mine in mines]
    chunks = len(mines)
    tile, model = mines[0].shape
    core = (lax.axis_index("replica") % 2).astype(jnp.int32).reshape(1)

    def kernel(core_ref, *refs):
        out_ref = refs[-1]
        for chunk in range(chunks):
            for side in range(2):

                @pl.when((pl.program_id(0) == chunk) & (pl.program_id(1) == side))
                def _():
                    @pl.when(core_ref[0] == side)
                    def _():
                        out_ref[...] = refs[chunk][...].astype(dtype)

                    @pl.when(core_ref[0] != side)
                    def _():
                        out_ref[...] = refs[chunks + chunk][...].astype(dtype)

    return pl.pallas_call(
        kernel,
        grid_spec=pltpu.PrefetchScalarGridSpec(
            num_scalar_prefetch=1,
            grid=(chunks, 2),
            in_specs=[pl.BlockSpec((tile, model), lambda chunk, side, core_ref: (0, 0))] * (2 * chunks),
            out_specs=pl.BlockSpec((tile, model), lambda chunk, side, core_ref: (2 * chunk + side, 0)),
        ),
        out_shape=jax.ShapeDtypeStruct((units, model), dtype),
        compiler_params=params(24),
        name="whole_grad",
    )(core, *mines, *others)


def joined(mine, other, axis):
    core = lax.axis_index("replica") % 2
    return jnp.where(
        core == 0,
        jnp.concatenate([mine, other], axis=axis),
        jnp.concatenate([other, mine], axis=axis),
    )


def core_join(block, axis):
    return joined(block, swapped(block, "replica", 1), axis)


def fetched(block):
    got = [swapped(block, "fsdp", mask) for mask in range(1, lax.axis_size("fsdp"))]
    return got, [swapped(part, "replica", 1) for part in got]


def gathered(block):
    group = lax.axis_size("fsdp")
    blocks, near = [block] + [None] * (group - 1), []
    for ring in range(1, group.bit_length()):
        masks = [mask for mask in range(1, group) if bin(mask).count("1") == ring]
        source = after(block, *near) if near else block
        near = [swapped(source, "fsdp", mask) for mask in masks]
        for mask, far in zip(masks, near):
            blocks[mask] = far
    return blocks


def passed_along(block, axis, distance):
    devices = range(lax.axis_size(axis))
    route = [(i - distance, i) for i in devices if i - distance in devices]
    return lax.ppermute(block, axis, route)


def contract(left, right, left_dim, right_dim):
    return lax.dot_general(
        left, right, (((left_dim,), (right_dim,)), ((), ())), preferred_element_type=jnp.float32
    )


def normed(value, gain):
    return value * lax.rsqrt(jnp.mean(value * value, axis=-1, keepdims=True) + EPS) * gain


def norm_back(value, gain, grad):
    _, pull = jax.vjp(normed, value, gain)
    return pull(grad)


def tables(places, half):
    freq = 10000.0 ** (-(2.0 * jnp.arange(half, dtype=jnp.float32)) / (2 * half))
    angle = places.astype(jnp.float32)[:, None] * freq[None, :]
    return (jnp.cos(angle), jnp.sin(angle))


def rotate(value, cosine, sine):
    half = value.shape[-1] // 2
    first = value[..., :half]
    second = value[..., half:]
    return jnp.concatenate(
        [first * cosine - second * sine, second * cosine + first * sine], axis=-1
    )


def head_post(raw, gain, cosine, sine):
    return rotate(normed(raw, gain), cosine, sine)


def per_device(
    hidden_in,
    out_grad,
    segments,
    positions,
    norm_in,
    query_weight,
    key_weight,
    value_weight,
    out_weight,
    norm_attn,
    norm_ffn,
    gate_weight,
    up_weight,
    down_weight,
    norm_out,
    query_gain,
    key_gain,
):
    rows = hidden_in.shape[0]
    rank = lax.axis_index("fsdp")
    group = lax.axis_size("fsdp")
    masks = range(1, group)
    head_size = key_weight.shape[1]
    heads = query_weight.shape[1] // head_size
    model = hidden_in.shape[1]
    own_model = norm_in.shape[0]
    own_head = query_gain.shape[0]
    hops = (WINDOW - 1) // rows + 1
    scale = head_size ** (-0.5)
    qkv_weights = (query_weight, key_weight, value_weight)
    wide = sum(weight.shape[1] for weight in qkv_weights)
    qkv_block = packed(qkv_weights)
    got, peers = fetched(qkv_block)
    gains = jnp.stack(
        [
            jnp.pad(gain, (0, own_model - gain.shape[0]))
            for gain in (norm_in, norm_attn, norm_ffn, norm_out, query_gain, key_gain)
        ]
    )
    gains = after(gains, *[got[mask - 1] for mask in masks if bin(mask).count("1") == 1])
    gain_stack = jnp.stack([gains] + [swapped(gains, "fsdp", mask) for mask in masks])
    w_qkv = unpacked(qkv_weights, got, peers)
    gain_rows = jnp.stack(
        [lax.dynamic_index_in_dim(gain_stack, rank ^ i, 0, keepdims=False) for i in range(group)], axis=1
    )
    gain_in, gain_attn, gain_ffn, gain_out = (gain_rows[i].reshape(-1) for i in range(4))
    gain_query, gain_key = (gain_rows[i, :, :own_head].reshape(-1) for i in (4, 5))
    residual_in = hidden_in.astype(jnp.float32)
    normed_in = normed(residual_in, gain_in).astype(jnp.bfloat16)
    qkv = jnp.dot(normed_in, w_qkv, preferred_element_type=jnp.float32)
    key_raw = qkv[:, heads * head_size : (heads + 1) * head_size]
    value_new = qkv[:, (heads + 1) * head_size :].astype(jnp.bfloat16)
    cosine, sine = tables(positions, head_size // 2)
    key_new = head_post(key_raw, gain_key, cosine, sine).astype(jnp.bfloat16)
    pair_new = jnp.concatenate([key_new, value_new], axis=1)
    got, peers = fetched(after(packed([out_weight]), pair_new))
    w_out = unpacked([out_weight], got, peers)
    parts = [pair_new]
    for step in range(1, hops + 1):
        parts.insert(0, passed_along(pair_new, "fsdp", step))
    pairs = jnp.concatenate(parts, axis=0)
    width = pairs.shape[0]
    seg_padded = jnp.concatenate([jnp.full((hops * rows,), -1, jnp.int32), segments], axis=0)
    key_segs = lax.dynamic_slice_in_dim(seg_padded, rank * rows, width, 0)
    query_segs = lax.dynamic_slice_in_dim(segments, rank * rows, rows, 0)
    attention_args = (
        qkv,
        gain_query[None, :],
        cosine,
        sine,
        pairs,
        query_segs[:, None],
        key_segs[None, :],
    )
    query_new, mixed = attention_forward(*attention_args, heads)
    attended = contract(mixed, w_out, 1, 1)
    resid = residual_in + normed(attended, gain_attn)
    ffn_in = normed(resid, gain_ffn).astype(jnp.bfloat16)
    ffn_blocks = gathered(ffn_in)
    hiddens, slopes, acts, parts = {}, {}, {}, {}
    rings = sorted(range(group), key=lambda mask: (bin(mask).count("1"), mask))
    last = None
    for mask in rings[1:] + [0]:
        if last is not None:
            ffn_blocks[mask] = after(ffn_blocks[mask], parts[last])
        hiddens[mask], slopes[mask], acts[mask], parts[mask] = ffn_forward(
            ffn_blocks[mask], gate_weight, up_weight, down_weight
        )
        last = mask
    branch = sum(
        (swapped(parts[mask], "fsdp", mask) if mask else parts[mask]).astype(jnp.float32)
        for mask in range(group)
    )
    result = resid + normed(branch, gain_out)
    hidden_out = result.astype(jnp.bfloat16)
    grad_result = out_grad.astype(jnp.float32)
    grad_branch, grad_gain_out = norm_back(branch, gain_out, grad_result)
    grad_branch_low = grad_branch.astype(jnp.bfloat16)
    pieces = gathered(grad_branch_low)
    units = gate_weight.shape[0]
    line = Line()

    def fresh(names, other, mine):
        far = swapped(other, "replica", 1)
        keys = [key for name in names for key in line_names(name, units)]
        return [(key, [(mine, spot), (far, spot)]) for spot, key in enumerate(keys)]

    grad_gates, grad_uppers, returned = {}, {}, {}
    final = rings[-1]
    last = None
    for mask in rings[:-1]:
        if last is not None:
            pieces[mask] = after(pieces[mask], part)
        grad_gates[mask], grad_uppers[mask], part = ffn_backward(
            pieces[mask], gate_weight, up_weight, down_weight, slopes[mask], acts[mask]
        )
        returned[mask] = swapped(part, "fsdp", mask) if mask else part
        last = mask
    pieces[final] = after(pieces[final], part)
    waiting = fresh(
        ["down"], *weight_grad([[hiddens[i] for i in range(group)]], [pieces[i] for i in range(group)])
    )
    gate_parts, upper_parts, parts = ffn_backward_blocks(
        [pieces[final]], gate_weight, up_weight, down_weight, [slopes[final]], [acts[final]]
    )
    grad_gates[final], grad_uppers[final] = gate_parts[0], upper_parts[0]
    returned[final] = swapped(parts[0], "fsdp", final)
    grad_gates[final] = line.advance(
        [waiting.pop(0)], after(grad_gates[final], *[returned[mask] for mask in rings[1:-1]])
    )
    other, mine = weight_grad(
        [[grad_gates[i] for i in range(group)], [grad_uppers[i] for i in range(group)]], ffn_blocks
    )
    other = line.advance([waiting.pop(0)] if waiting else [], after(other, returned[final]))
    waiting = fresh(["gate", "up"], other, mine)

    def advance(gate=None):
        return line.advance([waiting.pop(0)] if waiting else [], gate)

    grad_resid, grad_attended_low, grad_mixed, grad_gain_ffn, grad_gain_attn = resid_backward(
        [returned[mask] for mask in range(group)], resid, attended, out_grad, gain_ffn, gain_attn, w_out
    )
    grad_mixed = advance(grad_mixed)
    grad_query_low, grad_gain_query, grad_far, grad_pair = attention_backward(
        *attention_args, query_new, grad_mixed, heads
    )
    backs = []
    for step in range(1, hops + 1):
        grad_far = passed_along(grad_far, "fsdp", -1)
        backs.append(grad_far[-rows:])
        grad_far = grad_far[:-rows]
    grad_pair = advance(grad_pair)
    other, mine, grad_in = input_backward(
        grad_pair,
        backs,
        qkv,
        cosine,
        sine,
        gain_key,
        normed_in,
        grad_query_low,
        w_qkv,
        hidden_in,
        gain_in,
        grad_resid,
        grad_attended_low,
        mixed,
        [grad_gain_attn, grad_gain_ffn, grad_gain_out[None, :], grad_gain_query],
        group,
    )
    other = advance(other)
    weight_parts = owner_parts(other, mine)
    while waiting:
        weight_parts[0] = advance(weight_parts[0])
    line.advance([("weights", weight_parts)])
    grad_down = whole_grad(line, "down", units)
    grad_down = line.advance([], grad_down)
    grad_gate_w = whole_grad(line, "gate", units)
    grad_gate_w = line.advance([], grad_gate_w)
    grad_up_w = whole_grad(line, "up", units)
    owned = core_join(line.finished("weights"), 1).astype(jnp.float32)
    inner = heads * head_size
    columns = [0, inner, inner + head_size, inner + 2 * head_size, wide + inner]
    owned_query, owned_key, owned_value, owned_out = (
        owned[:own_model, columns[i] : columns[i + 1]] for i in range(4)
    )

    def owned_gain(row, size):
        return lax.dynamic_slice_in_dim(owned[own_model + row], rank * size, size, 0)

    owned_gain_in, owned_gain_attn, owned_gain_ffn, owned_gain_out = (
        owned_gain(row, own_model) for row in (0, 2, 3, 4)
    )
    owned_gain_key, owned_gain_query = (owned_gain(row, own_head) for row in (1, 5))
    return (
        hidden_out,
        grad_in,
        owned_gain_in,
        owned_query,
        owned_key,
        owned_value,
        owned_out,
        owned_gain_attn,
        owned_gain_ffn,
        grad_gate_w,
        grad_up_w,
        grad_down,
        owned_gain_out,
        owned_gain_query,
        owned_gain_key,
    )


def solution(mesh):
    return jax.shard_map(
        per_device,
        mesh=mesh,
        in_specs=(
            P(("replica", "fsdp"), None),
            P(("replica", "fsdp"), None),
            P("replica"),
            P(("replica", "fsdp")),
            P("fsdp"),
            P("fsdp", None),
            P("fsdp", None),
            P("fsdp", None),
            P("fsdp", None),
            P("fsdp"),
            P("fsdp"),
            P("fsdp", None),
            P("fsdp", None),
            P("fsdp", None),
            P("fsdp"),
            P("fsdp"),
            P("fsdp"),
        ),
        out_specs=(
            P(("replica", "fsdp"), None),
            P(("replica", "fsdp"), None),
            P("fsdp"),
            P("fsdp", None),
            P("fsdp", None),
            P("fsdp", None),
            P("fsdp", None),
            P("fsdp"),
            P("fsdp"),
            P("fsdp", None),
            P("fsdp", None),
            P("fsdp", None),
            P("fsdp"),
            P("fsdp"),
            P("fsdp"),
        ),
        check_vma=False,
    )
```

```python
import jax
import jax.numpy as jnp
from jax import lax
from jax.experimental import pallas as pl
from jax.experimental.pallas import tpu as pltpu
from jax.sharding import PartitionSpec as P

WINDOW = 512


EPS = 1e-06
NEG = -1e30


def swapped(block, axis, mask):
    route = [(i, i ^ mask) for i in range(lax.axis_size(axis))]
    return lax.ppermute(block, axis, route)


def added(left, right):
    total = left.astype(jnp.float32) + right.astype(jnp.float32)
    return lax.optimization_barrier(total.astype(jnp.bfloat16))


def params(mebibytes=48):
    return pltpu.CompilerParams(vmem_limit_bytes=mebibytes * 1024 * 1024)


def dot(left, right, left_dim, right_dim):
    return lax.dot_general(
        left, right, (((left_dim,), (right_dim,)), ((), ())), preferred_element_type=jnp.float32
    )


def after(array, *others):
    place = pl.BlockSpec(memory_space=pl.ANY)
    return pl.pallas_call(
        lambda *refs: None,
        out_shape=jax.ShapeDtypeStruct(array.shape, array.dtype),
        in_specs=[place] * (1 + len(others)),
        out_specs=place,
        input_output_aliases={0: 0},
        compiler_params=params(1),
        name="after",
    )(array, *others)


def scalar(value):
    return value.astype(jnp.int32).reshape(1)


def packed(weights):
    half = weights[0].shape[0] // 2
    wide = sum(weight.shape[1] for weight in weights)

    def kernel(core_ref, *refs):
        out_ref = refs[-1]
        for side in range(2):

            @pl.when(core_ref[0] == side)
            def _():
                at = 0
                for ref in refs[:-1]:
                    out_ref[:, at : at + ref.shape[1]] = ref[side * half : (side + 1) * half, :]
                    at += ref.shape[1]

    return pl.pallas_call(
        kernel,
        grid_spec=pltpu.PrefetchScalarGridSpec(
            num_scalar_prefetch=1,
            grid=(1,),
            in_specs=[pl.BlockSpec(weight.shape, lambda i, core_ref: (0, 0)) for weight in weights],
            out_specs=pl.BlockSpec((half, wide), lambda i, core_ref: (0, 0)),
        ),
        out_shape=jax.ShapeDtypeStruct((half, wide), jnp.bfloat16),
        compiler_params=params(16),
        name="pack",
    )(scalar(lax.axis_index("replica") % 2), *weights)


def unpacked(weights, got, peers):
    rows = weights[0].shape[0]
    half = rows // 2
    group = len(got) + 1
    wide = sum(weight.shape[1] for weight in weights)
    own = len(weights)

    def kernel(core_ref, rank_ref, *refs):
        out_ref = refs[-1]
        mask = rank_ref[0] ^ pl.program_id(0)

        @pl.when(mask == 0)
        def _():
            at = 0
            for ref in refs[:own]:
                out_ref[:, at : at + ref.shape[1]] = ref[...]
                at += ref.shape[1]

        for other in range(1, group):
            for side in range(2):

                @pl.when((mask == other) & (core_ref[0] == side))
                def _():
                    out_ref[side * half : (side + 1) * half, :] = refs[own + other - 1][:half, :]
                    out_ref[(1 - side) * half : (2 - side) * half, :] = refs[own + group - 2 + other][:half, :]

    arrays = list(weights) + list(got) + list(peers)
    return pl.pallas_call(
        kernel,
        grid_spec=pltpu.PrefetchScalarGridSpec(
            num_scalar_prefetch=2,
            grid=(group,),
            in_specs=[pl.BlockSpec(array.shape, lambda i, *refs: (0, 0)) for array in arrays],
            out_specs=pl.BlockSpec((rows, wide), lambda i, *refs: (i, 0)),
        ),
        out_shape=jax.ShapeDtypeStruct((group * rows, wide), jnp.bfloat16),
        compiler_params=params(24),
        name="unpack",
    )(scalar(lax.axis_index("replica") % 2), scalar(lax.axis_index("fsdp")), *arrays)


GELU_A = (2.0 / 3.141592653589793) ** 0.5
GELU_B = 0.044715


def ffn_forward(x, gate_weight, up_weight, down_weight):
    gate = contract(gate_weight, x, 1, 1)
    upper = contract(up_weight, x, 1, 1)
    square = gate * gate
    bend = jnp.tanh(GELU_A * gate * (1.0 + GELU_B * square))
    half = 0.5 + 0.5 * bend
    act = gate * half
    slope = half + 0.5 * gate * (1.0 - bend * bend) * (GELU_A * (1.0 + 3.0 * GELU_B * square))
    hidden = (act * upper).astype(jnp.bfloat16)
    part = contract(hidden, down_weight, 0, 0).astype(jnp.bfloat16)
    return hidden, (slope * upper).astype(jnp.bfloat16), act.astype(jnp.bfloat16), part


def ffn_backward(grad, gate_weight, up_weight, down_weight, slope, act):
    grad_hidden = contract(down_weight, grad, 1, 1)
    grad_gate = (grad_hidden * slope.astype(jnp.float32)).astype(jnp.bfloat16)
    grad_upper = (grad_hidden * act.astype(jnp.float32)).astype(jnp.bfloat16)
    part = contract(grad_gate, gate_weight, 0, 0) + contract(grad_upper, up_weight, 0, 0)
    return grad_gate, grad_upper, part.astype(jnp.bfloat16)


def tile_of(size, most):
    return max(tile for tile in range(16, most + 1, 16) if size % tile == 0)


def ffn_backward_blocks(grads, gate_weight, up_weight, down_weight, slopes, acts):
    count = len(grads)
    rows, model = grads[0].shape
    units = gate_weight.shape[0]
    tile = tile_of(units, 432)
    steps = units // tile

    def kernel(*refs):
        step = pl.program_id(0)
        grad_refs, refs = refs[:count], refs[count:]
        (gate_ref, up_ref, down_ref), refs = refs[:3], refs[3:]
        slope_refs, act_refs, refs = refs[:count], refs[count : 2 * count], refs[2 * count :]
        gate_outs, up_outs, part_outs, (grad_ref, acc) = (
            refs[:count],
            refs[count : 2 * count],
            refs[2 * count : 3 * count],
            refs[3 * count :],
        )

        @pl.when(step == 0)
        def _():
            for spot in range(count):
                grad_ref[spot * rows : (spot + 1) * rows, :] = grad_refs[spot][...]
            acc[...] = jnp.zeros_like(acc)

        grad_hidden = dot(down_ref[...], grad_ref[...], 1, 1)
        slope = jnp.concatenate([ref[...] for ref in slope_refs], axis=1).astype(jnp.float32)
        act = jnp.concatenate([ref[...] for ref in act_refs], axis=1).astype(jnp.float32)
        grad_gate = (grad_hidden * slope).astype(jnp.bfloat16)
        grad_upper = (grad_hidden * act).astype(jnp.bfloat16)
        for spot in range(count):
            gate_outs[spot][...] = grad_gate[:, spot * rows : (spot + 1) * rows]
            up_outs[spot][...] = grad_upper[:, spot * rows : (spot + 1) * rows]
        acc[...] += dot(grad_gate, gate_ref[...], 0, 0) + dot(grad_upper, up_ref[...], 0, 0)

        @pl.when(step == steps - 1)
        def _():
            for spot in range(count):
                part_outs[spot][...] = acc[spot * rows : (spot + 1) * rows, :].astype(jnp.bfloat16)

    weight = pl.BlockSpec((tile, model), lambda i: (i, 0))
    flat = pl.BlockSpec((tile, rows), lambda i: (i, 0))
    whole = pl.BlockSpec((rows, model), lambda i: (0, 0))
    kept = jax.ShapeDtypeStruct((units, rows), jnp.bfloat16)
    outs = pl.pallas_call(
        kernel,
        grid=(steps,),
        out_shape=[kept] * (2 * count) + [jax.ShapeDtypeStruct((rows, model), jnp.bfloat16)] * count,
        in_specs=[whole] * count + [weight] * 3 + [flat] * (2 * count),
        out_specs=[flat] * (2 * count) + [whole] * count,
        scratch_shapes=[
            pltpu.VMEM((count * rows, model), jnp.bfloat16),
            pltpu.VMEM((count * rows, model), jnp.float32),
        ],
        compiler_params=params(),
        name="ffn_backward",
    )(*grads, gate_weight, up_weight, down_weight, *slopes, *acts)
    return outs[:count], outs[count : 2 * count], outs[2 * count :]


def norm_pull(value, gain, grad):
    scale = lax.rsqrt(jnp.mean(value * value, axis=-1, keepdims=True) + EPS)
    unit = value * scale
    inner = grad * gain
    return scale * (inner - unit * jnp.mean(inner * unit, axis=-1, keepdims=True)), grad * unit


def resid_backward(parts, resid, attended, out_grad, gain_ffn, gain_attn, w_out):
    count = len(parts)
    rows, model = resid.shape
    tile = min(rows, 128)

    def kernel(*refs):
        part_refs, refs = refs[:count], refs[count:]
        resid_ref, attended_ref, out_ref, ffn_ref, attn_ref, weight_ref, refs = *refs[:6], refs[6:]
        grad_resid_ref, grad_attended_ref, grad_mixed_ref, ffn_grad_ref, attn_grad_ref = refs
        grad = sum(ref[...].astype(jnp.float32) for ref in part_refs)
        pulled, ffn_rows = norm_pull(resid_ref[...], ffn_ref[...].astype(jnp.float32), grad)
        grad_resid = out_ref[...].astype(jnp.float32) + pulled
        grad_resid_ref[...] = grad_resid
        pulled, attn_rows = norm_pull(attended_ref[...], attn_ref[...].astype(jnp.float32), grad_resid)
        grad_attended = pulled.astype(jnp.bfloat16)
        grad_attended_ref[...] = grad_attended
        grad_mixed_ref[...] = dot(grad_attended, weight_ref[...], 1, 0).astype(jnp.bfloat16)
        ffn_grad = jnp.sum(ffn_rows, axis=0, keepdims=True)
        attn_grad = jnp.sum(attn_rows, axis=0, keepdims=True)

        @pl.when(pl.program_id(0) == 0)
        def _():
            ffn_grad_ref[...] = ffn_grad
            attn_grad_ref[...] = attn_grad

        @pl.when(pl.program_id(0) > 0)
        def _():
            ffn_grad_ref[...] += ffn_grad
            attn_grad_ref[...] += attn_grad

    block = pl.BlockSpec((tile, model), lambda i: (i, 0))
    vector = pl.BlockSpec((1, model), lambda i: (0, 0))
    inner = w_out.shape[1]
    return pl.pallas_call(
        kernel,
        grid=(rows // tile,),
        in_specs=[block] * (count + 3) + [vector] * 2 + [pl.BlockSpec(w_out.shape, lambda i: (0, 0))],
        out_specs=[block, block, pl.BlockSpec((tile, inner), lambda i: (i, 0)), vector, vector],
        out_shape=[
            jax.ShapeDtypeStruct((rows, model), jnp.float32),
            jax.ShapeDtypeStruct((rows, model), jnp.bfloat16),
            jax.ShapeDtypeStruct((rows, inner), jnp.bfloat16),
            jax.ShapeDtypeStruct((1, model), jnp.float32),
            jax.ShapeDtypeStruct((1, model), jnp.float32),
        ],
        compiler_params=params(32),
        name="resid_backward",
    )(*parts, resid, attended, out_grad, gain_ffn[None, :], gain_attn[None, :], w_out)


def input_backward(
    own_pair, backs, qkv, cosine, sine, gain_key, normed_in, grad_query, w_qkv, hidden_in, gain_in, grad_resid,
    grad_attended, mixed, gain_grads, group,
):
    rows, model = hidden_in.shape
    size = own_pair.shape[1] // 2
    inner = grad_query.shape[1]
    own_rows = model // group
    half = inner + size
    hops = len(backs)
    count = len(gain_grads)

    def kernel(core_ref, *refs):
        pair_ref, refs = refs[0], refs[1:]
        back_refs, refs = refs[:hops], refs[hops:]
        (
            raw_ref, cos_ref, sin_ref, key_gain_ref, normed_ref, query_ref, weight_ref, x_ref, gain_ref, resid_ref,
            attended_ref, mixed_ref, refs,
        ) = *refs[:12], refs[12:]
        gain_refs, refs = refs[:count], refs[count:]
        other_ref, mine_ref, grad_in_ref, rows_ref = refs
        pair = pair_ref[...] + sum(ref[...].astype(jnp.float32) for ref in back_refs)
        first = pair[:, : size // 2]
        second = pair[:, size // 2 : size]
        turned = jnp.concatenate(
            [
                first * cos_ref[...] + second * sin_ref[...],
                second * cos_ref[...] - first * sin_ref[...],
            ],
            axis=-1,
        )
        pulled, key_rows = norm_pull(raw_ref[...], key_gain_ref[...].astype(jnp.float32), turned)
        grad_key = pulled.astype(jnp.bfloat16)
        grad_value = pair[:, size:].astype(jnp.bfloat16)
        grad_normed = (
            dot(query_ref[...], weight_ref[:, :inner], 1, 1)
            + dot(grad_key, weight_ref[:, inner:half], 1, 1)
            + dot(grad_value, weight_ref[:, half:], 1, 1)
        )
        pulled, in_rows = norm_pull(
            x_ref[...].astype(jnp.float32), gain_ref[...].astype(jnp.float32), grad_normed
        )
        grad_in_ref[...] = resid_ref[...] + pulled
        rows_ref[...] = jnp.zeros_like(rows_ref)
        rows_ref[0:1, :model] = jnp.sum(in_rows, axis=0, keepdims=True)
        rows_ref[1:2, :size] = jnp.sum(key_rows, axis=0, keepdims=True)
        for spot in range(count):
            rows_ref[2 + spot : 3 + spot, : gain_refs[spot].shape[1]] = gain_refs[spot][...].astype(
                jnp.float32
            )
        gains = rows_ref[...].astype(jnp.bfloat16)

        def write(ref, side):
            pieces = (
                [(normed_ref, query_ref[...], 0, inner), (normed_ref, grad_key, inner, half)]
                if side == 0
                else [(normed_ref, grad_value, 0, size), (attended_ref, mixed_ref[...], size, half)]
            )
            for left, right, begin, end in pieces:
                value = dot(left[...], right, 0, 0).astype(jnp.bfloat16)
                for owner in range(group):
                    ref[owner, :own_rows, begin:end] = value[owner * own_rows : (owner + 1) * own_rows]
            for owner in range(group):
                ref[owner, own_rows:, :] = gains

        for core in range(2):

            @pl.when(core_ref[0] == core)
            def _():
                write(other_ref, 1 - core)
                write(mine_ref, core)

    def whole(array):
        return pl.BlockSpec(array.shape, lambda i, core_ref: (0,) * len(array.shape))

    arrays = [
        own_pair, *backs, qkv, cosine, sine, gain_key[None, :], normed_in, grad_query, w_qkv, hidden_in,
        gain_in[None, :], grad_resid, grad_attended, mixed, *gain_grads,
    ]
    in_specs = [whole(array) for array in arrays]
    in_specs[1 + hops] = pl.BlockSpec((rows, size), lambda i, core_ref: (0, inner // size))
    shape = jax.ShapeDtypeStruct((group, own_rows + 16, half), jnp.bfloat16)
    grad_in = jax.ShapeDtypeStruct((rows, model), jnp.float32)
    return pl.pallas_call(
        kernel,
        grid_spec=pltpu.PrefetchScalarGridSpec(
            num_scalar_prefetch=1,
            grid=(1,),
            in_specs=in_specs,
            out_specs=[whole(shape), whole(shape), whole(grad_in)],
            scratch_shapes=[pltpu.VMEM((16, half), jnp.float32)],
        ),
        out_shape=[shape, shape, grad_in],
        compiler_params=params(),
        name="input_backward",
    )(scalar(lax.axis_index("replica") % 2), *arrays)


def owner_parts(other, mine):
    group, height, wide = mine.shape
    far = swapped(other, "replica", 1)

    def kernel(rank_ref, mine_ref, far_ref, *outs):
        total = mine_ref[...].astype(jnp.float32) + far_ref[...].astype(jnp.float32)
        for mask in range(group):

            @pl.when(pl.program_id(0) == mask)
            def _():
                outs[mask][...] = total.astype(jnp.bfloat16)

    block = pl.BlockSpec((None, height, wide), lambda i, rank_ref: (rank_ref[0] ^ i, 0, 0))
    parts = pl.pallas_call(
        kernel,
        grid_spec=pltpu.PrefetchScalarGridSpec(
            num_scalar_prefetch=1,
            grid=(group,),
            in_specs=[block, block],
            out_specs=[pl.BlockSpec((height, wide), lambda i, rank_ref: (0, 0))] * group,
        ),
        out_shape=[jax.ShapeDtypeStruct((height, wide), jnp.bfloat16)] * group,
        compiler_params=params(16),
        name="owner_parts",
    )(scalar(lax.axis_index("fsdp")), mine, far)
    return [parts[0]] + [swapped(parts[mask], "fsdp", mask) for mask in range(1, group)]


def chunks_of(units):
    return 2 if units % 64 == 0 else 1


def weight_grad(sets, rights):
    group = len(rights)
    count = len(sets)
    units, rows = sets[0][0].shape
    model = rights[0].shape[1]
    chunks = chunks_of(units)
    tile = units // (2 * chunks)

    def kernel(core_ref, *refs):
        right_refs, left_refs = refs[:group], refs[group:-4]
        other_ref, mine_ref, left_ref, right_ref = refs[-4:]

        @pl.when((pl.program_id(0) == 0) & (pl.program_id(1) == 0))
        def _():
            for spot in range(group):
                right_ref[spot * rows : (spot + 1) * rows, :] = right_refs[spot][...]

        for index in range(count):

            @pl.when(pl.program_id(1) == index)
            def _():
                for chunk in range(chunks):
                    for spot in range(group):
                        left_ref[
                            chunk * tile : (chunk + 1) * tile, spot * rows : (spot + 1) * rows
                        ] = left_refs[(index * chunks + chunk) * group + spot][...]

        value = dot(left_ref[...], right_ref[...], 1, 0).astype(jnp.bfloat16)

        @pl.when(pl.program_id(0) == 0)
        def _():
            for chunk in range(chunks):
                other_ref[chunk] = value[chunk * tile : (chunk + 1) * tile]

        @pl.when(pl.program_id(0) == 1)
        def _():
            for chunk in range(chunks):
                mine_ref[chunk] = value[chunk * tile : (chunk + 1) * tile]

    def left_spec(chunk):
        def index(side, spot, core_ref):
            return (2 * chunk + jnp.where(side == 0, 1 - core_ref[0], core_ref[0]), 0)

        return pl.BlockSpec((tile, rows), index)

    shape = jax.ShapeDtypeStruct((count * chunks, tile, model), jnp.bfloat16)
    block = (chunks, tile, model)
    return pl.pallas_call(
        kernel,
        grid_spec=pltpu.PrefetchScalarGridSpec(
            num_scalar_prefetch=1,
            grid=(2, count),
            in_specs=[pl.BlockSpec((rows, model), lambda side, spot, core_ref: (0, 0))] * group
            + [left_spec(chunk) for _ in range(count) for chunk in range(chunks) for _ in range(group)],
            out_specs=[
                pl.BlockSpec(
                    block, lambda side, spot, core_ref: (jnp.where(side == 0, spot, count - 1), 0, 0)
                ),
                pl.BlockSpec(block, lambda side, spot, core_ref: (jnp.where(side == 0, 0, spot), 0, 0)),
            ],
            scratch_shapes=[
                pltpu.VMEM((chunks * tile, group * rows), jnp.bfloat16),
                pltpu.VMEM((group * rows, model), jnp.bfloat16),
            ],
        ),
        out_shape=[shape, shape],
        compiler_params=params(),
        name="weight_grad",
    )(
        scalar(lax.axis_index("replica") % 2),
        *rights,
        *[left for lefts in sets for _ in range(chunks) for left in lefts],
    )


def allowed_mask(query_segs_ref, key_segs_ref, rows, width):
    gap = (
        width
        - rows
        + lax.broadcasted_iota(jnp.int32, (rows, width), 0)
        - lax.broadcasted_iota(jnp.int32, (rows, width), 1)
    )
    return (gap >= 0) & (gap < WINDOW) & (query_segs_ref[...] == key_segs_ref[...])


def head_probs(query, keys, allowed, scale):
    scores = jnp.where(allowed, dot(query, keys, 1, 1) * scale, NEG)
    expo = jnp.exp(scores - jnp.max(scores, axis=-1, keepdims=True))
    return expo / jnp.sum(expo, axis=-1, keepdims=True)


def attention_specs(rows, size, width, heads):
    head = pl.BlockSpec((rows, size), lambda h: (0, h))
    whole = lambda *shape: pl.BlockSpec(shape, lambda h: (0, 0))
    common = [
        head,
        whole(1, size),
        whole(rows, size // 2),
        whole(rows, size // 2),
        whole(width, 2 * size),
        whole(rows, 1),
        whole(1, width),
    ]
    return head, whole, common


def attention_forward(qkv, gain, cosine, sine, pairs, query_segs, key_segs, heads):
    rows, width, size = qkv.shape[0], pairs.shape[0], pairs.shape[1] // 2
    head, _, common = attention_specs(rows, size, width, heads)

    def kernel(raw_ref, gain_ref, cos_ref, sin_ref, pairs_ref, qseg_ref, kseg_ref, query_ref, mixed_ref):
        query = head_post(raw_ref[...], gain_ref[...], cos_ref[...], sin_ref[...]).astype(jnp.bfloat16)
        query_ref[...] = query
        allowed = allowed_mask(qseg_ref, kseg_ref, rows, width)
        probs = head_probs(query, pairs_ref[:, :size], allowed, size**-0.5).astype(jnp.bfloat16)
        mixed_ref[...] = dot(probs, pairs_ref[:, size:], 1, 0).astype(jnp.bfloat16)

    shape = jax.ShapeDtypeStruct((rows, heads * size), jnp.bfloat16)
    return pl.pallas_call(
        kernel,
        grid=(heads,),
        in_specs=common,
        out_specs=[head, head],
        out_shape=[shape, shape],
        compiler_params=params(32),
        name="attention_forward",
    )(qkv, gain, cosine, sine, pairs, query_segs, key_segs)


def attention_backward(qkv, gain, cosine, sine, pairs, query_segs, key_segs, query, grad_mixed, heads):
    rows, width, size = qkv.shape[0], pairs.shape[0], pairs.shape[1] // 2
    head, whole, common = attention_specs(rows, size, width, heads)
    before = width - rows

    def kernel(
        raw_ref, gain_ref, cos_ref, sin_ref, pairs_ref, qseg_ref, kseg_ref, query_ref, grad_ref,
        raw_grad_ref, gain_grad_ref, far_ref, own_ref, acc,
    ):
        step = pl.program_id(0)
        query = query_ref[...]
        grad = grad_ref[...]
        allowed = allowed_mask(qseg_ref, kseg_ref, rows, width)
        keys = pairs_ref[:, :size]
        probs = head_probs(query, keys, allowed, size**-0.5)
        grad_probs = dot(grad, pairs_ref[:, size:], 1, 1)
        delta = jnp.sum(grad_probs * probs, axis=-1, keepdims=True)
        grad_scores = (probs * (grad_probs - delta)).astype(jnp.bfloat16)
        grad_query = dot(grad_scores, keys, 1, 0) * size**-0.5
        grad_keys = dot(grad_scores, query, 0, 0) * size**-0.5
        grad_values = dot(probs.astype(jnp.bfloat16), grad, 0, 0)

        @pl.when(step == 0)
        def _():
            acc[:, :size] = grad_keys
            acc[:, size:] = grad_values

        @pl.when(step > 0)
        def _():
            acc[:, :size] += grad_keys
            acc[:, size:] += grad_values

        first = grad_query[:, : size // 2]
        second = grad_query[:, size // 2 :]
        cosine_part, sine_part = cos_ref[...], sin_ref[...]
        turned = jnp.concatenate(
            [
                first * cosine_part + second * sine_part,
                second * cosine_part - first * sine_part,
            ],
            axis=-1,
        )
        raw = raw_ref[...]
        scale = lax.rsqrt(jnp.mean(raw * raw, axis=-1, keepdims=True) + EPS)
        unit = raw * scale
        inner = turned * gain_ref[...].astype(jnp.float32)
        raw_grad = scale * (inner - unit * jnp.mean(inner * unit, axis=-1, keepdims=True))
        raw_grad_ref[...] = raw_grad.astype(jnp.bfloat16)
        gain_grad = jnp.sum(turned * unit, axis=0, keepdims=True)

        @pl.when(step == 0)
        def _():
            gain_grad_ref[...] = gain_grad

        @pl.when(step > 0)
        def _():
            gain_grad_ref[...] += gain_grad

        @pl.when(step == heads - 1)
        def _():
            far_ref[...] = acc[:before, :].astype(jnp.bfloat16)
            own_ref[...] = acc[before:, :]

    return pl.pallas_call(
        kernel,
        grid=(heads,),
        in_specs=common + [head, head],
        out_specs=[head, whole(1, size), whole(before, 2 * size), whole(rows, 2 * size)],
        out_shape=[
            jax.ShapeDtypeStruct((rows, heads * size), jnp.bfloat16),
            jax.ShapeDtypeStruct((1, size), jnp.float32),
            jax.ShapeDtypeStruct((before, 2 * size), jnp.bfloat16),
            jax.ShapeDtypeStruct((rows, 2 * size), jnp.float32),
        ],
        scratch_shapes=[pltpu.VMEM((width, 2 * size), jnp.float32)],
        compiler_params=params(32),
        name="attention_backward",
    )(qkv, gain, cosine, sine, pairs, query_segs, key_segs, query, grad_mixed)


def line_edges():
    places = lax.axis_size("replica") // 2
    outer = places // 2 - 1
    return places, outer


def exchanged(block, pairs):
    route = [(2 * a + core, 2 * b + core) for a, b in pairs for core in range(2)]
    return lax.ppermute(block, "replica", route)


class Line:
    def __init__(self):
        self.places, self.outer = line_edges()
        self.steps = 2 * self.outer + 1
        self.moving = []
        self.done = {}

    def advance(self, fresh, gate=None):
        places, outer, steps = self.places, self.outer, self.steps
        place = (lax.axis_index("replica") // 2).astype(jnp.int32).reshape(1)
        operands, plan = [], []

        def operand(entry):
            array, index = entry if isinstance(entry, tuple) else (entry, None)
            for spot, (known, known_index) in enumerate(operands):
                if known is array and known_index == index:
                    return spot
            operands.append((array, index))
            return len(operands) - 1

        for name, block, step, far in self.moving:
            plan.append((name, step + 1, [operand(block), operand(far)], step))
        for name, terms in fresh:
            plan.append((name, 0, [operand(term) for term in terms], None))
        if not plan:
            return gate
        sizes = [operands[spots[0]][0].shape[-2:] for _, _, spots, _ in plan]
        by_step = {step: index for index, (_, step, _, _) in enumerate(plan)}
        pairs = []
        for edge in range(outer):
            inward, outward = by_step.get(edge), by_step.get(2 * outer - edge)
            if inward is not None and outward is not None and sizes[inward] == sizes[outward]:
                pairs.append((edge, inward, outward))
        cuts = 3 if all(size[0] % 48 == 0 for size in sizes) else 1

        def kernel(place_ref, *refs):
            here = place_ref[0]
            inputs = refs[: len(operands)]
            if gate is not None:
                refs = refs[: len(operands)] + refs[len(operands) + 1 :]
            outputs = refs[len(operands) :]
            states = []
            for spot, (_, _, terms, last) in enumerate(plan):
                value = inputs[terms[0]][...]
                if len(terms) > 1:
                    far = inputs[terms[1]][...]
                    total = value.astype(jnp.float32)
                    for term in terms[1:]:
                        total = total + inputs[term][...].astype(jnp.float32)
                    total = total.astype(jnp.bfloat16)
                    if last is None:
                        value = total
                    elif last <= outer:
                        edge = last
                        value = jnp.where((here == edge + 1) | (here == places - 2 - edge), total, value)
                    else:
                        edge = 2 * outer - last
                        value = jnp.where((here == edge) | (here == places - 1 - edge), far, value)
                states.append(value)
                outputs[spot][...] = value
            for spot, (edge, inward, outward) in enumerate(pairs):
                outputs[len(plan) + spot][...] = jnp.where(
                    (here == edge) | (here == places - 1 - edge), states[inward], states[outward]
                )

        def spec(size, index):
            if index is None:
                return pl.BlockSpec((size[0] // cuts, size[1]), lambda i, place_ref: (i, 0))
            return pl.BlockSpec((None, size[0] // cuts, size[1]), lambda i, place_ref: (index, i, 0))

        in_specs = [spec(array.shape[-2:], index) for array, index in operands]
        arrays = [array for array, _ in operands]
        out_sizes = sizes + [sizes[inward] for _, inward, _ in pairs]
        out_specs = [spec(size, None) for size in out_sizes]
        out_shape = [jax.ShapeDtypeStruct(size, jnp.bfloat16) for size in out_sizes]
        aliases = {}
        if gate is not None:
            aliases = {1 + len(arrays): len(out_shape)}
            in_specs.append(pl.BlockSpec(memory_space=pl.ANY))
            out_specs.append(pl.BlockSpec(memory_space=pl.ANY))
            out_shape.append(jax.ShapeDtypeStruct(gate.shape, gate.dtype))
            arrays.append(gate)
        outs = pl.pallas_call(
            kernel,
            grid_spec=pltpu.PrefetchScalarGridSpec(
                num_scalar_prefetch=1, grid=(cuts,), in_specs=in_specs, out_specs=out_specs
            ),
            out_shape=out_shape,
            input_output_aliases=aliases,
            compiler_params=params(32),
            name="line_step",
        )(place, *arrays)
        received = {}
        for spot, (edge, inward, outward) in enumerate(pairs):
            ends = [(edge, edge + 1), (places - 1 - edge, places - 2 - edge)]
            far = exchanged(outs[len(plan) + spot], ends + [(b, a) for a, b in ends])
            received[inward] = received[outward] = far
        self.moving = []
        for index, (name, step, _, _) in enumerate(plan):
            block = outs[index]
            if step == steps:
                self.done[name] = block
                continue
            if index not in received:
                edge = step if step <= outer else 2 * outer - step
                route = [(edge, edge + 1), (places - 1 - edge, places - 2 - edge)]
                if step > outer:
                    route = [(b, a) for a, b in route]
                received[index] = exchanged(block, route)
            self.moving.append((name, block, step, received[index]))
        return outs[-1]

    def arrived(self):
        return [far for _, _, _, far in self.moving]

    def finished(self, name):
        while name not in self.done:
            self.advance([])
        return self.done[name]


def line_names(name, units):
    return [(name, chunk) for chunk in range(chunks_of(units))]


def whole_grad(line, name, units, dtype=jnp.float32):
    names = line_names(name, units)
    mines = [line.finished(chunk) for chunk in names]
    others = [swapped(mine, "replica", 1) for mine in mines]
    chunks = len(mines)
    tile, model = mines[0].shape
    core = (lax.axis_index("replica") % 2).astype(jnp.int32).reshape(1)

    def kernel(core_ref, *refs):
        out_ref = refs[-1]
        for chunk in range(chunks):
            for side in range(2):

                @pl.when((pl.program_id(0) == chunk) & (pl.program_id(1) == side))
                def _():
                    @pl.when(core_ref[0] == side)
                    def _():
                        out_ref[...] = refs[chunk][...].astype(dtype)

                    @pl.when(core_ref[0] != side)
                    def _():
                        out_ref[...] = refs[chunks + chunk][...].astype(dtype)

    return pl.pallas_call(
        kernel,
        grid_spec=pltpu.PrefetchScalarGridSpec(
            num_scalar_prefetch=1,
            grid=(chunks, 2),
            in_specs=[pl.BlockSpec((tile, model), lambda chunk, side, core_ref: (0, 0))] * (2 * chunks),
            out_specs=pl.BlockSpec((tile, model), lambda chunk, side, core_ref: (2 * chunk + side, 0)),
        ),
        out_shape=jax.ShapeDtypeStruct((units, model), dtype),
        compiler_params=params(24),
        name="whole_grad",
    )(core, *mines, *others)


def joined(mine, other, axis):
    core = lax.axis_index("replica") % 2
    return jnp.where(
        core == 0,
        jnp.concatenate([mine, other], axis=axis),
        jnp.concatenate([other, mine], axis=axis),
    )


def core_join(block, axis):
    return joined(block, swapped(block, "replica", 1), axis)


def fetched(block):
    got = [swapped(block, "fsdp", mask) for mask in range(1, lax.axis_size("fsdp"))]
    return got, [swapped(part, "replica", 1) for part in got]


def gathered(block):
    group = lax.axis_size("fsdp")
    blocks, near = [block] + [None] * (group - 1), []
    for ring in range(1, group.bit_length()):
        masks = [mask for mask in range(1, group) if bin(mask).count("1") == ring]
        source = after(block, *near) if near else block
        near = [swapped(source, "fsdp", mask) for mask in masks]
        for mask, far in zip(masks, near):
            blocks[mask] = far
    return blocks


def passed_along(block, axis, distance):
    devices = range(lax.axis_size(axis))
    route = [(i - distance, i) for i in devices if i - distance in devices]
    return lax.ppermute(block, axis, route)


def contract(left, right, left_dim, right_dim):
    return lax.dot_general(
        left, right, (((left_dim,), (right_dim,)), ((), ())), preferred_element_type=jnp.float32
    )


def normed(value, gain):
    return value * lax.rsqrt(jnp.mean(value * value, axis=-1, keepdims=True) + EPS) * gain


def norm_back(value, gain, grad):
    _, pull = jax.vjp(normed, value, gain)
    return pull(grad)


def tables(places, half):
    freq = 10000.0 ** (-(2.0 * jnp.arange(half, dtype=jnp.float32)) / (2 * half))
    angle = places.astype(jnp.float32)[:, None] * freq[None, :]
    return (jnp.cos(angle), jnp.sin(angle))


def rotate(value, cosine, sine):
    half = value.shape[-1] // 2
    first = value[..., :half]
    second = value[..., half:]
    return jnp.concatenate(
        [first * cosine - second * sine, second * cosine + first * sine], axis=-1
    )


def head_post(raw, gain, cosine, sine):
    return rotate(normed(raw, gain), cosine, sine)


def per_device(
    hidden_in,
    out_grad,
    segments,
    positions,
    norm_in,
    query_weight,
    key_weight,
    value_weight,
    out_weight,
    norm_attn,
    norm_ffn,
    gate_weight,
    up_weight,
    down_weight,
    norm_out,
    query_gain,
    key_gain,
):
    rows = hidden_in.shape[0]
    rank = lax.axis_index("fsdp")
    group = lax.axis_size("fsdp")
    masks = range(1, group)
    head_size = key_weight.shape[1]
    heads = query_weight.shape[1] // head_size
    model = hidden_in.shape[1]
    own_model = norm_in.shape[0]
    own_head = query_gain.shape[0]
    hops = (WINDOW - 1) // rows + 1
    scale = head_size ** (-0.5)
    qkv_weights = (query_weight, key_weight, value_weight)
    wide = sum(weight.shape[1] for weight in qkv_weights)
    qkv_block = packed(qkv_weights)
    got, peers = fetched(qkv_block)
    gains = jnp.stack(
        [
            jnp.pad(gain, (0, own_model - gain.shape[0]))
            for gain in (norm_in, norm_attn, norm_ffn, norm_out, query_gain, key_gain)
        ]
    )
    gains = after(gains, *[got[mask - 1] for mask in masks if bin(mask).count("1") == 1])
    gain_stack = jnp.stack([gains] + [swapped(gains, "fsdp", mask) for mask in masks])
    w_qkv = unpacked(qkv_weights, got, peers)
    gain_rows = jnp.stack(
        [lax.dynamic_index_in_dim(gain_stack, rank ^ i, 0, keepdims=False) for i in range(group)], axis=1
    )
    gain_in, gain_attn, gain_ffn, gain_out = (gain_rows[i].reshape(-1) for i in range(4))
    gain_query, gain_key = (gain_rows[i, :, :own_head].reshape(-1) for i in (4, 5))
    residual_in = hidden_in.astype(jnp.float32)
    normed_in = normed(residual_in, gain_in).astype(jnp.bfloat16)
    qkv = jnp.dot(normed_in, w_qkv, preferred_element_type=jnp.float32)
    key_raw = qkv[:, heads * head_size : (heads + 1) * head_size]
    value_new = qkv[:, (heads + 1) * head_size :].astype(jnp.bfloat16)
    cosine, sine = tables(positions, head_size // 2)
    key_new = head_post(key_raw, gain_key, cosine, sine).astype(jnp.bfloat16)
    pair_new = jnp.concatenate([key_new, value_new], axis=1)
    got, peers = fetched(after(packed([out_weight]), pair_new))
    w_out = unpacked([out_weight], got, peers)
    parts = [pair_new]
    for step in range(1, hops + 1):
        parts.insert(0, passed_along(pair_new, "fsdp", step))
    pairs = jnp.concatenate(parts, axis=0)
    width = pairs.shape[0]
    seg_padded = jnp.concatenate([jnp.full((hops * rows,), -1, jnp.int32), segments], axis=0)
    key_segs = lax.dynamic_slice_in_dim(seg_padded, rank * rows, width, 0)
    query_segs = lax.dynamic_slice_in_dim(segments, rank * rows, rows, 0)
    attention_args = (
        qkv,
        gain_query[None, :],
        cosine,
        sine,
        pairs,
        query_segs[:, None],
        key_segs[None, :],
    )
    query_new, mixed = attention_forward(*attention_args, heads)
    attended = contract(mixed, w_out, 1, 1)
    resid = residual_in + normed(attended, gain_attn)
    ffn_in = normed(resid, gain_ffn).astype(jnp.bfloat16)
    ffn_blocks = gathered(ffn_in)
    hiddens, slopes, acts, parts = {}, {}, {}, {}
    rings = sorted(range(group), key=lambda mask: (bin(mask).count("1"), mask))
    last = None
    for mask in rings[1:] + [0]:
        if last is not None:
            ffn_blocks[mask] = after(ffn_blocks[mask], parts[last])
        hiddens[mask], slopes[mask], acts[mask], parts[mask] = ffn_forward(
            ffn_blocks[mask], gate_weight, up_weight, down_weight
        )
        last = mask
    branch = sum(
        (swapped(parts[mask], "fsdp", mask) if mask else parts[mask]).astype(jnp.float32)
        for mask in range(group)
    )
    result = resid + normed(branch, gain_out)
    hidden_out = result.astype(jnp.bfloat16)
    grad_result = out_grad.astype(jnp.float32)
    grad_branch, grad_gain_out = norm_back(branch, gain_out, grad_result)
    grad_branch_low = grad_branch.astype(jnp.bfloat16)
    pieces = gathered(grad_branch_low)
    units = gate_weight.shape[0]
    line = Line()

    def fresh(names, other, mine):
        far = swapped(other, "replica", 1)
        keys = [key for name in names for key in line_names(name, units)]
        return [(key, [(mine, spot), (far, spot)]) for spot, key in enumerate(keys)]

    grad_gates, grad_uppers, returned = {}, {}, {}
    final = rings[-1]
    last = None
    for mask in rings[:-1]:
        if last is not None:
            pieces[mask] = after(pieces[mask], part)
        grad_gates[mask], grad_uppers[mask], part = ffn_backward(
            pieces[mask], gate_weight, up_weight, down_weight, slopes[mask], acts[mask]
        )
        returned[mask] = swapped(part, "fsdp", mask) if mask else part
        last = mask
    pieces[final] = after(pieces[final], part)
    waiting = fresh(
        ["down"], *weight_grad([[hiddens[i] for i in range(group)]], [pieces[i] for i in range(group)])
    )
    pieces[final] = line.advance([waiting.pop(0)], pieces[final])
    gate_parts, upper_parts, parts = ffn_backward_blocks(
        [pieces[final]], gate_weight, up_weight, down_weight, [slopes[final]], [acts[final]]
    )
    grad_gates[final], grad_uppers[final] = gate_parts[0], upper_parts[0]
    returned[final] = swapped(parts[0], "fsdp", final)
    other, mine = weight_grad(
        [[grad_gates[i] for i in range(group)], [grad_uppers[i] for i in range(group)]], ffn_blocks
    )
    other = line.advance([waiting.pop(0)] if waiting else [], after(other, *[returned[mask] for mask in masks]))
    waiting = fresh(["gate", "up"], other, mine)

    def advance(gate=None):
        return line.advance([waiting.pop(0)] if waiting else [], gate)

    grad_resid, grad_attended_low, grad_mixed, grad_gain_ffn, grad_gain_attn = resid_backward(
        [returned[mask] for mask in range(group)], resid, attended, out_grad, gain_ffn, gain_attn, w_out
    )
    grad_mixed = advance(grad_mixed)
    grad_query_low, grad_gain_query, grad_far, grad_pair = attention_backward(
        *attention_args, query_new, grad_mixed, heads
    )
    backs = [
        passed_along(grad_far[(hops - step) * rows : (hops - step + 1) * rows], "fsdp", -step)
        for step in range(1, hops + 1)
    ]
    other, mine, grad_in = input_backward(
        grad_pair,
        backs,
        qkv,
        cosine,
        sine,
        gain_key,
        normed_in,
        grad_query_low,
        w_qkv,
        hidden_in,
        gain_in,
        grad_resid,
        grad_attended_low,
        mixed,
        [grad_gain_attn, grad_gain_ffn, grad_gain_out[None, :], grad_gain_query],
        group,
    )
    other = advance(other)
    weight_parts = owner_parts(other, mine)
    weight_parts[0] = advance(weight_parts[0])
    near = [weight_parts[mask] for mask in masks if bin(mask).count("1") == 1]
    while waiting:
        weight_parts[0] = advance(after(weight_parts[0], *near))
    line.advance([("weights", weight_parts)])
    grad_down = whole_grad(line, "down", units)
    grad_down = line.advance([], grad_down)
    grad_gate_w = whole_grad(line, "gate", units)
    grad_gate_w = line.advance([], grad_gate_w)
    grad_up_w = whole_grad(line, "up", units)
    grad_up_w = line.advance([], grad_up_w)
    owned = core_join(line.finished("weights"), 1).astype(jnp.float32)
    inner = heads * head_size
    columns = [0, inner, inner + head_size, inner + 2 * head_size, wide + inner]
    owned_query, owned_key, owned_value, owned_out = (
        owned[:own_model, columns[i] : columns[i + 1]] for i in range(4)
    )

    def owned_gain(row, size):
        return lax.dynamic_slice_in_dim(owned[own_model + row], rank * size, size, 0)

    owned_gain_in, owned_gain_attn, owned_gain_ffn, owned_gain_out = (
        owned_gain(row, own_model) for row in (0, 2, 3, 4)
    )
    owned_gain_key, owned_gain_query = (owned_gain(row, own_head) for row in (1, 5))
    return (
        hidden_out,
        grad_in,
        owned_gain_in,
        owned_query,
        owned_key,
        owned_value,
        owned_out,
        owned_gain_attn,
        owned_gain_ffn,
        grad_gate_w,
        grad_up_w,
        grad_down,
        owned_gain_out,
        owned_gain_query,
        owned_gain_key,
    )


def solution(mesh):
    return jax.shard_map(
        per_device,
        mesh=mesh,
        in_specs=(
            P(("replica", "fsdp"), None),
            P(("replica", "fsdp"), None),
            P("replica"),
            P(("replica", "fsdp")),
            P("fsdp"),
            P("fsdp", None),
            P("fsdp", None),
            P("fsdp", None),
            P("fsdp", None),
            P("fsdp"),
            P("fsdp"),
            P("fsdp", None),
            P("fsdp", None),
            P("fsdp", None),
            P("fsdp"),
            P("fsdp"),
            P("fsdp"),
        ),
        out_specs=(
            P(("replica", "fsdp"), None),
            P(("replica", "fsdp"), None),
            P("fsdp"),
            P("fsdp", None),
            P("fsdp", None),
            P("fsdp", None),
            P("fsdp", None),
            P("fsdp"),
            P("fsdp"),
            P("fsdp", None),
            P("fsdp", None),
            P("fsdp", None),
            P("fsdp"),
            P("fsdp"),
            P("fsdp"),
        ),
        check_vma=False,
    )
```

```python
import jax
import jax.numpy as jnp
from jax import lax
from jax.experimental import pallas as pl
from jax.experimental.pallas import tpu as pltpu
from jax.sharding import PartitionSpec as P

WINDOW = 512


EPS = 1e-06
NEG = -1e30


def swapped(block, axis, mask):
    route = [(i, i ^ mask) for i in range(lax.axis_size(axis))]
    return lax.ppermute(block, axis, route)


def added(left, right):
    total = left.astype(jnp.float32) + right.astype(jnp.float32)
    return lax.optimization_barrier(total.astype(jnp.bfloat16))


def params(mebibytes=48):
    return pltpu.CompilerParams(vmem_limit_bytes=mebibytes * 1024 * 1024)


def dot(left, right, left_dim, right_dim):
    return lax.dot_general(
        left, right, (((left_dim,), (right_dim,)), ((), ())), preferred_element_type=jnp.float32
    )


def after(array, *others):
    place = pl.BlockSpec(memory_space=pl.ANY)
    return pl.pallas_call(
        lambda *refs: None,
        out_shape=jax.ShapeDtypeStruct(array.shape, array.dtype),
        in_specs=[place] * (1 + len(others)),
        out_specs=place,
        input_output_aliases={0: 0},
        compiler_params=params(1),
        name="after",
    )(array, *others)


def scalar(value):
    return value.astype(jnp.int32).reshape(1)


def packed(weights):
    half = weights[0].shape[0] // 2
    wide = sum(weight.shape[1] for weight in weights)

    def kernel(core_ref, *refs):
        out_ref = refs[-1]
        for side in range(2):

            @pl.when(core_ref[0] == side)
            def _():
                at = 0
                for ref in refs[:-1]:
                    out_ref[:, at : at + ref.shape[1]] = ref[side * half : (side + 1) * half, :]
                    at += ref.shape[1]

    return pl.pallas_call(
        kernel,
        grid_spec=pltpu.PrefetchScalarGridSpec(
            num_scalar_prefetch=1,
            grid=(1,),
            in_specs=[pl.BlockSpec(weight.shape, lambda i, core_ref: (0, 0)) for weight in weights],
            out_specs=pl.BlockSpec((half, wide), lambda i, core_ref: (0, 0)),
        ),
        out_shape=jax.ShapeDtypeStruct((half, wide), jnp.bfloat16),
        compiler_params=params(16),
        name="pack",
    )(scalar(lax.axis_index("replica") % 2), *weights)


def unpacked(weights, got, peers):
    rows = weights[0].shape[0]
    half = rows // 2
    group = len(got) + 1
    wide = sum(weight.shape[1] for weight in weights)
    own = len(weights)

    def kernel(core_ref, rank_ref, *refs):
        out_ref = refs[-1]
        mask = rank_ref[0] ^ pl.program_id(0)

        @pl.when(mask == 0)
        def _():
            at = 0
            for ref in refs[:own]:
                out_ref[:, at : at + ref.shape[1]] = ref[...]
                at += ref.shape[1]

        for other in range(1, group):
            for side in range(2):

                @pl.when((mask == other) & (core_ref[0] == side))
                def _():
                    out_ref[side * half : (side + 1) * half, :] = refs[own + other - 1][:half, :]
                    out_ref[(1 - side) * half : (2 - side) * half, :] = refs[own + group - 2 + other][:half, :]

    arrays = list(weights) + list(got) + list(peers)
    return pl.pallas_call(
        kernel,
        grid_spec=pltpu.PrefetchScalarGridSpec(
            num_scalar_prefetch=2,
            grid=(group,),
            in_specs=[pl.BlockSpec(array.shape, lambda i, *refs: (0, 0)) for array in arrays],
            out_specs=pl.BlockSpec((rows, wide), lambda i, *refs: (i, 0)),
        ),
        out_shape=jax.ShapeDtypeStruct((group * rows, wide), jnp.bfloat16),
        compiler_params=params(24),
        name="unpack",
    )(scalar(lax.axis_index("replica") % 2), scalar(lax.axis_index("fsdp")), *arrays)


GELU_A = (2.0 / 3.141592653589793) ** 0.5
GELU_B = 0.044715


def ffn_forward(x, gate_weight, up_weight, down_weight):
    gate = contract(gate_weight, x, 1, 1)
    upper = contract(up_weight, x, 1, 1)
    square = gate * gate
    bend = jnp.tanh(GELU_A * gate * (1.0 + GELU_B * square))
    half = 0.5 + 0.5 * bend
    act = gate * half
    slope = half + 0.5 * gate * (1.0 - bend * bend) * (GELU_A * (1.0 + 3.0 * GELU_B * square))
    hidden = (act * upper).astype(jnp.bfloat16)
    part = contract(hidden, down_weight, 0, 0).astype(jnp.bfloat16)
    return hidden, (slope * upper).astype(jnp.bfloat16), act.astype(jnp.bfloat16), part


def ffn_backward(grad, gate_weight, up_weight, down_weight, slope, act):
    grad_hidden = contract(down_weight, grad, 1, 1)
    grad_gate = (grad_hidden * slope.astype(jnp.float32)).astype(jnp.bfloat16)
    grad_upper = (grad_hidden * act.astype(jnp.float32)).astype(jnp.bfloat16)
    part = contract(grad_gate, gate_weight, 0, 0) + contract(grad_upper, up_weight, 0, 0)
    return grad_gate, grad_upper, part.astype(jnp.bfloat16)


def tile_of(size, most):
    return max(tile for tile in range(16, most + 1, 16) if size % tile == 0)


def ffn_backward_blocks(grads, gate_weight, up_weight, down_weight, slopes, acts):
    count = len(grads)
    rows, model = grads[0].shape
    units = gate_weight.shape[0]
    tile = tile_of(units, 432)
    steps = units // tile

    def kernel(*refs):
        step = pl.program_id(0)
        grad_refs, refs = refs[:count], refs[count:]
        (gate_ref, up_ref, down_ref), refs = refs[:3], refs[3:]
        slope_refs, act_refs, refs = refs[:count], refs[count : 2 * count], refs[2 * count :]
        gate_outs, up_outs, part_outs, (grad_ref, acc) = (
            refs[:count],
            refs[count : 2 * count],
            refs[2 * count : 3 * count],
            refs[3 * count :],
        )

        @pl.when(step == 0)
        def _():
            for spot in range(count):
                grad_ref[spot * rows : (spot + 1) * rows, :] = grad_refs[spot][...]
            acc[...] = jnp.zeros_like(acc)

        grad_hidden = dot(down_ref[...], grad_ref[...], 1, 1)
        slope = jnp.concatenate([ref[...] for ref in slope_refs], axis=1).astype(jnp.float32)
        act = jnp.concatenate([ref[...] for ref in act_refs], axis=1).astype(jnp.float32)
        grad_gate = (grad_hidden * slope).astype(jnp.bfloat16)
        grad_upper = (grad_hidden * act).astype(jnp.bfloat16)
        for spot in range(count):
            gate_outs[spot][...] = grad_gate[:, spot * rows : (spot + 1) * rows]
            up_outs[spot][...] = grad_upper[:, spot * rows : (spot + 1) * rows]
        acc[...] += dot(grad_gate, gate_ref[...], 0, 0) + dot(grad_upper, up_ref[...], 0, 0)

        @pl.when(step == steps - 1)
        def _():
            for spot in range(count):
                part_outs[spot][...] = acc[spot * rows : (spot + 1) * rows, :].astype(jnp.bfloat16)

    weight = pl.BlockSpec((tile, model), lambda i: (i, 0))
    flat = pl.BlockSpec((tile, rows), lambda i: (i, 0))
    whole = pl.BlockSpec((rows, model), lambda i: (0, 0))
    kept = jax.ShapeDtypeStruct((units, rows), jnp.bfloat16)
    outs = pl.pallas_call(
        kernel,
        grid=(steps,),
        out_shape=[kept] * (2 * count) + [jax.ShapeDtypeStruct((rows, model), jnp.bfloat16)] * count,
        in_specs=[whole] * count + [weight] * 3 + [flat] * (2 * count),
        out_specs=[flat] * (2 * count) + [whole] * count,
        scratch_shapes=[
            pltpu.VMEM((count * rows, model), jnp.bfloat16),
            pltpu.VMEM((count * rows, model), jnp.float32),
        ],
        compiler_params=params(),
        name="ffn_backward",
    )(*grads, gate_weight, up_weight, down_weight, *slopes, *acts)
    return outs[:count], outs[count : 2 * count], outs[2 * count :]


def norm_pull(value, gain, grad):
    scale = lax.rsqrt(jnp.mean(value * value, axis=-1, keepdims=True) + EPS)
    unit = value * scale
    inner = grad * gain
    return scale * (inner - unit * jnp.mean(inner * unit, axis=-1, keepdims=True)), grad * unit


def resid_backward(parts, resid, attended, out_grad, gain_ffn, gain_attn, w_out):
    count = len(parts)
    rows, model = resid.shape
    tile = min(rows, 128)

    def kernel(*refs):
        part_refs, refs = refs[:count], refs[count:]
        resid_ref, attended_ref, out_ref, ffn_ref, attn_ref, weight_ref, refs = *refs[:6], refs[6:]
        grad_resid_ref, grad_attended_ref, grad_mixed_ref, ffn_grad_ref, attn_grad_ref = refs
        grad = sum(ref[...].astype(jnp.float32) for ref in part_refs)
        pulled, ffn_rows = norm_pull(resid_ref[...], ffn_ref[...].astype(jnp.float32), grad)
        grad_resid = out_ref[...].astype(jnp.float32) + pulled
        grad_resid_ref[...] = grad_resid
        pulled, attn_rows = norm_pull(attended_ref[...], attn_ref[...].astype(jnp.float32), grad_resid)
        grad_attended = pulled.astype(jnp.bfloat16)
        grad_attended_ref[...] = grad_attended
        grad_mixed_ref[...] = dot(grad_attended, weight_ref[...], 1, 0).astype(jnp.bfloat16)
        ffn_grad = jnp.sum(ffn_rows, axis=0, keepdims=True)
        attn_grad = jnp.sum(attn_rows, axis=0, keepdims=True)

        @pl.when(pl.program_id(0) == 0)
        def _():
            ffn_grad_ref[...] = ffn_grad
            attn_grad_ref[...] = attn_grad

        @pl.when(pl.program_id(0) > 0)
        def _():
            ffn_grad_ref[...] += ffn_grad
            attn_grad_ref[...] += attn_grad

    block = pl.BlockSpec((tile, model), lambda i: (i, 0))
    vector = pl.BlockSpec((1, model), lambda i: (0, 0))
    inner = w_out.shape[1]
    return pl.pallas_call(
        kernel,
        grid=(rows // tile,),
        in_specs=[block] * (count + 3) + [vector] * 2 + [pl.BlockSpec(w_out.shape, lambda i: (0, 0))],
        out_specs=[block, block, pl.BlockSpec((tile, inner), lambda i: (i, 0)), vector, vector],
        out_shape=[
            jax.ShapeDtypeStruct((rows, model), jnp.float32),
            jax.ShapeDtypeStruct((rows, model), jnp.bfloat16),
            jax.ShapeDtypeStruct((rows, inner), jnp.bfloat16),
            jax.ShapeDtypeStruct((1, model), jnp.float32),
            jax.ShapeDtypeStruct((1, model), jnp.float32),
        ],
        compiler_params=params(32),
        name="resid_backward",
    )(*parts, resid, attended, out_grad, gain_ffn[None, :], gain_attn[None, :], w_out)


def input_backward(
    own_pair, backs, qkv, cosine, sine, gain_key, normed_in, grad_query, w_qkv, hidden_in, gain_in, grad_resid,
    grad_attended, mixed, gain_grads, group,
):
    rows, model = hidden_in.shape
    size = own_pair.shape[1] // 2
    inner = grad_query.shape[1]
    own_rows = model // group
    half = inner + size
    hops = len(backs)
    count = len(gain_grads)

    def kernel(core_ref, *refs):
        pair_ref, refs = refs[0], refs[1:]
        back_refs, refs = refs[:hops], refs[hops:]
        (
            raw_ref, cos_ref, sin_ref, key_gain_ref, normed_ref, query_ref, weight_ref, x_ref, gain_ref, resid_ref,
            attended_ref, mixed_ref, refs,
        ) = *refs[:12], refs[12:]
        gain_refs, refs = refs[:count], refs[count:]
        other_ref, mine_ref, grad_in_ref, rows_ref = refs
        pair = pair_ref[...] + sum(ref[...].astype(jnp.float32) for ref in back_refs)
        first = pair[:, : size // 2]
        second = pair[:, size // 2 : size]
        turned = jnp.concatenate(
            [
                first * cos_ref[...] + second * sin_ref[...],
                second * cos_ref[...] - first * sin_ref[...],
            ],
            axis=-1,
        )
        pulled, key_rows = norm_pull(raw_ref[...], key_gain_ref[...].astype(jnp.float32), turned)
        grad_key = pulled.astype(jnp.bfloat16)
        grad_value = pair[:, size:].astype(jnp.bfloat16)
        grad_normed = (
            dot(query_ref[...], weight_ref[:, :inner], 1, 1)
            + dot(grad_key, weight_ref[:, inner:half], 1, 1)
            + dot(grad_value, weight_ref[:, half:], 1, 1)
        )
        pulled, in_rows = norm_pull(
            x_ref[...].astype(jnp.float32), gain_ref[...].astype(jnp.float32), grad_normed
        )
        grad_in_ref[...] = resid_ref[...] + pulled
        rows_ref[...] = jnp.zeros_like(rows_ref)
        rows_ref[0:1, :model] = jnp.sum(in_rows, axis=0, keepdims=True)
        rows_ref[1:2, :size] = jnp.sum(key_rows, axis=0, keepdims=True)
        for spot in range(count):
            rows_ref[2 + spot : 3 + spot, : gain_refs[spot].shape[1]] = gain_refs[spot][...].astype(
                jnp.float32
            )
        gains = rows_ref[...].astype(jnp.bfloat16)

        def write(ref, side):
            pieces = (
                [(normed_ref, query_ref[...], 0, inner), (normed_ref, grad_key, inner, half)]
                if side == 0
                else [(normed_ref, grad_value, 0, size), (attended_ref, mixed_ref[...], size, half)]
            )
            for left, right, begin, end in pieces:
                value = dot(left[...], right, 0, 0).astype(jnp.bfloat16)
                for owner in range(group):
                    ref[owner, :own_rows, begin:end] = value[owner * own_rows : (owner + 1) * own_rows]
            for owner in range(group):
                ref[owner, own_rows:, :] = gains

        for core in range(2):

            @pl.when(core_ref[0] == core)
            def _():
                write(other_ref, 1 - core)
                write(mine_ref, core)

    def whole(array):
        return pl.BlockSpec(array.shape, lambda i, core_ref: (0,) * len(array.shape))

    arrays = [
        own_pair, *backs, qkv, cosine, sine, gain_key[None, :], normed_in, grad_query, w_qkv, hidden_in,
        gain_in[None, :], grad_resid, grad_attended, mixed, *gain_grads,
    ]
    in_specs = [whole(array) for array in arrays]
    in_specs[1 + hops] = pl.BlockSpec((rows, size), lambda i, core_ref: (0, inner // size))
    shape = jax.ShapeDtypeStruct((group, own_rows + 16, half), jnp.bfloat16)
    grad_in = jax.ShapeDtypeStruct((rows, model), jnp.float32)
    return pl.pallas_call(
        kernel,
        grid_spec=pltpu.PrefetchScalarGridSpec(
            num_scalar_prefetch=1,
            grid=(1,),
            in_specs=in_specs,
            out_specs=[whole(shape), whole(shape), whole(grad_in)],
            scratch_shapes=[pltpu.VMEM((16, half), jnp.float32)],
        ),
        out_shape=[shape, shape, grad_in],
        compiler_params=params(),
        name="input_backward",
    )(scalar(lax.axis_index("replica") % 2), *arrays)


def owner_parts(other, mine):
    group, height, wide = mine.shape
    far = swapped(other, "replica", 1)

    def kernel(rank_ref, mine_ref, far_ref, *outs):
        total = mine_ref[...].astype(jnp.float32) + far_ref[...].astype(jnp.float32)
        for mask in range(group):

            @pl.when(pl.program_id(0) == mask)
            def _():
                outs[mask][...] = total.astype(jnp.bfloat16)

    block = pl.BlockSpec((None, height, wide), lambda i, rank_ref: (rank_ref[0] ^ i, 0, 0))
    parts = pl.pallas_call(
        kernel,
        grid_spec=pltpu.PrefetchScalarGridSpec(
            num_scalar_prefetch=1,
            grid=(group,),
            in_specs=[block, block],
            out_specs=[pl.BlockSpec((height, wide), lambda i, rank_ref: (0, 0))] * group,
        ),
        out_shape=[jax.ShapeDtypeStruct((height, wide), jnp.bfloat16)] * group,
        compiler_params=params(16),
        name="owner_parts",
    )(scalar(lax.axis_index("fsdp")), mine, far)
    return [parts[0]] + [swapped(parts[mask], "fsdp", mask) for mask in range(1, group)]


def chunks_of(units):
    return 2 if units % 64 == 0 else 1


def weight_grad(sets, rights):
    group = len(rights)
    count = len(sets)
    units, rows = sets[0][0].shape
    model = rights[0].shape[1]
    chunks = chunks_of(units)
    tile = units // (2 * chunks)

    def kernel(core_ref, *refs):
        right_refs, left_refs = refs[:group], refs[group:-4]
        other_ref, mine_ref, left_ref, right_ref = refs[-4:]

        @pl.when((pl.program_id(0) == 0) & (pl.program_id(1) == 0))
        def _():
            for spot in range(group):
                right_ref[spot * rows : (spot + 1) * rows, :] = right_refs[spot][...]

        for index in range(count):

            @pl.when(pl.program_id(1) == index)
            def _():
                for chunk in range(chunks):
                    for spot in range(group):
                        left_ref[
                            chunk * tile : (chunk + 1) * tile, spot * rows : (spot + 1) * rows
                        ] = left_refs[(index * chunks + chunk) * group + spot][...]

        value = dot(left_ref[...], right_ref[...], 1, 0).astype(jnp.bfloat16)

        @pl.when(pl.program_id(0) == 0)
        def _():
            for chunk in range(chunks):
                other_ref[chunk] = value[chunk * tile : (chunk + 1) * tile]

        @pl.when(pl.program_id(0) == 1)
        def _():
            for chunk in range(chunks):
                mine_ref[chunk] = value[chunk * tile : (chunk + 1) * tile]

    def left_spec(chunk):
        def index(side, spot, core_ref):
            return (2 * chunk + jnp.where(side == 0, 1 - core_ref[0], core_ref[0]), 0)

        return pl.BlockSpec((tile, rows), index)

    shape = jax.ShapeDtypeStruct((count * chunks, tile, model), jnp.bfloat16)
    block = (chunks, tile, model)
    return pl.pallas_call(
        kernel,
        grid_spec=pltpu.PrefetchScalarGridSpec(
            num_scalar_prefetch=1,
            grid=(2, count),
            in_specs=[pl.BlockSpec((rows, model), lambda side, spot, core_ref: (0, 0))] * group
            + [left_spec(chunk) for _ in range(count) for chunk in range(chunks) for _ in range(group)],
            out_specs=[
                pl.BlockSpec(
                    block, lambda side, spot, core_ref: (jnp.where(side == 0, spot, count - 1), 0, 0)
                ),
                pl.BlockSpec(block, lambda side, spot, core_ref: (jnp.where(side == 0, 0, spot), 0, 0)),
            ],
            scratch_shapes=[
                pltpu.VMEM((chunks * tile, group * rows), jnp.bfloat16),
                pltpu.VMEM((group * rows, model), jnp.bfloat16),
            ],
        ),
        out_shape=[shape, shape],
        compiler_params=params(),
        name="weight_grad",
    )(
        scalar(lax.axis_index("replica") % 2),
        *rights,
        *[left for lefts in sets for _ in range(chunks) for left in lefts],
    )


def allowed_mask(query_segs_ref, key_segs_ref, rows, width):
    gap = (
        width
        - rows
        + lax.broadcasted_iota(jnp.int32, (rows, width), 0)
        - lax.broadcasted_iota(jnp.int32, (rows, width), 1)
    )
    return (gap >= 0) & (gap < WINDOW) & (query_segs_ref[...] == key_segs_ref[...])


def head_probs(query, keys, allowed, scale):
    scores = jnp.where(allowed, dot(query, keys, 1, 1) * scale, NEG)
    expo = jnp.exp(scores - jnp.max(scores, axis=-1, keepdims=True))
    return expo / jnp.sum(expo, axis=-1, keepdims=True)


def attention_specs(rows, size, width, heads):
    head = pl.BlockSpec((rows, size), lambda h: (0, h))
    whole = lambda *shape: pl.BlockSpec(shape, lambda h: (0, 0))
    common = [
        head,
        whole(1, size),
        whole(rows, size // 2),
        whole(rows, size // 2),
        whole(width, 2 * size),
        whole(rows, 1),
        whole(1, width),
    ]
    return head, whole, common


def attention_forward(qkv, gain, cosine, sine, pairs, query_segs, key_segs, heads):
    rows, width, size = qkv.shape[0], pairs.shape[0], pairs.shape[1] // 2
    head, _, common = attention_specs(rows, size, width, heads)

    def kernel(raw_ref, gain_ref, cos_ref, sin_ref, pairs_ref, qseg_ref, kseg_ref, query_ref, mixed_ref):
        query = head_post(raw_ref[...], gain_ref[...], cos_ref[...], sin_ref[...]).astype(jnp.bfloat16)
        query_ref[...] = query
        allowed = allowed_mask(qseg_ref, kseg_ref, rows, width)
        probs = head_probs(query, pairs_ref[:, :size], allowed, size**-0.5).astype(jnp.bfloat16)
        mixed_ref[...] = dot(probs, pairs_ref[:, size:], 1, 0).astype(jnp.bfloat16)

    shape = jax.ShapeDtypeStruct((rows, heads * size), jnp.bfloat16)
    return pl.pallas_call(
        kernel,
        grid=(heads,),
        in_specs=common,
        out_specs=[head, head],
        out_shape=[shape, shape],
        compiler_params=params(32),
        name="attention_forward",
    )(qkv, gain, cosine, sine, pairs, query_segs, key_segs)


def attention_backward(qkv, gain, cosine, sine, pairs, query_segs, key_segs, query, grad_mixed, heads):
    rows, width, size = qkv.shape[0], pairs.shape[0], pairs.shape[1] // 2
    head, whole, common = attention_specs(rows, size, width, heads)
    before = width - rows

    def kernel(
        raw_ref, gain_ref, cos_ref, sin_ref, pairs_ref, qseg_ref, kseg_ref, query_ref, grad_ref,
        raw_grad_ref, gain_grad_ref, far_ref, own_ref, acc,
    ):
        step = pl.program_id(0)
        query = query_ref[...]
        grad = grad_ref[...]
        allowed = allowed_mask(qseg_ref, kseg_ref, rows, width)
        keys = pairs_ref[:, :size]
        probs = head_probs(query, keys, allowed, size**-0.5)
        grad_probs = dot(grad, pairs_ref[:, size:], 1, 1)
        delta = jnp.sum(grad_probs * probs, axis=-1, keepdims=True)
        grad_scores = (probs * (grad_probs - delta)).astype(jnp.bfloat16)
        grad_query = dot(grad_scores, keys, 1, 0) * size**-0.5
        grad_keys = dot(grad_scores, query, 0, 0) * size**-0.5
        grad_values = dot(probs.astype(jnp.bfloat16), grad, 0, 0)

        @pl.when(step == 0)
        def _():
            acc[:, :size] = grad_keys
            acc[:, size:] = grad_values

        @pl.when(step > 0)
        def _():
            acc[:, :size] += grad_keys
            acc[:, size:] += grad_values

        first = grad_query[:, : size // 2]
        second = grad_query[:, size // 2 :]
        cosine_part, sine_part = cos_ref[...], sin_ref[...]
        turned = jnp.concatenate(
            [
                first * cosine_part + second * sine_part,
                second * cosine_part - first * sine_part,
            ],
            axis=-1,
        )
        raw = raw_ref[...]
        scale = lax.rsqrt(jnp.mean(raw * raw, axis=-1, keepdims=True) + EPS)
        unit = raw * scale
        inner = turned * gain_ref[...].astype(jnp.float32)
        raw_grad = scale * (inner - unit * jnp.mean(inner * unit, axis=-1, keepdims=True))
        raw_grad_ref[...] = raw_grad.astype(jnp.bfloat16)
        gain_grad = jnp.sum(turned * unit, axis=0, keepdims=True)

        @pl.when(step == 0)
        def _():
            gain_grad_ref[...] = gain_grad

        @pl.when(step > 0)
        def _():
            gain_grad_ref[...] += gain_grad

        @pl.when(step == heads - 1)
        def _():
            far_ref[...] = acc[:before, :].astype(jnp.bfloat16)
            own_ref[...] = acc[before:, :]

    return pl.pallas_call(
        kernel,
        grid=(heads,),
        in_specs=common + [head, head],
        out_specs=[head, whole(1, size), whole(before, 2 * size), whole(rows, 2 * size)],
        out_shape=[
            jax.ShapeDtypeStruct((rows, heads * size), jnp.bfloat16),
            jax.ShapeDtypeStruct((1, size), jnp.float32),
            jax.ShapeDtypeStruct((before, 2 * size), jnp.bfloat16),
            jax.ShapeDtypeStruct((rows, 2 * size), jnp.float32),
        ],
        scratch_shapes=[pltpu.VMEM((width, 2 * size), jnp.float32)],
        compiler_params=params(32),
        name="attention_backward",
    )(qkv, gain, cosine, sine, pairs, query_segs, key_segs, query, grad_mixed)


def line_edges():
    places = lax.axis_size("replica") // 2
    outer = places // 2 - 1
    return places, outer


def exchanged(block, pairs):
    route = [(2 * a + core, 2 * b + core) for a, b in pairs for core in range(2)]
    return lax.ppermute(block, "replica", route)


class Line:
    def __init__(self):
        self.places, self.outer = line_edges()
        self.steps = 2 * self.outer + 1
        self.moving = []
        self.done = {}

    def advance(self, fresh, gate=None):
        places, outer, steps = self.places, self.outer, self.steps
        place = (lax.axis_index("replica") // 2).astype(jnp.int32).reshape(1)
        operands, plan = [], []

        def operand(entry):
            array, index = entry if isinstance(entry, tuple) else (entry, None)
            for spot, (known, known_index) in enumerate(operands):
                if known is array and known_index == index:
                    return spot
            operands.append((array, index))
            return len(operands) - 1

        for name, block, step, far in self.moving:
            plan.append((name, step + 1, [operand(block), operand(far)], step))
        for name, terms in fresh:
            plan.append((name, 0, [operand(term) for term in terms], None))
        if not plan:
            return gate
        sizes = [operands[spots[0]][0].shape[-2:] for _, _, spots, _ in plan]
        by_step = {step: index for index, (_, step, _, _) in enumerate(plan)}
        pairs = []
        for edge in range(outer):
            inward, outward = by_step.get(edge), by_step.get(2 * outer - edge)
            if inward is not None and outward is not None and sizes[inward] == sizes[outward]:
                pairs.append((edge, inward, outward))
        cuts = 3 if all(size[0] % 48 == 0 for size in sizes) else 1

        def kernel(place_ref, *refs):
            here = place_ref[0]
            inputs = refs[: len(operands)]
            if gate is not None:
                refs = refs[: len(operands)] + refs[len(operands) + 1 :]
            outputs = refs[len(operands) :]
            states = []
            for spot, (_, _, terms, last) in enumerate(plan):
                value = inputs[terms[0]][...]
                if len(terms) > 1:
                    far = inputs[terms[1]][...]
                    total = value.astype(jnp.float32)
                    for term in terms[1:]:
                        total = total + inputs[term][...].astype(jnp.float32)
                    total = total.astype(jnp.bfloat16)
                    if last is None:
                        value = total
                    elif last <= outer:
                        edge = last
                        value = jnp.where((here == edge + 1) | (here == places - 2 - edge), total, value)
                    else:
                        edge = 2 * outer - last
                        value = jnp.where((here == edge) | (here == places - 1 - edge), far, value)
                states.append(value)
                outputs[spot][...] = value
            for spot, (edge, inward, outward) in enumerate(pairs):
                outputs[len(plan) + spot][...] = jnp.where(
                    (here == edge) | (here == places - 1 - edge), states[inward], states[outward]
                )

        def spec(size, index):
            if index is None:
                return pl.BlockSpec((size[0] // cuts, size[1]), lambda i, place_ref: (i, 0))
            return pl.BlockSpec((None, size[0] // cuts, size[1]), lambda i, place_ref: (index, i, 0))

        in_specs = [spec(array.shape[-2:], index) for array, index in operands]
        arrays = [array for array, _ in operands]
        out_sizes = sizes + [sizes[inward] for _, inward, _ in pairs]
        out_specs = [spec(size, None) for size in out_sizes]
        out_shape = [jax.ShapeDtypeStruct(size, jnp.bfloat16) for size in out_sizes]
        aliases = {}
        if gate is not None:
            aliases = {1 + len(arrays): len(out_shape)}
            in_specs.append(pl.BlockSpec(memory_space=pl.ANY))
            out_specs.append(pl.BlockSpec(memory_space=pl.ANY))
            out_shape.append(jax.ShapeDtypeStruct(gate.shape, gate.dtype))
            arrays.append(gate)
        outs = pl.pallas_call(
            kernel,
            grid_spec=pltpu.PrefetchScalarGridSpec(
                num_scalar_prefetch=1, grid=(cuts,), in_specs=in_specs, out_specs=out_specs
            ),
            out_shape=out_shape,
            input_output_aliases=aliases,
            compiler_params=params(32),
            name="line_step",
        )(place, *arrays)
        received = {}
        for spot, (edge, inward, outward) in enumerate(pairs):
            ends = [(edge, edge + 1), (places - 1 - edge, places - 2 - edge)]
            far = exchanged(outs[len(plan) + spot], ends + [(b, a) for a, b in ends])
            received[inward] = received[outward] = far
        self.moving = []
        for index, (name, step, _, _) in enumerate(plan):
            block = outs[index]
            if step == steps:
                self.done[name] = block
                continue
            if index not in received:
                edge = step if step <= outer else 2 * outer - step
                route = [(edge, edge + 1), (places - 1 - edge, places - 2 - edge)]
                if step > outer:
                    route = [(b, a) for a, b in route]
                received[index] = exchanged(block, route)
            self.moving.append((name, block, step, received[index]))
        return outs[-1]

    def arrived(self):
        return [far for _, _, _, far in self.moving]

    def finished(self, name):
        while name not in self.done:
            self.advance([])
        return self.done[name]


def line_names(name, units):
    return [(name, chunk) for chunk in range(chunks_of(units))]


def whole_grad(line, name, units, dtype=jnp.float32):
    names = line_names(name, units)
    mines = [line.finished(chunk) for chunk in names]
    others = [swapped(mine, "replica", 1) for mine in mines]
    chunks = len(mines)
    tile, model = mines[0].shape
    core = (lax.axis_index("replica") % 2).astype(jnp.int32).reshape(1)

    def kernel(core_ref, *refs):
        out_ref = refs[-1]
        for chunk in range(chunks):
            for side in range(2):

                @pl.when((pl.program_id(0) == chunk) & (pl.program_id(1) == side))
                def _():
                    @pl.when(core_ref[0] == side)
                    def _():
                        out_ref[...] = refs[chunk][...].astype(dtype)

                    @pl.when(core_ref[0] != side)
                    def _():
                        out_ref[...] = refs[chunks + chunk][...].astype(dtype)

    return pl.pallas_call(
        kernel,
        grid_spec=pltpu.PrefetchScalarGridSpec(
            num_scalar_prefetch=1,
            grid=(chunks, 2),
            in_specs=[pl.BlockSpec((tile, model), lambda chunk, side, core_ref: (0, 0))] * (2 * chunks),
            out_specs=pl.BlockSpec((tile, model), lambda chunk, side, core_ref: (2 * chunk + side, 0)),
        ),
        out_shape=jax.ShapeDtypeStruct((units, model), dtype),
        compiler_params=params(24),
        name="whole_grad",
    )(core, *mines, *others)


def joined(mine, other, axis):
    core = lax.axis_index("replica") % 2
    return jnp.where(
        core == 0,
        jnp.concatenate([mine, other], axis=axis),
        jnp.concatenate([other, mine], axis=axis),
    )


def core_join(block, axis):
    return joined(block, swapped(block, "replica", 1), axis)


def fetched(block):
    got = [swapped(block, "fsdp", mask) for mask in range(1, lax.axis_size("fsdp"))]
    return got, [swapped(part, "replica", 1) for part in got]


def gathered(block):
    group = lax.axis_size("fsdp")
    blocks, near = [block] + [None] * (group - 1), []
    for ring in range(1, group.bit_length()):
        masks = [mask for mask in range(1, group) if bin(mask).count("1") == ring]
        source = after(block, *near) if near else block
        near = [swapped(source, "fsdp", mask) for mask in masks]
        for mask, far in zip(masks, near):
            blocks[mask] = far
    return blocks


def passed_along(block, axis, distance):
    devices = range(lax.axis_size(axis))
    route = [(i - distance, i) for i in devices if i - distance in devices]
    return lax.ppermute(block, axis, route)


def contract(left, right, left_dim, right_dim):
    return lax.dot_general(
        left, right, (((left_dim,), (right_dim,)), ((), ())), preferred_element_type=jnp.float32
    )


def normed(value, gain):
    return value * lax.rsqrt(jnp.mean(value * value, axis=-1, keepdims=True) + EPS) * gain


def norm_back(value, gain, grad):
    _, pull = jax.vjp(normed, value, gain)
    return pull(grad)


def tables(places, half):
    freq = 10000.0 ** (-(2.0 * jnp.arange(half, dtype=jnp.float32)) / (2 * half))
    angle = places.astype(jnp.float32)[:, None] * freq[None, :]
    return (jnp.cos(angle), jnp.sin(angle))


def rotate(value, cosine, sine):
    half = value.shape[-1] // 2
    first = value[..., :half]
    second = value[..., half:]
    return jnp.concatenate(
        [first * cosine - second * sine, second * cosine + first * sine], axis=-1
    )


def head_post(raw, gain, cosine, sine):
    return rotate(normed(raw, gain), cosine, sine)


def per_device(
    hidden_in,
    out_grad,
    segments,
    positions,
    norm_in,
    query_weight,
    key_weight,
    value_weight,
    out_weight,
    norm_attn,
    norm_ffn,
    gate_weight,
    up_weight,
    down_weight,
    norm_out,
    query_gain,
    key_gain,
):
    rows = hidden_in.shape[0]
    rank = lax.axis_index("fsdp")
    group = lax.axis_size("fsdp")
    masks = range(1, group)
    head_size = key_weight.shape[1]
    heads = query_weight.shape[1] // head_size
    model = hidden_in.shape[1]
    own_model = norm_in.shape[0]
    own_head = query_gain.shape[0]
    hops = (WINDOW - 1) // rows + 1
    scale = head_size ** (-0.5)
    qkv_weights = (query_weight, key_weight, value_weight)
    wide = sum(weight.shape[1] for weight in qkv_weights)
    qkv_block = packed(qkv_weights)
    got, peers = fetched(qkv_block)
    gains = jnp.stack(
        [
            jnp.pad(gain, (0, own_model - gain.shape[0]))
            for gain in (norm_in, norm_attn, norm_ffn, norm_out, query_gain, key_gain)
        ]
    )
    gains = after(gains, *[got[mask - 1] for mask in masks if bin(mask).count("1") == 1])
    gain_stack = jnp.stack([gains] + [swapped(gains, "fsdp", mask) for mask in masks])
    w_qkv = unpacked(qkv_weights, got, peers)
    gain_rows = jnp.stack(
        [lax.dynamic_index_in_dim(gain_stack, rank ^ i, 0, keepdims=False) for i in range(group)], axis=1
    )
    gain_in, gain_attn, gain_ffn, gain_out = (gain_rows[i].reshape(-1) for i in range(4))
    gain_query, gain_key = (gain_rows[i, :, :own_head].reshape(-1) for i in (4, 5))
    residual_in = hidden_in.astype(jnp.float32)
    normed_in = normed(residual_in, gain_in).astype(jnp.bfloat16)
    qkv = jnp.dot(normed_in, w_qkv, preferred_element_type=jnp.float32)
    key_raw = qkv[:, heads * head_size : (heads + 1) * head_size]
    value_new = qkv[:, (heads + 1) * head_size :].astype(jnp.bfloat16)
    cosine, sine = tables(positions, head_size // 2)
    key_new = head_post(key_raw, gain_key, cosine, sine).astype(jnp.bfloat16)
    pair_new = jnp.concatenate([key_new, value_new], axis=1)
    got, peers = fetched(after(packed([out_weight]), pair_new))
    w_out = unpacked([out_weight], got, peers)
    parts = [pair_new]
    for step in range(1, hops + 1):
        parts.insert(0, passed_along(pair_new, "fsdp", step))
    pairs = jnp.concatenate(parts, axis=0)
    width = pairs.shape[0]
    seg_padded = jnp.concatenate([jnp.full((hops * rows,), -1, jnp.int32), segments], axis=0)
    key_segs = lax.dynamic_slice_in_dim(seg_padded, rank * rows, width, 0)
    query_segs = lax.dynamic_slice_in_dim(segments, rank * rows, rows, 0)
    attention_args = (
        qkv,
        gain_query[None, :],
        cosine,
        sine,
        pairs,
        query_segs[:, None],
        key_segs[None, :],
    )
    query_new, mixed = attention_forward(*attention_args, heads)
    attended = contract(mixed, w_out, 1, 1)
    resid = residual_in + normed(attended, gain_attn)
    ffn_in = normed(resid, gain_ffn).astype(jnp.bfloat16)
    ffn_blocks = gathered(ffn_in)
    hiddens, slopes, acts, parts = {}, {}, {}, {}
    rings = sorted(range(group), key=lambda mask: (bin(mask).count("1"), mask))
    last = None
    for mask in rings[1:] + [0]:
        if last is not None:
            ffn_blocks[mask] = after(ffn_blocks[mask], parts[last])
        hiddens[mask], slopes[mask], acts[mask], parts[mask] = ffn_forward(
            ffn_blocks[mask], gate_weight, up_weight, down_weight
        )
        last = mask
    branch = sum(
        (swapped(parts[mask], "fsdp", mask) if mask else parts[mask]).astype(jnp.float32)
        for mask in range(group)
    )
    result = resid + normed(branch, gain_out)
    hidden_out = result.astype(jnp.bfloat16)
    grad_result = out_grad.astype(jnp.float32)
    grad_branch, grad_gain_out = norm_back(branch, gain_out, grad_result)
    grad_branch_low = grad_branch.astype(jnp.bfloat16)
    pieces = gathered(grad_branch_low)
    units = gate_weight.shape[0]
    line = Line()

    def fresh(names, other, mine):
        far = swapped(other, "replica", 1)
        keys = [key for name in names for key in line_names(name, units)]
        return [(key, [(mine, spot), (far, spot)]) for spot, key in enumerate(keys)]

    grad_gates, grad_uppers, returned = {}, {}, {}
    final = rings[-1]
    last = None
    for mask in rings[:-1]:
        if last is not None:
            pieces[mask] = after(pieces[mask], part)
        grad_gates[mask], grad_uppers[mask], part = ffn_backward(
            pieces[mask], gate_weight, up_weight, down_weight, slopes[mask], acts[mask]
        )
        returned[mask] = swapped(part, "fsdp", mask) if mask else part
        last = mask
    pieces[final] = after(pieces[final], part)
    waiting = fresh(
        ["down"], *weight_grad([[hiddens[i] for i in range(group)]], [pieces[i] for i in range(group)])
    )
    pieces[final] = line.advance([waiting.pop(0)], pieces[final])
    gate_parts, upper_parts, parts = ffn_backward_blocks(
        [pieces[final]], gate_weight, up_weight, down_weight, [slopes[final]], [acts[final]]
    )
    grad_gates[final], grad_uppers[final] = gate_parts[0], upper_parts[0]
    returned[final] = swapped(parts[0], "fsdp", final)
    other, mine = weight_grad([[grad_gates[i] for i in range(group)]], ffn_blocks)
    other = after(other, *[returned[mask] for mask in rings[1:-1]])
    gate_chunks = fresh(["gate"], other, mine)
    grad_uppers[0] = line.advance(
        [waiting.pop(0)] if waiting else [], after(grad_uppers[0], other)
    )
    other, mine = weight_grad([[grad_uppers[i] for i in range(group)]], ffn_blocks)
    waiting = gate_chunks + fresh(["up"], after(other, returned[final]), mine)

    def advance(gate=None):
        return line.advance([waiting.pop(0)] if waiting else [], gate)

    grad_resid, grad_attended_low, grad_mixed, grad_gain_ffn, grad_gain_attn = resid_backward(
        [returned[mask] for mask in range(group)], resid, attended, out_grad, gain_ffn, gain_attn, w_out
    )
    grad_mixed = advance(grad_mixed)
    grad_query_low, grad_gain_query, grad_far, grad_pair = attention_backward(
        *attention_args, query_new, grad_mixed, heads
    )
    backs = [
        passed_along(grad_far[(hops - step) * rows : (hops - step + 1) * rows], "fsdp", -step)
        for step in range(1, hops + 1)
    ]
    grad_pair = advance(grad_pair)
    other, mine, grad_in = input_backward(
        grad_pair,
        backs,
        qkv,
        cosine,
        sine,
        gain_key,
        normed_in,
        grad_query_low,
        w_qkv,
        hidden_in,
        gain_in,
        grad_resid,
        grad_attended_low,
        mixed,
        [grad_gain_attn, grad_gain_ffn, grad_gain_out[None, :], grad_gain_query],
        group,
    )
    other = advance(other)
    weight_parts = owner_parts(other, mine)
    near = [weight_parts[mask] for mask in masks if bin(mask).count("1") == 1]
    while waiting:
        weight_parts[0] = advance(after(weight_parts[0], *near))
    line.advance([("weights", weight_parts)])
    grad_down = whole_grad(line, "down", units)
    grad_down = line.advance([], grad_down)
    grad_gate_w = whole_grad(line, "gate", units)
    grad_gate_w = line.advance([], grad_gate_w)
    grad_up_w = whole_grad(line, "up", units)
    grad_up_w = line.advance([], grad_up_w)
    owned = core_join(line.finished("weights"), 1).astype(jnp.float32)
    inner = heads * head_size
    columns = [0, inner, inner + head_size, inner + 2 * head_size, wide + inner]
    owned_query, owned_key, owned_value, owned_out = (
        owned[:own_model, columns[i] : columns[i + 1]] for i in range(4)
    )

    def owned_gain(row, size):
        return lax.dynamic_slice_in_dim(owned[own_model + row], rank * size, size, 0)

    owned_gain_in, owned_gain_attn, owned_gain_ffn, owned_gain_out = (
        owned_gain(row, own_model) for row in (0, 2, 3, 4)
    )
    owned_gain_key, owned_gain_query = (owned_gain(row, own_head) for row in (1, 5))
    return (
        hidden_out,
        grad_in,
        owned_gain_in,
        owned_query,
        owned_key,
        owned_value,
        owned_out,
        owned_gain_attn,
        owned_gain_ffn,
        grad_gate_w,
        grad_up_w,
        grad_down,
        owned_gain_out,
        owned_gain_query,
        owned_gain_key,
    )


def solution(mesh):
    return jax.shard_map(
        per_device,
        mesh=mesh,
        in_specs=(
            P(("replica", "fsdp"), None),
            P(("replica", "fsdp"), None),
            P("replica"),
            P(("replica", "fsdp")),
            P("fsdp"),
            P("fsdp", None),
            P("fsdp", None),
            P("fsdp", None),
            P("fsdp", None),
            P("fsdp"),
            P("fsdp"),
            P("fsdp", None),
            P("fsdp", None),
            P("fsdp", None),
            P("fsdp"),
            P("fsdp"),
            P("fsdp"),
        ),
        out_specs=(
            P(("replica", "fsdp"), None),
            P(("replica", "fsdp"), None),
            P("fsdp"),
            P("fsdp", None),
            P("fsdp", None),
            P("fsdp", None),
            P("fsdp", None),
            P("fsdp"),
            P("fsdp"),
            P("fsdp", None),
            P("fsdp", None),
            P("fsdp", None),
            P("fsdp"),
            P("fsdp"),
            P("fsdp"),
        ),
        check_vma=False,
    )
```

```python
import jax
import jax.numpy as jnp
from jax import lax
from jax.experimental import pallas as pl
from jax.experimental.pallas import tpu as pltpu
from jax.sharding import PartitionSpec as P

WINDOW = 512


EPS = 1e-06
NEG = -1e30


def swapped(block, axis, mask):
    route = [(i, i ^ mask) for i in range(lax.axis_size(axis))]
    return lax.ppermute(block, axis, route)


def added(left, right):
    total = left.astype(jnp.float32) + right.astype(jnp.float32)
    return lax.optimization_barrier(total.astype(jnp.bfloat16))


def params(mebibytes=48):
    return pltpu.CompilerParams(vmem_limit_bytes=mebibytes * 1024 * 1024)


def dot(left, right, left_dim, right_dim):
    return lax.dot_general(
        left, right, (((left_dim,), (right_dim,)), ((), ())), preferred_element_type=jnp.float32
    )


def after(array, *others):
    place = pl.BlockSpec(memory_space=pl.ANY)
    return pl.pallas_call(
        lambda *refs: None,
        out_shape=jax.ShapeDtypeStruct(array.shape, array.dtype),
        in_specs=[place] * (1 + len(others)),
        out_specs=place,
        input_output_aliases={0: 0},
        compiler_params=params(1),
        name="after",
    )(array, *others)


def scalar(value):
    return value.astype(jnp.int32).reshape(1)


def packed(weights):
    half = weights[0].shape[0] // 2
    wide = sum(weight.shape[1] for weight in weights)

    def kernel(core_ref, *refs):
        out_ref = refs[-1]
        for side in range(2):

            @pl.when(core_ref[0] == side)
            def _():
                at = 0
                for ref in refs[:-1]:
                    out_ref[:, at : at + ref.shape[1]] = ref[side * half : (side + 1) * half, :]
                    at += ref.shape[1]

    return pl.pallas_call(
        kernel,
        grid_spec=pltpu.PrefetchScalarGridSpec(
            num_scalar_prefetch=1,
            grid=(1,),
            in_specs=[pl.BlockSpec(weight.shape, lambda i, core_ref: (0, 0)) for weight in weights],
            out_specs=pl.BlockSpec((half, wide), lambda i, core_ref: (0, 0)),
        ),
        out_shape=jax.ShapeDtypeStruct((half, wide), jnp.bfloat16),
        compiler_params=params(16),
        name="pack",
    )(scalar(lax.axis_index("replica") % 2), *weights)


def unpacked(weights, got, peers):
    rows = weights[0].shape[0]
    half = rows // 2
    group = len(got) + 1
    wide = sum(weight.shape[1] for weight in weights)
    own = len(weights)

    def kernel(core_ref, rank_ref, *refs):
        out_ref = refs[-1]
        mask = rank_ref[0] ^ pl.program_id(0)

        @pl.when(mask == 0)
        def _():
            at = 0
            for ref in refs[:own]:
                out_ref[:, at : at + ref.shape[1]] = ref[...]
                at += ref.shape[1]

        for other in range(1, group):
            for side in range(2):

                @pl.when((mask == other) & (core_ref[0] == side))
                def _():
                    out_ref[side * half : (side + 1) * half, :] = refs[own + other - 1][:half, :]
                    out_ref[(1 - side) * half : (2 - side) * half, :] = refs[own + group - 2 + other][:half, :]

    arrays = list(weights) + list(got) + list(peers)
    return pl.pallas_call(
        kernel,
        grid_spec=pltpu.PrefetchScalarGridSpec(
            num_scalar_prefetch=2,
            grid=(group,),
            in_specs=[pl.BlockSpec(array.shape, lambda i, *refs: (0, 0)) for array in arrays],
            out_specs=pl.BlockSpec((rows, wide), lambda i, *refs: (i, 0)),
        ),
        out_shape=jax.ShapeDtypeStruct((group * rows, wide), jnp.bfloat16),
        compiler_params=params(24),
        name="unpack",
    )(scalar(lax.axis_index("replica") % 2), scalar(lax.axis_index("fsdp")), *arrays)


GELU_A = (2.0 / 3.141592653589793) ** 0.5
GELU_B = 0.044715


def ffn_forward(x, gate_weight, up_weight, down_weight):
    gate = contract(gate_weight, x, 1, 1)
    upper = contract(up_weight, x, 1, 1)
    square = gate * gate
    bend = jnp.tanh(GELU_A * gate * (1.0 + GELU_B * square))
    half = 0.5 + 0.5 * bend
    act = gate * half
    slope = half + 0.5 * gate * (1.0 - bend * bend) * (GELU_A * (1.0 + 3.0 * GELU_B * square))
    hidden = (act * upper).astype(jnp.bfloat16)
    part = contract(hidden, down_weight, 0, 0).astype(jnp.bfloat16)
    return hidden, (slope * upper).astype(jnp.bfloat16), act.astype(jnp.bfloat16), part


def ffn_backward(grad, gate_weight, up_weight, down_weight, slope, act):
    grad_hidden = contract(down_weight, grad, 1, 1)
    grad_gate = (grad_hidden * slope.astype(jnp.float32)).astype(jnp.bfloat16)
    grad_upper = (grad_hidden * act.astype(jnp.float32)).astype(jnp.bfloat16)
    part = contract(grad_gate, gate_weight, 0, 0) + contract(grad_upper, up_weight, 0, 0)
    return grad_gate, grad_upper, part.astype(jnp.bfloat16)


def tile_of(size, most):
    return max(tile for tile in range(16, most + 1, 16) if size % tile == 0)


def ffn_backward_blocks(grads, gate_weight, up_weight, down_weight, slopes, acts):
    count = len(grads)
    rows, model = grads[0].shape
    units = gate_weight.shape[0]
    tile = tile_of(units, 432)
    steps = units // tile

    def kernel(*refs):
        step = pl.program_id(0)
        grad_refs, refs = refs[:count], refs[count:]
        (gate_ref, up_ref, down_ref), refs = refs[:3], refs[3:]
        slope_refs, act_refs, refs = refs[:count], refs[count : 2 * count], refs[2 * count :]
        gate_outs, up_outs, part_outs, (grad_ref, acc) = (
            refs[:count],
            refs[count : 2 * count],
            refs[2 * count : 3 * count],
            refs[3 * count :],
        )

        @pl.when(step == 0)
        def _():
            for spot in range(count):
                grad_ref[spot * rows : (spot + 1) * rows, :] = grad_refs[spot][...]
            acc[...] = jnp.zeros_like(acc)

        grad_hidden = dot(down_ref[...], grad_ref[...], 1, 1)
        slope = jnp.concatenate([ref[...] for ref in slope_refs], axis=1).astype(jnp.float32)
        act = jnp.concatenate([ref[...] for ref in act_refs], axis=1).astype(jnp.float32)
        grad_gate = (grad_hidden * slope).astype(jnp.bfloat16)
        grad_upper = (grad_hidden * act).astype(jnp.bfloat16)
        for spot in range(count):
            gate_outs[spot][...] = grad_gate[:, spot * rows : (spot + 1) * rows]
            up_outs[spot][...] = grad_upper[:, spot * rows : (spot + 1) * rows]
        acc[...] += dot(grad_gate, gate_ref[...], 0, 0) + dot(grad_upper, up_ref[...], 0, 0)

        @pl.when(step == steps - 1)
        def _():
            for spot in range(count):
                part_outs[spot][...] = acc[spot * rows : (spot + 1) * rows, :].astype(jnp.bfloat16)

    weight = pl.BlockSpec((tile, model), lambda i: (i, 0))
    flat = pl.BlockSpec((tile, rows), lambda i: (i, 0))
    whole = pl.BlockSpec((rows, model), lambda i: (0, 0))
    kept = jax.ShapeDtypeStruct((units, rows), jnp.bfloat16)
    outs = pl.pallas_call(
        kernel,
        grid=(steps,),
        out_shape=[kept] * (2 * count) + [jax.ShapeDtypeStruct((rows, model), jnp.bfloat16)] * count,
        in_specs=[whole] * count + [weight] * 3 + [flat] * (2 * count),
        out_specs=[flat] * (2 * count) + [whole] * count,
        scratch_shapes=[
            pltpu.VMEM((count * rows, model), jnp.bfloat16),
            pltpu.VMEM((count * rows, model), jnp.float32),
        ],
        compiler_params=params(),
        name="ffn_backward",
    )(*grads, gate_weight, up_weight, down_weight, *slopes, *acts)
    return outs[:count], outs[count : 2 * count], outs[2 * count :]


def norm_pull(value, gain, grad):
    scale = lax.rsqrt(jnp.mean(value * value, axis=-1, keepdims=True) + EPS)
    unit = value * scale
    inner = grad * gain
    return scale * (inner - unit * jnp.mean(inner * unit, axis=-1, keepdims=True)), grad * unit


def resid_backward(parts, resid, attended, out_grad, gain_ffn, gain_attn, w_out):
    count = len(parts)
    rows, model = resid.shape
    tile = min(rows, 128)

    def kernel(*refs):
        part_refs, refs = refs[:count], refs[count:]
        resid_ref, attended_ref, out_ref, ffn_ref, attn_ref, weight_ref, refs = *refs[:6], refs[6:]
        grad_resid_ref, grad_attended_ref, grad_mixed_ref, ffn_grad_ref, attn_grad_ref = refs
        grad = sum(ref[...].astype(jnp.float32) for ref in part_refs)
        pulled, ffn_rows = norm_pull(resid_ref[...], ffn_ref[...].astype(jnp.float32), grad)
        grad_resid = out_ref[...].astype(jnp.float32) + pulled
        grad_resid_ref[...] = grad_resid
        pulled, attn_rows = norm_pull(attended_ref[...], attn_ref[...].astype(jnp.float32), grad_resid)
        grad_attended = pulled.astype(jnp.bfloat16)
        grad_attended_ref[...] = grad_attended
        grad_mixed_ref[...] = dot(grad_attended, weight_ref[...], 1, 0).astype(jnp.bfloat16)
        ffn_grad = jnp.sum(ffn_rows, axis=0, keepdims=True)
        attn_grad = jnp.sum(attn_rows, axis=0, keepdims=True)

        @pl.when(pl.program_id(0) == 0)
        def _():
            ffn_grad_ref[...] = ffn_grad
            attn_grad_ref[...] = attn_grad

        @pl.when(pl.program_id(0) > 0)
        def _():
            ffn_grad_ref[...] += ffn_grad
            attn_grad_ref[...] += attn_grad

    block = pl.BlockSpec((tile, model), lambda i: (i, 0))
    vector = pl.BlockSpec((1, model), lambda i: (0, 0))
    inner = w_out.shape[1]
    return pl.pallas_call(
        kernel,
        grid=(rows // tile,),
        in_specs=[block] * (count + 3) + [vector] * 2 + [pl.BlockSpec(w_out.shape, lambda i: (0, 0))],
        out_specs=[block, block, pl.BlockSpec((tile, inner), lambda i: (i, 0)), vector, vector],
        out_shape=[
            jax.ShapeDtypeStruct((rows, model), jnp.float32),
            jax.ShapeDtypeStruct((rows, model), jnp.bfloat16),
            jax.ShapeDtypeStruct((rows, inner), jnp.bfloat16),
            jax.ShapeDtypeStruct((1, model), jnp.float32),
            jax.ShapeDtypeStruct((1, model), jnp.float32),
        ],
        compiler_params=params(32),
        name="resid_backward",
    )(*parts, resid, attended, out_grad, gain_ffn[None, :], gain_attn[None, :], w_out)


def input_backward(
    own_pair, backs, qkv, cosine, sine, gain_key, normed_in, grad_query, w_qkv, hidden_in, gain_in, grad_resid,
    grad_attended, mixed, gain_grads, group,
):
    rows, model = hidden_in.shape
    size = own_pair.shape[1] // 2
    inner = grad_query.shape[1]
    own_rows = model // group
    half = inner + size
    hops = len(backs)
    count = len(gain_grads)

    def kernel(core_ref, *refs):
        pair_ref, refs = refs[0], refs[1:]
        back_refs, refs = refs[:hops], refs[hops:]
        (
            raw_ref, cos_ref, sin_ref, key_gain_ref, normed_ref, query_ref, weight_ref, x_ref, gain_ref, resid_ref,
            attended_ref, mixed_ref, refs,
        ) = *refs[:12], refs[12:]
        gain_refs, refs = refs[:count], refs[count:]
        other_ref, mine_ref, grad_in_ref, rows_ref = refs
        pair = pair_ref[...] + sum(ref[...].astype(jnp.float32) for ref in back_refs)
        first = pair[:, : size // 2]
        second = pair[:, size // 2 : size]
        turned = jnp.concatenate(
            [
                first * cos_ref[...] + second * sin_ref[...],
                second * cos_ref[...] - first * sin_ref[...],
            ],
            axis=-1,
        )
        pulled, key_rows = norm_pull(raw_ref[...], key_gain_ref[...].astype(jnp.float32), turned)
        grad_key = pulled.astype(jnp.bfloat16)
        grad_value = pair[:, size:].astype(jnp.bfloat16)
        grad_normed = (
            dot(query_ref[...], weight_ref[:, :inner], 1, 1)
            + dot(grad_key, weight_ref[:, inner:half], 1, 1)
            + dot(grad_value, weight_ref[:, half:], 1, 1)
        )
        pulled, in_rows = norm_pull(
            x_ref[...].astype(jnp.float32), gain_ref[...].astype(jnp.float32), grad_normed
        )
        grad_in_ref[...] = resid_ref[...] + pulled
        rows_ref[...] = jnp.zeros_like(rows_ref)
        rows_ref[0:1, :model] = jnp.sum(in_rows, axis=0, keepdims=True)
        rows_ref[1:2, :size] = jnp.sum(key_rows, axis=0, keepdims=True)
        for spot in range(count):
            rows_ref[2 + spot : 3 + spot, : gain_refs[spot].shape[1]] = gain_refs[spot][...].astype(
                jnp.float32
            )
        gains = rows_ref[...].astype(jnp.bfloat16)

        def write(ref, side):
            pieces = (
                [(normed_ref, query_ref[...], 0, inner), (normed_ref, grad_key, inner, half)]
                if side == 0
                else [(normed_ref, grad_value, 0, size), (attended_ref, mixed_ref[...], size, half)]
            )
            for left, right, begin, end in pieces:
                value = dot(left[...], right, 0, 0).astype(jnp.bfloat16)
                for owner in range(group):
                    ref[owner, :own_rows, begin:end] = value[owner * own_rows : (owner + 1) * own_rows]
            for owner in range(group):
                ref[owner, own_rows:, :] = gains

        for core in range(2):

            @pl.when(core_ref[0] == core)
            def _():
                write(other_ref, 1 - core)
                write(mine_ref, core)

    def whole(array):
        return pl.BlockSpec(array.shape, lambda i, core_ref: (0,) * len(array.shape))

    arrays = [
        own_pair, *backs, qkv, cosine, sine, gain_key[None, :], normed_in, grad_query, w_qkv, hidden_in,
        gain_in[None, :], grad_resid, grad_attended, mixed, *gain_grads,
    ]
    in_specs = [whole(array) for array in arrays]
    in_specs[1 + hops] = pl.BlockSpec((rows, size), lambda i, core_ref: (0, inner // size))
    shape = jax.ShapeDtypeStruct((group, own_rows + 16, half), jnp.bfloat16)
    grad_in = jax.ShapeDtypeStruct((rows, model), jnp.float32)
    return pl.pallas_call(
        kernel,
        grid_spec=pltpu.PrefetchScalarGridSpec(
            num_scalar_prefetch=1,
            grid=(1,),
            in_specs=in_specs,
            out_specs=[whole(shape), whole(shape), whole(grad_in)],
            scratch_shapes=[pltpu.VMEM((16, half), jnp.float32)],
        ),
        out_shape=[shape, shape, grad_in],
        compiler_params=params(),
        name="input_backward",
    )(scalar(lax.axis_index("replica") % 2), *arrays)


def owner_parts(other, mine):
    group, height, wide = mine.shape
    far = swapped(other, "replica", 1)

    def kernel(rank_ref, mine_ref, far_ref, *outs):
        total = mine_ref[...].astype(jnp.float32) + far_ref[...].astype(jnp.float32)
        for mask in range(group):

            @pl.when(pl.program_id(0) == mask)
            def _():
                outs[mask][...] = total.astype(jnp.bfloat16)

    block = pl.BlockSpec((None, height, wide), lambda i, rank_ref: (rank_ref[0] ^ i, 0, 0))
    parts = pl.pallas_call(
        kernel,
        grid_spec=pltpu.PrefetchScalarGridSpec(
            num_scalar_prefetch=1,
            grid=(group,),
            in_specs=[block, block],
            out_specs=[pl.BlockSpec((height, wide), lambda i, rank_ref: (0, 0))] * group,
        ),
        out_shape=[jax.ShapeDtypeStruct((height, wide), jnp.bfloat16)] * group,
        compiler_params=params(16),
        name="owner_parts",
    )(scalar(lax.axis_index("fsdp")), mine, far)
    return [parts[0]] + [swapped(parts[mask], "fsdp", mask) for mask in range(1, group)]


def chunks_of(units):
    return 2 if units % 64 == 0 else 1


def weight_grad(sets, rights):
    group = len(rights)
    count = len(sets)
    units, rows = sets[0][0].shape
    model = rights[0].shape[1]
    chunks = chunks_of(units)
    tile = units // (2 * chunks)

    def kernel(core_ref, *refs):
        right_refs, left_refs = refs[:group], refs[group:-4]
        other_ref, mine_ref, left_ref, right_ref = refs[-4:]

        @pl.when((pl.program_id(0) == 0) & (pl.program_id(1) == 0))
        def _():
            for spot in range(group):
                right_ref[spot * rows : (spot + 1) * rows, :] = right_refs[spot][...]

        for index in range(count):

            @pl.when(pl.program_id(1) == index)
            def _():
                for chunk in range(chunks):
                    for spot in range(group):
                        left_ref[
                            chunk * tile : (chunk + 1) * tile, spot * rows : (spot + 1) * rows
                        ] = left_refs[(index * chunks + chunk) * group + spot][...]

        value = dot(left_ref[...], right_ref[...], 1, 0).astype(jnp.bfloat16)

        @pl.when(pl.program_id(0) == 0)
        def _():
            for chunk in range(chunks):
                other_ref[chunk] = value[chunk * tile : (chunk + 1) * tile]

        @pl.when(pl.program_id(0) == 1)
        def _():
            for chunk in range(chunks):
                mine_ref[chunk] = value[chunk * tile : (chunk + 1) * tile]

    def left_spec(chunk):
        def index(side, spot, core_ref):
            return (2 * chunk + jnp.where(side == 0, 1 - core_ref[0], core_ref[0]), 0)

        return pl.BlockSpec((tile, rows), index)

    shape = jax.ShapeDtypeStruct((count * chunks, tile, model), jnp.bfloat16)
    block = (chunks, tile, model)
    return pl.pallas_call(
        kernel,
        grid_spec=pltpu.PrefetchScalarGridSpec(
            num_scalar_prefetch=1,
            grid=(2, count),
            in_specs=[pl.BlockSpec((rows, model), lambda side, spot, core_ref: (0, 0))] * group
            + [left_spec(chunk) for _ in range(count) for chunk in range(chunks) for _ in range(group)],
            out_specs=[
                pl.BlockSpec(
                    block, lambda side, spot, core_ref: (jnp.where(side == 0, spot, count - 1), 0, 0)
                ),
                pl.BlockSpec(block, lambda side, spot, core_ref: (jnp.where(side == 0, 0, spot), 0, 0)),
            ],
            scratch_shapes=[
                pltpu.VMEM((chunks * tile, group * rows), jnp.bfloat16),
                pltpu.VMEM((group * rows, model), jnp.bfloat16),
            ],
        ),
        out_shape=[shape, shape],
        compiler_params=params(),
        name="weight_grad",
    )(
        scalar(lax.axis_index("replica") % 2),
        *rights,
        *[left for lefts in sets for _ in range(chunks) for left in lefts],
    )


def allowed_mask(query_segs_ref, key_segs_ref, rows, width):
    gap = (
        width
        - rows
        + lax.broadcasted_iota(jnp.int32, (rows, width), 0)
        - lax.broadcasted_iota(jnp.int32, (rows, width), 1)
    )
    return (gap >= 0) & (gap < WINDOW) & (query_segs_ref[...] == key_segs_ref[...])


def head_probs(query, keys, allowed, scale):
    scores = jnp.where(allowed, dot(query, keys, 1, 1) * scale, NEG)
    expo = jnp.exp(scores - jnp.max(scores, axis=-1, keepdims=True))
    return expo / jnp.sum(expo, axis=-1, keepdims=True)


def attention_specs(rows, size, width, heads):
    head = pl.BlockSpec((rows, size), lambda h: (0, h))
    whole = lambda *shape: pl.BlockSpec(shape, lambda h: (0, 0))
    common = [
        head,
        whole(1, size),
        whole(rows, size // 2),
        whole(rows, size // 2),
        whole(width, 2 * size),
        whole(rows, 1),
        whole(1, width),
    ]
    return head, whole, common


def attention_forward(qkv, gain, cosine, sine, pairs, query_segs, key_segs, heads):
    rows, width, size = qkv.shape[0], pairs.shape[0], pairs.shape[1] // 2
    head, _, common = attention_specs(rows, size, width, heads)

    def kernel(raw_ref, gain_ref, cos_ref, sin_ref, pairs_ref, qseg_ref, kseg_ref, query_ref, mixed_ref):
        query = head_post(raw_ref[...], gain_ref[...], cos_ref[...], sin_ref[...]).astype(jnp.bfloat16)
        query_ref[...] = query
        allowed = allowed_mask(qseg_ref, kseg_ref, rows, width)
        probs = head_probs(query, pairs_ref[:, :size], allowed, size**-0.5).astype(jnp.bfloat16)
        mixed_ref[...] = dot(probs, pairs_ref[:, size:], 1, 0).astype(jnp.bfloat16)

    shape = jax.ShapeDtypeStruct((rows, heads * size), jnp.bfloat16)
    return pl.pallas_call(
        kernel,
        grid=(heads,),
        in_specs=common,
        out_specs=[head, head],
        out_shape=[shape, shape],
        compiler_params=params(32),
        name="attention_forward",
    )(qkv, gain, cosine, sine, pairs, query_segs, key_segs)


def attention_backward(qkv, gain, cosine, sine, pairs, query_segs, key_segs, query, grad_mixed, heads):
    rows, width, size = qkv.shape[0], pairs.shape[0], pairs.shape[1] // 2
    head, whole, common = attention_specs(rows, size, width, heads)
    before = width - rows

    def kernel(
        raw_ref, gain_ref, cos_ref, sin_ref, pairs_ref, qseg_ref, kseg_ref, query_ref, grad_ref,
        raw_grad_ref, gain_grad_ref, far_ref, own_ref, acc,
    ):
        step = pl.program_id(0)
        query = query_ref[...]
        grad = grad_ref[...]
        allowed = allowed_mask(qseg_ref, kseg_ref, rows, width)
        keys = pairs_ref[:, :size]
        probs = head_probs(query, keys, allowed, size**-0.5)
        grad_probs = dot(grad, pairs_ref[:, size:], 1, 1)
        delta = jnp.sum(grad_probs * probs, axis=-1, keepdims=True)
        grad_scores = (probs * (grad_probs - delta)).astype(jnp.bfloat16)
        grad_query = dot(grad_scores, keys, 1, 0) * size**-0.5
        grad_keys = dot(grad_scores, query, 0, 0) * size**-0.5
        grad_values = dot(probs.astype(jnp.bfloat16), grad, 0, 0)

        @pl.when(step == 0)
        def _():
            acc[:, :size] = grad_keys
            acc[:, size:] = grad_values

        @pl.when(step > 0)
        def _():
            acc[:, :size] += grad_keys
            acc[:, size:] += grad_values

        first = grad_query[:, : size // 2]
        second = grad_query[:, size // 2 :]
        cosine_part, sine_part = cos_ref[...], sin_ref[...]
        turned = jnp.concatenate(
            [
                first * cosine_part + second * sine_part,
                second * cosine_part - first * sine_part,
            ],
            axis=-1,
        )
        raw = raw_ref[...]
        scale = lax.rsqrt(jnp.mean(raw * raw, axis=-1, keepdims=True) + EPS)
        unit = raw * scale
        inner = turned * gain_ref[...].astype(jnp.float32)
        raw_grad = scale * (inner - unit * jnp.mean(inner * unit, axis=-1, keepdims=True))
        raw_grad_ref[...] = raw_grad.astype(jnp.bfloat16)
        gain_grad = jnp.sum(turned * unit, axis=0, keepdims=True)

        @pl.when(step == 0)
        def _():
            gain_grad_ref[...] = gain_grad

        @pl.when(step > 0)
        def _():
            gain_grad_ref[...] += gain_grad

        @pl.when(step == heads - 1)
        def _():
            far_ref[...] = acc[:before, :].astype(jnp.bfloat16)
            own_ref[...] = acc[before:, :]

    return pl.pallas_call(
        kernel,
        grid=(heads,),
        in_specs=common + [head, head],
        out_specs=[head, whole(1, size), whole(before, 2 * size), whole(rows, 2 * size)],
        out_shape=[
            jax.ShapeDtypeStruct((rows, heads * size), jnp.bfloat16),
            jax.ShapeDtypeStruct((1, size), jnp.float32),
            jax.ShapeDtypeStruct((before, 2 * size), jnp.bfloat16),
            jax.ShapeDtypeStruct((rows, 2 * size), jnp.float32),
        ],
        scratch_shapes=[pltpu.VMEM((width, 2 * size), jnp.float32)],
        compiler_params=params(32),
        name="attention_backward",
    )(qkv, gain, cosine, sine, pairs, query_segs, key_segs, query, grad_mixed)


def line_edges():
    places = lax.axis_size("replica") // 2
    outer = places // 2 - 1
    return places, outer


def exchanged(block, pairs):
    route = [(2 * a + core, 2 * b + core) for a, b in pairs for core in range(2)]
    return lax.ppermute(block, "replica", route)


class Line:
    def __init__(self):
        self.places, self.outer = line_edges()
        self.steps = 2 * self.outer + 1
        self.moving = []
        self.done = {}

    def advance(self, fresh, gate=None):
        places, outer, steps = self.places, self.outer, self.steps
        place = (lax.axis_index("replica") // 2).astype(jnp.int32).reshape(1)
        operands, plan = [], []

        def operand(entry):
            array, index = entry if isinstance(entry, tuple) else (entry, None)
            for spot, (known, known_index) in enumerate(operands):
                if known is array and known_index == index:
                    return spot
            operands.append((array, index))
            return len(operands) - 1

        for name, block, step, far in self.moving:
            plan.append((name, step + 1, [operand(block), operand(far)], step))
        for name, terms in fresh:
            plan.append((name, 0, [operand(term) for term in terms], None))
        if not plan:
            return gate
        sizes = [operands[spots[0]][0].shape[-2:] for _, _, spots, _ in plan]
        by_step = {step: index for index, (_, step, _, _) in enumerate(plan)}
        pairs = []
        for edge in range(outer):
            inward, outward = by_step.get(edge), by_step.get(2 * outer - edge)
            if inward is not None and outward is not None and sizes[inward] == sizes[outward]:
                pairs.append((edge, inward, outward))
        cuts = 3 if all(size[0] % 48 == 0 for size in sizes) else 1

        def kernel(place_ref, *refs):
            here = place_ref[0]
            inputs = refs[: len(operands)]
            if gate is not None:
                refs = refs[: len(operands)] + refs[len(operands) + 1 :]
            outputs = refs[len(operands) :]
            states = []
            for spot, (_, _, terms, last) in enumerate(plan):
                value = inputs[terms[0]][...]
                if len(terms) > 1:
                    far = inputs[terms[1]][...]
                    total = value.astype(jnp.float32)
                    for term in terms[1:]:
                        total = total + inputs[term][...].astype(jnp.float32)
                    total = total.astype(jnp.bfloat16)
                    if last is None:
                        value = total
                    elif last <= outer:
                        edge = last
                        value = jnp.where((here == edge + 1) | (here == places - 2 - edge), total, value)
                    else:
                        edge = 2 * outer - last
                        value = jnp.where((here == edge) | (here == places - 1 - edge), far, value)
                states.append(value)
                outputs[spot][...] = value
            for spot, (edge, inward, outward) in enumerate(pairs):
                outputs[len(plan) + spot][...] = jnp.where(
                    (here == edge) | (here == places - 1 - edge), states[inward], states[outward]
                )

        def spec(size, index):
            if index is None:
                return pl.BlockSpec((size[0] // cuts, size[1]), lambda i, place_ref: (i, 0))
            return pl.BlockSpec((None, size[0] // cuts, size[1]), lambda i, place_ref: (index, i, 0))

        in_specs = [spec(array.shape[-2:], index) for array, index in operands]
        arrays = [array for array, _ in operands]
        out_sizes = sizes + [sizes[inward] for _, inward, _ in pairs]
        out_specs = [spec(size, None) for size in out_sizes]
        out_shape = [jax.ShapeDtypeStruct(size, jnp.bfloat16) for size in out_sizes]
        aliases = {}
        if gate is not None:
            aliases = {1 + len(arrays): len(out_shape)}
            in_specs.append(pl.BlockSpec(memory_space=pl.ANY))
            out_specs.append(pl.BlockSpec(memory_space=pl.ANY))
            out_shape.append(jax.ShapeDtypeStruct(gate.shape, gate.dtype))
            arrays.append(gate)
        outs = pl.pallas_call(
            kernel,
            grid_spec=pltpu.PrefetchScalarGridSpec(
                num_scalar_prefetch=1, grid=(cuts,), in_specs=in_specs, out_specs=out_specs
            ),
            out_shape=out_shape,
            input_output_aliases=aliases,
            compiler_params=params(32),
            name="line_step",
        )(place, *arrays)
        received = {}
        for spot, (edge, inward, outward) in enumerate(pairs):
            ends = [(edge, edge + 1), (places - 1 - edge, places - 2 - edge)]
            far = exchanged(outs[len(plan) + spot], ends + [(b, a) for a, b in ends])
            received[inward] = received[outward] = far
        self.moving = []
        for index, (name, step, _, _) in enumerate(plan):
            block = outs[index]
            if step == steps:
                self.done[name] = block
                continue
            if index not in received:
                edge = step if step <= outer else 2 * outer - step
                route = [(edge, edge + 1), (places - 1 - edge, places - 2 - edge)]
                if step > outer:
                    route = [(b, a) for a, b in route]
                received[index] = exchanged(block, route)
            self.moving.append((name, block, step, received[index]))
        return outs[-1]

    def arrived(self):
        return [far for _, _, _, far in self.moving]

    def finished(self, name):
        while name not in self.done:
            self.advance([])
        return self.done[name]


def line_names(name, units):
    return [(name, chunk) for chunk in range(chunks_of(units))]


def whole_grad(line, name, units, dtype=jnp.float32):
    names = line_names(name, units)
    mines = [line.finished(chunk) for chunk in names]
    others = [swapped(mine, "replica", 1) for mine in mines]
    chunks = len(mines)
    tile, model = mines[0].shape
    core = (lax.axis_index("replica") % 2).astype(jnp.int32).reshape(1)

    def kernel(core_ref, *refs):
        out_ref = refs[-1]
        for chunk in range(chunks):
            for side in range(2):

                @pl.when((pl.program_id(0) == chunk) & (pl.program_id(1) == side))
                def _():
                    @pl.when(core_ref[0] == side)
                    def _():
                        out_ref[...] = refs[chunk][...].astype(dtype)

                    @pl.when(core_ref[0] != side)
                    def _():
                        out_ref[...] = refs[chunks + chunk][...].astype(dtype)

    return pl.pallas_call(
        kernel,
        grid_spec=pltpu.PrefetchScalarGridSpec(
            num_scalar_prefetch=1,
            grid=(chunks, 2),
            in_specs=[pl.BlockSpec((tile, model), lambda chunk, side, core_ref: (0, 0))] * (2 * chunks),
            out_specs=pl.BlockSpec((tile, model), lambda chunk, side, core_ref: (2 * chunk + side, 0)),
        ),
        out_shape=jax.ShapeDtypeStruct((units, model), dtype),
        compiler_params=params(24),
        name="whole_grad",
    )(core, *mines, *others)


def joined(mine, other, axis):
    core = lax.axis_index("replica") % 2
    return jnp.where(
        core == 0,
        jnp.concatenate([mine, other], axis=axis),
        jnp.concatenate([other, mine], axis=axis),
    )


def core_join(block, axis):
    return joined(block, swapped(block, "replica", 1), axis)


def fetched(block):
    got = [swapped(block, "fsdp", mask) for mask in range(1, lax.axis_size("fsdp"))]
    return got, [swapped(part, "replica", 1) for part in got]


def gathered(block):
    group = lax.axis_size("fsdp")
    blocks, near = [block] + [None] * (group - 1), []
    for ring in range(1, group.bit_length()):
        masks = [mask for mask in range(1, group) if bin(mask).count("1") == ring]
        source = after(block, *near) if near else block
        near = [swapped(source, "fsdp", mask) for mask in masks]
        for mask, far in zip(masks, near):
            blocks[mask] = far
    return blocks


def passed_along(block, axis, distance):
    devices = range(lax.axis_size(axis))
    route = [(i - distance, i) for i in devices if i - distance in devices]
    return lax.ppermute(block, axis, route)


def contract(left, right, left_dim, right_dim):
    return lax.dot_general(
        left, right, (((left_dim,), (right_dim,)), ((), ())), preferred_element_type=jnp.float32
    )


def normed(value, gain):
    return value * lax.rsqrt(jnp.mean(value * value, axis=-1, keepdims=True) + EPS) * gain


def norm_back(value, gain, grad):
    _, pull = jax.vjp(normed, value, gain)
    return pull(grad)


def tables(places, half):
    freq = 10000.0 ** (-(2.0 * jnp.arange(half, dtype=jnp.float32)) / (2 * half))
    angle = places.astype(jnp.float32)[:, None] * freq[None, :]
    return (jnp.cos(angle), jnp.sin(angle))


def rotate(value, cosine, sine):
    half = value.shape[-1] // 2
    first = value[..., :half]
    second = value[..., half:]
    return jnp.concatenate(
        [first * cosine - second * sine, second * cosine + first * sine], axis=-1
    )


def head_post(raw, gain, cosine, sine):
    return rotate(normed(raw, gain), cosine, sine)


def per_device(
    hidden_in,
    out_grad,
    segments,
    positions,
    norm_in,
    query_weight,
    key_weight,
    value_weight,
    out_weight,
    norm_attn,
    norm_ffn,
    gate_weight,
    up_weight,
    down_weight,
    norm_out,
    query_gain,
    key_gain,
):
    rows = hidden_in.shape[0]
    rank = lax.axis_index("fsdp")
    group = lax.axis_size("fsdp")
    masks = range(1, group)
    head_size = key_weight.shape[1]
    heads = query_weight.shape[1] // head_size
    model = hidden_in.shape[1]
    own_model = norm_in.shape[0]
    own_head = query_gain.shape[0]
    hops = (WINDOW - 1) // rows + 1
    scale = head_size ** (-0.5)
    qkv_weights = (query_weight, key_weight, value_weight)
    wide = sum(weight.shape[1] for weight in qkv_weights)
    qkv_block = packed(qkv_weights)
    got, peers = fetched(qkv_block)
    gains = jnp.stack(
        [
            jnp.pad(gain, (0, own_model - gain.shape[0]))
            for gain in (norm_in, norm_attn, norm_ffn, norm_out, query_gain, key_gain)
        ]
    )
    gains = after(gains, *[got[mask - 1] for mask in masks if bin(mask).count("1") == 1])
    gain_stack = jnp.stack([gains] + [swapped(gains, "fsdp", mask) for mask in masks])
    w_qkv = unpacked(qkv_weights, got, peers)
    gain_rows = jnp.stack(
        [lax.dynamic_index_in_dim(gain_stack, rank ^ i, 0, keepdims=False) for i in range(group)], axis=1
    )
    gain_in, gain_attn, gain_ffn, gain_out = (gain_rows[i].reshape(-1) for i in range(4))
    gain_query, gain_key = (gain_rows[i, :, :own_head].reshape(-1) for i in (4, 5))
    residual_in = hidden_in.astype(jnp.float32)
    normed_in = normed(residual_in, gain_in).astype(jnp.bfloat16)
    qkv = jnp.dot(normed_in, w_qkv, preferred_element_type=jnp.float32)
    key_raw = qkv[:, heads * head_size : (heads + 1) * head_size]
    value_new = qkv[:, (heads + 1) * head_size :].astype(jnp.bfloat16)
    cosine, sine = tables(positions, head_size // 2)
    key_new = head_post(key_raw, gain_key, cosine, sine).astype(jnp.bfloat16)
    pair_new = jnp.concatenate([key_new, value_new], axis=1)
    got, peers = fetched(after(packed([out_weight]), pair_new))
    w_out = unpacked([out_weight], got, peers)
    parts = [pair_new]
    for step in range(1, hops + 1):
        parts.insert(0, passed_along(pair_new, "fsdp", step))
    pairs = jnp.concatenate(parts, axis=0)
    width = pairs.shape[0]
    seg_padded = jnp.concatenate([jnp.full((hops * rows,), -1, jnp.int32), segments], axis=0)
    key_segs = lax.dynamic_slice_in_dim(seg_padded, rank * rows, width, 0)
    query_segs = lax.dynamic_slice_in_dim(segments, rank * rows, rows, 0)
    attention_args = (
        qkv,
        gain_query[None, :],
        cosine,
        sine,
        pairs,
        query_segs[:, None],
        key_segs[None, :],
    )
    query_new, mixed = attention_forward(*attention_args, heads)
    attended = contract(mixed, w_out, 1, 1)
    resid = residual_in + normed(attended, gain_attn)
    ffn_in = normed(resid, gain_ffn).astype(jnp.bfloat16)
    ffn_blocks = gathered(ffn_in)
    hiddens, slopes, acts, parts = {}, {}, {}, {}
    rings = sorted(range(group), key=lambda mask: (bin(mask).count("1"), mask))
    last = None
    for mask in rings[1:] + [0]:
        if last is not None:
            ffn_blocks[mask] = after(ffn_blocks[mask], parts[last])
        hiddens[mask], slopes[mask], acts[mask], parts[mask] = ffn_forward(
            ffn_blocks[mask], gate_weight, up_weight, down_weight
        )
        last = mask
    branch = sum(
        (swapped(parts[mask], "fsdp", mask) if mask else parts[mask]).astype(jnp.float32)
        for mask in range(group)
    )
    result = resid + normed(branch, gain_out)
    hidden_out = result.astype(jnp.bfloat16)
    grad_result = out_grad.astype(jnp.float32)
    grad_branch, grad_gain_out = norm_back(branch, gain_out, grad_result)
    grad_branch_low = grad_branch.astype(jnp.bfloat16)
    pieces = gathered(grad_branch_low)
    units = gate_weight.shape[0]
    line = Line()

    def fresh(names, other, mine):
        far = swapped(other, "replica", 1)
        keys = [key for name in names for key in line_names(name, units)]
        return [(key, [(mine, spot), (far, spot)]) for spot, key in enumerate(keys)]

    grad_gates, grad_uppers, returned = {}, {}, {}
    final = rings[-1]
    last = None
    for mask in rings[:-1]:
        if last is not None:
            pieces[mask] = after(pieces[mask], part)
        grad_gates[mask], grad_uppers[mask], part = ffn_backward(
            pieces[mask], gate_weight, up_weight, down_weight, slopes[mask], acts[mask]
        )
        returned[mask] = swapped(part, "fsdp", mask) if mask else part
        last = mask
    pieces[final] = after(pieces[final], part)
    waiting = fresh(
        ["down"], *weight_grad([[hiddens[i] for i in range(group)]], [pieces[i] for i in range(group)])
    )
    pieces[final] = line.advance([waiting.pop(0)], pieces[final])
    gate_parts, upper_parts, parts = ffn_backward_blocks(
        [pieces[final]], gate_weight, up_weight, down_weight, [slopes[final]], [acts[final]]
    )
    grad_gates[final], grad_uppers[final] = gate_parts[0], upper_parts[0]
    returned[final] = swapped(parts[0], "fsdp", final)
    other, mine = weight_grad([[grad_gates[i] for i in range(group)]], ffn_blocks)
    other = after(other, *[returned[mask] for mask in rings[1:-1]])
    gate_chunks = fresh(["gate"], other, mine)
    grad_uppers[0] = line.advance(
        [waiting.pop(0)] if waiting else [], after(grad_uppers[0], other)
    )
    up_other, mine = weight_grad([[grad_uppers[i] for i in range(group)]], ffn_blocks)
    waiting = gate_chunks + fresh(["up"], up_other, mine)
    returned[0] = after(returned[0], up_other)

    def advance(gate=None):
        return line.advance([waiting.pop(0)] if waiting else [], gate)

    grad_resid, grad_attended_low, grad_mixed, grad_gain_ffn, grad_gain_attn = resid_backward(
        [returned[mask] for mask in range(group)], resid, attended, out_grad, gain_ffn, gain_attn, w_out
    )
    grad_mixed = advance(grad_mixed)
    grad_query_low, grad_gain_query, grad_far, grad_pair = attention_backward(
        *attention_args, query_new, grad_mixed, heads
    )
    backs = [
        passed_along(grad_far[(hops - step) * rows : (hops - step + 1) * rows], "fsdp", -step)
        for step in range(1, hops + 1)
    ]
    grad_pair = advance(after(grad_pair, *backs))
    other, mine, grad_in = input_backward(
        grad_pair,
        backs,
        qkv,
        cosine,
        sine,
        gain_key,
        normed_in,
        grad_query_low,
        w_qkv,
        hidden_in,
        gain_in,
        grad_resid,
        grad_attended_low,
        mixed,
        [grad_gain_attn, grad_gain_ffn, grad_gain_out[None, :], grad_gain_query],
        group,
    )
    other = advance(other)
    weight_parts = owner_parts(other, mine)
    near = [weight_parts[mask] for mask in masks if bin(mask).count("1") == 1]
    while waiting:
        weight_parts[0] = advance(after(weight_parts[0], *near))
    line.advance([("weights", weight_parts)])
    grad_down = whole_grad(line, "down", units)
    grad_down = line.advance([], grad_down)
    grad_gate_w = whole_grad(line, "gate", units)
    grad_gate_w = line.advance([], grad_gate_w)
    grad_up_w = whole_grad(line, "up", units)
    grad_up_w = line.advance([], grad_up_w)
    owned = core_join(line.finished("weights"), 1).astype(jnp.float32)
    inner = heads * head_size
    columns = [0, inner, inner + head_size, inner + 2 * head_size, wide + inner]
    owned_query, owned_key, owned_value, owned_out = (
        owned[:own_model, columns[i] : columns[i + 1]] for i in range(4)
    )

    def owned_gain(row, size):
        return lax.dynamic_slice_in_dim(owned[own_model + row], rank * size, size, 0)

    owned_gain_in, owned_gain_attn, owned_gain_ffn, owned_gain_out = (
        owned_gain(row, own_model) for row in (0, 2, 3, 4)
    )
    owned_gain_key, owned_gain_query = (owned_gain(row, own_head) for row in (1, 5))
    return (
        hidden_out,
        grad_in,
        owned_gain_in,
        owned_query,
        owned_key,
        owned_value,
        owned_out,
        owned_gain_attn,
        owned_gain_ffn,
        grad_gate_w,
        grad_up_w,
        grad_down,
        owned_gain_out,
        owned_gain_query,
        owned_gain_key,
    )


def solution(mesh):
    return jax.shard_map(
        per_device,
        mesh=mesh,
        in_specs=(
            P(("replica", "fsdp"), None),
            P(("replica", "fsdp"), None),
            P("replica"),
            P(("replica", "fsdp")),
            P("fsdp"),
            P("fsdp", None),
            P("fsdp", None),
            P("fsdp", None),
            P("fsdp", None),
            P("fsdp"),
            P("fsdp"),
            P("fsdp", None),
            P("fsdp", None),
            P("fsdp", None),
            P("fsdp"),
            P("fsdp"),
            P("fsdp"),
        ),
        out_specs=(
            P(("replica", "fsdp"), None),
            P(("replica", "fsdp"), None),
            P("fsdp"),
            P("fsdp", None),
            P("fsdp", None),
            P("fsdp", None),
            P("fsdp", None),
            P("fsdp"),
            P("fsdp"),
            P("fsdp", None),
            P("fsdp", None),
            P("fsdp", None),
            P("fsdp"),
            P("fsdp"),
            P("fsdp"),
        ),
        check_vma=False,
    )
```
